32 devices in a mesh: ctx: 8 (over z, core), exp: 4 (over y, x).
Axes of the slice: x: 2, y: 2, z: 4, core: 2. Of those that a mesh axis runs over, the one named last changes fastest.
Arguments:
- block_input: bfloat16 [4, 2048, 1280], P('exp', 'ctx'), may hold values from -6 to 6
- cotangent: bfloat16 [4, 2048, 1280], P('exp', 'ctx'), may hold values from -6 to 6
- routes: int32 [4, 2048, 7], P('exp', 'ctx'), may hold values from 0 to 15, all different within a row; in each aligned block of 256 rows (0 to 255, 256 to 511, ..., all dimensions but the last counted through in order) at most 168 rows name the same one
- attn_gain: bfloat16 [1280], P(('ctx', 'exp')), may hold values from 0.25 to 1.75
- query_key_value_weight: bfloat16 [1280, 3840], P(('ctx', 'exp')), may hold values from -0.15625 to 0.15625
- attention_output_weight: bfloat16 [1280, 1280], P(('ctx', 'exp')), may hold values from -2.5 to 2.5
- ffn_gain: bfloat16 [1280], P(('ctx', 'exp')), may hold values from 0.25 to 1.75
- routing_weight: bfloat16 [1280, 16], P(('ctx', 'exp')), may hold values from -0.078125 to 0.078125
- common_expert_gate_up_weight: bfloat16 [1280, 1792], P(('ctx', 'exp')), may hold values from -0.15625 to 0.15625
- common_expert_down_weight: bfloat16 [896, 1280], P(('ctx', 'exp')), may hold values from -0.25 to 0.25
- expert_gate_up: bfloat16 [16, 1280, 1792], P('exp', 'ctx'), may hold values from -0.15625 to 0.15625
- expert_down: bfloat16 [16, 896, 1280], P('exp', 'ctx'), may hold values from -0.75 to 0.75
Outputs:
- layer_out: bfloat16 [4, 2048, 1280], P('exp', 'ctx')
- input_grad: float32 [4, 2048, 1280], P('exp', 'ctx')
- attn_gain_grad: float32 [1280], P(('ctx', 'exp'))
- qkv_weight_grad: float32 [1280, 3840], P(('ctx', 'exp'))
- out_weight_grad: float32 [1280, 1280], P(('ctx', 'exp'))
- ffn_gain_grad: float32 [1280], P(('ctx', 'exp'))
- router_weight_grad: float32 [1280, 16], P(('ctx', 'exp'))
- shared_gate_up_grad: float32 [1280, 1792], P(('ctx', 'exp'))
- shared_down_grad: float32 [896, 1280], P(('ctx', 'exp'))
- expert_gate_up_grad: float32 [16, 1280, 1792], P('exp', 'ctx')
- expert_down_grad: float32 [16, 896, 1280], P('exp', 'ctx')
The draws below stay inside these ranges and needn't reach their ends.
Inputs may be any that keep to these rules, and one draw needn't show every extreme that they name: `routes`: the 7 experts of a token differ. Among the 256 rows of one device no expert is named by more than 168 rows, and in every draw some expert is named by exactly 168 rows of some device.
All inputs are finite; a program needn't handle non-finite values.
Results may differ from the reference program's by a relative error of at most 0.019.
Values may be sent and summed in bfloat16 or wider, within the bound.
No kernel may reach another device: no remote copies, remote signals or barrier semaphores. Data moves between devices by JAX's collectives and lax.ppermute only.
A program may use at most 320 MiB of HBM per device.

```python
import math
import jax
import jax.numpy as jnp
import numpy as np
from jax import lax

D = 1280
HEADS = 10
HEAD_DIM = 128
FF = 896
TOP = 7
TOK_DEV = 256
SEQS = 4
LENGTH = 2048
EXPERTS = 16
CAP = 168
N_CTX = 8


def steps_of(key, extent, pieces, low, largest):
    level = 1.0
    for position, blocks in pieces:
        steps = jax.random.uniform(jax.random.fold_in(jax.random.fold_in(key, 6), position), (blocks,), jnp.float32, low / len(pieces), largest / len(pieces))
        level = level * jnp.repeat(jnp.exp(steps), extent[position] // blocks).reshape((-1,) + (1,) * (len(extent) - 1 - position))
    return level


def routed_block(stream_key, own, number, rows, count, top, most, skew):
    sequence = jax.random.permutation(stream_key, count)
    packed, usual = shares(count, rows * top, most, skew, True), shares(count, rows * top, most, skew, False)
    places = jnp.arange(count)

    def named(sizes, rotation):
        used = int((sizes > 0).sum())
        fixed = max(1, used // 4)
        passed = fixed + (places - fixed + rotation * (used - fixed)) % max(1, count - fixed)
        return jnp.zeros((count,), jnp.int32).at[sequence[jnp.where(places < fixed, places, passed)]].set(jnp.asarray(sizes, jnp.int32))

    sizes = jnp.where(number % 4 == 0, named(packed, number // 4), named(usual, number - number // 4 - 1))
    mixed = jax.random.permutation(jax.random.fold_in(own, 3), count)
    donor, receiver = mixed[0:count // 2 * 2:2], mixed[1:count // 2 * 2:2]
    room = jnp.minimum(sizes[donor] - 1, most - sizes[receiver]) // 2
    room = jnp.where((donor == sequence[0]) | (receiver == sequence[0]) | (sizes[receiver] == 0), 0, jnp.maximum(room, 0))
    passed = jax.random.randint(jax.random.fold_in(own, 4), (count // 2,), 0, 1 << 20) % (room + 1)
    sizes = sizes.at[donor].add(-passed).at[receiver].add(passed)
    labels = jnp.searchsorted(jnp.cumsum(sizes), jnp.arange(rows * top), side="right").astype(jnp.int32)
    listing = labels.reshape(top, rows).T
    listing = listing[jax.random.permutation(jax.random.fold_in(own, 1), rows)]
    rotation = jax.random.randint(jax.random.fold_in(own, 2), (rows, 1), 0, top)
    return jnp.take_along_axis(listing, (jnp.arange(top)[None, :] + rotation) % top, axis=1)


def shares(number_of, total, limit, lean, full):
    loads = [(1 << 20) // math.isqrt(grade ** lean) + 1 for grade in range(1, number_of + 1)]
    largest = limit if full else min(limit, max(-(-total // number_of), total * loads[0] // sum(loads)))
    least = 1 if total - largest >= number_of - 1 else 0
    holding, surplus = [largest] + [least] * (number_of - 1), total - largest - least * (number_of - 1)
    while surplus > 0:
        movable = [i for i in range(1, number_of) if holding[i] < largest] or [i for i in range(1, number_of) if holding[i] < limit]
        pool, budget = sum([loads[i] for i in movable]), surplus
        for i in movable:
            more = min(limit - holding[i], max(1, budget * loads[i] // pool), surplus)
            holding[i] = holding[i] + more
            surplus = surplus - more
    return np.array(holding)


def centred(stream_key, dims, spread, limit, split=(), kind=jnp.bfloat16):
    array = spread * jax.random.normal(stream_key, dims, jnp.float32)
    if split:
        array = array * steps_of(stream_key, dims, split, -0.22, 0.18)
    return jnp.clip(array, -limit, limit).astype(kind)


def setup_inputs(seed: int = 0) -> dict:
    splits = jax.random.split(jax.random.key(seed), 13)
    block_input = centred(splits[0], (SEQS, LENGTH, D), 1.0, 6.0, ((0, 4), (1, 8)))
    cotangent = centred(splits[1], (SEQS, LENGTH, D), 1.0, 6.0, ((0, 4), (1, 8)))
    routes_keys = jax.random.split(jax.random.fold_in(splits[2], 1), SEQS * LENGTH // TOK_DEV)
    routes_turns = jax.random.permutation(jax.random.fold_in(splits[2], 3), SEQS * LENGTH // TOK_DEV)
    routes = jax.vmap(lambda own, number: routed_block(jax.random.fold_in(splits[2], 2), own, number, TOK_DEV, EXPERTS, TOP, CAP, 1))(routes_keys, routes_turns).reshape((SEQS, LENGTH, TOP))
    attn_gain = jnp.clip(1.0 + 0.15 * jax.random.normal(splits[3], (D,), jnp.float32), 0.25, 1.75).astype(jnp.bfloat16)
    query_key_value_weight = centred(splits[4], (D, 3 * D), D ** -0.5, 0.15625, ((0, 32),))
    attention_output_weight = centred(splits[5], (D, D), (max(D // 256, 1)) ** -0.5, 2.5, ((0, 32),))
    ffn_gain = jnp.clip(1.0 + 0.15 * jax.random.normal(splits[6], (D,), jnp.float32), 0.25, 1.75).astype(jnp.bfloat16)
    routing_weight = centred(splits[7], (D, EXPERTS), (4 * D) ** -0.5, 0.078125, ((0, 32),))
    common_expert_gate_up_weight = centred(splits[8], (D, 2 * FF), D ** -0.5, 0.15625, ((0, 32),))
    common_expert_down_weight = centred(splits[9], (FF, D), (FF // 2) ** -0.5, 0.25, ((0, 32),))
    expert_gate_up = centred(splits[10], (EXPERTS, D, 2 * FF), D ** -0.5, 0.15625, ((0, 4), (1, 8)))
    expert_down = centred(splits[11], (EXPERTS, FF, D), (FF // 16) ** -0.5, 0.75, ((0, 4), (1, 8)))
    return dict(block_input=block_input, cotangent=cotangent, routes=routes, attn_gain=attn_gain, query_key_value_weight=query_key_value_weight, attention_output_weight=attention_output_weight, ffn_gain=ffn_gain, routing_weight=routing_weight, common_expert_gate_up_weight=common_expert_gate_up_weight, common_expert_down_weight=common_expert_down_weight, expert_gate_up=expert_gate_up, expert_down=expert_down)


norm_eps = 1e-06
rope_base = 10000.0
masked_value = -1000000000.0
highest_matmul_precision = lax.Precision.HIGHEST

@jax.custom_vjp
def low(v):
    return lax.optimization_barrier(v.astype(jnp.bfloat16)).astype(jnp.float32)

@jax.custom_vjp
def reduced_precision_back(v):
    return v

def low_keep(v):
    return (low(v), None)

def low_pass(kept, grad):
    return (grad,)

def back_keep(v):
    return (v, None)

def back_low(kept, grad):
    return (low(grad),)
low.defvjp(low_keep, low_pass)
reduced_precision_back.defvjp(back_keep, back_low)

def dealt_positions(row_index, tok_dev, n_ctx):
    halfway = tok_dev // 2
    device = row_index // tok_dev
    within = row_index % tok_dev
    early_pos = device * halfway + within
    late_pos = (2 * n_ctx - 1 - device) * halfway + within - halfway
    return jnp.where(within < halfway, early_pos, late_pos).astype(jnp.int32)

def rope_tables(positions, head_dim):
    halfway = head_dim // 2
    frequency = rope_base ** (-(jnp.arange(halfway).astype(jnp.float32) * 2.0 / head_dim))
    angles = positions.astype(jnp.float32)[:, None] * frequency[None, :]
    angles = jnp.concatenate([angles, angles], axis=1)
    return (jnp.cos(angles), jnp.sin(angles))

def rotate(vector, cosines, sine_table):
    halfway = vector.shape[-1] // 2
    turned = jnp.concatenate([-vector[..., halfway:], vector[..., :halfway]], axis=-1)
    return vector * cosines + turned * sine_table

def attend_rows(queries, key_rows, value_rows, allowed):
    scores = jnp.einsum('bhd,lhd->hbl', queries, key_rows, precision=highest_matmul_precision) * HEAD_DIM ** (-0.5)
    scores = reduced_precision_back(scores)
    scores = jnp.where(allowed[None], scores, masked_value)
    probabilities = jax.nn.softmax(scores, axis=-1)
    return jnp.einsum('hbl,lhd->bhd', low(probabilities), value_rows, precision=highest_matmul_precision)

def layer_forward(tokens_in, attn_gain, query_key_value_weight, attention_output_weight, ffn_gain, routing_weight, common_expert_gate_up_weight, common_expert_down_weight, expert_gate_up, expert_down, routes):
    sequences, length, model_width = tokens_in.shape
    positions = dealt_positions(jnp.arange(length).astype(jnp.int32), TOK_DEV, N_CTX)
    cosines, sine_table = rope_tables(positions, HEAD_DIM)
    cosines = cosines[:, None, :]
    sine_table = sine_table[:, None, :]
    block_rows = math.gcd(512, length)
    allowed = (positions[None, :] <= positions[:, None]).reshape(length // block_rows, block_rows, length)
    inv_one = lax.rsqrt(lax.optimization_barrier(jnp.mean(tokens_in * tokens_in, axis=-1, keepdims=True)) + norm_eps)
    first_normalized = low(tokens_in * inv_one * attn_gain)
    attention_projected = reduced_precision_back(jnp.einsum('rot,tm->rom', first_normalized, query_key_value_weight, precision=highest_matmul_precision))
    head_shape = (sequences, length, HEADS, HEAD_DIM)
    queries = low(rotate(attention_projected[..., :model_width].reshape(head_shape), cosines, sine_table))
    key_rows = low(rotate(attention_projected[..., model_width:2 * model_width].reshape(head_shape), cosines, sine_table))
    value_rows = low(attention_projected[..., 2 * model_width:].reshape(head_shape))
    stepper = jax.checkpoint(attend_rows)

    def per_sequence(element):
        query_seq, key_seq, value_seq = element
        query_blocks = query_seq.reshape(length // block_rows, block_rows, HEADS, HEAD_DIM)
        return lax.map(lambda couple: stepper(couple[0], key_seq, value_seq, couple[1]), (query_blocks, allowed))
    merged_head_output = lax.map(per_sequence, (queries, key_rows, value_rows)).reshape(sequences, length, model_width)
    merged_head_output = low(reduced_precision_back(merged_head_output))
    attention_result = reduced_precision_back(jnp.einsum('rot,tm->rom', merged_head_output, attention_output_weight, precision=highest_matmul_precision))
    residual = tokens_in + attention_result
    inv_two = lax.rsqrt(lax.optimization_barrier(jnp.mean(residual * residual, axis=-1, keepdims=True)) + norm_eps)
    second_normalized = low(residual * inv_two * ffn_gain)
    common_expert_preactivation = reduced_precision_back(jnp.einsum('jrb,bi->jri', second_normalized, common_expert_gate_up_weight, precision=highest_matmul_precision))
    common_expert_hidden = low(jax.nn.silu(common_expert_preactivation[..., :FF]) * common_expert_preactivation[..., FF:])
    common_expert_output = jnp.einsum('qgn,nm->qgm', common_expert_hidden, common_expert_down_weight, precision=highest_matmul_precision)
    router_scores = reduced_precision_back(jnp.einsum('rot,tm->rom', second_normalized, routing_weight, precision=highest_matmul_precision))
    route_table = (routes[..., None] == jnp.arange(EXPERTS, dtype=jnp.int32)).astype(jnp.float32)
    chosen = lax.optimization_barrier(jnp.sum(route_table * router_scores[:, :, None, :], axis=-1))
    gate_weights = jax.nn.softmax(chosen, axis=-1)
    spread_gates = lax.optimization_barrier(jnp.sum(route_table * gate_weights[..., None], axis=2))
    flattened = second_normalized.reshape(sequences * length, model_width)
    columns = spread_gates.reshape(sequences * length, EXPERTS).T

    def expert_term(running, element):
        weight_in, weight_out, column = element
        row_block = reduced_precision_back(flattened)
        expert_pre = reduced_precision_back(jnp.dot(row_block, weight_in, precision=highest_matmul_precision))
        hidden = low(jax.nn.silu(expert_pre[:, :FF]) * expert_pre[:, FF:])
        output = low(reduced_precision_back(jnp.dot(hidden, weight_out, precision=highest_matmul_precision)))
        return (running + column[:, None] * output, None)
    routed, _ = lax.scan(jax.checkpoint(expert_term), jnp.zeros_like(flattened), (expert_gate_up, expert_down, columns))
    return residual + common_expert_output + routed.reshape(sequences, length, model_width)

def reference(block_input, cotangent, routes, attn_gain, query_key_value_weight, attention_output_weight, ffn_gain, routing_weight, common_expert_gate_up_weight, common_expert_down_weight, expert_gate_up, expert_down):
    floats = tuple((member.astype(jnp.float32) for member in (block_input, attn_gain, query_key_value_weight, attention_output_weight, ffn_gain, routing_weight, common_expert_gate_up_weight, common_expert_down_weight, expert_gate_up, expert_down)))

    def closed(*arrays):
        return layer_forward(*arrays, routes)
    result, pullback = jax.vjp(closed, *floats)
    gradients = pullback(cotangent.astype(jnp.float32))
    return (result.astype(jnp.bfloat16), gradients[0], gradients[1], gradients[2], gradients[3], gradients[4], gradients[5], gradients[6], gradients[7], gradients[8], gradients[9])
```

```python
import functools

import jax
import jax.numpy as jnp
import numpy as np
from jax import lax
from jax.experimental import pallas as pl
from jax.experimental.pallas import tpu as pltpu
from jax.sharding import Mesh
from jax.sharding import PartitionSpec as P

HEADS = 10
HEAD_DIM = 128
FF = 896
TOP = 7

norm_eps = 1e-06
rope_base = 10000.0
masked_value = -1e30
LOG2E = 1.4426950408889634

BF = jnp.bfloat16
F32 = jnp.float32
VMEM_LIMIT = 56 * 1024 * 1024


def rope_tables(positions, head_dim):
    halfway = head_dim // 2
    frequency = rope_base ** (-(jnp.arange(halfway).astype(F32) * 2.0 / head_dim))
    angles = positions.astype(F32)[:, None] * frequency[None, :]
    angles = jnp.concatenate([angles, angles], axis=1)
    return (jnp.cos(angles), jnp.sin(angles))


def rotate(vector, cosines, sine_table):
    halfway = vector.shape[-1] // 2
    turned = jnp.concatenate([-vector[..., halfway:], vector[..., :halfway]], axis=-1)
    return vector * cosines + turned * sine_table


def unrotate(gradient, cosines, sine_table):
    halfway = gradient.shape[-1] // 2
    moved = gradient * sine_table
    turned = jnp.concatenate([moved[..., halfway:], -moved[..., :halfway]], axis=-1)
    return gradient * cosines + turned


def rms_scale(values):
    return lax.rsqrt(jnp.mean(values * values, axis=1, keepdims=True) + norm_eps)


def norm_back(grad_in, values, inv_rms, gain_vec):
    scaled = grad_in * gain_vec
    return inv_rms * scaled - values * inv_rms**3 * jnp.mean(scaled * values, axis=1, keepdims=True)


def dot(a, b, dims=((1,), (0,))):
    return lax.dot_general(a, b, (dims, ((), ())), preferred_element_type=F32)


NT = ((1,), (1,))
TN = ((0,), (0,))


def shift(value, axis):
    n = lax.axis_size(axis)
    return lax.ppermute(value, axis, [(i, (i + 1) % n) for i in range(n)])


def ring_gather(value, axis):
    parts = [value]
    for _ in range(1, lax.axis_size(axis)):
        parts.append(shift(parts[-1], axis))
    return parts


def ring_sum(blocks, axis):
    n = len(blocks)
    if n == 1:
        return blocks[0].astype(F32)
    moving = blocks[1].astype(BF)
    for k in range(2, n):
        moving = (shift(moving, axis).astype(F32) + blocks[k].astype(F32)).astype(BF)
    return shift(moving, axis).astype(F32) + blocks[0].astype(F32)


def to_order(parts, axis):
    n = len(parts)
    index = lax.axis_index(axis)
    if n == 1:
        return parts[0][None]
    if n == 2:
        first = jnp.where(index == 0, parts[0], parts[1])
        second = jnp.where(index == 0, parts[1], parts[0])
        return jnp.stack([first, second])
    back = parts[::-1]
    return lax.dynamic_slice_in_dim(jnp.stack(back + back), n - 1 - index, n, axis=0)


def ring_blocks(value, axis, dim):
    n = lax.axis_size(axis)
    index = lax.axis_index(axis)
    return [
        lax.dynamic_index_in_dim(value, lax.rem(index - k + n, n), dim, keepdims=False)
        for k in range(n)
    ]


def dense_gather(shard):
    rows, width = shard.shape
    along_q = to_order(ring_gather(shard, "q"), "q")
    nq = along_q.shape[0]
    half = nq // 2
    one = to_order(ring_gather(along_q[:half], "b"), "b")
    two = to_order(ring_gather(along_q[half:], "a"), "a")
    one = to_order(ring_gather(one, "a"), "a")
    two = to_order(ring_gather(two, "b"), "b")
    plane = jnp.concatenate(
        [jnp.moveaxis(one, 2, 0), jnp.moveaxis(jnp.swapaxes(two, 0, 1), 2, 0)], axis=0
    )
    whole = to_order(ring_gather(plane, "r"), "r")
    return jnp.moveaxis(whole, 0, 1).reshape(-1, width)


def dense_sum(whole, n_rows):
    width = whole.shape[1]
    nq, nr, na, nb = (lax.axis_size(axis) for axis in ("q", "r", "a", "b"))
    value = whole.reshape(nq, nr, na, nb, n_rows, width)
    value = ring_sum(ring_blocks(value, "r", 1), "r").astype(BF)
    half = nq // 2
    one, two = value[:half], value[half:]
    one = ring_sum(ring_blocks(one, "a", 1), "a").astype(BF)
    two = ring_sum(ring_blocks(two, "b", 2), "b").astype(BF)
    one = ring_sum(ring_blocks(one, "b", 1), "b")
    two = ring_sum(ring_blocks(two, "a", 1), "a")
    value = jnp.concatenate([one, two], axis=0).astype(BF)
    return ring_sum(ring_blocks(value, "q", 0), "q")


def plane_gather(rows):
    half = rows.shape[0] // 2
    one = jnp.stack(ring_gather(rows[:half], "b"))
    two = jnp.stack(ring_gather(rows[half:], "a"))
    return (jnp.stack(ring_gather(one, "a")), jnp.stack(ring_gather(two, "b")))


def plane_sum(one, two):
    na, nb = one.shape[:2]
    first = ring_sum([one[k] for k in range(na)], "a")
    second = ring_sum([two[k] for k in range(nb)], "b")
    first = ring_sum([first[k] for k in range(nb)], "b")
    second = ring_sum([second[k] for k in range(na)], "a")
    return jnp.concatenate([first, second], axis=0)


def allowed_mask(own, other, n_ctx, half):
    row = lax.broadcasted_iota(jnp.int32, (2 * half, 2 * half), 0)
    col = lax.broadcasted_iota(jnp.int32, (2 * half, 2 * half), 1)
    last = 2 * n_ctx - 1
    query = row + jnp.where(row < half, own * half, (last - own) * half - half)
    key = col + jnp.where(col < half, other * half, (last - other) * half - half)
    return key <= query


def attend_kernel(n_ctx, n_src, first, last, place_ref, q_ref, *refs):
    kv_refs, refs = refs[:n_src], refs[n_src:]
    if not first:
        acc_in, ml_in = refs[:2]
        refs = refs[2:]
    out_ref, ml_ref = refs
    queries = q_ref[...]
    tok = queries.shape[0]
    scores = []
    for s in range(n_src):
        raw = dot(queries, kv_refs[s][0], NT) * (HEAD_DIM ** (-0.5) * LOG2E)
        mask = allowed_mask(place_ref[0], place_ref[1 + s], n_ctx, tok // 2)
        scores.append(jnp.where(mask, raw, masked_value))
    peak = functools.reduce(jnp.maximum, [jnp.max(s, axis=1, keepdims=True) for s in scores])
    if not first:
        old_peak = ml_in[0][:, 0:1]
        old_sum = ml_in[0][:, 64:65]
        peak = jnp.maximum(peak, old_peak)
    total = jnp.zeros_like(peak)
    mixed = jnp.zeros((tok, HEAD_DIM), F32)
    for s in range(n_src):
        raised = jnp.exp2(scores[s] - peak)
        total = total + jnp.sum(raised, axis=1, keepdims=True)
        mixed = mixed + dot(raised.astype(BF), kv_refs[s][1])
    if not first:
        decay = jnp.exp2(old_peak - peak)
        total = total + old_sum * decay
        mixed = mixed + acc_in[...] * decay
    if last:
        out_ref[...] = (mixed / total).astype(BF)
        ml_ref[0] = jnp.broadcast_to(peak + jnp.log2(total), (tok, 128))
    else:
        out_ref[...] = mixed
        lane = lax.broadcasted_iota(jnp.int32, (tok, 128), 1)
        ml_ref[0] = jnp.where(lane < 64, peak, total)


def attend_chunk(places, queries, kv_list, state, last, n_ctx):
    tok, width = queries.shape
    head = pl.BlockSpec((tok, HEAD_DIM), lambda h, p: (0, h))
    pair = pl.BlockSpec((2, tok, HEAD_DIM), lambda h, p: (0, 0, h))
    rows = pl.BlockSpec((1, tok, 128), lambda h, p: (h, 0, 0))
    first = state is None
    n = len(kv_list)
    pairs = tok * tok * n * HEADS
    return pl.pallas_call(
        functools.partial(attend_kernel, n_ctx, n, first, last),
        grid_spec=pltpu.PrefetchScalarGridSpec(
            num_scalar_prefetch=1,
            grid=(HEADS,),
            in_specs=[head] + [pair] * n + ([] if first else [head, rows]),
            out_specs=[head, rows],
        ),
        out_shape=[
            jax.ShapeDtypeStruct((tok, width), BF if last else F32),
            jax.ShapeDtypeStruct((HEADS, tok, 128), F32),
        ],
        compiler_params=pltpu.CompilerParams(vmem_limit_bytes=VMEM_LIMIT // 2),
        cost_estimate=pl.CostEstimate(
            flops=4 * pairs * HEAD_DIM * 4, bytes_accessed=8 * tok * width, transcendentals=pairs
        ),
        name="attend",
    )(places, queries, *kv_list, *(() if first else state))


def attend_back_kernel(n_ctx, n_src, first, place_ref, q_ref, do_ref, o_ref, lse_ref, *refs):
    kv_refs, refs = refs[:n_src], refs[n_src:]
    if not first:
        dq_in, refs = refs[0], refs[1:]
    dq_ref, dkv_refs = refs[0], refs[1:]
    queries = q_ref[...]
    grad = do_ref[...]
    tok = queries.shape[0]
    lse = lse_ref[0][:, 0:1]
    delta = jnp.sum(grad.astype(F32) * o_ref[...].astype(F32), axis=1, keepdims=True)
    scale = HEAD_DIM ** (-0.5)
    grad_query = jnp.zeros((tok, HEAD_DIM), F32)
    for s in range(n_src):
        keys, values = kv_refs[s][0], kv_refs[s][1]
        raw = dot(queries, keys, NT) * (scale * LOG2E)
        mask = allowed_mask(place_ref[0], place_ref[1 + s], n_ctx, tok // 2)
        probs = jnp.exp2(jnp.where(mask, raw, masked_value) - lse)
        grad_probs = dot(grad, values, NT)
        grad_scores = (probs * (grad_probs - delta)).astype(BF)
        grad_query = grad_query + dot(grad_scores, keys)
        dkv_refs[s][0] = (dot(grad_scores, queries, TN) * scale).astype(dkv_refs[s].dtype)
        dkv_refs[s][1] = dot(probs.astype(BF), grad, TN).astype(dkv_refs[s].dtype)
    grad_query = grad_query * scale
    if not first:
        grad_query = grad_query + dq_in[...]
    dq_ref[...] = grad_query


def attend_back_chunk(places, queries, grad, mixed, lse, kv_list, dq, n_ctx):
    tok, width = queries.shape
    head = pl.BlockSpec((tok, HEAD_DIM), lambda h, p: (0, h))
    pair = pl.BlockSpec((2, tok, HEAD_DIM), lambda h, p: (0, 0, h))
    rows = pl.BlockSpec((1, tok, 128), lambda h, p: (h, 0, 0))
    first = dq is None
    n = len(kv_list)
    pairs = tok * tok * n * HEADS
    out = pl.pallas_call(
        functools.partial(attend_back_kernel, n_ctx, n, first),
        grid_spec=pltpu.PrefetchScalarGridSpec(
            num_scalar_prefetch=1,
            grid=(HEADS,),
            in_specs=[head, head, head, rows] + [pair] * n + ([] if first else [head]),
            out_specs=[head] + [pair] * n,
        ),
        out_shape=[jax.ShapeDtypeStruct((tok, width), F32)]
        + [jax.ShapeDtypeStruct((2, tok, width), F32 if s == 0 else BF) for s in range(n)],
        compiler_params=pltpu.CompilerParams(vmem_limit_bytes=VMEM_LIMIT // 2),
        cost_estimate=pl.CostEstimate(
            flops=10 * pairs * HEAD_DIM * 4, bytes_accessed=16 * tok * width, transcendentals=pairs
        ),
        name="attend_back",
    )(places, queries, grad, mixed, lse, *kv_list, *(() if first else (dq,)))
    return out[0], out[1:]


def expert_kernel(
    slots, e_ref, rank_ref, c0, c1, g0, g1, wr_ref, w1_ref, w2_ref,
    y0, y1, d0, d1, dg_ref, x_ref, h_ref, dey_ref, deg_ref,
):
    n_src = c0.shape[1]
    half = c0.shape[2]
    tok = 2 * half
    experts = wr_ref.shape[0]
    me = e_ref[0]
    picks, rows, grads, weights = [], [], [], []
    own = lax.broadcasted_iota(jnp.int32, (experts, tok), 0) == me
    slot = lax.broadcasted_iota(jnp.int32, (slots, tok), 0).astype(F32)
    for s in range(n_src):
        tokens = jnp.concatenate([c0[0, s], c1[s, 0]], axis=0)
        cot = jnp.concatenate([g0[0, s], g1[s, 0]], axis=0)
        rank = rank_ref[0, s, 0]
        logits = dot(wr_ref[...], tokens, NT)
        logits = jnp.where(rank >= 0, logits, masked_value)
        raised = jnp.where(rank >= 0, jnp.exp(logits - jnp.max(logits, axis=0, keepdims=True)), 0.0)
        gates = raised / jnp.sum(raised, axis=0, keepdims=True)
        gate_row = jnp.sum(jnp.where(own, gates, 0.0), axis=0, keepdims=True)
        rank_row = jnp.sum(jnp.where(own, rank, 0.0), axis=0, keepdims=True)
        pick = jnp.where(slot == rank_row, 1.0, 0.0)
        weights.append(jnp.sum(pick * gate_row, axis=1, keepdims=True))
        pick_low = pick.astype(BF)
        picks.append((pick, pick_low))
        rows.append(dot(pick_low, tokens).astype(BF))
        grads.append(dot(pick_low, cot))
    x = jnp.concatenate(rows, axis=0)
    grad = jnp.concatenate(grads, axis=0)
    weight = jnp.concatenate(weights, axis=0)
    x_ref[...] = x
    dey = (weight * grad).astype(BF)
    dey_ref[...] = dey
    pre = dot(x, w1_ref[...])
    gate, up = pre[:, :FF], pre[:, FF:]
    sig = jax.nn.sigmoid(gate)
    act = gate * sig
    hidden = (act * up).astype(BF)
    h_ref[...] = hidden
    grad_hidden = dot(dey, w2_ref[...], NT)
    deg = jnp.concatenate(
        [
            (grad_hidden * up * sig * (1.0 + gate * (1.0 - sig))).astype(BF),
            (grad_hidden * act).astype(BF),
        ],
        axis=1,
    )
    deg_ref[...] = deg
    dec = dot(deg, w1_ref[...], NT).astype(BF)
    ey = dot(hidden, w2_ref[...]).astype(BF).astype(F32)
    dgate = jnp.sum(grad * ey, axis=1, keepdims=True)
    weighted = (weight * ey).astype(BF)
    for s in range(n_src):
        part = slice(s * slots, (s + 1) * slots)
        pick, pick_low = picks[s]
        back = dot(pick_low, dec[part], TN).astype(BF)
        d0[0, s] = back[:half]
        d1[s, 0] = back[half:]
        back = dot(pick_low, weighted[part], TN).astype(BF)
        y0[0, s] = back[:half]
        y1[s, 0] = back[half:]
        dg_ref[0, s] = jnp.sum(pick * dgate[part], axis=0, keepdims=True)


def expert_chunk(chunk, expert, ranks, c, g, router_t, w1, w2, slots):
    na, nb, half, width = c[0].shape
    experts = router_t.shape[0]
    one = pl.BlockSpec((1, nb, half, width), lambda i, e: (i, 0, 0, 0))
    two = pl.BlockSpec((nb, 1, half, width), lambda i, e: (0, i, 0, 0))

    def fixed(shape):
        return pl.BlockSpec(shape, lambda i, e: (0,) * len(shape), pipeline_mode=pl.Buffered(1))

    def by_rows(n):
        return pl.BlockSpec((nb * slots, n), lambda i, e: (i, 0))

    n_rows = na * nb * slots
    return pl.pallas_call(
        functools.partial(expert_kernel, slots),
        grid_spec=pltpu.PrefetchScalarGridSpec(
            num_scalar_prefetch=1,
            grid=(na,),
            in_specs=[
                pl.BlockSpec((1, nb, 1, experts, 2 * half), lambda i, e: (i, 0, chunk, 0, 0)),
                one, two, one, two,
                fixed(router_t.shape), fixed(w1.shape), fixed(w2.shape),
            ],
            out_specs=[
                one, two, one, two,
                pl.BlockSpec((1, nb, 1, 2 * half), lambda i, e: (i, 0, 0, 0)),
                by_rows(width), by_rows(FF), by_rows(width), by_rows(2 * FF),
            ],
        ),
        out_shape=[
            jax.ShapeDtypeStruct((na, nb, half, width), BF),
            jax.ShapeDtypeStruct((nb, na, half, width), BF),
            jax.ShapeDtypeStruct((na, nb, half, width), BF),
            jax.ShapeDtypeStruct((nb, na, half, width), BF),
            jax.ShapeDtypeStruct((na, nb, 1, 2 * half), F32),
            jax.ShapeDtypeStruct((n_rows, width), BF),
            jax.ShapeDtypeStruct((n_rows, FF), BF),
            jax.ShapeDtypeStruct((n_rows, width), BF),
            jax.ShapeDtypeStruct((n_rows, 2 * FF), BF),
        ],
        compiler_params=pltpu.CompilerParams(vmem_limit_bytes=VMEM_LIMIT),
        cost_estimate=pl.CostEstimate(
            flops=n_rows * width * FF * 12, bytes_accessed=30_000_000, transcendentals=n_rows * FF
        ),
        name="experts",
    )(expert, ranks, *c, *g, router_t, w1, w2)


def body(
    n_experts,
    block_input,
    cotangent,
    routes,
    attn_gain,
    query_key_value_weight,
    attention_output_weight,
    ffn_gain,
    routing_weight,
    common_expert_gate_up_weight,
    common_expert_down_weight,
    expert_gate_up,
    expert_down,
):
    nq, nr, na, nb = (lax.axis_size(axis) for axis in ("q", "r", "a", "b"))
    q_at, r_at, a_at, b_at = (lax.axis_index(axis) for axis in ("q", "r", "a", "b"))
    n_ctx = nq * nr
    n_exp = na * nb
    ctx_rank = q_at * nr + r_at
    exp_rank = a_at * nb + b_at
    tok = block_input.shape[1]
    width = block_input.shape[2]
    half = tok // 2
    capacity = min(tok, 3 * TOP * tok // (2 * n_experts))
    slots = -(-capacity // 16) * 16
    row = jnp.arange(tok, dtype=jnp.int32)
    local_pos = jnp.where(
        row < half, ctx_rank * half + row, (2 * n_ctx - 1 - ctx_rank) * half + row - half
    )
    cosines, sine_table = rope_tables(local_pos, HEAD_DIM)
    cosines = cosines[:, None, :]
    sine_table = sine_table[:, None, :]
    head_shape = (tok, HEADS, HEAD_DIM)
    tokens_in = block_input[0].astype(F32)
    grad_low = cotangent[0]
    out_grad = grad_low.astype(F32)

    named = jnp.any(
        routes[0][:, :, None] == jnp.arange(n_experts, dtype=jnp.int32)[None, None, :], axis=1
    )
    before = (row[:, None] < row[None, :]).astype(BF)
    rank = dot(named.astype(BF).T, before)
    rank = jnp.where(named.T, rank, -1.0)
    ranks = jnp.stack(ring_gather(rank, "q"))
    ranks = jnp.stack(ring_gather(ranks, "b"))
    ranks = jnp.stack(ring_gather(ranks, "a"))

    own_rows = query_key_value_weight.shape[0]
    small = jnp.concatenate(
        [
            attn_gain[:, None],
            ffn_gain[:, None],
            routing_weight,
            jnp.zeros((own_rows, 126 - n_experts), BF),
        ],
        axis=1,
    )
    small = dense_gather(small)
    gain_one = small[:, 0].astype(F32)
    gain_two = small[:, 1].astype(F32)
    router = small[:, 2 : 2 + n_experts]
    qkv_weight = dense_gather(query_key_value_weight)
    out_weight = dense_gather(attention_output_weight)
    shared_in = dense_gather(common_expert_gate_up_weight)
    shared_out = dense_gather(common_expert_down_weight)

    def own_expert(stack):
        rows = lax.all_to_all(stack, "q", split_axis=0, concat_axis=0, tiled=True)
        whole = to_order(ring_gather(rows, "r"), "r")
        return jnp.moveaxis(whole, 0, 1).reshape(-1, stack.shape[2])

    w1 = own_expert(expert_gate_up)
    w2 = own_expert(expert_down)

    inv_one = rms_scale(tokens_in)
    normed = (tokens_in * inv_one * gain_one).astype(BF)
    projected = dot(normed, qkv_weight)
    queries = rotate(projected[:, :width].reshape(head_shape), cosines, sine_table)
    queries = queries.astype(BF).reshape(tok, width)
    keys = rotate(projected[:, width : 2 * width].reshape(head_shape), cosines, sine_table)
    keys = keys.astype(BF).reshape(tok, width)
    kv_own = jnp.stack([keys, projected[:, 2 * width :].astype(BF)])
    kv_chunks = [ring_gather(part, "r") for part in ring_gather(kv_own, "q")]
    places = [
        jnp.stack(
            [ctx_rank]
            + [
                lax.rem(q_at - k + nq, nq) * nr + lax.rem(r_at - s + nr, nr)
                for s in range(nr)
            ]
        ).astype(jnp.int32)
        for k in range(nq)
    ]
    state = None
    for k in range(nq):
        state = attend_chunk(places[k], queries, kv_chunks[k], state, k == nq - 1, n_ctx)
    mixed, lse = state

    g_planes = [plane_gather(part) for part in ring_gather(grad_low, "q")]

    residual = tokens_in + dot(mixed, out_weight)
    inv_two = rms_scale(residual)
    second = (residual * inv_two * gain_two).astype(BF)
    c_planes = [plane_gather(part) for part in ring_gather(second, "q")]
    expert = (exp_rank * nq + q_at).astype(jnp.int32).reshape(1)
    results = [
        expert_chunk(k, expert, ranks, c_planes[k], g_planes[k], router.T, w1, w2, slots)
        for k in range(nq)
    ]
    dec_sums = [None] * nq
    for k in list(range(1, nq)) + [0]:
        dec_sums[k] = plane_sum(results[k][2], results[k][3])
    routed_grad = ring_sum(dec_sums, "q")
    y_sums = [plane_sum(result[0], result[1]) for result in results]
    routed_sum = ring_sum(y_sums, "q")

    shared_pre = dot(second, shared_in)
    shared_gate, shared_up = shared_pre[:, :FF], shared_pre[:, FF:]
    shared_sig = jax.nn.sigmoid(shared_gate)
    shared_hidden = (shared_gate * shared_sig * shared_up).astype(BF)
    layer_out = (residual + dot(shared_hidden, shared_out) + routed_sum).astype(BF)

    logits = jnp.where(named, dot(second, router), masked_value)
    raised = jnp.where(named, jnp.exp(logits - jnp.max(logits, axis=1, keepdims=True)), 0.0)
    gates = raised / jnp.sum(raised, axis=1, keepdims=True)
    dgate = jnp.stack([result[4].reshape(na, nb, tok) for result in results])
    dgate = to_order([dgate[k] for k in range(nq)], "q")
    dgate = to_order([dgate[:, k] for k in range(na)], "a")
    dgate = to_order([dgate[:, :, k] for k in range(nb)], "b")
    dgate = jnp.transpose(dgate, (2, 1, 0, 3))
    dgate = lax.all_to_all(dgate, "q", split_axis=0, concat_axis=0, tiled=True)
    dgate = lax.all_to_all(dgate, "a", split_axis=1, concat_axis=1, tiled=True)
    dgate = lax.all_to_all(dgate, "b", split_axis=2, concat_axis=2, tiled=True)
    dgate = jnp.transpose(dgate, (1, 2, 0, 3)).reshape(n_experts, tok).T
    grad_logits = gates * (dgate - jnp.sum(gates * dgate, axis=1, keepdims=True))
    grad_logits = grad_logits.astype(BF)

    shared_hidden_grad = dot(grad_low, shared_out, NT)
    shared_pre_grad = jnp.concatenate(
        [
            shared_hidden_grad * shared_up * shared_sig * (1.0 + shared_gate * (1.0 - shared_sig)),
            shared_hidden_grad * shared_gate * shared_sig,
        ],
        axis=1,
    ).astype(BF)
    second_grad = (
        dot(shared_pre_grad, shared_in, NT) + dot(grad_logits, router, NT) + routed_grad
    )
    ffn_gain_grad = jnp.sum(second_grad * residual * inv_two, axis=0)
    residual_grad = out_grad + norm_back(second_grad, residual, inv_two, gain_two)
    mixed_grad = residual_grad.astype(BF)
    heads_grad = dot(mixed_grad, out_weight, NT).astype(BF)

    dq = None
    kv_sums = [None] * nq
    for k in list(range(1, nq)) + [0]:
        dq, parts = attend_back_chunk(
            places[k], queries, heads_grad, mixed, lse, kv_chunks[k], dq, n_ctx
        )
        kv_sums[k] = ring_sum(parts, "r")
    kv_grad = ring_sum(kv_sums, "q")

    xs, hs, deys, degs = (
        jnp.concatenate([result[i] for result in results], axis=0) for i in range(5, 9)
    )

    def expert_rows(whole):
        value = whole.reshape(nq, nr, -1, whole.shape[1])
        value = ring_sum(ring_blocks(value, "r", 1), "r").astype(BF)
        return lax.all_to_all(value, "q", split_axis=0, concat_axis=0, tiled=True).astype(F32)

    gate_up_grad = expert_rows(dot(xs, degs, TN).astype(BF))
    down_grad = expert_rows(dot(hs, deys, TN).astype(BF))

    down_rows = common_expert_down_weight.shape[0]
    shared_down_grad = dense_sum(dot(shared_hidden, grad_low, TN).astype(BF), down_rows)
    shared_in_grad = dense_sum(dot(second, shared_pre_grad, TN).astype(BF), own_rows)
    out_weight_grad = dense_sum(dot(mixed, mixed_grad, TN).astype(BF), own_rows)
    router_grad = dot(second, grad_logits, TN)

    query_back = unrotate(dq.reshape(head_shape), cosines, sine_table).reshape(tok, width)
    key_back = unrotate(kv_grad[0].reshape(head_shape), cosines, sine_table).reshape(tok, width)
    qkv_back = jnp.concatenate([query_back, key_back, kv_grad[1]], axis=1).astype(BF)
    normed_grad = dot(qkv_back, qkv_weight, NT)
    attn_gain_grad = jnp.sum(normed_grad * tokens_in * inv_one, axis=0)
    input_grad = residual_grad + norm_back(normed_grad, tokens_in, inv_one, gain_one)
    qkv_weight_grad = dense_sum(dot(normed, qkv_back, TN).astype(BF), own_rows)
    small_grad = jnp.concatenate(
        [
            attn_gain_grad[:, None],
            ffn_gain_grad[:, None],
            router_grad,
            jnp.zeros((width, 126 - n_experts), F32),
        ],
        axis=1,
    )
    small_grad = dense_sum(small_grad, own_rows)
    return (
        layer_out[None],
        input_grad[None],
        small_grad[:, 0],
        qkv_weight_grad,
        out_weight_grad,
        small_grad[:, 1],
        small_grad[:, 2 : 2 + n_experts],
        shared_in_grad,
        shared_down_grad,
        gate_up_grad,
        down_grad,
    )


def solution(mesh):
    n_ctx, n_exp = mesh.shape["ctx"], mesh.shape["exp"]

    def layer(*args):
        n_experts = args[10].shape[0]
        nq = n_experts // n_exp
        nb = 2
        fine = Mesh(
            np.asarray(mesh.devices).reshape(nq, n_ctx // nq, n_exp // nb, nb), ("q", "r", "a", "b")
        )
        ctx, exp, every = ("q", "r"), ("a", "b"), ("q", "r", "a", "b")
        tokens, flat, rows = P(exp, ctx, None), P(every), P(every, None)
        run = jax.shard_map(
            functools.partial(body, n_experts),
            mesh=fine,
            in_specs=(
                tokens, tokens, tokens, flat, rows, rows, flat, rows, rows, rows, tokens, tokens,
            ),
            out_specs=(tokens, tokens, flat, rows, rows, flat, rows, rows, rows, tokens, tokens),
            check_vma=False,
        )
        return run(*args)

    return layer
```

```python
import functools

import jax
import jax.numpy as jnp
import numpy as np
from jax import lax
from jax.experimental import pallas as pl
from jax.experimental.pallas import tpu as pltpu
from jax.sharding import Mesh
from jax.sharding import PartitionSpec as P

HEADS = 10
HEAD_DIM = 128
FF = 896
TOP = 7

norm_eps = 1e-06
rope_base = 10000.0
masked_value = -1e30
LOG2E = 1.4426950408889634

BF = jnp.bfloat16
F32 = jnp.float32
VMEM_LIMIT = 56 * 1024 * 1024


def rope_tables(positions, head_dim):
    halfway = head_dim // 2
    frequency = rope_base ** (-(jnp.arange(halfway).astype(F32) * 2.0 / head_dim))
    angles = positions.astype(F32)[:, None] * frequency[None, :]
    angles = jnp.concatenate([angles, angles], axis=1)
    return (jnp.cos(angles), jnp.sin(angles))


def rms_scale(values):
    return lax.rsqrt(jnp.mean(values * values, axis=1, keepdims=True) + norm_eps)


def norm_back(grad_in, values, inv_rms, gain_vec):
    scaled = grad_in * gain_vec
    return inv_rms * scaled - values * inv_rms**3 * jnp.mean(scaled * values, axis=1, keepdims=True)


def dot(a, b, dims=((1,), (0,))):
    return lax.dot_general(a, b, (dims, ((), ())), preferred_element_type=F32)


NT = ((1,), (1,))
TN = ((0,), (0,))


def shift(value, axis):
    n = lax.axis_size(axis)
    return lax.ppermute(value, axis, [(i, (i + 1) % n) for i in range(n)])


def ring_gather(value, axis):
    parts = [value]
    for _ in range(1, lax.axis_size(axis)):
        parts.append(shift(parts[-1], axis))
    return parts


def ring_sum(blocks, axis):
    n = len(blocks)
    if n == 1:
        return blocks[0].astype(F32)
    moving = blocks[1].astype(BF)
    for k in range(2, n):
        moving = (shift(moving, axis).astype(F32) + blocks[k].astype(F32)).astype(BF)
    return shift(moving, axis).astype(F32) + blocks[0].astype(F32)


def ring_blocks(arrays, axis, dim):
    n = lax.axis_size(axis)
    index = lax.axis_index(axis)
    out = []
    for k in range(n):
        at = lax.rem(index - k + n, n)
        parts = [lax.dynamic_index_in_dim(v, at, dim, keepdims=False) for v in arrays]
        out.append(parts[0] if len(parts) == 1 else jnp.concatenate(parts, axis=-1))
    return out


def after(value, *events):
    return lax.optimization_barrier((value, *events))[0]


def place_kernel(counts, columns, index_ref, *refs):
    n = len(counts)
    pieces, outs, sems = refs[:n], refs[n:-1], refs[-1]
    t = 0
    for piece, count in zip(pieces, counts):
        for j in range(count):
            at = index_ref[t]
            t += 1
            for o, (low, high) in enumerate(columns):
                pltpu.make_async_copy(
                    piece.at[j, :, pl.ds(low, high - low)], outs[o].at[at], sems.at[o]
                ).start()
    for o in range(len(columns)):
        pltpu.make_async_copy(outs[o], outs[o], sems.at[o]).wait()


def place(index, pieces, widths):
    rows, total = pieces[0].shape[-2:]
    pieces = [piece.reshape(-1, rows, total) for piece in pieces]
    counts = [piece.shape[0] for piece in pieces]
    edges = np.cumsum([0] + list(widths))
    columns = [(int(low), int(high)) for low, high in zip(edges[:-1], edges[1:])]
    n = sum(counts)
    anywhere = pl.BlockSpec(memory_space=pl.ANY)
    outs = pl.pallas_call(
        functools.partial(place_kernel, counts, columns),
        grid_spec=pltpu.PrefetchScalarGridSpec(
            num_scalar_prefetch=1,
            grid=(1,),
            in_specs=[anywhere] * len(pieces),
            out_specs=[anywhere] * len(widths),
            scratch_shapes=[pltpu.SemaphoreType.DMA((len(widths),))],
        ),
        out_shape=[jax.ShapeDtypeStruct((n, rows, w), pieces[0].dtype) for w in widths],
        cost_estimate=pl.CostEstimate(
            flops=0, bytes_accessed=4 * n * rows * total, transcendentals=0
        ),
        name="place",
    )(index, *pieces)
    return [out.reshape(n * rows, w) for out, w in zip(outs, widths)]


def dense_rings(along_q):
    half = len(along_q) // 2
    na, nb = lax.axis_size("a"), lax.axis_size("b")
    one = jnp.stack(ring_gather(jnp.stack(along_q[:half]), "b"))
    two = jnp.stack(ring_gather(jnp.stack(along_q[half:]), "a"))
    pieces = ring_gather(one, "a") + ring_gather(two, "b")
    steps = [[(kq, ka, kb) for kb in range(nb) for kq in range(half)] for ka in range(na)]
    steps += [
        [(kq, ka, kb) for ka in range(na) for kq in range(half, len(along_q))] for kb in range(nb)
    ]
    return pieces, steps


def dense_place(pieces, steps, widths):
    nq, nr, na, nb = (lax.axis_size(axis) for axis in ("q", "r", "a", "b"))
    moved = [ring_gather(piece, "r") for piece in pieces]
    order = [(k, *s) for k in range(nr) for part in steps for s in part]
    kr, kq, ka, kb = (np.array(column, np.int32) for column in zip(*order))
    index = lax.rem(lax.axis_index("q") - kq + nq, nq) * nr
    index = index + lax.rem(lax.axis_index("r") - kr + nr, nr)
    index = index * na + lax.rem(lax.axis_index("a") - ka + na, na)
    index = index * nb + lax.rem(lax.axis_index("b") - kb + nb, nb)
    arrays = [moved[p][k] for k in range(nr) for p in range(len(pieces))]
    return place(index.astype(jnp.int32), arrays, widths)


def dense_sum(wholes, n_rows):
    nq, nr, na, nb = (lax.axis_size(axis) for axis in ("q", "r", "a", "b"))
    values = [whole.reshape(nq, nr, na, nb, n_rows, whole.shape[1]) for whole in wholes]
    value = ring_sum(ring_blocks(values, "r", 1), "r").astype(BF)
    half = nq // 2
    one, two = value[:half], value[half:]
    one = ring_sum(ring_blocks([one], "a", 1), "a").astype(BF)
    two = ring_sum(ring_blocks([two], "b", 2), "b").astype(BF)
    one = ring_sum(ring_blocks([one], "b", 1), "b")
    two = ring_sum(ring_blocks([two], "a", 1), "a")
    value = jnp.concatenate([one, two], axis=0).astype(BF)
    return ring_sum(ring_blocks([value], "q", 0), "q")


def plane_gather(rows):
    half = rows.shape[-2] // 2
    one = jnp.stack(ring_gather(rows[..., :half, :], "b"))
    two = jnp.stack(ring_gather(rows[..., half:, :], "a"))
    return (jnp.stack(ring_gather(one, "a")), ring_gather(two, "b"))


def plane_sum(one, two, dim=0):
    first = ring_sum(one, "a")
    second = ring_sum(two, "b")
    first = ring_sum([lax.index_in_dim(first, k, dim, False) for k in range(len(two))], "b")
    second = ring_sum([lax.index_in_dim(second, k, dim, False) for k in range(len(one))], "a")
    return jnp.concatenate([first, second], axis=-2)


def project_kernel(n_query, x_ref, w_ref, cos_ref, sin_ref, q_ref, kv_ref):
    j = pl.program_id(0)
    made = dot(x_ref[...], w_ref[...])

    def turned():
        parts = []
        for low in range(0, made.shape[1], HEAD_DIM):
            u = made[:, low : low + HEAD_DIM]
            parts.append(u * cos_ref[...] + pltpu.roll(u, HEAD_DIM // 2, 1) * sin_ref[...])
        return jnp.concatenate(parts, axis=1).astype(BF)

    @pl.when(j < n_query)
    def _():
        q_ref[...] = turned()

    @pl.when((j >= n_query) & (j < 2 * n_query))
    def _():
        kv_ref[0] = turned()

    @pl.when(j >= 2 * n_query)
    def _():
        kv_ref[0] = made.astype(BF)


def project(normed, weight, cosines, signed_sine):
    tok, width = normed.shape
    block = 2 * HEAD_DIM
    n = width // block
    table = pl.BlockSpec((tok, HEAD_DIM), lambda j: (0, 0))
    return pl.pallas_call(
        functools.partial(project_kernel, n),
        grid=(3 * n,),
        in_specs=[
            pl.BlockSpec((tok, width), lambda j: (0, 0)),
            pl.BlockSpec((width, block), lambda j: (0, j)),
            table,
            table,
        ],
        out_specs=[
            pl.BlockSpec((tok, block), lambda j: (0, jnp.minimum(j, n - 1))),
            pl.BlockSpec(
                (1, tok, block),
                lambda j: (jnp.maximum(j - n, 0) // n, 0, jnp.maximum(j - n, 0) % n),
            ),
        ],
        out_shape=[
            jax.ShapeDtypeStruct((tok, width), BF),
            jax.ShapeDtypeStruct((2, tok, width), BF),
        ],
        compiler_params=pltpu.CompilerParams(vmem_limit_bytes=VMEM_LIMIT // 2),
        cost_estimate=pl.CostEstimate(
            flops=6 * tok * width * width, bytes_accessed=6 * width * width, transcendentals=0
        ),
        name="project",
    )(normed, weight, cosines, signed_sine)


def turn_back(grad, cos, signed_sine):
    return grad * cos - pltpu.roll(grad, HEAD_DIM // 2, 1) * signed_sine


def finish_kernel(moved_ref, own_ref, cos_ref, sin_ref, out_ref):
    keys = moved_ref[0].astype(F32) + own_ref[0]
    out_ref[0] = turn_back(keys, cos_ref[...], sin_ref[...]).astype(BF)
    out_ref[1] = (moved_ref[1].astype(F32) + own_ref[1]).astype(BF)


def finish_keys(moved, own, cosines, signed_sine):
    _, tok, width = own.shape
    pair = pl.BlockSpec((2, tok, HEAD_DIM), lambda h: (0, 0, h))
    table = pl.BlockSpec((tok, HEAD_DIM), lambda h: (0, 0))
    return pl.pallas_call(
        finish_kernel,
        grid=(width // HEAD_DIM,),
        in_specs=[pair, pair, table, table],
        out_specs=pair,
        out_shape=jax.ShapeDtypeStruct((2, tok, width), BF),
        cost_estimate=pl.CostEstimate(
            flops=10 * tok * width, bytes_accessed=16 * tok * width, transcendentals=0
        ),
        name="finish_keys",
    )(moved, own, cosines, signed_sine)


def allowed_mask(own, other, n_ctx, half):
    row = lax.broadcasted_iota(jnp.int32, (2 * half, 2 * half), 0)
    col = lax.broadcasted_iota(jnp.int32, (2 * half, 2 * half), 1)
    last = 2 * n_ctx - 1
    query = row + jnp.where(row < half, own * half, (last - own) * half - half)
    key = col + jnp.where(col < half, other * half, (last - other) * half - half)
    return key <= query


def attend_kernel(n_ctx, n_src, first, last, place_ref, q_ref, *refs):
    kv_refs, refs = refs[:n_src], refs[n_src:]
    if not first:
        acc_in, ml_in = refs[:2]
        refs = refs[2:]
    out_ref, ml_ref = refs
    queries = q_ref[...]
    tok = queries.shape[0]
    scores = []
    for s in range(n_src):
        raw = dot(queries, kv_refs[s][0], NT) * (HEAD_DIM ** (-0.5) * LOG2E)
        mask = allowed_mask(place_ref[0], place_ref[1 + s], n_ctx, tok // 2)
        scores.append(jnp.where(mask, raw, masked_value))
    peak = functools.reduce(jnp.maximum, [jnp.max(s, axis=1, keepdims=True) for s in scores])
    if not first:
        old_peak = ml_in[0][:, 0:1]
        old_sum = ml_in[0][:, 64:65]
        peak = jnp.maximum(peak, old_peak)
    total = jnp.zeros_like(peak)
    mixed = jnp.zeros((tok, HEAD_DIM), F32)
    for s in range(n_src):
        raised = jnp.exp2(scores[s] - peak)
        total = total + jnp.sum(raised, axis=1, keepdims=True)
        mixed = mixed + dot(raised.astype(BF), kv_refs[s][1])
    if not first:
        decay = jnp.exp2(old_peak - peak)
        total = total + old_sum * decay
        mixed = mixed + acc_in[...] * decay
    if last:
        out_ref[...] = (mixed / total).astype(BF)
        ml_ref[0] = jnp.broadcast_to(peak + jnp.log2(total), (tok, 128))
    else:
        out_ref[...] = mixed
        lane = lax.broadcasted_iota(jnp.int32, (tok, 128), 1)
        ml_ref[0] = jnp.where(lane < 64, peak, total)


def attend_chunk(places, queries, kv_list, state, last, n_ctx):
    tok, width = queries.shape
    head = pl.BlockSpec((tok, HEAD_DIM), lambda h, p: (0, h))
    pair = pl.BlockSpec((2, tok, HEAD_DIM), lambda h, p: (0, 0, h))
    rows = pl.BlockSpec((1, tok, 128), lambda h, p: (h, 0, 0))
    first = state is None
    n = len(kv_list)
    pairs = tok * tok * n * HEADS
    return pl.pallas_call(
        functools.partial(attend_kernel, n_ctx, n, first, last),
        grid_spec=pltpu.PrefetchScalarGridSpec(
            num_scalar_prefetch=1,
            grid=(HEADS,),
            in_specs=[head] + [pair] * n + ([] if first else [head, rows]),
            out_specs=[head, rows],
        ),
        out_shape=[
            jax.ShapeDtypeStruct((tok, width), BF if last else F32),
            jax.ShapeDtypeStruct((HEADS, tok, 128), F32),
        ],
        compiler_params=pltpu.CompilerParams(vmem_limit_bytes=VMEM_LIMIT // 2),
        cost_estimate=pl.CostEstimate(
            flops=4 * pairs * HEAD_DIM * 4, bytes_accessed=8 * tok * width, transcendentals=pairs
        ),
        name="attend",
    )(places, queries, *kv_list, *(() if first else state))


def attend_back_kernel(
    n_ctx, n_src, first, last, place_ref, q_ref, do_ref, o_ref, lse_ref, cos_ref, sin_ref, *refs
):
    kv_refs, refs = refs[:n_src], refs[n_src:]
    if not first:
        dq_in, refs = refs[0], refs[1:]
    dq_ref, dkv_refs = refs[0], refs[1:]
    queries = q_ref[...]
    grad = do_ref[...]
    tok = queries.shape[0]
    lse = lse_ref[0][:, 0:1]
    delta = jnp.sum(grad.astype(F32) * o_ref[...].astype(F32), axis=1, keepdims=True)
    scale = HEAD_DIM ** (-0.5)
    grad_query = jnp.zeros((tok, HEAD_DIM), F32)
    for s in range(n_src):
        keys, values = kv_refs[s][0], kv_refs[s][1]
        raw = dot(queries, keys, NT) * (scale * LOG2E)
        mask = allowed_mask(place_ref[0], place_ref[1 + s], n_ctx, tok // 2)
        probs = jnp.exp2(jnp.where(mask, raw, masked_value) - lse)
        grad_probs = dot(grad, values, NT)
        grad_scores = (probs * (grad_probs - delta)).astype(BF)
        grad_query = grad_query + dot(grad_scores, keys)
        dkv_refs[s][0] = (dot(grad_scores, queries, TN) * scale).astype(dkv_refs[s].dtype)
        dkv_refs[s][1] = dot(probs.astype(BF), grad, TN).astype(dkv_refs[s].dtype)
    grad_query = grad_query * scale
    if not first:
        grad_query = grad_query + dq_in[...]
    if last:
        grad_query = turn_back(grad_query, cos_ref[...], sin_ref[...]).astype(BF)
    dq_ref[...] = grad_query


def attend_back_chunk(places, queries, grad, mixed, lse, tables, kv_list, dq, last, n_ctx):
    tok, width = queries.shape
    head = pl.BlockSpec((tok, HEAD_DIM), lambda h, p: (0, h))
    pair = pl.BlockSpec((2, tok, HEAD_DIM), lambda h, p: (0, 0, h))
    rows = pl.BlockSpec((1, tok, 128), lambda h, p: (h, 0, 0))
    table = pl.BlockSpec((tok, HEAD_DIM), lambda h, p: (0, 0))
    first = dq is None
    n = len(kv_list)
    pairs = tok * tok * n * HEADS
    out = pl.pallas_call(
        functools.partial(attend_back_kernel, n_ctx, n, first, last),
        grid_spec=pltpu.PrefetchScalarGridSpec(
            num_scalar_prefetch=1,
            grid=(HEADS,),
            in_specs=[head, head, head, rows, table, table] + [pair] * n + ([] if first else [head]),
            out_specs=[head] + [pair] * n,
        ),
        out_shape=[jax.ShapeDtypeStruct((tok, width), BF if last else F32)]
        + [jax.ShapeDtypeStruct((2, tok, width), F32 if s == 0 else BF) for s in range(n)],
        compiler_params=pltpu.CompilerParams(vmem_limit_bytes=VMEM_LIMIT // 2),
        cost_estimate=pl.CostEstimate(
            flops=10 * pairs * HEAD_DIM * 4, bytes_accessed=16 * tok * width, transcendentals=pairs
        ),
        name="attend_back",
    )(places, queries, grad, mixed, lse, *tables, *kv_list, *(() if first else (dq,)))
    return out[0], out[1:]


def expert_kernel(slots, na, nb, n_kept, e_ref, rank_ref, c0, *refs):
    c1, refs = refs[:nb], refs[nb:]
    g0, g1, refs = refs[0], refs[1 : 1 + nb], refs[1 + nb :]
    wr_ref, w1_ref, w2_ref = refs[:3]
    refs = refs[3 + n_kept :]
    d0, d1, refs = refs[:na], refs[na : na + nb], refs[na + nb :]
    dg_ref, x_ref, h_ref, dey_ref, deg_ref = refs[:5]
    y0, y1 = refs[5 : 5 + na], refs[5 + na :]
    half = c0.shape[2]
    tok = 2 * half
    experts = wr_ref.shape[0]
    me = e_ref[0]
    step = pl.program_id(0)
    picks, rows, grads, weights = [], [], [], []
    own = lax.broadcasted_iota(jnp.int32, (experts, tok), 0) == me
    slot = lax.broadcasted_iota(jnp.int32, (slots, tok), 0).astype(F32)
    for s in range(nb):
        tokens = jnp.concatenate([c0[0, s], c1[s][0]], axis=0)
        cot = jnp.concatenate([g0[0, s, 0], g1[s][0, 0]], axis=0)
        rank = rank_ref[0, s, 0]
        logits = dot(wr_ref[...], tokens, NT)
        logits = jnp.where(rank >= 0, logits, masked_value)
        raised = jnp.where(rank >= 0, jnp.exp(logits - jnp.max(logits, axis=0, keepdims=True)), 0.0)
        gates = raised / jnp.sum(raised, axis=0, keepdims=True)
        gate_row = jnp.sum(jnp.where(own, gates, 0.0), axis=0, keepdims=True)
        rank_row = jnp.sum(jnp.where(own, rank, 0.0), axis=0, keepdims=True)
        pick = jnp.where(slot == rank_row, 1.0, 0.0)
        weights.append(jnp.sum(pick * gate_row, axis=1, keepdims=True))
        pick_low = pick.astype(BF)
        picks.append((pick, pick_low))
        rows.append(dot(pick_low, tokens).astype(BF))
        grads.append(dot(pick_low, cot))
    x = jnp.concatenate(rows, axis=0)
    grad = jnp.concatenate(grads, axis=0)
    weight = jnp.concatenate(weights, axis=0)
    x_ref[...] = x
    dey = (weight * grad).astype(BF)
    dey_ref[...] = dey
    pre = dot(x, w1_ref[...])
    gate, up = pre[:, :FF], pre[:, FF:]
    sig = jax.nn.sigmoid(gate)
    act = gate * sig
    hidden = (act * up).astype(BF)
    h_ref[...] = hidden
    grad_hidden = dot(dey, w2_ref[...], NT)
    deg = jnp.concatenate(
        [
            (grad_hidden * up * sig * (1.0 + gate * (1.0 - sig))).astype(BF),
            (grad_hidden * act).astype(BF),
        ],
        axis=1,
    )
    deg_ref[...] = deg
    dec = dot(deg, w1_ref[...], NT).astype(BF)
    ey = dot(hidden, w2_ref[...]).astype(BF).astype(F32)
    dgate = jnp.sum(grad * ey, axis=1, keepdims=True)
    weighted = (weight * ey).astype(BF)
    d_first, y_first = [], []
    for s in range(nb):
        part = slice(s * slots, (s + 1) * slots)
        pick, pick_low = picks[s]
        back = dot(pick_low, dec[part], TN).astype(BF)
        d_first.append(back[:half])
        d1[s][0] = back[half:]
        back = dot(pick_low, weighted[part], TN).astype(BF)
        y_first.append(back[:half])
        y1[s][0, 0] = back[half:]
        dg_ref[0, s] = jnp.sum(pick * dgate[part], axis=0, keepdims=True)
    for k in range(na):

        @pl.when(step == k)
        def _(k=k):
            for s in range(nb):
                d0[k][s] = d_first[s]
                y0[k][0, s] = y_first[s]


def expert_chunk(chunk, nq, expert, ranks, c, g, router_t, w1, w2, kept, slots):
    na, nb, half, width = c[0].shape
    experts = router_t.shape[0]
    one = pl.BlockSpec((1, nb, half, width), lambda i, e: (i, 0, 0, 0))
    two = pl.BlockSpec((1, half, width), lambda i, e: (i, 0, 0))
    g_one = pl.BlockSpec((1, nb, 1, half, width), lambda i, e: (i, 0, chunk, 0, 0))
    g_two = pl.BlockSpec((1, 1, half, width), lambda i, e: (i, chunk, 0, 0))

    def fixed(shape):
        return pl.BlockSpec(shape, lambda i, e: (0,) * len(shape), pipeline_mode=pl.Buffered(1))

    def by_rows(n):
        return pl.BlockSpec((nb * slots, n), lambda i, e: (chunk * na + i, 0))

    n_rows = na * nb * slots
    kept_shapes = (
        [jax.ShapeDtypeStruct((nq * n_rows, n), BF) for n in (width, FF, width, 2 * FF)]
        + [jax.ShapeDtypeStruct((nq, nb, half, width), BF)] * na
        + [jax.ShapeDtypeStruct((nq, na, half, width), BF)] * nb
    )
    n_kept = 0 if kept is None else len(kept)
    n_in = 1 + 1 + (1 + nb) * 2 + 3
    n_out = na + nb + 1
    out = pl.pallas_call(
        functools.partial(expert_kernel, slots, na, nb, n_kept),
        grid_spec=pltpu.PrefetchScalarGridSpec(
            num_scalar_prefetch=1,
            grid=(na,),
            in_specs=[
                pl.BlockSpec((1, nb, 1, experts, 2 * half), lambda i, e: (i, 0, chunk, 0, 0)),
                one, *[two] * nb, g_one, *[g_two] * nb,
                fixed(router_t.shape), fixed(w1.shape), fixed(w2.shape),
                *[pl.BlockSpec(memory_space=pl.ANY)] * n_kept,
            ],
            out_specs=[
                *[pl.BlockSpec((nb, half, width), lambda i, e: (0, 0, 0))] * na,
                *[two] * nb,
                pl.BlockSpec((1, nb, 1, 2 * half), lambda i, e: (i, 0, 0, 0)),
                by_rows(width), by_rows(FF), by_rows(width), by_rows(2 * FF),
                *[pl.BlockSpec((1, nb, half, width), lambda i, e: (chunk, 0, 0, 0))] * na,
                *[pl.BlockSpec((1, 1, half, width), lambda i, e: (chunk, i, 0, 0))] * nb,
            ],
        ),
        out_shape=[jax.ShapeDtypeStruct((nb, half, width), BF)] * na
        + [jax.ShapeDtypeStruct((na, half, width), BF)] * nb
        + [jax.ShapeDtypeStruct((na, nb, 1, 2 * half), F32)]
        + kept_shapes,
        input_output_aliases={n_in + k: n_out + k for k in range(n_kept)},
        compiler_params=pltpu.CompilerParams(vmem_limit_bytes=VMEM_LIMIT),
        cost_estimate=pl.CostEstimate(
            flops=n_rows * width * FF * 12, bytes_accessed=30_000_000, transcendentals=n_rows * FF
        ),
        name="experts",
    )(expert, ranks, c[0], *c[1], g[0], *g[1], router_t, w1, w2, *(() if kept is None else kept))
    return out[:na], out[na : na + nb], out[na + nb], out[n_out:]


def body(
    n_experts,
    block_input,
    cotangent,
    routes,
    attn_gain,
    query_key_value_weight,
    attention_output_weight,
    ffn_gain,
    routing_weight,
    common_expert_gate_up_weight,
    common_expert_down_weight,
    expert_gate_up,
    expert_down,
):
    nq, nr, na, nb = (lax.axis_size(axis) for axis in ("q", "r", "a", "b"))
    q_at, r_at, a_at, b_at = (lax.axis_index(axis) for axis in ("q", "r", "a", "b"))
    n_ctx = nq * nr
    n_exp = na * nb
    ctx_rank = q_at * nr + r_at
    exp_rank = a_at * nb + b_at
    tok = block_input.shape[1]
    width = block_input.shape[2]
    half = tok // 2
    capacity = min(tok, 3 * TOP * tok // (2 * n_experts))
    slots = -(-capacity // 16) * 16
    row = jnp.arange(tok, dtype=jnp.int32)
    local_pos = jnp.where(
        row < half, ctx_rank * half + row, (2 * n_ctx - 1 - ctx_rank) * half + row - half
    )
    cosines, sines = rope_tables(local_pos, HEAD_DIM)
    sines = jnp.where(jnp.arange(HEAD_DIM)[None, :] < HEAD_DIM // 2, -sines, sines)
    tables = (cosines, sines)
    tokens_in = block_input[0].astype(F32)
    grad_low = cotangent[0]
    out_grad = grad_low.astype(F32)
    own_rows = query_key_value_weight.shape[0]
    down_rows = common_expert_down_weight.shape[0]

    zeros = jnp.zeros((own_rows, 127), BF)
    front = jnp.concatenate([query_key_value_weight, attn_gain[:, None], zeros], axis=1)
    front_q = ring_gather(front, "q")

    named = jnp.any(
        routes[0][:, :, None] == jnp.arange(n_experts, dtype=jnp.int32)[None, None, :], axis=1
    )
    before = (row[:, None] < row[None, :]).astype(BF)
    rank = dot(named.astype(BF).T, before)
    rank = jnp.where(named.T, rank, -1.0)
    ranks = jnp.stack(ring_gather(rank, "q"))
    ranks = jnp.stack(ring_gather(ranks, "b"))
    ranks = jnp.stack(ring_gather(ranks, "a"))

    rest = jnp.concatenate(
        [
            attention_output_weight,
            common_expert_gate_up_weight,
            common_expert_down_weight.reshape(own_rows, -1),
            ffn_gain[:, None],
            routing_weight,
            zeros[:, n_experts:],
        ],
        axis=1,
    )
    flat = common_expert_down_weight.size // own_rows
    g_q = ring_gather(after(grad_low, front_q[-1]), "q")
    rest_q = ring_gather(after(rest, g_q[-1]), "q")
    front_pieces, front_steps = dense_rings(front_q)
    rest_pieces, rest_steps = dense_rings([after(part, *front_pieces) for part in rest_q])
    g_stack = after(jnp.stack(g_q), *rest_pieces)
    g_one, g_two = plane_gather(g_stack)

    def own_expert(stack):
        rows = lax.all_to_all(stack, "q", split_axis=0, concat_axis=0, tiled=True)
        parts = ring_gather(rows, "r")
        kr = np.repeat(np.arange(nr, dtype=np.int32), nq)
        kq = np.tile(np.arange(nq, dtype=np.int32), nr)
        index = kq * nr + lax.rem(r_at - kr + nr, nr)
        return place(index.astype(jnp.int32), parts, [stack.shape[2]])[0]

    w2 = own_expert(after(expert_down, rest_q[-1]))

    qkv_weight, front_small = dense_place(front_pieces, front_steps, [3 * width, 128])
    gain_one = front_small[:, 0].astype(F32)
    inv_one = rms_scale(tokens_in)
    normed = (tokens_in * inv_one * gain_one).astype(BF)
    queries, kv_own = project(normed, qkv_weight, *tables)
    kv_q = ring_gather(kv_own, "q")
    kv_chunks = [ring_gather(part, "r") for part in kv_q]
    w1 = own_expert(after(expert_gate_up, kv_q[-1]))
    places = [
        jnp.stack(
            [ctx_rank]
            + [
                lax.rem(q_at - k + nq, nq) * nr + lax.rem(r_at - s + nr, nr)
                for s in range(nr)
            ]
        ).astype(jnp.int32)
        for k in range(nq)
    ]
    state = None
    for k in range(nq):
        state = attend_chunk(places[k], queries, kv_chunks[k], state, k == nq - 1, n_ctx)
    mixed, lse = state

    out_weight, shared_in, shared_out, rest_small = dense_place(
        rest_pieces, rest_steps, [width, 2 * FF, flat, 128]
    )
    shared_out = shared_out.reshape(-1, width)
    gain_two = rest_small[:, 0].astype(F32)
    router = rest_small[:, 1 : 1 + n_experts]
    residual = tokens_in + dot(mixed, out_weight)
    inv_two = rms_scale(residual)
    second = (residual * inv_two * gain_two).astype(BF)
    c_planes = [plane_gather(part) for part in ring_gather(second, "q")]
    expert = (exp_rank * nq + q_at).astype(jnp.int32).reshape(1)
    router_t = router.T
    kept = None
    dec_parts, dgates = [], []
    for k in range(nq):
        one, two, dgate, kept = expert_chunk(
            k, nq, expert, ranks, c_planes[k], (g_one, g_two), router_t, w1, w2, kept, slots
        )
        dec_parts.append((one, two))
        dgates.append(dgate.reshape(na * nb, tok))
    dec_sums = [None] * nq
    for k in list(range(1, nq)) + [0]:
        dec_sums[k] = plane_sum(*dec_parts[k])
    routed_grad = ring_sum(dec_sums, "q")
    y_one, y_two = kept[4 : 4 + na], kept[4 + na :]
    y_one = [after(y_one[0], routed_grad)] + [after(v, routed_grad) for v in y_one[1:]]
    y_two = [after(y_two[0], routed_grad)] + [after(v, routed_grad) for v in y_two[1:]]
    y_sums = plane_sum(y_one, y_two, 1)
    routed_sum = ring_sum([y_sums[k] for k in range(nq)], "q")

    shared_pre = dot(second, shared_in)
    shared_gate, shared_up = shared_pre[:, :FF], shared_pre[:, FF:]
    shared_sig = jax.nn.sigmoid(shared_gate)
    shared_hidden = (shared_gate * shared_sig * shared_up).astype(BF)
    layer_out = (residual + dot(shared_hidden, shared_out) + routed_sum).astype(BF)

    logits = jnp.where(named, dot(second, router), masked_value)
    raised = jnp.where(named, jnp.exp(logits - jnp.max(logits, axis=1, keepdims=True)), 0.0)
    gates = raised / jnp.sum(raised, axis=1, keepdims=True)
    n_all = nq * na * nb
    spot = np.arange(n_all, dtype=np.int32)
    spot = (
        lax.rem(q_at - spot // (na * nb) + nq, nq) * (na * nb)
        + lax.rem(a_at - spot // nb % na + na, na) * nb
        + lax.rem(b_at - spot % nb + nb, nb)
    )
    dgate = jnp.concatenate(dgates, axis=0)[spot]
    dgate = lax.all_to_all(dgate, ("q", "a", "b"), split_axis=0, concat_axis=0, tiled=True)
    dgate = jnp.swapaxes(dgate.reshape(nq, na * nb, tok), 0, 1).reshape(n_experts, tok).T
    grad_logits = gates * (dgate - jnp.sum(gates * dgate, axis=1, keepdims=True))
    grad_logits = grad_logits.astype(BF)

    shared_hidden_grad = dot(grad_low, shared_out, NT)
    shared_pre_grad = jnp.concatenate(
        [
            shared_hidden_grad * shared_up * shared_sig * (1.0 + shared_gate * (1.0 - shared_sig)),
            shared_hidden_grad * shared_gate * shared_sig,
        ],
        axis=1,
    ).astype(BF)
    second_grad = (
        dot(shared_pre_grad, shared_in, NT) + dot(grad_logits, router, NT) + routed_grad
    )
    ffn_gain_grad = jnp.sum(second_grad * residual * inv_two, axis=0)
    residual_grad = out_grad + norm_back(second_grad, residual, inv_two, gain_two)
    mixed_grad = residual_grad.astype(BF)
    heads_grad = dot(mixed_grad, out_weight, NT).astype(BF)

    dq = None
    moving = None
    for k in list(range(1, nq)) + [0]:
        dq, parts = attend_back_chunk(
            places[k], queries, heads_grad, mixed, lse, tables, kv_chunks[k], dq, k == 0, n_ctx
        )
        term = ring_sum(parts, "r")
        if k == 1:
            moving = term.astype(BF)
        elif k:
            moving = (shift(moving, "q").astype(F32) + term).astype(BF)
    kv_back = finish_keys(shift(moving, "q"), term, *tables)

    xs, hs, deys, degs = kept[:4]

    def expert_rows(whole):
        value = whole.reshape(nq, nr, -1, whole.shape[1])
        value = ring_sum(ring_blocks([value], "r", 1), "r").astype(BF)
        return lax.all_to_all(value, "q", split_axis=0, concat_axis=0, tiled=True).astype(F32)

    gate_up_grad = expert_rows(dot(xs, degs, TN).astype(BF))
    down_grad = expert_rows(dot(hs, deys, TN).astype(BF))

    rest_grad = dense_sum(
        [
            dot(mixed, mixed_grad, TN).astype(BF),
            dot(second, shared_pre_grad, TN).astype(BF),
            dot(shared_hidden, grad_low, TN).astype(BF).reshape(width, flat),
            jnp.concatenate(
                [
                    ffn_gain_grad[:, None],
                    dot(second, grad_logits, TN),
                    jnp.zeros((width, 127 - n_experts), F32),
                ],
                axis=1,
            ).astype(BF),
        ],
        own_rows,
    )
    query_grad = dense_sum([dot(normed, dq, TN).astype(BF)], own_rows)
    normed_grad = dot(dq, qkv_weight[:, :width], NT)
    normed_grad += dot(kv_back[0], qkv_weight[:, width : 2 * width], NT)
    normed_grad += dot(kv_back[1], qkv_weight[:, 2 * width :], NT)
    attn_gain_grad = jnp.sum(normed_grad * tokens_in * inv_one, axis=0)
    input_grad = residual_grad + norm_back(normed_grad, tokens_in, inv_one, gain_one)
    kv_weight_grad = dense_sum(
        [
            dot(normed, kv_back[0], TN).astype(BF),
            dot(normed, kv_back[1], TN).astype(BF),
            jnp.concatenate(
                [attn_gain_grad[:, None], jnp.zeros((width, 127), F32)], axis=1
            ).astype(BF),
        ],
        own_rows,
    )
    at_in, at_out = width + 2 * FF, width + 2 * FF + flat
    return (
        layer_out[None],
        input_grad[None],
        kv_weight_grad[:, 2 * width],
        jnp.concatenate([query_grad, kv_weight_grad[:, : 2 * width]], axis=1),
        rest_grad[:, :width],
        rest_grad[:, at_out],
        rest_grad[:, at_out + 1 : at_out + 1 + n_experts],
        rest_grad[:, width:at_in],
        rest_grad[:, at_in:at_out].reshape(down_rows, width),
        gate_up_grad,
        down_grad,
    )


def solution(mesh):
    n_ctx, n_exp = mesh.shape["ctx"], mesh.shape["exp"]

    def layer(*args):
        n_experts = args[10].shape[0]
        nq = n_experts // n_exp
        nb = 2
        fine = Mesh(
            np.asarray(mesh.devices).reshape(nq, n_ctx // nq, n_exp // nb, nb), ("q", "r", "a", "b")
        )
        ctx, exp, every = ("q", "r"), ("a", "b"), ("q", "r", "a", "b")
        tokens, flat, rows = P(exp, ctx, None), P(every), P(every, None)
        run = jax.shard_map(
            functools.partial(body, n_experts),
            mesh=fine,
            in_specs=(
                tokens, tokens, tokens, flat, rows, rows, flat, rows, rows, rows, tokens, tokens,
            ),
            out_specs=(tokens, tokens, flat, rows, rows, flat, rows, rows, rows, tokens, tokens),
            check_vma=False,
        )
        return run(*args)

    return layer
```

```python
import functools

import jax
import jax.numpy as jnp
import numpy as np
from jax import lax
from jax.experimental import pallas as pl
from jax.experimental.pallas import tpu as pltpu
from jax.sharding import Mesh
from jax.sharding import PartitionSpec as P

HEADS = 10
HEAD_DIM = 128
FF = 896
TOP = 7

norm_eps = 1e-06
rope_base = 10000.0
masked_value = -1e30
LOG2E = 1.4426950408889634

BF = jnp.bfloat16
F32 = jnp.float32
VMEM_LIMIT = 56 * 1024 * 1024


def rope_tables(positions, head_dim):
    halfway = head_dim // 2
    frequency = rope_base ** (-(jnp.arange(halfway).astype(F32) * 2.0 / head_dim))
    angles = positions.astype(F32)[:, None] * frequency[None, :]
    angles = jnp.concatenate([angles, angles], axis=1)
    return (jnp.cos(angles), jnp.sin(angles))


def rms_scale(values):
    return lax.rsqrt(jnp.mean(values * values, axis=1, keepdims=True) + norm_eps)


def norm_back(grad_in, values, inv_rms, gain_vec):
    scaled = grad_in * gain_vec
    return inv_rms * scaled - values * inv_rms**3 * jnp.mean(scaled * values, axis=1, keepdims=True)


def dot(a, b, dims=((1,), (0,))):
    return lax.dot_general(a, b, (dims, ((), ())), preferred_element_type=F32)


NT = ((1,), (1,))
TN = ((0,), (0,))


def shift(value, axis):
    n = lax.axis_size(axis)
    return lax.ppermute(value, axis, [(i, (i + 1) % n) for i in range(n)])


def ring_gather(value, axis):
    parts = [value]
    for _ in range(1, lax.axis_size(axis)):
        parts.append(shift(parts[-1], axis))
    return parts


def ring_sum(blocks, axis):
    n = len(blocks)
    if n == 1:
        return blocks[0].astype(F32)
    moving = blocks[1].astype(BF)
    for k in range(2, n):
        moving = (shift(moving, axis).astype(F32) + blocks[k].astype(F32)).astype(BF)
    return shift(moving, axis).astype(F32) + blocks[0].astype(F32)


def ring_blocks(arrays, axis, dim):
    n = lax.axis_size(axis)
    index = lax.axis_index(axis)
    out = []
    for k in range(n):
        at = lax.rem(index - k + n, n)
        parts = [lax.dynamic_index_in_dim(v, at, dim, keepdims=False) for v in arrays]
        out.append(parts[0] if len(parts) == 1 else jnp.concatenate(parts, axis=-1))
    return out


def after(value, *events):
    return lax.optimization_barrier((value, *events))[0]


def place_kernel(counts, columns, index_ref, *refs):
    n = len(counts)
    pieces, outs, sems = refs[:n], refs[n:-1], refs[-1]
    t = 0
    for piece, count in zip(pieces, counts):
        for j in range(count):
            at = index_ref[t]
            t += 1
            for o, (low, high) in enumerate(columns):
                pltpu.make_async_copy(
                    piece.at[j, :, pl.ds(low, high - low)], outs[o].at[at], sems.at[o]
                ).start()
    for o in range(len(columns)):
        pltpu.make_async_copy(outs[o], outs[o], sems.at[o]).wait()


def place(index, pieces, widths):
    rows, total = pieces[0].shape[-2:]
    pieces = [piece.reshape(-1, rows, total) for piece in pieces]
    counts = [piece.shape[0] for piece in pieces]
    edges = np.cumsum([0] + list(widths))
    columns = [(int(low), int(high)) for low, high in zip(edges[:-1], edges[1:])]
    n = sum(counts)
    outs = pl.pallas_call(
        functools.partial(place_kernel, counts, columns),
        in_specs=[pl.BlockSpec(memory_space=pltpu.SMEM)]
        + [pl.BlockSpec(memory_space=pl.ANY)] * len(pieces),
        out_specs=[pl.BlockSpec(memory_space=pltpu.VMEM)] * len(widths),
        scratch_shapes=[pltpu.SemaphoreType.DMA((len(widths),))],
        out_shape=[jax.ShapeDtypeStruct((n, rows, w), pieces[0].dtype) for w in widths],
        compiler_params=pltpu.CompilerParams(vmem_limit_bytes=VMEM_LIMIT // 2),
        cost_estimate=pl.CostEstimate(
            flops=0, bytes_accessed=4 * n * rows * total, transcendentals=0
        ),
        name="place",
    )(index, *pieces)
    return [out.reshape(n * rows, w) for out, w in zip(outs, widths)]


def dense_rings(along_q):
    half = len(along_q) // 2
    na, nb = lax.axis_size("a"), lax.axis_size("b")
    one = jnp.stack(ring_gather(jnp.stack(along_q[:half]), "b"))
    two = jnp.stack(ring_gather(jnp.stack(along_q[half:]), "a"))
    pieces = ring_gather(one, "a") + ring_gather(two, "b")
    steps = [[(kq, ka, kb) for kb in range(nb) for kq in range(half)] for ka in range(na)]
    steps += [
        [(kq, ka, kb) for ka in range(na) for kq in range(half, len(along_q))] for kb in range(nb)
    ]
    return pieces, steps


def dense_place(pieces, steps, widths):
    nq, nr, na, nb = (lax.axis_size(axis) for axis in ("q", "r", "a", "b"))
    moved = [ring_gather(piece, "r") for piece in pieces]
    order = [(k, *s) for k in range(nr) for part in steps for s in part]
    kr, kq, ka, kb = (np.array(column, np.int32) for column in zip(*order))
    index = lax.rem(lax.axis_index("q") - kq + nq, nq) * nr
    index = index + lax.rem(lax.axis_index("r") - kr + nr, nr)
    index = index * na + lax.rem(lax.axis_index("a") - ka + na, na)
    index = index * nb + lax.rem(lax.axis_index("b") - kb + nb, nb)
    arrays = [moved[p][k] for k in range(nr) for p in range(len(pieces))]
    return place(index.astype(jnp.int32), arrays, widths)


def dense_sum(wholes, n_rows):
    nq, nr, na, nb = (lax.axis_size(axis) for axis in ("q", "r", "a", "b"))
    values = [whole.reshape(nq, nr, na, nb, n_rows, whole.shape[1]) for whole in wholes]
    value = ring_sum(ring_blocks(values, "r", 1), "r").astype(BF)
    half = nq // 2
    one, two = value[:half], value[half:]
    one = ring_sum(ring_blocks([one], "a", 1), "a").astype(BF)
    two = ring_sum(ring_blocks([two], "b", 2), "b").astype(BF)
    one = ring_sum(ring_blocks([one], "b", 1), "b")
    two = ring_sum(ring_blocks([two], "a", 1), "a")
    value = jnp.concatenate([one, two], axis=0).astype(BF)
    return ring_sum(ring_blocks([value], "q", 0), "q")


def plane_gather(rows):
    half = rows.shape[-2] // 2
    one = jnp.stack(ring_gather(rows[..., :half, :], "b"))
    two = jnp.stack(ring_gather(rows[..., half:, :], "a"))
    return (jnp.stack(ring_gather(one, "a")), ring_gather(two, "b"))


def plane_sum(one, two, dim=0):
    first = ring_sum(one, "a")
    second = ring_sum(two, "b")
    first = ring_sum([lax.index_in_dim(first, k, dim, False) for k in range(len(two))], "b")
    second = ring_sum([lax.index_in_dim(second, k, dim, False) for k in range(len(one))], "a")
    return jnp.concatenate([first, second], axis=-2)


def project_kernel(n_query, x_ref, w_ref, cos_ref, sin_ref, q_ref, kv_ref):
    j = pl.program_id(0)
    made = dot(x_ref[...], w_ref[...])

    def turned():
        parts = []
        for low in range(0, made.shape[1], HEAD_DIM):
            u = made[:, low : low + HEAD_DIM]
            parts.append(u * cos_ref[...] + pltpu.roll(u, HEAD_DIM // 2, 1) * sin_ref[...])
        return jnp.concatenate(parts, axis=1).astype(BF)

    @pl.when(j < n_query)
    def _():
        q_ref[...] = turned()

    @pl.when((j >= n_query) & (j < 2 * n_query))
    def _():
        kv_ref[0] = turned()

    @pl.when(j >= 2 * n_query)
    def _():
        kv_ref[0] = made.astype(BF)


def project(normed, weight, cosines, signed_sine):
    tok, width = normed.shape
    block = 2 * HEAD_DIM
    n = width // block
    table = pl.BlockSpec((tok, HEAD_DIM), lambda j: (0, 0))
    return pl.pallas_call(
        functools.partial(project_kernel, n),
        grid=(3 * n,),
        in_specs=[
            pl.BlockSpec((tok, width), lambda j: (0, 0)),
            pl.BlockSpec((width, block), lambda j: (0, j)),
            table,
            table,
        ],
        out_specs=[
            pl.BlockSpec((tok, block), lambda j: (0, jnp.minimum(j, n - 1))),
            pl.BlockSpec(
                (1, tok, block),
                lambda j: (jnp.maximum(j - n, 0) // n, 0, jnp.maximum(j - n, 0) % n),
            ),
        ],
        out_shape=[
            jax.ShapeDtypeStruct((tok, width), BF),
            jax.ShapeDtypeStruct((2, tok, width), BF),
        ],
        compiler_params=pltpu.CompilerParams(vmem_limit_bytes=VMEM_LIMIT // 2),
        cost_estimate=pl.CostEstimate(
            flops=6 * tok * width * width, bytes_accessed=6 * width * width, transcendentals=0
        ),
        name="project",
    )(normed, weight, cosines, signed_sine)


def turn_back(grad, cos, signed_sine):
    return grad * cos - pltpu.roll(grad, HEAD_DIM // 2, 1) * signed_sine


def finish_kernel(moved_ref, own_ref, cos_ref, sin_ref, out_ref):
    keys = moved_ref[0].astype(F32) + own_ref[0]
    out_ref[0] = turn_back(keys, cos_ref[...], sin_ref[...]).astype(BF)
    out_ref[1] = (moved_ref[1].astype(F32) + own_ref[1]).astype(BF)


def finish_keys(moved, own, cosines, signed_sine):
    _, tok, width = own.shape
    pair = pl.BlockSpec((2, tok, HEAD_DIM), lambda h: (0, 0, h))
    table = pl.BlockSpec((tok, HEAD_DIM), lambda h: (0, 0))
    return pl.pallas_call(
        finish_kernel,
        grid=(width // HEAD_DIM,),
        in_specs=[pair, pair, table, table],
        out_specs=pair,
        out_shape=jax.ShapeDtypeStruct((2, tok, width), BF),
        cost_estimate=pl.CostEstimate(
            flops=10 * tok * width, bytes_accessed=16 * tok * width, transcendentals=0
        ),
        name="finish_keys",
    )(moved, own, cosines, signed_sine)


def allowed_mask(own, other, n_ctx, half):
    row = lax.broadcasted_iota(jnp.int32, (2 * half, 2 * half), 0)
    col = lax.broadcasted_iota(jnp.int32, (2 * half, 2 * half), 1)
    last = 2 * n_ctx - 1
    query = row + jnp.where(row < half, own * half, (last - own) * half - half)
    key = col + jnp.where(col < half, other * half, (last - other) * half - half)
    return key <= query


def attend_kernel(n_ctx, n_src, first, last, place_ref, q_ref, *refs):
    kv_refs, refs = refs[:n_src], refs[n_src:]
    if not first:
        acc_in, ml_in = refs[:2]
        refs = refs[2:]
    out_ref, ml_ref = refs
    queries = q_ref[...]
    tok = queries.shape[0]
    scores = []
    for s in range(n_src):
        raw = dot(queries, kv_refs[s][0], NT) * (HEAD_DIM ** (-0.5) * LOG2E)
        mask = allowed_mask(place_ref[0], place_ref[1 + s], n_ctx, tok // 2)
        scores.append(jnp.where(mask, raw, masked_value))
    peak = functools.reduce(jnp.maximum, [jnp.max(s, axis=1, keepdims=True) for s in scores])
    if not first:
        old_peak = ml_in[0][:, 0:1]
        old_sum = ml_in[0][:, 64:65]
        peak = jnp.maximum(peak, old_peak)
    total = jnp.zeros_like(peak)
    mixed = jnp.zeros((tok, HEAD_DIM), F32)
    for s in range(n_src):
        raised = jnp.exp2(scores[s] - peak)
        total = total + jnp.sum(raised, axis=1, keepdims=True)
        mixed = mixed + dot(raised.astype(BF), kv_refs[s][1])
    if not first:
        decay = jnp.exp2(old_peak - peak)
        total = total + old_sum * decay
        mixed = mixed + acc_in[...] * decay
    if last:
        out_ref[...] = (mixed / total).astype(BF)
        ml_ref[0] = jnp.broadcast_to(peak + jnp.log2(total), (tok, 128))
    else:
        out_ref[...] = mixed
        lane = lax.broadcasted_iota(jnp.int32, (tok, 128), 1)
        ml_ref[0] = jnp.where(lane < 64, peak, total)


def attend_chunk(places, queries, kv_list, state, last, n_ctx):
    tok, width = queries.shape
    head = pl.BlockSpec((tok, HEAD_DIM), lambda h, p: (0, h))
    pair = pl.BlockSpec((2, tok, HEAD_DIM), lambda h, p: (0, 0, h))
    rows = pl.BlockSpec((1, tok, 128), lambda h, p: (h, 0, 0))
    first = state is None
    n = len(kv_list)
    pairs = tok * tok * n * HEADS
    return pl.pallas_call(
        functools.partial(attend_kernel, n_ctx, n, first, last),
        grid_spec=pltpu.PrefetchScalarGridSpec(
            num_scalar_prefetch=1,
            grid=(HEADS,),
            in_specs=[head] + [pair] * n + ([] if first else [head, rows]),
            out_specs=[head, rows],
        ),
        out_shape=[
            jax.ShapeDtypeStruct((tok, width), BF if last else F32),
            jax.ShapeDtypeStruct((HEADS, tok, 128), F32),
        ],
        compiler_params=pltpu.CompilerParams(vmem_limit_bytes=VMEM_LIMIT // 2),
        cost_estimate=pl.CostEstimate(
            flops=4 * pairs * HEAD_DIM * 4, bytes_accessed=8 * tok * width, transcendentals=pairs
        ),
        name="attend",
    )(places, queries, *kv_list, *(() if first else state))


def attend_back_kernel(
    n_ctx, n_src, first, last, place_ref, q_ref, do_ref, o_ref, lse_ref, cos_ref, sin_ref, *refs
):
    kv_refs, refs = refs[:n_src], refs[n_src:]
    if not first:
        dq_in, refs = refs[0], refs[1:]
    dq_ref, dkv_refs = refs[0], refs[1:]
    queries = q_ref[...]
    grad = do_ref[...]
    tok = queries.shape[0]
    lse = lse_ref[0][:, 0:1]
    delta = jnp.sum(grad.astype(F32) * o_ref[...].astype(F32), axis=1, keepdims=True)
    scale = HEAD_DIM ** (-0.5)
    grad_query = jnp.zeros((tok, HEAD_DIM), F32)
    for s in range(n_src):
        keys, values = kv_refs[s][0], kv_refs[s][1]
        raw = dot(queries, keys, NT) * (scale * LOG2E)
        mask = allowed_mask(place_ref[0], place_ref[1 + s], n_ctx, tok // 2)
        probs = jnp.exp2(jnp.where(mask, raw, masked_value) - lse)
        grad_probs = dot(grad, values, NT)
        grad_scores = (probs * (grad_probs - delta)).astype(BF)
        grad_query = grad_query + dot(grad_scores, keys)
        dkv_refs[s][0] = (dot(grad_scores, queries, TN) * scale).astype(dkv_refs[s].dtype)
        dkv_refs[s][1] = dot(probs.astype(BF), grad, TN).astype(dkv_refs[s].dtype)
    grad_query = grad_query * scale
    if not first:
        grad_query = grad_query + dq_in[...]
    if last:
        grad_query = turn_back(grad_query, cos_ref[...], sin_ref[...]).astype(BF)
    dq_ref[...] = grad_query


def attend_back_chunk(places, queries, grad, mixed, lse, tables, kv_list, dq, last, n_ctx):
    tok, width = queries.shape
    head = pl.BlockSpec((tok, HEAD_DIM), lambda h, p: (0, h))
    pair = pl.BlockSpec((2, tok, HEAD_DIM), lambda h, p: (0, 0, h))
    rows = pl.BlockSpec((1, tok, 128), lambda h, p: (h, 0, 0))
    table = pl.BlockSpec((tok, HEAD_DIM), lambda h, p: (0, 0))
    first = dq is None
    n = len(kv_list)
    pairs = tok * tok * n * HEADS
    out = pl.pallas_call(
        functools.partial(attend_back_kernel, n_ctx, n, first, last),
        grid_spec=pltpu.PrefetchScalarGridSpec(
            num_scalar_prefetch=1,
            grid=(HEADS,),
            in_specs=[head, head, head, rows, table, table] + [pair] * n + ([] if first else [head]),
            out_specs=[head] + [pair] * n,
        ),
        out_shape=[jax.ShapeDtypeStruct((tok, width), BF if last else F32)]
        + [jax.ShapeDtypeStruct((2, tok, width), F32 if s == 0 else BF) for s in range(n)],
        compiler_params=pltpu.CompilerParams(vmem_limit_bytes=VMEM_LIMIT // 2),
        cost_estimate=pl.CostEstimate(
            flops=10 * pairs * HEAD_DIM * 4, bytes_accessed=16 * tok * width, transcendentals=pairs
        ),
        name="attend_back",
    )(places, queries, grad, mixed, lse, *tables, *kv_list, *(() if first else (dq,)))
    return out[0], out[1:]


def expert_kernel(slots, na, nb, n_kept, e_ref, rank_ref, c0, *refs):
    c1, refs = refs[:nb], refs[nb:]
    g0, g1, refs = refs[0], refs[1 : 1 + nb], refs[1 + nb :]
    wr_ref, w1_ref, w2_ref = refs[:3]
    refs = refs[3 + n_kept :]
    d0, d1, refs = refs[:na], refs[na : na + nb], refs[na + nb :]
    dg_ref, x_ref, h_ref, dey_ref, deg_ref = refs[:5]
    y0, y1 = refs[5 : 5 + na], refs[5 + na :]
    half = c0.shape[2]
    tok = 2 * half
    experts = wr_ref.shape[0]
    me = e_ref[0]
    step = pl.program_id(0)
    picks, rows, grads, weights = [], [], [], []
    own = lax.broadcasted_iota(jnp.int32, (experts, tok), 0) == me
    slot = lax.broadcasted_iota(jnp.int32, (slots, tok), 0).astype(F32)
    for s in range(nb):
        tokens = jnp.concatenate([c0[0, s], c1[s][0]], axis=0)
        cot = jnp.concatenate([g0[0, s, 0], g1[s][0, 0]], axis=0)
        rank = rank_ref[0, s, 0]
        logits = dot(wr_ref[...], tokens, NT)
        logits = jnp.where(rank >= 0, logits, masked_value)
        raised = jnp.where(rank >= 0, jnp.exp(logits - jnp.max(logits, axis=0, keepdims=True)), 0.0)
        gates = raised / jnp.sum(raised, axis=0, keepdims=True)
        gate_row = jnp.sum(jnp.where(own, gates, 0.0), axis=0, keepdims=True)
        rank_row = jnp.sum(jnp.where(own, rank, 0.0), axis=0, keepdims=True)
        pick = jnp.where(slot == rank_row, 1.0, 0.0)
        weights.append(jnp.sum(pick * gate_row, axis=1, keepdims=True))
        pick_low = pick.astype(BF)
        picks.append((pick, pick_low))
        rows.append(dot(pick_low, tokens).astype(BF))
        grads.append(dot(pick_low, cot))
    x = jnp.concatenate(rows, axis=0)
    grad = jnp.concatenate(grads, axis=0)
    weight = jnp.concatenate(weights, axis=0)
    x_ref[...] = x
    dey = (weight * grad).astype(BF)
    dey_ref[...] = dey
    pre = dot(x, w1_ref[...])
    gate, up = pre[:, :FF], pre[:, FF:]
    sig = jax.nn.sigmoid(gate)
    act = gate * sig
    hidden = (act * up).astype(BF)
    h_ref[...] = hidden
    grad_hidden = dot(dey, w2_ref[...], NT)
    deg = jnp.concatenate(
        [
            (grad_hidden * up * sig * (1.0 + gate * (1.0 - sig))).astype(BF),
            (grad_hidden * act).astype(BF),
        ],
        axis=1,
    )
    deg_ref[...] = deg
    dec = dot(deg, w1_ref[...], NT).astype(BF)
    ey = dot(hidden, w2_ref[...]).astype(BF).astype(F32)
    dgate = jnp.sum(grad * ey, axis=1, keepdims=True)
    weighted = (weight * ey).astype(BF)
    d_first, y_first = [], []
    for s in range(nb):
        part = slice(s * slots, (s + 1) * slots)
        pick, pick_low = picks[s]
        back = dot(pick_low, dec[part], TN).astype(BF)
        d_first.append(back[:half])
        d1[s][0] = back[half:]
        back = dot(pick_low, weighted[part], TN).astype(BF)
        y_first.append(back[:half])
        y1[s][0, 0] = back[half:]
        dg_ref[0, s] = jnp.sum(pick * dgate[part], axis=0, keepdims=True)
    for k in range(na):

        @pl.when(step == k)
        def _(k=k):
            for s in range(nb):
                d0[k][s] = d_first[s]
                y0[k][0, s] = y_first[s]


def expert_chunk(chunk, nq, expert, ranks, c, g, router_t, w1, w2, kept, slots):
    na, nb, half, width = c[0].shape
    experts = router_t.shape[0]
    one = pl.BlockSpec((1, nb, half, width), lambda i, e: (i, 0, 0, 0))
    two = pl.BlockSpec((1, half, width), lambda i, e: (i, 0, 0))
    g_one = pl.BlockSpec((1, nb, 1, half, width), lambda i, e: (i, 0, chunk, 0, 0))
    g_two = pl.BlockSpec((1, 1, half, width), lambda i, e: (i, chunk, 0, 0))

    def fixed(shape):
        return pl.BlockSpec(shape, lambda i, e: (0,) * len(shape), pipeline_mode=pl.Buffered(1))

    def by_rows(n):
        return pl.BlockSpec((nb * slots, n), lambda i, e: (chunk * na + i, 0))

    n_rows = na * nb * slots
    kept_shapes = (
        [jax.ShapeDtypeStruct((nq * n_rows, n), BF) for n in (width, FF, width, 2 * FF)]
        + [jax.ShapeDtypeStruct((nq, nb, half, width), BF)] * na
        + [jax.ShapeDtypeStruct((nq, na, half, width), BF)] * nb
    )
    n_kept = 0 if kept is None else len(kept)
    n_in = 1 + 1 + (1 + nb) * 2 + 3
    n_out = na + nb + 1
    out = pl.pallas_call(
        functools.partial(expert_kernel, slots, na, nb, n_kept),
        grid_spec=pltpu.PrefetchScalarGridSpec(
            num_scalar_prefetch=1,
            grid=(na,),
            in_specs=[
                pl.BlockSpec((1, nb, 1, experts, 2 * half), lambda i, e: (i, 0, chunk, 0, 0)),
                one, *[two] * nb, g_one, *[g_two] * nb,
                fixed(router_t.shape), fixed(w1.shape), fixed(w2.shape),
                *[pl.BlockSpec(memory_space=pl.ANY)] * n_kept,
            ],
            out_specs=[
                *[pl.BlockSpec((nb, half, width), lambda i, e: (0, 0, 0))] * na,
                *[two] * nb,
                pl.BlockSpec((1, nb, 1, 2 * half), lambda i, e: (i, 0, 0, 0)),
                by_rows(width), by_rows(FF), by_rows(width), by_rows(2 * FF),
                *[pl.BlockSpec((1, nb, half, width), lambda i, e: (chunk, 0, 0, 0))] * na,
                *[pl.BlockSpec((1, 1, half, width), lambda i, e: (chunk, i, 0, 0))] * nb,
            ],
        ),
        out_shape=[jax.ShapeDtypeStruct((nb, half, width), BF)] * na
        + [jax.ShapeDtypeStruct((na, half, width), BF)] * nb
        + [jax.ShapeDtypeStruct((na, nb, 1, 2 * half), F32)]
        + kept_shapes,
        input_output_aliases={n_in + k: n_out + k for k in range(n_kept)},
        compiler_params=pltpu.CompilerParams(vmem_limit_bytes=VMEM_LIMIT),
        cost_estimate=pl.CostEstimate(
            flops=n_rows * width * FF * 12, bytes_accessed=30_000_000, transcendentals=n_rows * FF
        ),
        name="experts",
    )(expert, ranks, c[0], *c[1], g[0], *g[1], router_t, w1, w2, *(() if kept is None else kept))
    return out[:na], out[na : na + nb], out[na + nb], out[n_out:]


def body(
    n_experts,
    block_input,
    cotangent,
    routes,
    attn_gain,
    query_key_value_weight,
    attention_output_weight,
    ffn_gain,
    routing_weight,
    common_expert_gate_up_weight,
    common_expert_down_weight,
    expert_gate_up,
    expert_down,
):
    nq, nr, na, nb = (lax.axis_size(axis) for axis in ("q", "r", "a", "b"))
    q_at, r_at, a_at, b_at = (lax.axis_index(axis) for axis in ("q", "r", "a", "b"))
    n_ctx = nq * nr
    n_exp = na * nb
    ctx_rank = q_at * nr + r_at
    exp_rank = a_at * nb + b_at
    tok = block_input.shape[1]
    width = block_input.shape[2]
    half = tok // 2
    capacity = min(tok, 3 * TOP * tok // (2 * n_experts))
    slots = -(-capacity // 16) * 16
    row = jnp.arange(tok, dtype=jnp.int32)
    local_pos = jnp.where(
        row < half, ctx_rank * half + row, (2 * n_ctx - 1 - ctx_rank) * half + row - half
    )
    cosines, sines = rope_tables(local_pos, HEAD_DIM)
    sines = jnp.where(jnp.arange(HEAD_DIM)[None, :] < HEAD_DIM // 2, -sines, sines)
    tables = (cosines, sines)
    tokens_in = block_input[0].astype(F32)
    grad_low = cotangent[0]
    out_grad = grad_low.astype(F32)
    own_rows = query_key_value_weight.shape[0]
    down_rows = common_expert_down_weight.shape[0]

    zeros = jnp.zeros((own_rows, 127), BF)
    front = jnp.concatenate([query_key_value_weight, attn_gain[:, None], zeros], axis=1)
    front_q = ring_gather(front, "q")

    named = jnp.any(
        routes[0][:, :, None] == jnp.arange(n_experts, dtype=jnp.int32)[None, None, :], axis=1
    )
    before = (row[:, None] < row[None, :]).astype(BF)
    rank = dot(named.astype(BF).T, before)
    rank = jnp.where(named.T, rank, -1.0)
    ranks = jnp.stack(ring_gather(rank, "q"))
    ranks = jnp.stack(ring_gather(ranks, "b"))
    ranks = jnp.stack(ring_gather(ranks, "a"))

    rest = jnp.concatenate(
        [
            attention_output_weight,
            common_expert_gate_up_weight,
            common_expert_down_weight.reshape(own_rows, -1),
            ffn_gain[:, None],
            routing_weight,
            zeros[:, n_experts:],
        ],
        axis=1,
    )
    flat = common_expert_down_weight.size // own_rows
    g_q = ring_gather(after(grad_low, front_q[-1]), "q")
    rest_q = ring_gather(after(rest, g_q[-1]), "q")
    front_pieces, front_steps = dense_rings(front_q)
    rest_pieces, rest_steps = dense_rings([after(part, *front_pieces) for part in rest_q])
    g_stack = after(jnp.stack(g_q), *rest_pieces)
    g_one, g_two = plane_gather(g_stack)

    def own_expert(stack):
        rows = lax.all_to_all(stack, "q", split_axis=0, concat_axis=0, tiled=True)
        parts = ring_gather(rows, "r")
        kr = np.repeat(np.arange(nr, dtype=np.int32), nq)
        kq = np.tile(np.arange(nq, dtype=np.int32), nr)
        index = kq * nr + lax.rem(r_at - kr + nr, nr)
        return place(index.astype(jnp.int32), parts, [stack.shape[2]])[0]

    w2 = own_expert(after(expert_down, rest_q[-1]))

    qkv_weight, front_small = dense_place(front_pieces, front_steps, [3 * width, 128])
    gain_one = front_small[:, 0].astype(F32)
    inv_one = rms_scale(tokens_in)
    normed = (tokens_in * inv_one * gain_one).astype(BF)
    queries, kv_own = project(normed, qkv_weight, *tables)
    kv_q = ring_gather(kv_own, "q")
    kv_chunks = [ring_gather(part, "r") for part in kv_q]
    w1 = own_expert(after(expert_gate_up, kv_q[-1]))
    places = [
        jnp.stack(
            [ctx_rank]
            + [
                lax.rem(q_at - k + nq, nq) * nr + lax.rem(r_at - s + nr, nr)
                for s in range(nr)
            ]
        ).astype(jnp.int32)
        for k in range(nq)
    ]
    state = None
    for k in range(nq):
        state = attend_chunk(places[k], queries, kv_chunks[k], state, k == nq - 1, n_ctx)
    mixed, lse = state

    out_weight, shared_in, shared_out, rest_small = dense_place(
        rest_pieces, rest_steps, [width, 2 * FF, flat, 128]
    )
    shared_out = shared_out.reshape(-1, width)
    gain_two = rest_small[:, 0].astype(F32)
    router = rest_small[:, 1 : 1 + n_experts]
    residual = tokens_in + dot(mixed, out_weight)
    inv_two = rms_scale(residual)
    second = (residual * inv_two * gain_two).astype(BF)
    c_planes = [plane_gather(part) for part in ring_gather(second, "q")]
    expert = (exp_rank * nq + q_at).astype(jnp.int32).reshape(1)
    router_t = router.T
    kept = None
    dec_parts, dgates = [], []
    for k in range(nq):
        one, two, dgate, kept = expert_chunk(
            k, nq, expert, ranks, c_planes[k], (g_one, g_two), router_t, w1, w2, kept, slots
        )
        dec_parts.append((one, two))
        dgates.append(dgate.reshape(na * nb, tok))
    dec_sums = [None] * nq
    for k in list(range(1, nq)) + [0]:
        dec_sums[k] = plane_sum(*dec_parts[k])
    routed_grad = ring_sum(dec_sums, "q")
    y_one, y_two = kept[4 : 4 + na], kept[4 + na :]
    y_one = [after(y_one[0], routed_grad)] + [after(v, routed_grad) for v in y_one[1:]]
    y_two = [after(y_two[0], routed_grad)] + [after(v, routed_grad) for v in y_two[1:]]
    y_sums = plane_sum(y_one, y_two, 1)
    routed_sum = ring_sum([y_sums[k] for k in range(nq)], "q")

    shared_pre = dot(second, shared_in)
    shared_gate, shared_up = shared_pre[:, :FF], shared_pre[:, FF:]
    shared_sig = jax.nn.sigmoid(shared_gate)
    shared_hidden = (shared_gate * shared_sig * shared_up).astype(BF)
    layer_out = (residual + dot(shared_hidden, shared_out) + routed_sum).astype(BF)

    logits = jnp.where(named, dot(second, router), masked_value)
    raised = jnp.where(named, jnp.exp(logits - jnp.max(logits, axis=1, keepdims=True)), 0.0)
    gates = raised / jnp.sum(raised, axis=1, keepdims=True)
    n_all = nq * na * nb
    spot = np.arange(n_all, dtype=np.int32)
    spot = (
        lax.rem(q_at - spot // (na * nb) + nq, nq) * (na * nb)
        + lax.rem(a_at - spot // nb % na + na, na) * nb
        + lax.rem(b_at - spot % nb + nb, nb)
    )
    dgate = jnp.concatenate(dgates, axis=0)[spot]
    dgate = lax.all_to_all(dgate, ("q", "a", "b"), split_axis=0, concat_axis=0, tiled=True)
    dgate = jnp.swapaxes(dgate.reshape(nq, na * nb, tok), 0, 1).reshape(n_experts, tok).T
    grad_logits = gates * (dgate - jnp.sum(gates * dgate, axis=1, keepdims=True))
    grad_logits = grad_logits.astype(BF)

    shared_hidden_grad = dot(grad_low, shared_out, NT)
    shared_pre_grad = jnp.concatenate(
        [
            shared_hidden_grad * shared_up * shared_sig * (1.0 + shared_gate * (1.0 - shared_sig)),
            shared_hidden_grad * shared_gate * shared_sig,
        ],
        axis=1,
    ).astype(BF)
    second_grad = (
        dot(shared_pre_grad, shared_in, NT) + dot(grad_logits, router, NT) + routed_grad
    )
    ffn_gain_grad = jnp.sum(second_grad * residual * inv_two, axis=0)
    residual_grad = out_grad + norm_back(second_grad, residual, inv_two, gain_two)
    mixed_grad = residual_grad.astype(BF)
    heads_grad = dot(mixed_grad, out_weight, NT).astype(BF)

    dq = None
    moving = None
    for k in list(range(1, nq)) + [0]:
        dq, parts = attend_back_chunk(
            places[k], queries, heads_grad, mixed, lse, tables, kv_chunks[k], dq, k == 0, n_ctx
        )
        term = ring_sum(parts, "r")
        if k == 1:
            moving = term.astype(BF)
        elif k:
            moving = (shift(moving, "q").astype(F32) + term).astype(BF)
    kv_back = finish_keys(shift(moving, "q"), term, *tables)

    xs, hs, deys, degs = kept[:4]

    def expert_rows(whole):
        value = whole.reshape(nq, nr, -1, whole.shape[1])
        value = ring_sum(ring_blocks([value], "r", 1), "r").astype(BF)
        return lax.all_to_all(value, "q", split_axis=0, concat_axis=0, tiled=True).astype(F32)

    gate_up_grad = expert_rows(dot(xs, degs, TN).astype(BF))
    down_grad = expert_rows(dot(hs, deys, TN).astype(BF))

    rest_grad = dense_sum(
        [
            dot(mixed, mixed_grad, TN).astype(BF),
            dot(second, shared_pre_grad, TN).astype(BF),
            dot(shared_hidden, grad_low, TN).astype(BF).reshape(width, flat),
            jnp.concatenate(
                [
                    ffn_gain_grad[:, None],
                    dot(second, grad_logits, TN),
                    jnp.zeros((width, 127 - n_experts), F32),
                ],
                axis=1,
            ).astype(BF),
        ],
        own_rows,
    )
    query_grad = dense_sum([dot(normed, dq, TN).astype(BF)], own_rows)
    normed_grad = dot(dq, qkv_weight[:, :width], NT)
    normed_grad += dot(kv_back[0], qkv_weight[:, width : 2 * width], NT)
    normed_grad += dot(kv_back[1], qkv_weight[:, 2 * width :], NT)
    attn_gain_grad = jnp.sum(normed_grad * tokens_in * inv_one, axis=0)
    input_grad = residual_grad + norm_back(normed_grad, tokens_in, inv_one, gain_one)
    kv_weight_grad = dense_sum(
        [
            dot(normed, kv_back[0], TN).astype(BF),
            dot(normed, kv_back[1], TN).astype(BF),
            jnp.concatenate(
                [attn_gain_grad[:, None], jnp.zeros((width, 127), F32)], axis=1
            ).astype(BF),
        ],
        own_rows,
    )
    at_in, at_out = width + 2 * FF, width + 2 * FF + flat
    return (
        layer_out[None],
        input_grad[None],
        kv_weight_grad[:, 2 * width],
        jnp.concatenate([query_grad, kv_weight_grad[:, : 2 * width]], axis=1),
        rest_grad[:, :width],
        rest_grad[:, at_out],
        rest_grad[:, at_out + 1 : at_out + 1 + n_experts],
        rest_grad[:, width:at_in],
        rest_grad[:, at_in:at_out].reshape(down_rows, width),
        gate_up_grad,
        down_grad,
    )


def solution(mesh):
    n_ctx, n_exp = mesh.shape["ctx"], mesh.shape["exp"]

    def layer(*args):
        n_experts = args[10].shape[0]
        nq = n_experts // n_exp
        nb = 2
        fine = Mesh(
            np.asarray(mesh.devices).reshape(nq, n_ctx // nq, n_exp // nb, nb), ("q", "r", "a", "b")
        )
        ctx, exp, every = ("q", "r"), ("a", "b"), ("q", "r", "a", "b")
        tokens, flat, rows = P(exp, ctx, None), P(every), P(every, None)
        run = jax.shard_map(
            functools.partial(body, n_experts),
            mesh=fine,
            in_specs=(
                tokens, tokens, tokens, flat, rows, rows, flat, rows, rows, rows, tokens, tokens,
            ),
            out_specs=(tokens, tokens, flat, rows, rows, flat, rows, rows, rows, tokens, tokens),
            check_vma=False,
        )
        return run(*args)

    return layer
```

```python
import functools

import jax
import jax.numpy as jnp
import numpy as np
from jax import lax
from jax.experimental import pallas as pl
from jax.experimental.pallas import tpu as pltpu
from jax.sharding import Mesh
from jax.sharding import PartitionSpec as P

HEADS = 10
HEAD_DIM = 128
FF = 896
TOP = 7

norm_eps = 1e-06
rope_base = 10000.0
masked_value = -1e30
LOG2E = 1.4426950408889634

BF = jnp.bfloat16
F32 = jnp.float32
VMEM_LIMIT = 56 * 1024 * 1024


def rope_tables(positions, head_dim):
    halfway = head_dim // 2
    frequency = rope_base ** (-(jnp.arange(halfway).astype(F32) * 2.0 / head_dim))
    angles = positions.astype(F32)[:, None] * frequency[None, :]
    angles = jnp.concatenate([angles, angles], axis=1)
    return (jnp.cos(angles), jnp.sin(angles))


def rms_scale(values):
    return lax.rsqrt(jnp.mean(values * values, axis=1, keepdims=True) + norm_eps)


def norm_back(grad_in, values, inv_rms, gain_vec):
    scaled = grad_in * gain_vec
    return inv_rms * scaled - values * inv_rms**3 * jnp.mean(scaled * values, axis=1, keepdims=True)


def dot(a, b, dims=((1,), (0,))):
    return lax.dot_general(a, b, (dims, ((), ())), preferred_element_type=F32)


NT = ((1,), (1,))
TN = ((0,), (0,))


def shift(value, axis):
    n = lax.axis_size(axis)
    return lax.ppermute(value, axis, [(i, (i + 1) % n) for i in range(n)])


def ring_gather(value, axis):
    parts = [value]
    for _ in range(1, lax.axis_size(axis)):
        parts.append(shift(parts[-1], axis))
    return parts


def shift_by(value, axis, k):
    n = lax.axis_size(axis)
    return lax.ppermute(value, axis, [(i, (i + k) % n) for i in range(n)])


def direct_gather(value, axis):
    return [value] + [shift_by(value, axis, k) for k in range(1, lax.axis_size(axis))]


def ring_sum(blocks, axis):
    n = len(blocks)
    if n == 1:
        return blocks[0].astype(F32)
    moving = blocks[1].astype(BF)
    for k in range(2, n):
        moving = (shift(moving, axis).astype(F32) + blocks[k].astype(F32)).astype(BF)
    return shift(moving, axis).astype(F32) + blocks[0].astype(F32)


def ring_blocks(arrays, axis, dim):
    n = lax.axis_size(axis)
    index = lax.axis_index(axis)
    out = []
    for k in range(n):
        at = lax.rem(index - k + n, n)
        parts = [lax.dynamic_index_in_dim(v, at, dim, keepdims=False) for v in arrays]
        out.append(parts[0] if len(parts) == 1 else jnp.concatenate(parts, axis=-1))
    return out


def after(value, *events):
    if not events:
        return value
    return lax.optimization_barrier((value, *events))[0]


def place_kernel(counts, columns, index_ref, *refs):
    n = len(counts)
    pieces, outs, sems = refs[:n], refs[n:-1], refs[-1]
    t = 0
    for piece, count in zip(pieces, counts):
        for j in range(count):
            at = index_ref[t]
            t += 1
            for o, (low, high) in enumerate(columns):
                pltpu.make_async_copy(
                    piece.at[j, :, pl.ds(low, high - low)], outs[o].at[at], sems.at[o]
                ).start()
    for o in range(len(columns)):
        pltpu.make_async_copy(outs[o], outs[o], sems.at[o]).wait()


def place(index, pieces, widths):
    rows, total = pieces[0].shape[-2:]
    pieces = [piece.reshape(-1, rows, total) for piece in pieces]
    counts = [piece.shape[0] for piece in pieces]
    edges = np.cumsum([0] + list(widths))
    columns = [(int(low), int(high)) for low, high in zip(edges[:-1], edges[1:])]
    n = sum(counts)
    outs = pl.pallas_call(
        functools.partial(place_kernel, counts, columns),
        in_specs=[pl.BlockSpec(memory_space=pltpu.SMEM)]
        + [pl.BlockSpec(memory_space=pl.ANY)] * len(pieces),
        out_specs=[pl.BlockSpec(memory_space=pltpu.VMEM)] * len(widths),
        scratch_shapes=[pltpu.SemaphoreType.DMA((len(widths),))],
        out_shape=[jax.ShapeDtypeStruct((n, rows, w), pieces[0].dtype) for w in widths],
        compiler_params=pltpu.CompilerParams(vmem_limit_bytes=VMEM_LIMIT // 2),
        cost_estimate=pl.CostEstimate(
            flops=0, bytes_accessed=4 * n * rows * total, transcendentals=0
        ),
        name="place",
    )(index, *pieces)
    return [out.reshape(n * rows, w) for out, w in zip(outs, widths)]


def dense_steps(nq):
    half, na, nb = nq // 2, lax.axis_size("a"), lax.axis_size("b")
    steps = [[(kq, ka, kb) for kb in range(nb) for kq in range(half)] for ka in range(na)]
    return steps + [
        [(kq, ka, kb) for ka in range(na) for kq in range(half, nq)] for kb in range(nb)
    ]


def dense_start(along_q):
    half = len(along_q) // 2
    one = jnp.stack(ring_gather(jnp.stack(along_q[:half]), "b"))
    two = jnp.stack(ring_gather(jnp.stack(along_q[half:]), "a"))
    return one, two


def dense_end(one, two):
    return ring_gather(one, "a") + ring_gather(two, "b")


def dense_place(pieces, steps, widths):
    nq, nr, na, nb = (lax.axis_size(axis) for axis in ("q", "r", "a", "b"))
    moved = [ring_gather(piece, "r") for piece in pieces]
    order = [(k, *s) for k in range(nr) for part in steps for s in part]
    kr, kq, ka, kb = (np.array(column, np.int32) for column in zip(*order))
    index = lax.rem(lax.axis_index("q") - kq + nq, nq) * nr
    index = index + lax.rem(lax.axis_index("r") - kr + nr, nr)
    index = index * na + lax.rem(lax.axis_index("a") - ka + na, na)
    index = index * nb + lax.rem(lax.axis_index("b") - kb + nb, nb)
    arrays = [moved[p][k] for k in range(nr) for p in range(len(pieces))]
    return place(index.astype(jnp.int32), arrays, widths)


def dense_sum(wholes, n_rows, middle=(), late=()):
    nq, nr, na, nb = (lax.axis_size(axis) for axis in ("q", "r", "a", "b"))
    values = [whole.reshape(nq, nr, na, nb, n_rows, whole.shape[1]) for whole in wholes]
    value = ring_sum(ring_blocks(values, "r", 1), "r").astype(BF)
    half = nq // 2
    one, two = value[:half], value[half:]
    one = ring_sum(ring_blocks([one], "a", 1), "a").astype(BF)
    two = ring_sum(ring_blocks([two], "b", 2), "b").astype(BF)
    one, two = after(one, *middle), after(two, *middle)
    one = ring_sum(ring_blocks([one], "b", 1), "b")
    two = ring_sum(ring_blocks([two], "a", 1), "a")
    value = after(jnp.concatenate([one, two], axis=0).astype(BF), *late)
    return ring_sum(ring_blocks([value], "q", 0), "q")


def plane_gather(rows, even, event=()):
    inner, outer = ("b", "a") if even else ("a", "b")
    first = after(jnp.stack(ring_gather(rows, inner)), *event)
    parts = ring_gather(first, outer)
    return [jnp.stack(parts)] if even else parts


def sum_start(parts, even):
    return ring_sum(parts, "a" if even else "b")


def sum_end(first, even, dim=0):
    n = first.shape[dim]
    return ring_sum(
        [lax.index_in_dim(first, k, dim, False) for k in range(n)], "b" if even else "a"
    )


def project_kernel(n_query, x_ref, w_ref, cos_ref, sin_ref, q_ref, kv_ref):
    j = pl.program_id(0)
    made = dot(x_ref[...], w_ref[...])

    def turned():
        parts = []
        for low in range(0, made.shape[1], HEAD_DIM):
            u = made[:, low : low + HEAD_DIM]
            parts.append(u * cos_ref[...] + pltpu.roll(u, HEAD_DIM // 2, 1) * sin_ref[...])
        return jnp.concatenate(parts, axis=1).astype(BF)

    @pl.when(j < n_query)
    def _():
        q_ref[...] = turned()

    @pl.when((j >= n_query) & (j < 2 * n_query))
    def _():
        kv_ref[0] = turned()

    @pl.when(j >= 2 * n_query)
    def _():
        kv_ref[0] = made.astype(BF)


def project(normed, weight, cosines, signed_sine):
    tok, width = normed.shape
    block = 2 * HEAD_DIM
    n = width // block
    table = pl.BlockSpec((tok, HEAD_DIM), lambda j: (0, 0))
    return pl.pallas_call(
        functools.partial(project_kernel, n),
        grid=(3 * n,),
        in_specs=[
            pl.BlockSpec((tok, width), lambda j: (0, 0)),
            pl.BlockSpec((width, block), lambda j: (0, j)),
            table,
            table,
        ],
        out_specs=[
            pl.BlockSpec((tok, block), lambda j: (0, jnp.minimum(j, n - 1))),
            pl.BlockSpec(
                (1, tok, block),
                lambda j: (jnp.maximum(j - n, 0) // n, 0, jnp.maximum(j - n, 0) % n),
            ),
        ],
        out_shape=[
            jax.ShapeDtypeStruct((tok, width), BF),
            jax.ShapeDtypeStruct((2, tok, width), BF),
        ],
        compiler_params=pltpu.CompilerParams(vmem_limit_bytes=VMEM_LIMIT // 2),
        cost_estimate=pl.CostEstimate(
            flops=6 * tok * width * width, bytes_accessed=6 * width * width, transcendentals=0
        ),
        name="project",
    )(normed, weight, cosines, signed_sine)


def turn_back(grad, cos, signed_sine):
    return grad * cos - pltpu.roll(grad, HEAD_DIM // 2, 1) * signed_sine


def finish_kernel(moved_ref, own_ref, cos_ref, sin_ref, out_ref):
    keys = moved_ref[0].astype(F32) + own_ref[0]
    out_ref[0] = turn_back(keys, cos_ref[...], sin_ref[...]).astype(BF)
    out_ref[1] = (moved_ref[1].astype(F32) + own_ref[1]).astype(BF)


def finish_keys(moved, own, cosines, signed_sine):
    _, tok, width = own.shape
    pair = pl.BlockSpec((2, tok, HEAD_DIM), lambda h: (0, 0, h))
    table = pl.BlockSpec((tok, HEAD_DIM), lambda h: (0, 0))
    return pl.pallas_call(
        finish_kernel,
        grid=(width // HEAD_DIM,),
        in_specs=[pair, pair, table, table],
        out_specs=pair,
        out_shape=jax.ShapeDtypeStruct((2, tok, width), BF),
        cost_estimate=pl.CostEstimate(
            flops=10 * tok * width, bytes_accessed=16 * tok * width, transcendentals=0
        ),
        name="finish_keys",
    )(moved, own, cosines, signed_sine)


def allowed_mask(own, other, n_ctx, half):
    row = lax.broadcasted_iota(jnp.int32, (2 * half, 2 * half), 0)
    col = lax.broadcasted_iota(jnp.int32, (2 * half, 2 * half), 1)
    last = 2 * n_ctx - 1
    query = row + jnp.where(row < half, own * half, (last - own) * half - half)
    key = col + jnp.where(col < half, other * half, (last - other) * half - half)
    return key <= query


def attend_kernel(n_ctx, n_src, first, last, place_ref, q_ref, *refs):
    kv_refs, refs = refs[:n_src], refs[n_src:]
    if not first:
        acc_in, ml_in = refs[:2]
        refs = refs[2:]
    out_ref, ml_ref = refs
    queries = q_ref[...]
    tok = queries.shape[0]
    scores = []
    for s in range(n_src):
        raw = dot(queries, kv_refs[s][0], NT) * (HEAD_DIM ** (-0.5) * LOG2E)
        mask = allowed_mask(place_ref[0], place_ref[1 + s], n_ctx, tok // 2)
        scores.append(jnp.where(mask, raw, masked_value))
    peak = functools.reduce(jnp.maximum, [jnp.max(s, axis=1, keepdims=True) for s in scores])
    if not first:
        old_peak = ml_in[0][:, 0:1]
        old_sum = ml_in[0][:, 64:65]
        peak = jnp.maximum(peak, old_peak)
    total = jnp.zeros_like(peak)
    mixed = jnp.zeros((tok, HEAD_DIM), F32)
    for s in range(n_src):
        raised = jnp.exp2(scores[s] - peak)
        total = total + jnp.sum(raised, axis=1, keepdims=True)
        mixed = mixed + dot(raised.astype(BF), kv_refs[s][1])
    if not first:
        decay = jnp.exp2(old_peak - peak)
        total = total + old_sum * decay
        mixed = mixed + acc_in[...] * decay
    if last:
        out_ref[...] = (mixed / total).astype(BF)
        ml_ref[0] = jnp.broadcast_to(peak + jnp.log2(total), (tok, 128))
    else:
        out_ref[...] = mixed
        lane = lax.broadcasted_iota(jnp.int32, (tok, 128), 1)
        ml_ref[0] = jnp.where(lane < 64, peak, total)


def attend_chunk(places, queries, kv_list, state, last, n_ctx):
    tok, width = queries.shape
    head = pl.BlockSpec((tok, HEAD_DIM), lambda h, p: (0, h))
    pair = pl.BlockSpec((2, tok, HEAD_DIM), lambda h, p: (0, 0, h))
    rows = pl.BlockSpec((1, tok, 128), lambda h, p: (h, 0, 0))
    first = state is None
    n = len(kv_list)
    pairs = tok * tok * n * HEADS
    return pl.pallas_call(
        functools.partial(attend_kernel, n_ctx, n, first, last),
        grid_spec=pltpu.PrefetchScalarGridSpec(
            num_scalar_prefetch=1,
            grid=(HEADS,),
            in_specs=[head] + [pair] * n + ([] if first else [head, rows]),
            out_specs=[head, rows],
        ),
        out_shape=[
            jax.ShapeDtypeStruct((tok, width), BF if last else F32),
            jax.ShapeDtypeStruct((HEADS, tok, 128), F32),
        ],
        compiler_params=pltpu.CompilerParams(vmem_limit_bytes=VMEM_LIMIT // 2),
        cost_estimate=pl.CostEstimate(
            flops=4 * pairs * HEAD_DIM * 4, bytes_accessed=8 * tok * width, transcendentals=pairs
        ),
        name="attend",
    )(places, queries, *kv_list, *(() if first else state))


def attend_back_kernel(
    n_ctx, n_src, first, last, place_ref, q_ref, do_ref, o_ref, lse_ref, cos_ref, sin_ref, *refs
):
    kv_refs, refs = refs[:n_src], refs[n_src:]
    if not first:
        dq_in, refs = refs[0], refs[1:]
    dq_ref, dkv_refs = refs[0], refs[1:]
    queries = q_ref[...]
    grad = do_ref[...]
    tok = queries.shape[0]
    lse = lse_ref[0][:, 0:1]
    delta = jnp.sum(grad.astype(F32) * o_ref[...].astype(F32), axis=1, keepdims=True)
    scale = HEAD_DIM ** (-0.5)
    grad_query = jnp.zeros((tok, HEAD_DIM), F32)
    for s in range(n_src):
        keys, values = kv_refs[s][0], kv_refs[s][1]
        raw = dot(queries, keys, NT) * (scale * LOG2E)
        mask = allowed_mask(place_ref[0], place_ref[1 + s], n_ctx, tok // 2)
        probs = jnp.exp2(jnp.where(mask, raw, masked_value) - lse)
        grad_probs = dot(grad, values, NT)
        grad_scores = (probs * (grad_probs - delta)).astype(BF)
        grad_query = grad_query + dot(grad_scores, keys)
        dkv_refs[s][0] = (dot(grad_scores, queries, TN) * scale).astype(dkv_refs[s].dtype)
        dkv_refs[s][1] = dot(probs.astype(BF), grad, TN).astype(dkv_refs[s].dtype)
    grad_query = grad_query * scale
    if not first:
        grad_query = grad_query + dq_in[...]
    if last:
        grad_query = turn_back(grad_query, cos_ref[...], sin_ref[...]).astype(BF)
    dq_ref[...] = grad_query


def attend_back_chunk(places, queries, grad, mixed, lse, tables, kv_list, dq, last, n_ctx):
    tok, width = queries.shape
    head = pl.BlockSpec((tok, HEAD_DIM), lambda h, p: (0, h))
    pair = pl.BlockSpec((2, tok, HEAD_DIM), lambda h, p: (0, 0, h))
    rows = pl.BlockSpec((1, tok, 128), lambda h, p: (h, 0, 0))
    table = pl.BlockSpec((tok, HEAD_DIM), lambda h, p: (0, 0))
    first = dq is None
    n = len(kv_list)
    pairs = tok * tok * n * HEADS
    out = pl.pallas_call(
        functools.partial(attend_back_kernel, n_ctx, n, first, last),
        grid_spec=pltpu.PrefetchScalarGridSpec(
            num_scalar_prefetch=1,
            grid=(HEADS,),
            in_specs=[head, head, head, rows, table, table] + [pair] * n + ([] if first else [head]),
            out_specs=[head] + [pair] * n,
        ),
        out_shape=[jax.ShapeDtypeStruct((tok, width), BF if last else F32)]
        + [jax.ShapeDtypeStruct((2, tok, width), F32 if s == 0 else BF) for s in range(n)],
        compiler_params=pltpu.CompilerParams(vmem_limit_bytes=VMEM_LIMIT // 2),
        cost_estimate=pl.CostEstimate(
            flops=10 * pairs * HEAD_DIM * 4, bytes_accessed=16 * tok * width, transcendentals=pairs
        ),
        name="attend_back",
    )(places, queries, grad, mixed, lse, *tables, *kv_list, *(() if first else (dq,)))
    return out[0], out[1:]


def expert_kernel(slots, na, nb, even, n_kept, e_ref, rank_ref, *refs):
    n_in, n_sum = (1, na) if even else (nb, nb)
    c_refs, g_ref, refs = refs[:n_in], refs[n_in], refs[n_in + 1 :]
    wr_ref, w1_ref, w2_ref = refs[:3]
    refs = refs[3 + n_kept :]
    d_refs, dg_ref, refs = refs[:n_sum], refs[n_sum], refs[n_sum + 1 :]
    x_ref, h_ref, dey_ref, deg_ref = refs[:4]
    y_refs = refs[4:]
    tok = g_ref.shape[3]
    experts = wr_ref.shape[0]
    me = e_ref[0]
    step = pl.program_id(0)
    picks, rows, grads, weights = [], [], [], []
    own = lax.broadcasted_iota(jnp.int32, (experts, tok), 0) == me
    slot = lax.broadcasted_iota(jnp.int32, (slots, tok), 0).astype(F32)
    for s in range(nb):
        tokens = c_refs[0][0, s] if even else c_refs[s][0]
        cot = g_ref[0, 0, lax.rem(e_ref[3] - s + nb, nb)]
        rank = rank_ref[0, s, 0]
        logits = dot(wr_ref[...], tokens, NT)
        logits = jnp.where(rank >= 0, logits, masked_value)
        raised = jnp.where(rank >= 0, jnp.exp(logits - jnp.max(logits, axis=0, keepdims=True)), 0.0)
        gates = raised / jnp.sum(raised, axis=0, keepdims=True)
        gate_row = jnp.sum(jnp.where(own, gates, 0.0), axis=0, keepdims=True)
        rank_row = jnp.sum(jnp.where(own, rank, 0.0), axis=0, keepdims=True)
        pick = jnp.where(slot == rank_row, 1.0, 0.0)
        weights.append(jnp.sum(pick * gate_row, axis=1, keepdims=True))
        pick_low = pick.astype(BF)
        picks.append((pick, pick_low))
        rows.append(dot(pick_low, tokens).astype(BF))
        grads.append(dot(pick_low, cot))
    x = jnp.concatenate(rows, axis=0)
    grad = jnp.concatenate(grads, axis=0)
    weight = jnp.concatenate(weights, axis=0)
    x_ref[...] = x
    dey = (weight * grad).astype(BF)
    dey_ref[...] = dey
    pre = dot(x, w1_ref[...])
    gate, up = pre[:, :FF], pre[:, FF:]
    sig = jax.nn.sigmoid(gate)
    act = gate * sig
    hidden = (act * up).astype(BF)
    h_ref[...] = hidden
    grad_hidden = dot(dey, w2_ref[...], NT)
    deg = jnp.concatenate(
        [
            (grad_hidden * up * sig * (1.0 + gate * (1.0 - sig))).astype(BF),
            (grad_hidden * act).astype(BF),
        ],
        axis=1,
    )
    deg_ref[...] = deg
    dec = dot(deg, w1_ref[...], NT).astype(BF)
    ey = dot(hidden, w2_ref[...]).astype(BF).astype(F32)
    dgate = jnp.sum(grad * ey, axis=1, keepdims=True)
    weighted = (weight * ey).astype(BF)
    d_all, y_all = [], []
    for s in range(nb):
        part = slice(s * slots, (s + 1) * slots)
        pick, pick_low = picks[s]
        d_all.append(dot(pick_low, dec[part], TN).astype(BF))
        y_all.append(dot(pick_low, weighted[part], TN).astype(BF))
        if not even:
            d_refs[s][0] = d_all[s]
            y_refs[s][0, 0] = y_all[s]
        dg_ref[0, s] = jnp.sum(pick * dgate[part], axis=0, keepdims=True)
    if even:
        for k in range(na):

            @pl.when(step == k)
            def _(k=k):
                for s in range(nb):
                    d_refs[k][s] = d_all[s]
                    y_refs[k][0, s] = y_all[s]


def expert_chunk(chunk, nq, na, nb, expert, ranks, c, g, router_t, w1, w2, kept, y_kept, slots):
    even = chunk % 2 == 0
    tok, width = c[0].shape[-2:]
    experts = router_t.shape[0]
    plane = pl.BlockSpec(
        (1, 1, nb, tok, width),
        lambda i, e: (lax.rem(e[1] - chunk + nq, nq), lax.rem(e[2] - i + na, na), 0, 0, 0),
    )
    one = pl.BlockSpec((1, nb, tok, width), lambda i, e: (i, 0, 0, 0))
    two = pl.BlockSpec((1, tok, width), lambda i, e: (i, 0, 0))

    def fixed(shape):
        return pl.BlockSpec(shape, lambda i, e: (0,) * len(shape), pipeline_mode=pl.Buffered(1))

    def by_rows(n):
        return pl.BlockSpec((nb * slots, n), lambda i, e: (chunk * na + i, 0))

    n_rows = na * nb * slots
    n_half = nq // 2
    if even:
        d_specs = [pl.BlockSpec((nb, tok, width), lambda i, e: (0, 0, 0))] * na
        y_specs = [pl.BlockSpec((1, nb, tok, width), lambda i, e: (chunk // 2, 0, 0, 0))] * na
        d_shapes = [jax.ShapeDtypeStruct((nb, tok, width), BF)] * na
        y_shapes = [jax.ShapeDtypeStruct((n_half, nb, tok, width), BF)] * na
    else:
        d_specs = [two] * nb
        y_specs = [pl.BlockSpec((1, 1, tok, width), lambda i, e: (chunk // 2, i, 0, 0))] * nb
        d_shapes = [jax.ShapeDtypeStruct((na, tok, width), BF)] * nb
        y_shapes = [jax.ShapeDtypeStruct((n_half, na, tok, width), BF)] * nb
    held = [*(kept or ()), *(y_kept or ())]
    n_in = 1 + 1 + len(c) + 1 + 3
    n_out = len(d_shapes) + 1
    aliases = {n_in + k: n_out + k for k in range(len(kept or ()))}
    for k in range(len(y_kept or ())):
        aliases[n_in + len(kept or ()) + k] = n_out + 4 + k
    out = pl.pallas_call(
        functools.partial(expert_kernel, slots, na, nb, even, len(held)),
        grid_spec=pltpu.PrefetchScalarGridSpec(
            num_scalar_prefetch=1,
            grid=(na,),
            in_specs=[
                pl.BlockSpec((1, nb, 1, experts, tok), lambda i, e: (i, 0, chunk, 0, 0)),
                *([one] if even else [two] * nb), plane,
                fixed(router_t.shape), fixed(w1.shape), fixed(w2.shape),
                *[pl.BlockSpec(memory_space=pl.ANY)] * len(held),
            ],
            out_specs=[
                *d_specs,
                pl.BlockSpec((1, nb, 1, tok), lambda i, e: (i, 0, 0, 0)),
                by_rows(width), by_rows(FF), by_rows(width), by_rows(2 * FF),
                *y_specs,
            ],
        ),
        out_shape=[
            *d_shapes,
            jax.ShapeDtypeStruct((na, nb, 1, tok), F32),
            *[jax.ShapeDtypeStruct((nq * n_rows, n), BF) for n in (width, FF, width, 2 * FF)],
            *y_shapes,
        ],
        input_output_aliases=aliases,
        compiler_params=pltpu.CompilerParams(vmem_limit_bytes=VMEM_LIMIT),
        cost_estimate=pl.CostEstimate(
            flops=n_rows * width * FF * 12, bytes_accessed=30_000_000, transcendentals=n_rows * FF
        ),
        name="experts",
    )(expert, ranks, *c, g, router_t, w1, w2, *held)
    n_d = len(d_shapes)
    return out[:n_d], out[n_d], out[n_out : n_out + 4], out[n_out + 4 :]


def body(
    n_experts,
    block_input,
    cotangent,
    routes,
    attn_gain,
    query_key_value_weight,
    attention_output_weight,
    ffn_gain,
    routing_weight,
    common_expert_gate_up_weight,
    common_expert_down_weight,
    expert_gate_up,
    expert_down,
):
    nq, nr, na, nb = (lax.axis_size(axis) for axis in ("q", "r", "a", "b"))
    q_at, r_at, a_at, b_at = (lax.axis_index(axis) for axis in ("q", "r", "a", "b"))
    n_ctx = nq * nr
    n_exp = na * nb
    ctx_rank = q_at * nr + r_at
    exp_rank = a_at * nb + b_at
    tok = block_input.shape[1]
    width = block_input.shape[2]
    half = tok // 2
    capacity = min(tok, 3 * TOP * tok // (2 * n_experts))
    slots = -(-capacity // 16) * 16
    row = jnp.arange(tok, dtype=jnp.int32)
    local_pos = jnp.where(
        row < half, ctx_rank * half + row, (2 * n_ctx - 1 - ctx_rank) * half + row - half
    )
    cosines, sines = rope_tables(local_pos, HEAD_DIM)
    sines = jnp.where(jnp.arange(HEAD_DIM)[None, :] < HEAD_DIM // 2, -sines, sines)
    tables = (cosines, sines)
    tokens_in = block_input[0].astype(F32)
    grad_low = cotangent[0]
    out_grad = grad_low.astype(F32)
    own_rows = query_key_value_weight.shape[0]
    down_rows = common_expert_down_weight.shape[0]

    named = jnp.any(
        routes[0][:, :, None] == jnp.arange(n_experts, dtype=jnp.int32)[None, None, :], axis=1
    )
    before = (row[:, None] < row[None, :]).astype(BF)
    rank = dot(named.astype(BF).T, before)
    rank = jnp.where(named.T, rank, -1.0)
    ranks = jnp.stack(direct_gather(rank, "q"))
    ranks = jnp.stack(ring_gather(ranks, "b"))
    ranks = jnp.stack(ring_gather(ranks, "a"))

    zeros = jnp.zeros((own_rows, 127), BF)
    front = jnp.concatenate([query_key_value_weight, attn_gain[:, None], zeros], axis=1)
    front_q = ring_gather(front, "q")
    rest = jnp.concatenate(
        [
            attention_output_weight,
            common_expert_gate_up_weight,
            common_expert_down_weight.reshape(own_rows, -1),
            ffn_gain[:, None],
            routing_weight,
            zeros[:, n_experts:],
        ],
        axis=1,
    )
    flat = common_expert_down_weight.size // own_rows
    front_q[-1] = after(front_q[-1], ranks)
    steps = dense_steps(nq)
    front_first = dense_start(front_q)

    def own_rows_of(stack, event):
        return lax.all_to_all(after(stack, event), "q", split_axis=0, concat_axis=0, tiled=True)

    def own_expert(rows):
        parts = ring_gather(rows, "r")
        kr = np.repeat(np.arange(nr, dtype=np.int32), nq)
        kq = np.tile(np.arange(nq, dtype=np.int32), nr)
        index = kq * nr + lax.rem(r_at - kr + nr, nr)
        return place(index.astype(jnp.int32), parts, [rows.shape[2]])[0]

    w1_rows = own_rows_of(expert_gate_up, front_q[-1])
    front_pieces = dense_end(*front_first)
    qkv_weight, front_small = dense_place(front_pieces, steps, [3 * width, 128])
    rest = lax.all_gather(rest, ("q", "r", "a", "b"), axis=0, tiled=True)
    g_all = lax.all_gather(grad_low, ("q", "a", "b"), axis=0, tiled=True)
    g_all = g_all.reshape(nq, na, nb, tok, width)

    kv_chunks = []
    gain_one = front_small[:, 0].astype(F32)
    inv_one = rms_scale(tokens_in)
    normed = after((tokens_in * inv_one * gain_one).astype(BF), w1_rows)
    queries, kv_own = project(normed, qkv_weight, *tables)
    places = [
        jnp.stack(
            [ctx_rank]
            + [
                lax.rem(q_at - k + nq, nq) * nr + lax.rem(r_at - s + nr, nr)
                for s in range(nr)
            ]
        ).astype(jnp.int32)
        for k in range(nq)
    ]
    state = None
    arrived = kv_own
    for k in range(nq):
        chunk = ring_gather(arrived, "r")
        if k < nq - 1:
            coming = shift(arrived, "q")
        state = attend_chunk(places[k], queries, chunk, state, k == nq - 1, n_ctx)
        kv_chunks.append(chunk)
        if k < nq - 1:
            arrived = after(coming, state[0]) if k < nq - 2 else coming
    mixed, lse = state
    w1, w2 = own_expert(w1_rows), own_expert(own_rows_of(expert_down, arrived))

    at_in, at_out = width + 2 * FF, width + 2 * FF + flat
    out_weight, shared_in = rest[:, :width], rest[:, width:at_in]
    shared_out = rest[:, at_in:at_out].reshape(-1, width)
    rest_small = rest[:, at_out:]
    gain_two = rest_small[:, 0].astype(F32)
    router = rest_small[:, 1 : 1 + n_experts]
    residual = tokens_in + dot(mixed, out_weight)
    inv_two = rms_scale(residual)
    second = (residual * inv_two * gain_two).astype(BF)
    expert = jnp.stack([exp_rank * nq + q_at, q_at, a_at, b_at]).astype(jnp.int32)
    router_t = router.T
    kept = None
    ys = [None, None]
    dec_parts, dgates = [], []
    c_q = ring_gather(second, "q")
    for k in range(nq):
        c = plane_gather(c_q[k], k % 2 == 0, () if k < 2 else (dgates[0],))
        dec, dgate, kept, ys[k % 2] = expert_chunk(
            k, nq, na, nb, expert, ranks, c, g_all, router_t, w1, w2, kept, ys[k % 2], slots
        )
        dec_parts.append(dec)
        dgates.append(dgate.reshape(na * nb, tok))
    dec_parts[0] = [after(v, dgates[-1]) for v in dec_parts[0]]
    firsts = [sum_start(dec_parts[k], k % 2 == 0) for k in range(nq)]
    dec_sums = [sum_end(firsts[k], k % 2 == 0) for k in range(nq)]
    xs, hs, deys, degs = kept[:4]
    down_term = dot(after(hs, firsts[nq - 2]), deys, TN).astype(BF)
    gate_up_term = dot(after(xs, firsts[nq - 1]), degs, TN).astype(BF)
    moving = dec_sums[1].astype(BF)
    for k in range(2, nq):
        term = dec_sums[k]
        if k >= nq - 2:
            term = after(term, down_term if k == nq - 2 else gate_up_term)
        moving = (shift(moving, "q").astype(F32) + term).astype(BF)
    routed_grad = shift(moving, "q").astype(F32) + dec_sums[0]

    def expert_rows(whole, *events):
        value = whole.reshape(nq, nr, -1, whole.shape[1])
        value = ring_sum(ring_blocks([value], "r", 1), "r").astype(BF)
        value = after(value, *events)
        return lax.all_to_all(value, "q", split_axis=0, concat_axis=0, tiled=True)

    gate_up_rows_low = expert_rows(gate_up_term)

    shared_pre = dot(second, shared_in)
    shared_gate, shared_up = shared_pre[:, :FF], shared_pre[:, FF:]
    shared_sig = jax.nn.sigmoid(shared_gate)
    shared_hidden = (shared_gate * shared_sig * shared_up).astype(BF)

    logits = jnp.where(named, dot(second, router), masked_value)
    raised = jnp.where(named, jnp.exp(logits - jnp.max(logits, axis=1, keepdims=True)), 0.0)
    gates = raised / jnp.sum(raised, axis=1, keepdims=True)
    n_all = nq * na * nb
    spot = np.arange(n_all, dtype=np.int32)
    spot = (
        lax.rem(q_at - spot // (na * nb) + nq, nq) * (na * nb)
        + lax.rem(a_at - spot // nb % na + na, na) * nb
        + lax.rem(b_at - spot % nb + nb, nb)
    )
    dgate = jnp.concatenate(dgates, axis=0)[spot]
    dgate = lax.all_to_all(dgate, ("q", "a", "b"), split_axis=0, concat_axis=0, tiled=True)
    dgate = jnp.swapaxes(dgate.reshape(nq, na * nb, tok), 0, 1).reshape(n_experts, tok).T
    grad_logits = gates * (dgate - jnp.sum(gates * dgate, axis=1, keepdims=True))
    grad_logits = grad_logits.astype(BF)

    shared_hidden_grad = dot(grad_low, shared_out, NT)
    shared_pre_grad = jnp.concatenate(
        [
            shared_hidden_grad * shared_up * shared_sig * (1.0 + shared_gate * (1.0 - shared_sig)),
            shared_hidden_grad * shared_gate * shared_sig,
        ],
        axis=1,
    ).astype(BF)
    every = ("q", "r", "a", "b")
    shared_grad = jnp.concatenate(
        [
            dot(second, shared_pre_grad, TN).astype(BF),
            dot(shared_hidden, grad_low, TN).astype(BF).reshape(width, flat),
        ],
        axis=1,
    )
    shared_grad = lax.psum_scatter(shared_grad, every, scatter_dimension=0, tiled=True)
    second_grad = (
        dot(shared_pre_grad, shared_in, NT) + dot(grad_logits, router, NT) + routed_grad
    )
    ffn_gain_grad = jnp.sum(second_grad * residual * inv_two, axis=0)
    residual_grad = out_grad + norm_back(second_grad, residual, inv_two, gain_two)
    mixed_grad = residual_grad.astype(BF)
    heads_grad = dot(mixed_grad, out_weight, NT).astype(BF)

    dq = None
    moving = None
    held = after(heads_grad, shared_grad, gate_up_rows_low)
    for step, k in enumerate(list(range(1, nq)) + [0]):
        if step == 2:
            held = after(held, moving)
        dq, parts = attend_back_chunk(
            places[k], queries, held, mixed, lse, tables, kv_chunks[k], dq, k == 0, n_ctx
        )
        term = ring_sum(parts, "r")
        if k == 1:
            moving = term.astype(BF)
            first_move = moving
        elif k:
            moving = (shift(moving, "q").astype(F32) + term).astype(BF)
    last_move = moving
    kv_back = finish_keys(shift(moving, "q"), term, *tables)

    y_sums = []
    for even in (True, False):
        first = sum_start([after(v, routed_grad) for v in ys[0 if even else 1]], even)
        y_sums.append(sum_end(after(first, first_move), even, 1))
    y_sums = after(y_sums, kv_back)
    routed_sum = ring_sum([y_sums[k % 2][k // 2] for k in range(nq)], "q")
    layer_out = (residual + dot(shared_hidden, shared_out) + routed_sum).astype(BF)


    down_rows_low = expert_rows(down_term, last_move)
    gate_up_grad, down_grad = gate_up_rows_low.astype(F32), down_rows_low.astype(F32)
    out_part = lax.psum_scatter(
        dot(mixed, mixed_grad, TN).astype(BF), every, scatter_dimension=0, tiled=True
    )
    shared_grad, out_part = shared_grad.astype(F32), out_part.astype(F32)
    query_grad = dense_sum([after(dot(normed, dq, TN).astype(BF), last_move)], own_rows)
    normed_grad = dot(dq, qkv_weight[:, :width], NT)
    normed_grad += dot(kv_back[0], qkv_weight[:, width : 2 * width], NT)
    normed_grad += dot(kv_back[1], qkv_weight[:, 2 * width :], NT)
    attn_gain_grad = jnp.sum(normed_grad * tokens_in * inv_one, axis=0)
    input_grad = residual_grad + norm_back(normed_grad, tokens_in, inv_one, gain_one)
    kv_weight_grad = dense_sum(
        [
            dot(normed, kv_back[0], TN).astype(BF),
            dot(normed, kv_back[1], TN).astype(BF),
            jnp.concatenate(
                [
                    attn_gain_grad[:, None],
                    ffn_gain_grad[:, None],
                    dot(second, grad_logits, TN),
                    jnp.zeros((width, 126 - n_experts), F32),
                ],
                axis=1,
            ).astype(BF),
        ],
        own_rows,
    )
    return (
        layer_out[None],
        input_grad[None],
        kv_weight_grad[:, 2 * width],
        jnp.concatenate([query_grad, kv_weight_grad[:, : 2 * width]], axis=1),
        out_part,
        kv_weight_grad[:, 2 * width + 1],
        kv_weight_grad[:, 2 * width + 2 : 2 * width + 2 + n_experts],
        shared_grad[:, : 2 * FF],
        shared_grad[:, 2 * FF :].reshape(down_rows, width),
        gate_up_grad,
        down_grad,
    )


def solution(mesh):
    n_ctx, n_exp = mesh.shape["ctx"], mesh.shape["exp"]

    def layer(*args):
        n_experts = args[10].shape[0]
        nq = n_experts // n_exp
        nb = 2
        fine = Mesh(
            np.asarray(mesh.devices).reshape(nq, n_ctx // nq, n_exp // nb, nb), ("q", "r", "a", "b")
        )
        ctx, exp, every = ("q", "r"), ("a", "b"), ("q", "r", "a", "b")
        tokens, flat, rows = P(exp, ctx, None), P(every), P(every, None)
        run = jax.shard_map(
            functools.partial(body, n_experts),
            mesh=fine,
            in_specs=(
                tokens, tokens, tokens, flat, rows, rows, flat, rows, rows, rows, tokens, tokens,
            ),
            out_specs=(tokens, tokens, flat, rows, rows, flat, rows, rows, rows, tokens, tokens),
            check_vma=False,
        )
        return run(*args)

    return layer
```

```python
import functools

import jax
import jax.numpy as jnp
import numpy as np
from jax import lax
from jax.experimental import pallas as pl
from jax.experimental.pallas import tpu as pltpu
from jax.sharding import Mesh
from jax.sharding import PartitionSpec as P

HEADS = 10
HEAD_DIM = 128
FF = 896
TOP = 7

norm_eps = 1e-06
rope_base = 10000.0
masked_value = -1e30
LOG2E = 1.4426950408889634

BF = jnp.bfloat16
F32 = jnp.float32
VMEM_LIMIT = 56 * 1024 * 1024


def rope_tables(positions, head_dim):
    halfway = head_dim // 2
    frequency = rope_base ** (-(jnp.arange(halfway).astype(F32) * 2.0 / head_dim))
    angles = positions.astype(F32)[:, None] * frequency[None, :]
    angles = jnp.concatenate([angles, angles], axis=1)
    return (jnp.cos(angles), jnp.sin(angles))


def rms_scale(values):
    return lax.rsqrt(jnp.mean(values * values, axis=1, keepdims=True) + norm_eps)


def norm_back(grad_in, values, inv_rms, gain_vec):
    scaled = grad_in * gain_vec
    return inv_rms * scaled - values * inv_rms**3 * jnp.mean(scaled * values, axis=1, keepdims=True)


def dot(a, b, dims=((1,), (0,))):
    return lax.dot_general(a, b, (dims, ((), ())), preferred_element_type=F32)


NT = ((1,), (1,))
TN = ((0,), (0,))


def shift(value, axis):
    n = lax.axis_size(axis)
    return lax.ppermute(value, axis, [(i, (i + 1) % n) for i in range(n)])


def ring_gather(value, axis):
    parts = [value]
    for _ in range(1, lax.axis_size(axis)):
        parts.append(shift(parts[-1], axis))
    return parts


def shift_by(value, axis, k):
    n = lax.axis_size(axis)
    return lax.ppermute(value, axis, [(i, (i + k) % n) for i in range(n)])


def direct_gather(value, axis):
    return [value] + [shift_by(value, axis, k) for k in range(1, lax.axis_size(axis))]


def ring_sum(blocks, axis, events=()):
    n = len(blocks)
    if n == 1:
        return blocks[0].astype(F32)
    moving = blocks[1].astype(BF)
    for k in range(2, n):
        moving = after(shift(moving, axis), *events)
        moving = (moving.astype(F32) + blocks[k].astype(F32)).astype(BF)
    return after(shift(moving, axis), *events).astype(F32) + blocks[0].astype(F32)


def ring_blocks(arrays, axis, dim):
    n = lax.axis_size(axis)
    index = lax.axis_index(axis)
    out = []
    for k in range(n):
        at = lax.rem(index - k + n, n)
        parts = [lax.dynamic_index_in_dim(v, at, dim, keepdims=False) for v in arrays]
        out.append(parts[0] if len(parts) == 1 else jnp.concatenate(parts, axis=-1))
    return out


def after(value, *events):
    if not events:
        return value
    return lax.optimization_barrier((value, *events))[0]


def place_kernel(counts, cuts, index_ref, *refs):
    n = len(counts)
    pieces, outs, sems = refs[:n], refs[n:-1], refs[-1]
    t = 0
    for piece, count in zip(pieces, counts):
        for j in range(count):
            at = index_ref[t]
            t += 1
            for o, (rows, low, high) in enumerate(cuts):
                pltpu.make_async_copy(
                    piece.at[j, pl.ds(*rows), pl.ds(low, high - low)], outs[o].at[at], sems.at[o]
                ).start()
    for o in range(len(cuts)):
        pltpu.make_async_copy(outs[o], outs[o], sems.at[o]).wait()


def place(index, pieces, cuts):
    rows, total = pieces[0].shape[-2:]
    pieces = [piece.reshape(-1, rows, total) for piece in pieces]
    counts = [piece.shape[0] for piece in pieces]
    n = sum(counts)
    outs = pl.pallas_call(
        functools.partial(place_kernel, counts, cuts),
        in_specs=[pl.BlockSpec(memory_space=pltpu.SMEM)]
        + [pl.BlockSpec(memory_space=pl.ANY)] * len(pieces),
        out_specs=[pl.BlockSpec(memory_space=pltpu.VMEM)] * len(cuts),
        scratch_shapes=[pltpu.SemaphoreType.DMA((len(cuts),))],
        out_shape=[
            jax.ShapeDtypeStruct((n, c[0][1], c[2] - c[1]), pieces[0].dtype) for c in cuts
        ],
        compiler_params=pltpu.CompilerParams(vmem_limit_bytes=VMEM_LIMIT // 2),
        cost_estimate=pl.CostEstimate(
            flops=0, bytes_accessed=4 * n * rows * total, transcendentals=0
        ),
        name="place",
    )(index, *pieces)
    return [out.reshape(-1, out.shape[2]) for out in outs]


def dense_steps(nq):
    half, na, nb = nq // 2, lax.axis_size("a"), lax.axis_size("b")
    steps = [[(kq, ka, kb) for kb in range(nb) for kq in range(half)] for ka in range(na)]
    return steps + [
        [(kq, ka, kb) for ka in range(na) for kq in range(half, nq)] for kb in range(nb)
    ]


def dense_start(along_q):
    half = len(along_q) // 2
    one = jnp.stack(ring_gather(jnp.stack(along_q[:half]), "b"))
    two = jnp.stack(ring_gather(jnp.stack(along_q[half:]), "a"))
    return one, two


def dense_end(one, two):
    return ring_gather(one, "a") + ring_gather(two, "b")


def dense_place(pieces, steps, widths, due=()):
    nq, nr, na, nb = (lax.axis_size(axis) for axis in ("q", "r", "a", "b"))
    rows, width = pieces[0].shape[-2:]
    flat = [piece.reshape(-1, rows, width) for piece in pieces]
    groups = [[0, na], [k for k in range(na + nb) if k not in (0, na)]]
    arrays, order = [], []
    for group in groups:
        own = jnp.concatenate([flat[k] for k in group], axis=0)
        if group is groups[1]:
            own = after(own, *due)
        entries = [s for k in group for s in steps[k]]
        for kr, part in enumerate(ring_gather(own, "r")):
            arrays.append(part)
            order += [(kr, *s) for s in entries]
    kr, kq, ka, kb = (np.array(column, np.int32) for column in zip(*order))
    index = lax.rem(lax.axis_index("q") - kq + nq, nq) * nr
    index = index + lax.rem(lax.axis_index("r") - kr + nr, nr)
    index = index * na + lax.rem(lax.axis_index("a") - ka + na, na)
    index = index * nb + lax.rem(lax.axis_index("b") - kb + nb, nb)
    edges = np.cumsum([0] + list(widths))
    cuts = [((0, rows), int(low), int(high)) for low, high in zip(edges[:-1], edges[1:])]
    return place(index.astype(jnp.int32), arrays, cuts)


def dense_sum_core(wholes, n_rows):
    nq, nr, na, nb = (lax.axis_size(axis) for axis in ("q", "r", "a", "b"))
    values = [whole.reshape(nq, nr, na, nb, n_rows, whole.shape[1]) for whole in wholes]
    return ring_sum(ring_blocks(values, "r", 1), "r").astype(BF)


def dense_sum_first(value):
    half = value.shape[0] // 2
    one = ring_sum(ring_blocks([value[:half]], "a", 1), "a").astype(BF)
    two = ring_sum(ring_blocks([value[half:]], "b", 2), "b").astype(BF)
    return one, two


def dense_sum_second(one, two):
    one = ring_sum(ring_blocks([one], "b", 1), "b")
    two = ring_sum(ring_blocks([two], "a", 1), "a")
    return jnp.concatenate([one, two], axis=0).astype(BF)


def dense_sum_last(value):
    return ring_sum(ring_blocks([value], "q", 0), "q")


def plane_gather(rows, even, first=None):
    inner, outer = ("b", "a") if even else ("a", "b")
    if first is None:
        first = jnp.stack(ring_gather(rows, inner))
    parts = ring_gather(first, outer)
    return [jnp.stack(parts)] if even else parts


def sum_start(parts, even, events=()):
    return ring_sum(parts, "a" if even else "b", events)


def sum_end(first, even, dim=0, events=()):
    n = first.shape[dim]
    parts = [lax.index_in_dim(first, k, dim, False) for k in range(n)]
    return ring_sum(parts, "b" if even else "a", events)


def project_kernel(n_query, x_ref, w_ref, cos_ref, sin_ref, q_ref, kv_ref):
    j = pl.program_id(0)
    made = dot(x_ref[...], w_ref[...])

    def turned():
        parts = []
        for low in range(0, made.shape[1], HEAD_DIM):
            u = made[:, low : low + HEAD_DIM]
            parts.append(u * cos_ref[...] + pltpu.roll(u, HEAD_DIM // 2, 1) * sin_ref[...])
        return jnp.concatenate(parts, axis=1).astype(BF)

    @pl.when(j < n_query)
    def _():
        q_ref[...] = turned()

    @pl.when((j >= n_query) & (j < 2 * n_query))
    def _():
        kv_ref[0] = turned()

    @pl.when(j >= 2 * n_query)
    def _():
        kv_ref[0] = made.astype(BF)


def project(normed, weight, cosines, signed_sine):
    tok, width = normed.shape
    block = 2 * HEAD_DIM
    n = width // block
    table = pl.BlockSpec((tok, HEAD_DIM), lambda j: (0, 0))
    return pl.pallas_call(
        functools.partial(project_kernel, n),
        grid=(3 * n,),
        in_specs=[
            pl.BlockSpec((tok, width), lambda j: (0, 0)),
            pl.BlockSpec((width, block), lambda j: (0, j)),
            table,
            table,
        ],
        out_specs=[
            pl.BlockSpec((tok, block), lambda j: (0, jnp.minimum(j, n - 1))),
            pl.BlockSpec(
                (1, tok, block),
                lambda j: (jnp.maximum(j - n, 0) // n, 0, jnp.maximum(j - n, 0) % n),
            ),
        ],
        out_shape=[
            jax.ShapeDtypeStruct((tok, width), BF),
            jax.ShapeDtypeStruct((2, tok, width), BF),
        ],
        compiler_params=pltpu.CompilerParams(vmem_limit_bytes=VMEM_LIMIT // 2),
        cost_estimate=pl.CostEstimate(
            flops=6 * tok * width * width, bytes_accessed=6 * width * width, transcendentals=0
        ),
        name="project",
    )(normed, weight, cosines, signed_sine)


def turn_back(grad, cos, signed_sine):
    return grad * cos - pltpu.roll(grad, HEAD_DIM // 2, 1) * signed_sine


def finish_kernel(moved_ref, own_ref, cos_ref, sin_ref, out_ref):
    keys = moved_ref[0].astype(F32) + own_ref[0]
    out_ref[0] = turn_back(keys, cos_ref[...], sin_ref[...]).astype(BF)
    out_ref[1] = (moved_ref[1].astype(F32) + own_ref[1]).astype(BF)


def finish_keys(moved, own, cosines, signed_sine):
    _, tok, width = own.shape
    pair = pl.BlockSpec((2, tok, HEAD_DIM), lambda h: (0, 0, h))
    table = pl.BlockSpec((tok, HEAD_DIM), lambda h: (0, 0))
    return pl.pallas_call(
        finish_kernel,
        grid=(width // HEAD_DIM,),
        in_specs=[pair, pair, table, table],
        out_specs=pair,
        out_shape=jax.ShapeDtypeStruct((2, tok, width), BF),
        cost_estimate=pl.CostEstimate(
            flops=10 * tok * width, bytes_accessed=16 * tok * width, transcendentals=0
        ),
        name="finish_keys",
    )(moved, own, cosines, signed_sine)


def allowed_mask(own, other, n_ctx, half):
    row = lax.broadcasted_iota(jnp.int32, (2 * half, 2 * half), 0)
    col = lax.broadcasted_iota(jnp.int32, (2 * half, 2 * half), 1)
    last = 2 * n_ctx - 1
    query = row + jnp.where(row < half, own * half, (last - own) * half - half)
    key = col + jnp.where(col < half, other * half, (last - other) * half - half)
    return key <= query


def attend_kernel(n_ctx, n_src, first, last, place_ref, q_ref, *refs):
    kv_refs, refs = refs[:n_src], refs[n_src:]
    if not first:
        acc_in, ml_in = refs[:2]
        refs = refs[2:]
    out_ref, ml_ref = refs
    queries = q_ref[...]
    tok = queries.shape[0]
    scores = []
    for s in range(n_src):
        raw = dot(queries, kv_refs[s][0], NT) * (HEAD_DIM ** (-0.5) * LOG2E)
        mask = allowed_mask(place_ref[0], place_ref[1 + s], n_ctx, tok // 2)
        scores.append(jnp.where(mask, raw, masked_value))
    peak = functools.reduce(jnp.maximum, [jnp.max(s, axis=1, keepdims=True) for s in scores])
    if not first:
        old_peak = ml_in[0][:, 0:1]
        old_sum = ml_in[0][:, 64:65]
        peak = jnp.maximum(peak, old_peak)
    total = jnp.zeros_like(peak)
    mixed = jnp.zeros((tok, HEAD_DIM), F32)
    for s in range(n_src):
        raised = jnp.exp2(scores[s] - peak)
        total = total + jnp.sum(raised, axis=1, keepdims=True)
        mixed = mixed + dot(raised.astype(BF), kv_refs[s][1])
    if not first:
        decay = jnp.exp2(old_peak - peak)
        total = total + old_sum * decay
        mixed = mixed + acc_in[...] * decay
    if last:
        out_ref[...] = (mixed / total).astype(BF)
        ml_ref[0] = jnp.broadcast_to(peak + jnp.log2(total), (tok, 128))
    else:
        out_ref[...] = mixed
        lane = lax.broadcasted_iota(jnp.int32, (tok, 128), 1)
        ml_ref[0] = jnp.where(lane < 64, peak, total)


def attend_chunk(places, queries, kv_list, state, last, n_ctx):
    tok, width = queries.shape
    head = pl.BlockSpec((tok, HEAD_DIM), lambda h, p: (0, h))
    pair = pl.BlockSpec((2, tok, HEAD_DIM), lambda h, p: (0, 0, h))
    rows = pl.BlockSpec((1, tok, 128), lambda h, p: (h, 0, 0))
    first = state is None
    n = len(kv_list)
    pairs = tok * tok * n * HEADS
    return pl.pallas_call(
        functools.partial(attend_kernel, n_ctx, n, first, last),
        grid_spec=pltpu.PrefetchScalarGridSpec(
            num_scalar_prefetch=1,
            grid=(HEADS,),
            in_specs=[head] + [pair] * n + ([] if first else [head, rows]),
            out_specs=[head, rows],
        ),
        out_shape=[
            jax.ShapeDtypeStruct((tok, width), BF if last else F32),
            jax.ShapeDtypeStruct((HEADS, tok, 128), F32),
        ],
        compiler_params=pltpu.CompilerParams(vmem_limit_bytes=VMEM_LIMIT // 2),
        cost_estimate=pl.CostEstimate(
            flops=4 * pairs * HEAD_DIM * 4, bytes_accessed=8 * tok * width, transcendentals=pairs
        ),
        name="attend",
    )(places, queries, *kv_list, *(() if first else state))


def attend_back_kernel(
    n_ctx, n_src, first, last, place_ref, q_ref, do_ref, o_ref, lse_ref, cos_ref, sin_ref, *refs
):
    kv_refs, refs = refs[:n_src], refs[n_src:]
    if not first:
        dq_in, refs = refs[0], refs[1:]
    dq_ref, dkv_refs = refs[0], refs[1:]
    queries = q_ref[...]
    grad = do_ref[...]
    tok = queries.shape[0]
    lse = lse_ref[0][:, 0:1]
    delta = jnp.sum(grad.astype(F32) * o_ref[...].astype(F32), axis=1, keepdims=True)
    scale = HEAD_DIM ** (-0.5)
    grad_query = jnp.zeros((tok, HEAD_DIM), F32)
    for s in range(n_src):
        keys, values = kv_refs[s][0], kv_refs[s][1]
        raw = dot(queries, keys, NT) * (scale * LOG2E)
        mask = allowed_mask(place_ref[0], place_ref[1 + s], n_ctx, tok // 2)
        probs = jnp.exp2(jnp.where(mask, raw, masked_value) - lse)
        grad_probs = dot(grad, values, NT)
        grad_scores = (probs * (grad_probs - delta)).astype(BF)
        grad_query = grad_query + dot(grad_scores, keys)
        dkv_refs[s][0] = (dot(grad_scores, queries, TN) * scale).astype(dkv_refs[s].dtype)
        dkv_refs[s][1] = dot(probs.astype(BF), grad, TN).astype(dkv_refs[s].dtype)
    grad_query = grad_query * scale
    if not first:
        grad_query = grad_query + dq_in[...]
    if last:
        grad_query = turn_back(grad_query, cos_ref[...], sin_ref[...]).astype(BF)
    dq_ref[...] = grad_query


def attend_back_chunk(places, queries, grad, mixed, lse, tables, kv_list, dq, last, n_ctx):
    tok, width = queries.shape
    head = pl.BlockSpec((tok, HEAD_DIM), lambda h, p: (0, h))
    pair = pl.BlockSpec((2, tok, HEAD_DIM), lambda h, p: (0, 0, h))
    rows = pl.BlockSpec((1, tok, 128), lambda h, p: (h, 0, 0))
    table = pl.BlockSpec((tok, HEAD_DIM), lambda h, p: (0, 0))
    first = dq is None
    n = len(kv_list)
    pairs = tok * tok * n * HEADS
    out = pl.pallas_call(
        functools.partial(attend_back_kernel, n_ctx, n, first, last),
        grid_spec=pltpu.PrefetchScalarGridSpec(
            num_scalar_prefetch=1,
            grid=(HEADS,),
            in_specs=[head, head, head, rows, table, table] + [pair] * n + ([] if first else [head]),
            out_specs=[head] + [pair] * n,
        ),
        out_shape=[jax.ShapeDtypeStruct((tok, width), BF if last else F32)]
        + [jax.ShapeDtypeStruct((2, tok, width), F32 if s == 0 else BF) for s in range(n)],
        compiler_params=pltpu.CompilerParams(vmem_limit_bytes=VMEM_LIMIT // 2),
        cost_estimate=pl.CostEstimate(
            flops=10 * pairs * HEAD_DIM * 4, bytes_accessed=16 * tok * width, transcendentals=pairs
        ),
        name="attend_back",
    )(places, queries, grad, mixed, lse, *tables, *kv_list, *(() if first else (dq,)))
    return out[0], out[1:]


def expert_kernel(slots, na, nb, even, n_kept, e_ref, rank_ref, *refs):
    n_in, n_sum = (1, na) if even else (nb, nb)
    c_refs, g_refs, refs = refs[:n_in], refs[n_in : 2 * n_in], refs[2 * n_in :]
    wr_ref, w1_ref, w2_ref = refs[:3]
    refs = refs[3 + n_kept :]
    d_refs, dg_ref, refs = refs[:n_sum], refs[n_sum], refs[n_sum + 1 :]
    x_ref, h_ref, dey_ref, deg_ref = refs[:4]
    y_refs = refs[4:]
    tok = g_refs[0].shape[-2]
    experts = wr_ref.shape[0]
    me = e_ref[0]
    step = pl.program_id(0)
    picks, rows, grads, weights = [], [], [], []
    own = lax.broadcasted_iota(jnp.int32, (experts, tok), 0) == me
    slot = lax.broadcasted_iota(jnp.int32, (slots, tok), 0).astype(F32)
    for s in range(nb):
        tokens = c_refs[0][0, s] if even else c_refs[s][0]
        cot = g_refs[0][0, s, 0] if even else g_refs[s][0, 0]
        rank = rank_ref[0, s, 0]
        logits = dot(wr_ref[...], tokens, NT)
        logits = jnp.where(rank >= 0, logits, masked_value)
        raised = jnp.where(rank >= 0, jnp.exp(logits - jnp.max(logits, axis=0, keepdims=True)), 0.0)
        gates = raised / jnp.sum(raised, axis=0, keepdims=True)
        gate_row = jnp.sum(jnp.where(own, gates, 0.0), axis=0, keepdims=True)
        rank_row = jnp.sum(jnp.where(own, rank, 0.0), axis=0, keepdims=True)
        pick = jnp.where(slot == rank_row, 1.0, 0.0)
        weights.append(jnp.sum(pick * gate_row, axis=1, keepdims=True))
        pick_low = pick.astype(BF)
        picks.append((pick, pick_low))
        rows.append(dot(pick_low, tokens).astype(BF))
        grads.append(dot(pick_low, cot))
    x = jnp.concatenate(rows, axis=0)
    grad = jnp.concatenate(grads, axis=0)
    weight = jnp.concatenate(weights, axis=0)
    x_ref[...] = x
    dey = (weight * grad).astype(BF)
    dey_ref[...] = dey
    pre = dot(x, w1_ref[...])
    gate, up = pre[:, :FF], pre[:, FF:]
    sig = jax.nn.sigmoid(gate)
    act = gate * sig
    hidden = (act * up).astype(BF)
    h_ref[...] = hidden
    grad_hidden = dot(dey, w2_ref[...], NT)
    deg = jnp.concatenate(
        [
            (grad_hidden * up * sig * (1.0 + gate * (1.0 - sig))).astype(BF),
            (grad_hidden * act).astype(BF),
        ],
        axis=1,
    )
    deg_ref[...] = deg
    dec = dot(deg, w1_ref[...], NT).astype(BF)
    ey = dot(hidden, w2_ref[...]).astype(BF).astype(F32)
    dgate = jnp.sum(grad * ey, axis=1, keepdims=True)
    weighted = (weight * ey).astype(BF)
    d_all, y_all = [], []
    for s in range(nb):
        part = slice(s * slots, (s + 1) * slots)
        pick, pick_low = picks[s]
        d_all.append(dot(pick_low, dec[part], TN).astype(BF))
        y_all.append(dot(pick_low, weighted[part], TN).astype(BF))
        if not even:
            d_refs[s][0] = d_all[s]
            y_refs[s][0, 0] = y_all[s]
        dg_ref[0, s] = jnp.sum(pick * dgate[part], axis=0, keepdims=True)
    if even:
        for k in range(na):

            @pl.when(step == k)
            def _(k=k):
                for s in range(nb):
                    d_refs[k][s] = d_all[s]
                    y_refs[k][0, s] = y_all[s]


def expert_chunk(chunk, nq, na, nb, expert, ranks, c, g, router_t, w1, w2, kept, y_kept, slots):
    even = chunk % 2 == 0
    tok, width = c[0].shape[-2:]
    experts = router_t.shape[0]
    g_one = pl.BlockSpec((1, nb, 1, tok, width), lambda i, e: (i, 0, chunk // 2, 0, 0))
    g_two = pl.BlockSpec((1, 1, tok, width), lambda i, e: (i, chunk // 2, 0, 0))
    one = pl.BlockSpec((1, nb, tok, width), lambda i, e: (i, 0, 0, 0))
    two = pl.BlockSpec((1, tok, width), lambda i, e: (i, 0, 0))

    def fixed(shape):
        return pl.BlockSpec(shape, lambda i, e: (0,) * len(shape), pipeline_mode=pl.Buffered(1))

    def by_rows(n):
        return pl.BlockSpec((nb * slots, n), lambda i, e: (chunk * na + i, 0))

    n_rows = na * nb * slots
    n_half = nq // 2
    if even:
        d_specs = [pl.BlockSpec((nb, tok, width), lambda i, e: (0, 0, 0))] * na
        y_specs = [pl.BlockSpec((1, nb, tok, width), lambda i, e: (chunk // 2, 0, 0, 0))] * na
        d_shapes = [jax.ShapeDtypeStruct((nb, tok, width), BF)] * na
        y_shapes = [jax.ShapeDtypeStruct((n_half, nb, tok, width), BF)] * na
    else:
        d_specs = [two] * nb
        y_specs = [pl.BlockSpec((1, 1, tok, width), lambda i, e: (chunk // 2, i, 0, 0))] * nb
        d_shapes = [jax.ShapeDtypeStruct((na, tok, width), BF)] * nb
        y_shapes = [jax.ShapeDtypeStruct((n_half, na, tok, width), BF)] * nb
    held = [*(kept or ()), *(y_kept or ())]
    n_in = 1 + 1 + len(c) + len(g) + 3
    n_out = len(d_shapes) + 1
    aliases = {n_in + k: n_out + k for k in range(len(kept or ()))}
    for k in range(len(y_kept or ())):
        aliases[n_in + len(kept or ()) + k] = n_out + 4 + k
    out = pl.pallas_call(
        functools.partial(expert_kernel, slots, na, nb, even, len(held)),
        grid_spec=pltpu.PrefetchScalarGridSpec(
            num_scalar_prefetch=1,
            grid=(na,),
            in_specs=[
                pl.BlockSpec((1, nb, 1, experts, tok), lambda i, e: (i, 0, chunk, 0, 0)),
                *([one, g_one] if even else [two] * nb + [g_two] * nb),
                fixed(router_t.shape), fixed(w1.shape), fixed(w2.shape),
                *[pl.BlockSpec(memory_space=pl.ANY)] * len(held),
            ],
            out_specs=[
                *d_specs,
                pl.BlockSpec((1, nb, 1, tok), lambda i, e: (i, 0, 0, 0)),
                by_rows(width), by_rows(FF), by_rows(width), by_rows(2 * FF),
                *y_specs,
            ],
        ),
        out_shape=[
            *d_shapes,
            jax.ShapeDtypeStruct((na, nb, 1, tok), F32),
            *[jax.ShapeDtypeStruct((nq * n_rows, n), BF) for n in (width, FF, width, 2 * FF)],
            *y_shapes,
        ],
        input_output_aliases=aliases,
        compiler_params=pltpu.CompilerParams(vmem_limit_bytes=VMEM_LIMIT),
        cost_estimate=pl.CostEstimate(
            flops=n_rows * width * FF * 12, bytes_accessed=30_000_000, transcendentals=n_rows * FF
        ),
        name="experts",
    )(expert, ranks, *c, *g, router_t, w1, w2, *held)
    n_d = len(d_shapes)
    return out[:n_d], out[n_d], out[n_out : n_out + 4], out[n_out + 4 :]


def body(
    n_experts,
    block_input,
    cotangent,
    routes,
    attn_gain,
    query_key_value_weight,
    attention_output_weight,
    ffn_gain,
    routing_weight,
    common_expert_gate_up_weight,
    common_expert_down_weight,
    expert_gate_up,
    expert_down,
):
    nq, nr, na, nb = (lax.axis_size(axis) for axis in ("q", "r", "a", "b"))
    q_at, r_at, a_at, b_at = (lax.axis_index(axis) for axis in ("q", "r", "a", "b"))
    n_ctx = nq * nr
    n_exp = na * nb
    ctx_rank = q_at * nr + r_at
    exp_rank = a_at * nb + b_at
    tok = block_input.shape[1]
    width = block_input.shape[2]
    half = tok // 2
    capacity = min(tok, 3 * TOP * tok // (2 * n_experts))
    slots = -(-capacity // 16) * 16
    row = jnp.arange(tok, dtype=jnp.int32)
    local_pos = jnp.where(
        row < half, ctx_rank * half + row, (2 * n_ctx - 1 - ctx_rank) * half + row - half
    )
    cosines, sines = rope_tables(local_pos, HEAD_DIM)
    sines = jnp.where(jnp.arange(HEAD_DIM)[None, :] < HEAD_DIM // 2, -sines, sines)
    tables = (cosines, sines)
    tokens_in = block_input[0].astype(F32)
    grad_low = cotangent[0]
    out_grad = grad_low.astype(F32)
    own_rows = query_key_value_weight.shape[0]
    down_rows = common_expert_down_weight.shape[0]

    named = jnp.any(
        routes[0][:, :, None] == jnp.arange(n_experts, dtype=jnp.int32)[None, None, :], axis=1
    )
    before = (row[:, None] < row[None, :]).astype(BF)
    rank = dot(named.astype(BF).T, before)
    rank = jnp.where(named.T, rank, -1.0)
    ranks = jnp.stack(direct_gather(rank, "q"))
    ranks = jnp.stack(ring_gather(ranks, "b"))
    ranks = jnp.stack(ring_gather(ranks, "a"))

    zeros = jnp.zeros((own_rows, 127), BF)
    front = jnp.concatenate([query_key_value_weight, attn_gain[:, None], zeros], axis=1)
    front_q = ring_gather(front, "q")
    rest = jnp.concatenate(
        [
            attention_output_weight,
            common_expert_gate_up_weight,
            common_expert_down_weight.reshape(own_rows, -1),
            ffn_gain[:, None],
            routing_weight,
            zeros[:, n_experts:],
        ],
        axis=1,
    )
    flat = common_expert_down_weight.size // own_rows
    front_q[-1] = after(front_q[-1], ranks)
    steps = dense_steps(nq)
    front_first = dense_start(front_q)

    gu_rows = expert_gate_up.shape[1]
    folded = expert_down.reshape(nq, -1, 2 * FF)
    both = jnp.concatenate([expert_gate_up, folded], axis=1)

    rest_q = ring_gather(after(rest, front_q[-1]), "q")
    g_q = [after(grad_low, rest_q[-1])]
    g_q.append(shift(g_q[0], "q"))
    front_pieces = dense_end(*front_first)
    qkv_weight, front_small = dense_place(
        front_pieces, steps, [3 * width, 128], (rest_q[-2],)
    )
    for _ in range(nq - 2):
        g_q.append(shift(g_q[-1], "q"))
    rest_first = dense_start([after(part, *front_pieces) for part in rest_q])

    kv_chunks = []
    gain_one = front_small[:, 0].astype(F32)
    inv_one = rms_scale(tokens_in)
    normed = after((tokens_in * inv_one * gain_one).astype(BF), g_q[1], *rest_first)
    queries, kv_own = project(normed, qkv_weight, *tables)
    places = [
        jnp.stack(
            [ctx_rank]
            + [
                lax.rem(q_at - k + nq, nq) * nr + lax.rem(r_at - s + nr, nr)
                for s in range(nr)
            ]
        ).astype(jnp.int32)
        for k in range(nq)
    ]
    rest_pieces = dense_end(*rest_first)
    state = None
    arrived = kv_own
    for k in range(nq):
        chunk = ring_gather(arrived, "r")
        due = ()
        if k < nq - 1:
            coming = shift(arrived, "q")
        if k == 1:
            g_even, g_odd = (after(jnp.stack(g_q[low::2]), *rest_pieces) for low in (0, 1))
            g_even = jnp.stack(ring_gather(g_even, "b"))
            g_odd = jnp.stack(ring_gather(g_odd, "a"))
        state = attend_chunk(places[k], queries, chunk, state, k == nq - 1, n_ctx)
        kv_chunks.append(chunk)
        if k < nq - 1:
            if k == 0:
                due = (state[0], g_q[nq - 2], *rest_pieces)
            if k == 1:
                due = (state[0], g_even, g_odd)
            if k == 2:
                g_even, g_odd = ring_gather(g_even, "a"), ring_gather(g_odd, "b")
                due = (state[0], *g_even, *g_odd)
            arrived = after(coming, *due)
    mixed, lse = state
    both = lax.all_to_all(after(both, arrived), "q", split_axis=0, concat_axis=0, tiled=True)
    out_weight, shared_in, shared_out, rest_small = dense_place(
        rest_pieces, steps, [width, 2 * FF, flat, 128]
    )
    shared_out = shared_out.reshape(-1, width)
    gain_two = rest_small[:, 0].astype(F32)
    router = rest_small[:, 1 : 1 + n_experts]
    residual = tokens_in + dot(mixed, out_weight)
    inv_two = rms_scale(residual)
    second = (residual * inv_two * gain_two).astype(BF)
    expert = jnp.stack([exp_rank * nq + q_at, q_at, a_at, b_at]).astype(jnp.int32)
    router_t = router.T
    kept = None
    ys = [None, None]
    sum_first, dgates = [], []
    c_q = ring_gather(second, "q")
    c_start = jnp.stack(ring_gather(c_q[0], "b"))
    both = ring_gather(after(both, c_start), "r")
    kr = np.repeat(np.arange(nr, dtype=np.int32), nq)
    kq = np.tile(np.arange(nq, dtype=np.int32), nr)
    index = kq * nr + lax.rem(r_at - kr + nr, nr)
    w1, w2 = place(
        index.astype(jnp.int32),
        both,
        [((0, gu_rows), 0, 2 * FF), ((gu_rows, folded.shape[1]), 0, 2 * FF)],
    )
    w2 = w2.reshape(-1, width)
    g_even = [jnp.stack(g_even)]
    for k in range(nq):
        rows = c_q[k] if k < 2 else after(c_q[k], dgates[0])
        first = c_start
        if k:
            first = jnp.stack(ring_gather(rows, "ba"[k % 2]))
        if k == 1:
            first = after(first, w1)
        c = plane_gather(rows, k % 2 == 0, first)
        dec, dgate, kept, ys[k % 2] = expert_chunk(
            k, nq, na, nb, expert, ranks, c, (g_even, g_odd)[k % 2], router_t, w1, w2, kept, ys[k % 2], slots
        )
        sum_first.append(sum_start(dec, k % 2 == 0))
        dgates.append(dgate.reshape(na * nb, tok))
    firsts = sum_first
    dec_sums = [sum_end(firsts[k], k % 2 == 0) for k in range(nq)]
    xs, hs, deys, degs = kept[:4]
    down_term = dot(hs, deys, TN).astype(BF)
    gate_up_term = dot(xs, degs, TN).astype(BF)
    terms = [
        gate_up_term.reshape(nq, nr, gu_rows, 2 * FF),
        down_term.reshape(nq, nr, -1, 2 * FF),
    ]
    at = [lax.rem(r_at - k + nr, nr) for k in range(nr)]
    expert_rows = ring_sum(
        [
            jnp.concatenate(
                [lax.dynamic_index_in_dim(t, i, 1, keepdims=False) for t in terms], axis=1
            )
            for i in at
        ],
        "r",
    ).astype(BF)
    moving = dec_sums[1].astype(BF)
    for k in range(2, nq):
        term = dec_sums[k]
        if k == 2:
            term = after(term, expert_rows)
        moving = (shift(moving, "q").astype(F32) + term).astype(BF)
    routed_grad = shift(moving, "q").astype(F32) + dec_sums[0]

    expert_rows = lax.all_to_all(expert_rows, "q", split_axis=0, concat_axis=0, tiled=True)

    later = after(second, dgates[0])
    shared_pre = dot(later, shared_in)
    shared_gate, shared_up = shared_pre[:, :FF], shared_pre[:, FF:]
    shared_sig = jax.nn.sigmoid(shared_gate)
    shared_hidden = (shared_gate * shared_sig * shared_up).astype(BF)

    logits = jnp.where(named, dot(later, router), masked_value)
    raised = jnp.where(named, jnp.exp(logits - jnp.max(logits, axis=1, keepdims=True)), 0.0)
    gates = raised / jnp.sum(raised, axis=1, keepdims=True)
    n_all = nq * na * nb
    spot = np.arange(n_all, dtype=np.int32)
    spot = (
        lax.rem(q_at - spot // (na * nb) + nq, nq) * (na * nb)
        + lax.rem(a_at - spot // nb % na + na, na) * nb
        + lax.rem(b_at - spot % nb + nb, nb)
    )
    dgate = jnp.concatenate(dgates, axis=0)[spot]
    dgate = lax.all_to_all(dgate, ("q", "a", "b"), split_axis=0, concat_axis=0, tiled=True)
    dgate = jnp.swapaxes(dgate.reshape(nq, na * nb, tok), 0, 1).reshape(n_experts, tok).T
    grad_logits = gates * (dgate - jnp.sum(gates * dgate, axis=1, keepdims=True))
    grad_logits = grad_logits.astype(BF)

    shared_hidden_grad = dot(grad_low, shared_out, NT)
    shared_pre_grad = jnp.concatenate(
        [
            shared_hidden_grad * shared_up * shared_sig * (1.0 + shared_gate * (1.0 - shared_sig)),
            shared_hidden_grad * shared_gate * shared_sig,
        ],
        axis=1,
    ).astype(BF)
    second_grad = (
        dot(shared_pre_grad, shared_in, NT) + dot(grad_logits, router, NT) + routed_grad
    )
    ffn_gain_grad = jnp.sum(second_grad * residual * inv_two, axis=0)
    residual_grad = out_grad + norm_back(second_grad, residual, inv_two, gain_two)
    mixed_grad = residual_grad.astype(BF)
    heads_grad = dot(mixed_grad, out_weight, NT).astype(BF)

    y_first = [
        sum_start([after(v, routed_grad) for v in ys[p]], p == 0) for p in (0, 1)
    ]
    dq = None
    moving = None
    held = heads_grad
    for step, k in enumerate(list(range(1, nq)) + [0]):
        if step == 2:
            held = after(held, moving, expert_rows)
        dq, parts = attend_back_chunk(
            places[k], queries, held, mixed, lse, tables, kv_chunks[k], dq, k == 0, n_ctx
        )
        term = ring_sum(parts, "r")
        if k == 1:
            moving = term.astype(BF)
            first_move = moving
        elif k:
            moving = (shift(moving, "q").astype(F32) + term).astype(BF)
    late = dense_sum_core(
        [
            dot(normed, dq, TN).astype(BF),
            dot(mixed, mixed_grad, TN).astype(BF),
            dot(later, shared_pre_grad, TN).astype(BF),
            dot(shared_hidden, grad_low, TN).astype(BF).reshape(width, flat),
        ],
        own_rows,
    )
    y_sums = [sum_end(after(y_first[p], dq), p == 0, 1) for p in (0, 1)]
    late = dense_sum_first(late)
    kv_back = finish_keys(shift(moving, "q"), after(term, *late), *tables)

    gate_up_grad = expert_rows[:, :gu_rows].astype(F32)
    down_grad = expert_rows[:, gu_rows:].reshape(nq, -1, width).astype(F32)
    normed_grad = dot(dq, qkv_weight[:, :width], NT)
    normed_grad += dot(kv_back[0], qkv_weight[:, width : 2 * width], NT)
    normed_grad += dot(kv_back[1], qkv_weight[:, 2 * width :], NT)
    attn_gain_grad = jnp.sum(normed_grad * tokens_in * inv_one, axis=0)
    input_grad = residual_grad + norm_back(normed_grad, tokens_in, inv_one, gain_one)
    small_grad = jnp.concatenate(
        [
            attn_gain_grad[:, None],
            ffn_gain_grad[:, None],
            dot(second, grad_logits, TN),
            jnp.zeros((width, 126 - n_experts), F32),
        ],
        axis=1,
    ).astype(BF)
    key_value = dense_sum_core(
        [
            dot(normed, kv_back[0], TN).astype(BF),
            dot(normed, kv_back[1], TN).astype(BF),
            small_grad,
        ],
        own_rows,
    )
    y_sums = after(y_sums, kv_back)
    y_terms = [y_sums[k % 2][k // 2] for k in range(nq)]
    late = dense_sum_second(*late)
    first_kv = dense_sum_first(key_value)
    last_kv = dense_sum_second(*first_kv)
    y_moving = y_terms[1].astype(BF)
    events = [(key_value,), first_kv, (late,)]
    for k in range(2, nq + 1):
        y_moving = after(shift(y_moving, "q"), *events[min(k - 2, 2)])
        routed_sum = y_moving.astype(F32) + y_terms[k % nq]
        y_moving = routed_sum.astype(BF)
    late_grad = dense_sum_last(after(late, *first_kv))
    kv_weight_grad = dense_sum_last(last_kv)
    layer_out = (residual + dot(shared_hidden, shared_out) + routed_sum).astype(BF)
    at_out, at_shared, at_down = width, 2 * width, 2 * width + 2 * FF
    return (
        layer_out[None],
        input_grad[None],
        kv_weight_grad[:, 2 * width],
        jnp.concatenate([late_grad[:, :at_out], kv_weight_grad[:, : 2 * width]], axis=1),
        late_grad[:, at_out:at_shared],
        kv_weight_grad[:, 2 * width + 1],
        kv_weight_grad[:, 2 * width + 2 : 2 * width + 2 + n_experts],
        late_grad[:, at_shared:at_down],
        late_grad[:, at_down:].reshape(down_rows, width),
        gate_up_grad,
        down_grad,
    )


def solution(mesh):
    n_ctx, n_exp = mesh.shape["ctx"], mesh.shape["exp"]

    def layer(*args):
        n_experts = args[10].shape[0]
        nq = n_experts // n_exp
        nb = 2
        fine = Mesh(
            np.asarray(mesh.devices).reshape(nq, n_ctx // nq, n_exp // nb, nb), ("q", "r", "a", "b")
        )
        ctx, exp, every = ("q", "r"), ("a", "b"), ("q", "r", "a", "b")
        tokens, flat, rows = P(exp, ctx, None), P(every), P(every, None)
        run = jax.shard_map(
            functools.partial(body, n_experts),
            mesh=fine,
            in_specs=(
                tokens, tokens, tokens, flat, rows, rows, flat, rows, rows, rows, tokens, tokens,
            ),
            out_specs=(tokens, tokens, flat, rows, rows, flat, rows, rows, rows, tokens, tokens),
            check_vma=False,
        )
        return run(*args)

    return layer
```

```python
import functools

import jax
import jax.numpy as jnp
import numpy as np
from jax import lax
from jax.experimental import pallas as pl
from jax.experimental.pallas import tpu as pltpu
from jax.sharding import Mesh
from jax.sharding import PartitionSpec as P

HEADS = 10
HEAD_DIM = 128
FF = 896
TOP = 7

norm_eps = 1e-06
rope_base = 10000.0
masked_value = -1e30
LOG2E = 1.4426950408889634

BF = jnp.bfloat16
F32 = jnp.float32
VMEM_LIMIT = 56 * 1024 * 1024


def rope_tables(positions, head_dim):
    halfway = head_dim // 2
    frequency = rope_base ** (-(jnp.arange(halfway).astype(F32) * 2.0 / head_dim))
    angles = positions.astype(F32)[:, None] * frequency[None, :]
    angles = jnp.concatenate([angles, angles], axis=1)
    return (jnp.cos(angles), jnp.sin(angles))


def rms_scale(values):
    return lax.rsqrt(jnp.mean(values * values, axis=1, keepdims=True) + norm_eps)


def norm_back(grad_in, values, inv_rms, gain_vec):
    scaled = grad_in * gain_vec
    return inv_rms * scaled - values * inv_rms**3 * jnp.mean(scaled * values, axis=1, keepdims=True)


def dot(a, b, dims=((1,), (0,))):
    return lax.dot_general(a, b, (dims, ((), ())), preferred_element_type=F32)


NT = ((1,), (1,))
TN = ((0,), (0,))


def shift(value, axis):
    n = lax.axis_size(axis)
    return lax.ppermute(value, axis, [(i, (i + 1) % n) for i in range(n)])


def ring_gather(value, axis):
    parts = [value]
    for _ in range(1, lax.axis_size(axis)):
        parts.append(shift(parts[-1], axis))
    return parts


def shift_by(value, axis, k):
    n = lax.axis_size(axis)
    return lax.ppermute(value, axis, [(i, (i + k) % n) for i in range(n)])


def direct_gather(value, axis):
    return [value] + [shift_by(value, axis, k) for k in range(1, lax.axis_size(axis))]


def ring_sum(blocks, axis, events=()):
    n = len(blocks)
    if n == 1:
        return blocks[0].astype(F32)
    moving = blocks[1].astype(BF)
    for k in range(2, n):
        moving = after(shift(moving, axis), *events)
        moving = (moving.astype(F32) + blocks[k].astype(F32)).astype(BF)
    return after(shift(moving, axis), *events).astype(F32) + blocks[0].astype(F32)


def ring_blocks(arrays, axis, dim):
    n = lax.axis_size(axis)
    index = lax.axis_index(axis)
    out = []
    for k in range(n):
        at = lax.rem(index - k + n, n)
        parts = [lax.dynamic_index_in_dim(v, at, dim, keepdims=False) for v in arrays]
        out.append(parts[0] if len(parts) == 1 else jnp.concatenate(parts, axis=-1))
    return out


ORDER = {
    "g": "f3",
    "mid0": "r1",
    "core2": "r3",
    "rs1": "fp",
    "norm": "rs g2",
    "gs1": "rp",
    "arr1": "g3 rp",
    "arr2": "s rp",
    "arr3": "s gf",
    "wa": "a3",
    "wc": "cs",
    "c1b": "w",
    "c2b": "k0",
    "c3a": "k0",
    "c3b": "k0",
    "gu": "s2",
    "dn": "gu",
    "t2": "gu dn",
    "ea": "t",
    "sh": "k2",
    "B2": "er",
    "B3": "er",
    "y1": "rg",
    "y2": "q",
    "fin": "late ys",
    "y3": "b",
    "late2": "b",
    "kv2": "l",
    "yz2": "kv",
    "yz4": "l",
    "late3": "f",
}


def pick(name, value, **events):
    chosen = [events[key] for key in ORDER.get(name, "").split() if key in events]
    return after(value, *jax.tree.leaves(chosen))


def after(value, *events):
    if not events:
        return value
    return lax.optimization_barrier((value, *events))[0]


def place_kernel(counts, cuts, index_ref, *refs):
    n = len(counts)
    pieces, outs, sems = refs[:n], refs[n:-1], refs[-1]
    t = 0
    for piece, count in zip(pieces, counts):
        for j in range(count):
            at = index_ref[t]
            t += 1
            for o, (rows, low, high) in enumerate(cuts):
                pltpu.make_async_copy(
                    piece.at[j, pl.ds(*rows), pl.ds(low, high - low)], outs[o].at[at], sems.at[o]
                ).start()
    for o in range(len(cuts)):
        pltpu.make_async_copy(outs[o], outs[o], sems.at[o]).wait()


def place(index, pieces, cuts):
    rows, total = pieces[0].shape[-2:]
    pieces = [piece.reshape(-1, rows, total) for piece in pieces]
    counts = [piece.shape[0] for piece in pieces]
    n = sum(counts)
    outs = pl.pallas_call(
        functools.partial(place_kernel, counts, cuts),
        in_specs=[pl.BlockSpec(memory_space=pltpu.SMEM)]
        + [pl.BlockSpec(memory_space=pl.ANY)] * len(pieces),
        out_specs=[pl.BlockSpec(memory_space=pltpu.VMEM)] * len(cuts),
        scratch_shapes=[pltpu.SemaphoreType.DMA((len(cuts),))],
        out_shape=[
            jax.ShapeDtypeStruct((n, c[0][1], c[2] - c[1]), pieces[0].dtype) for c in cuts
        ],
        compiler_params=pltpu.CompilerParams(vmem_limit_bytes=VMEM_LIMIT // 2),
        cost_estimate=pl.CostEstimate(
            flops=0, bytes_accessed=4 * n * rows * total, transcendentals=0
        ),
        name="place",
    )(index, *pieces)
    return [out.reshape(-1, out.shape[2]) for out in outs]


def dense_steps(nq):
    half, na, nb = nq // 2, lax.axis_size("a"), lax.axis_size("b")
    steps = [[(kq, ka, kb) for kb in range(nb) for kq in range(half)] for ka in range(na)]
    return steps + [
        [(kq, ka, kb) for ka in range(na) for kq in range(half, nq)] for kb in range(nb)
    ]


def dense_start(along_q):
    half = len(along_q) // 2
    one = jnp.stack(ring_gather(jnp.stack(along_q[:half]), "b"))
    two = jnp.stack(ring_gather(jnp.stack(along_q[half:]), "a"))
    return one, two


def dense_end(one, two):
    return ring_gather(one, "a") + ring_gather(two, "b")


def dense_place(pieces, steps, widths, due=()):
    nq, nr, na, nb = (lax.axis_size(axis) for axis in ("q", "r", "a", "b"))
    rows, width = pieces[0].shape[-2:]
    flat = [piece.reshape(-1, rows, width) for piece in pieces]
    groups = [[0, na], [k for k in range(na + nb) if k not in (0, na)]]
    arrays, order = [], []
    for group in groups:
        own = jnp.concatenate([flat[k] for k in group], axis=0)
        if group is groups[1]:
            own = after(own, *due)
        entries = [s for k in group for s in steps[k]]
        for kr, part in enumerate(ring_gather(own, "r")):
            arrays.append(part)
            order += [(kr, *s) for s in entries]
    kr, kq, ka, kb = (np.array(column, np.int32) for column in zip(*order))
    index = lax.rem(lax.axis_index("q") - kq + nq, nq) * nr
    index = index + lax.rem(lax.axis_index("r") - kr + nr, nr)
    index = index * na + lax.rem(lax.axis_index("a") - ka + na, na)
    index = index * nb + lax.rem(lax.axis_index("b") - kb + nb, nb)
    edges = np.cumsum([0] + list(widths))
    cuts = [((0, rows), int(low), int(high)) for low, high in zip(edges[:-1], edges[1:])]
    return place(index.astype(jnp.int32), arrays, cuts)


def dense_sum_core(wholes, n_rows):
    nq, nr, na, nb = (lax.axis_size(axis) for axis in ("q", "r", "a", "b"))
    values = [whole.reshape(nq, nr, na, nb, n_rows, whole.shape[1]) for whole in wholes]
    return ring_sum(ring_blocks(values, "r", 1), "r").astype(BF)


def dense_sum_first(value):
    half = value.shape[0] // 2
    one = ring_sum(ring_blocks([value[:half]], "a", 1), "a").astype(BF)
    two = ring_sum(ring_blocks([value[half:]], "b", 2), "b").astype(BF)
    return one, two


def dense_sum_second(one, two):
    one = ring_sum(ring_blocks([one], "b", 1), "b")
    two = ring_sum(ring_blocks([two], "a", 1), "a")
    return jnp.concatenate([one, two], axis=0).astype(BF)


def dense_sum_last(value):
    return ring_sum(ring_blocks([value], "q", 0), "q")


def plane_gather(rows, even, first=None):
    inner, outer = ("b", "a") if even else ("a", "b")
    if first is None:
        first = jnp.stack(ring_gather(rows, inner))
    parts = ring_gather(first, outer)
    return [jnp.stack(parts)] if even else parts


def sum_start(parts, even, events=()):
    return ring_sum(parts, "a" if even else "b", events)


def sum_end(first, even, dim=0, events=()):
    n = first.shape[dim]
    parts = [lax.index_in_dim(first, k, dim, False) for k in range(n)]
    return ring_sum(parts, "b" if even else "a", events)


def project_kernel(n_query, x_ref, w_ref, cos_ref, sin_ref, q_ref, kv_ref):
    j = pl.program_id(0)
    made = dot(x_ref[...], w_ref[...])

    def turned():
        parts = []
        for low in range(0, made.shape[1], HEAD_DIM):
            u = made[:, low : low + HEAD_DIM]
            parts.append(u * cos_ref[...] + pltpu.roll(u, HEAD_DIM // 2, 1) * sin_ref[...])
        return jnp.concatenate(parts, axis=1).astype(BF)

    @pl.when(j < n_query)
    def _():
        q_ref[...] = turned()

    @pl.when((j >= n_query) & (j < 2 * n_query))
    def _():
        kv_ref[0] = turned()

    @pl.when(j >= 2 * n_query)
    def _():
        kv_ref[0] = made.astype(BF)


def project(normed, weight, cosines, signed_sine):
    tok, width = normed.shape
    block = 2 * HEAD_DIM
    n = width // block
    table = pl.BlockSpec((tok, HEAD_DIM), lambda j: (0, 0))
    return pl.pallas_call(
        functools.partial(project_kernel, n),
        grid=(3 * n,),
        in_specs=[
            pl.BlockSpec((tok, width), lambda j: (0, 0)),
            pl.BlockSpec((width, block), lambda j: (0, j)),
            table,
            table,
        ],
        out_specs=[
            pl.BlockSpec((tok, block), lambda j: (0, jnp.minimum(j, n - 1))),
            pl.BlockSpec(
                (1, tok, block),
                lambda j: (jnp.maximum(j - n, 0) // n, 0, jnp.maximum(j - n, 0) % n),
            ),
        ],
        out_shape=[
            jax.ShapeDtypeStruct((tok, width), BF),
            jax.ShapeDtypeStruct((2, tok, width), BF),
        ],
        compiler_params=pltpu.CompilerParams(vmem_limit_bytes=VMEM_LIMIT // 2),
        cost_estimate=pl.CostEstimate(
            flops=6 * tok * width * width, bytes_accessed=6 * width * width, transcendentals=0
        ),
        name="project",
    )(normed, weight, cosines, signed_sine)


def turn_back(grad, cos, signed_sine):
    return grad * cos - pltpu.roll(grad, HEAD_DIM // 2, 1) * signed_sine


def finish_kernel(moved_ref, own_ref, cos_ref, sin_ref, out_ref):
    keys = moved_ref[0].astype(F32) + own_ref[0]
    out_ref[0] = turn_back(keys, cos_ref[...], sin_ref[...]).astype(BF)
    out_ref[1] = (moved_ref[1].astype(F32) + own_ref[1]).astype(BF)


def finish_keys(moved, own, cosines, signed_sine):
    _, tok, width = own.shape
    pair = pl.BlockSpec((2, tok, HEAD_DIM), lambda h: (0, 0, h))
    table = pl.BlockSpec((tok, HEAD_DIM), lambda h: (0, 0))
    return pl.pallas_call(
        finish_kernel,
        grid=(width // HEAD_DIM,),
        in_specs=[pair, pair, table, table],
        out_specs=pair,
        out_shape=jax.ShapeDtypeStruct((2, tok, width), BF),
        cost_estimate=pl.CostEstimate(
            flops=10 * tok * width, bytes_accessed=16 * tok * width, transcendentals=0
        ),
        name="finish_keys",
    )(moved, own, cosines, signed_sine)


def allowed_mask(own, other, n_ctx, half):
    row = lax.broadcasted_iota(jnp.int32, (2 * half, 2 * half), 0)
    col = lax.broadcasted_iota(jnp.int32, (2 * half, 2 * half), 1)
    last = 2 * n_ctx - 1
    query = row + jnp.where(row < half, own * half, (last - own) * half - half)
    key = col + jnp.where(col < half, other * half, (last - other) * half - half)
    return key <= query


def attend_kernel(n_ctx, n_src, first, last, place_ref, q_ref, *refs):
    kv_refs, refs = refs[:n_src], refs[n_src:]
    if not first:
        acc_in, ml_in = refs[:2]
        refs = refs[2:]
    out_ref, ml_ref = refs
    queries = q_ref[...]
    tok = queries.shape[0]
    scores = []
    for s in range(n_src):
        raw = dot(queries, kv_refs[s][0], NT) * (HEAD_DIM ** (-0.5) * LOG2E)
        mask = allowed_mask(place_ref[0], place_ref[1 + s], n_ctx, tok // 2)
        scores.append(jnp.where(mask, raw, masked_value))
    peak = functools.reduce(jnp.maximum, [jnp.max(s, axis=1, keepdims=True) for s in scores])
    if not first:
        old_peak = ml_in[0][:, 0:1]
        old_sum = ml_in[0][:, 64:65]
        peak = jnp.maximum(peak, old_peak)
    total = jnp.zeros_like(peak)
    mixed = jnp.zeros((tok, HEAD_DIM), F32)
    for s in range(n_src):
        raised = jnp.exp2(scores[s] - peak)
        total = total + jnp.sum(raised, axis=1, keepdims=True)
        mixed = mixed + dot(raised.astype(BF), kv_refs[s][1])
    if not first:
        decay = jnp.exp2(old_peak - peak)
        total = total + old_sum * decay
        mixed = mixed + acc_in[...] * decay
    if last:
        out_ref[...] = (mixed / total).astype(BF)
        ml_ref[0] = jnp.broadcast_to(peak + jnp.log2(total), (tok, 128))
    else:
        out_ref[...] = mixed
        lane = lax.broadcasted_iota(jnp.int32, (tok, 128), 1)
        ml_ref[0] = jnp.where(lane < 64, peak, total)


def attend_chunk(places, queries, kv_list, state, last, n_ctx):
    tok, width = queries.shape
    head = pl.BlockSpec((tok, HEAD_DIM), lambda h, p: (0, h))
    pair = pl.BlockSpec((2, tok, HEAD_DIM), lambda h, p: (0, 0, h))
    rows = pl.BlockSpec((1, tok, 128), lambda h, p: (h, 0, 0))
    first = state is None
    n = len(kv_list)
    pairs = tok * tok * n * HEADS
    return pl.pallas_call(
        functools.partial(attend_kernel, n_ctx, n, first, last),
        grid_spec=pltpu.PrefetchScalarGridSpec(
            num_scalar_prefetch=1,
            grid=(HEADS,),
            in_specs=[head] + [pair] * n + ([] if first else [head, rows]),
            out_specs=[head, rows],
        ),
        out_shape=[
            jax.ShapeDtypeStruct((tok, width), BF if last else F32),
            jax.ShapeDtypeStruct((HEADS, tok, 128), F32),
        ],
        compiler_params=pltpu.CompilerParams(vmem_limit_bytes=VMEM_LIMIT // 2),
        cost_estimate=pl.CostEstimate(
            flops=4 * pairs * HEAD_DIM * 4, bytes_accessed=8 * tok * width, transcendentals=pairs
        ),
        name="attend",
    )(places, queries, *kv_list, *(() if first else state))


def attend_back_kernel(
    n_ctx, n_src, first, last, place_ref, q_ref, do_ref, o_ref, lse_ref, cos_ref, sin_ref, *refs
):
    kv_refs, refs = refs[:n_src], refs[n_src:]
    if not first:
        dq_in, refs = refs[0], refs[1:]
    dq_ref, dkv_refs = refs[0], refs[1:]
    queries = q_ref[...]
    grad = do_ref[...]
    tok = queries.shape[0]
    lse = lse_ref[0][:, 0:1]
    delta = jnp.sum(grad.astype(F32) * o_ref[...].astype(F32), axis=1, keepdims=True)
    scale = HEAD_DIM ** (-0.5)
    grad_query = jnp.zeros((tok, HEAD_DIM), F32)
    for s in range(n_src):
        keys, values = kv_refs[s][0], kv_refs[s][1]
        raw = dot(queries, keys, NT) * (scale * LOG2E)
        mask = allowed_mask(place_ref[0], place_ref[1 + s], n_ctx, tok // 2)
        probs = jnp.exp2(jnp.where(mask, raw, masked_value) - lse)
        grad_probs = dot(grad, values, NT)
        grad_scores = (probs * (grad_probs - delta)).astype(BF)
        grad_query = grad_query + dot(grad_scores, keys)
        dkv_refs[s][0] = (dot(grad_scores, queries, TN) * scale).astype(dkv_refs[s].dtype)
        dkv_refs[s][1] = dot(probs.astype(BF), grad, TN).astype(dkv_refs[s].dtype)
    grad_query = grad_query * scale
    if not first:
        grad_query = grad_query + dq_in[...]
    if last:
        grad_query = turn_back(grad_query, cos_ref[...], sin_ref[...]).astype(BF)
    dq_ref[...] = grad_query


def attend_back_chunk(places, queries, grad, mixed, lse, tables, kv_list, dq, last, n_ctx):
    tok, width = queries.shape
    head = pl.BlockSpec((tok, HEAD_DIM), lambda h, p: (0, h))
    pair = pl.BlockSpec((2, tok, HEAD_DIM), lambda h, p: (0, 0, h))
    rows = pl.BlockSpec((1, tok, 128), lambda h, p: (h, 0, 0))
    table = pl.BlockSpec((tok, HEAD_DIM), lambda h, p: (0, 0))
    first = dq is None
    n = len(kv_list)
    pairs = tok * tok * n * HEADS
    out = pl.pallas_call(
        functools.partial(attend_back_kernel, n_ctx, n, first, last),
        grid_spec=pltpu.PrefetchScalarGridSpec(
            num_scalar_prefetch=1,
            grid=(HEADS,),
            in_specs=[head, head, head, rows, table, table] + [pair] * n + ([] if first else [head]),
            out_specs=[head] + [pair] * n,
        ),
        out_shape=[jax.ShapeDtypeStruct((tok, width), BF if last else F32)]
        + [jax.ShapeDtypeStruct((2, tok, width), F32 if s == 0 else BF) for s in range(n)],
        compiler_params=pltpu.CompilerParams(vmem_limit_bytes=VMEM_LIMIT // 2),
        cost_estimate=pl.CostEstimate(
            flops=10 * pairs * HEAD_DIM * 4, bytes_accessed=16 * tok * width, transcendentals=pairs
        ),
        name="attend_back",
    )(places, queries, grad, mixed, lse, *tables, *kv_list, *(() if first else (dq,)))
    return out[0], out[1:]


def expert_kernel(slots, na, nb, even, n_kept, e_ref, rank_ref, *refs):
    n_in, n_sum = (1, na) if even else (nb, nb)
    c_refs, g_refs, refs = refs[:n_in], refs[n_in : 2 * n_in], refs[2 * n_in :]
    wr_ref, w1_ref, w2_ref = refs[:3]
    refs = refs[3 + n_kept :]
    d_refs, dg_ref, refs = refs[:n_sum], refs[n_sum], refs[n_sum + 1 :]
    x_ref, h_ref, dey_ref, deg_ref = refs[:4]
    y_refs = refs[4:]
    tok = g_refs[0].shape[-2]
    experts = wr_ref.shape[0]
    me = e_ref[0]
    step = pl.program_id(0)
    picks, rows, grads, weights = [], [], [], []
    own = lax.broadcasted_iota(jnp.int32, (experts, tok), 0) == me
    slot = lax.broadcasted_iota(jnp.int32, (slots, tok), 0).astype(F32)
    for s in range(nb):
        tokens = c_refs[0][0, s] if even else c_refs[s][0]
        cot = g_refs[0][0, s, 0] if even else g_refs[s][0, 0]
        rank = rank_ref[0, s, 0]
        logits = dot(wr_ref[...], tokens, NT)
        logits = jnp.where(rank >= 0, logits, masked_value)
        raised = jnp.where(rank >= 0, jnp.exp(logits - jnp.max(logits, axis=0, keepdims=True)), 0.0)
        gates = raised / jnp.sum(raised, axis=0, keepdims=True)
        gate_row = jnp.sum(jnp.where(own, gates, 0.0), axis=0, keepdims=True)
        rank_row = jnp.sum(jnp.where(own, rank, 0.0), axis=0, keepdims=True)
        pick = jnp.where(slot == rank_row, 1.0, 0.0)
        weights.append(jnp.sum(pick * gate_row, axis=1, keepdims=True))
        pick_low = pick.astype(BF)
        picks.append((pick, pick_low))
        rows.append(dot(pick_low, tokens).astype(BF))
        grads.append(dot(pick_low, cot))
    x = jnp.concatenate(rows, axis=0)
    grad = jnp.concatenate(grads, axis=0)
    weight = jnp.concatenate(weights, axis=0)
    x_ref[...] = x
    dey = (weight * grad).astype(BF)
    dey_ref[...] = dey
    pre = dot(x, w1_ref[...])
    gate, up = pre[:, :FF], pre[:, FF:]
    sig = jax.nn.sigmoid(gate)
    act = gate * sig
    hidden = (act * up).astype(BF)
    h_ref[...] = hidden
    grad_hidden = dot(dey, w2_ref[...], NT)
    deg = jnp.concatenate(
        [
            (grad_hidden * up * sig * (1.0 + gate * (1.0 - sig))).astype(BF),
            (grad_hidden * act).astype(BF),
        ],
        axis=1,
    )
    deg_ref[...] = deg
    dec = dot(deg, w1_ref[...], NT).astype(BF)
    ey = dot(hidden, w2_ref[...]).astype(BF).astype(F32)
    dgate = jnp.sum(grad * ey, axis=1, keepdims=True)
    weighted = (weight * ey).astype(BF)
    d_all, y_all = [], []
    for s in range(nb):
        part = slice(s * slots, (s + 1) * slots)
        pick, pick_low = picks[s]
        d_all.append(dot(pick_low, dec[part], TN).astype(BF))
        y_all.append(dot(pick_low, weighted[part], TN).astype(BF))
        if not even:
            d_refs[s][0] = d_all[s]
            y_refs[s][0, 0] = y_all[s]
        dg_ref[0, s] = jnp.sum(pick * dgate[part], axis=0, keepdims=True)
    if even:
        for k in range(na):

            @pl.when(step == k)
            def _(k=k):
                for s in range(nb):
                    d_refs[k][s] = d_all[s]
                    y_refs[k][0, s] = y_all[s]


def expert_chunk(chunk, nq, na, nb, expert, ranks, c, g, router_t, w1, w2, kept, y_kept, slots):
    even = chunk % 2 == 0
    tok, width = c[0].shape[-2:]
    experts = router_t.shape[0]
    g_one = pl.BlockSpec((1, nb, 1, tok, width), lambda i, e: (i, 0, chunk // 2, 0, 0))
    g_two = pl.BlockSpec((1, 1, tok, width), lambda i, e: (i, chunk // 2, 0, 0))
    one = pl.BlockSpec((1, nb, tok, width), lambda i, e: (i, 0, 0, 0))
    two = pl.BlockSpec((1, tok, width), lambda i, e: (i, 0, 0))

    def fixed(shape):
        return pl.BlockSpec(shape, lambda i, e: (0,) * len(shape), pipeline_mode=pl.Buffered(1))

    def by_rows(n):
        return pl.BlockSpec((nb * slots, n), lambda i, e: (chunk * na + i, 0))

    n_rows = na * nb * slots
    n_half = nq // 2
    if even:
        d_specs = [pl.BlockSpec((nb, tok, width), lambda i, e: (0, 0, 0))] * na
        y_specs = [pl.BlockSpec((1, nb, tok, width), lambda i, e: (chunk // 2, 0, 0, 0))] * na
        d_shapes = [jax.ShapeDtypeStruct((nb, tok, width), BF)] * na
        y_shapes = [jax.ShapeDtypeStruct((n_half, nb, tok, width), BF)] * na
    else:
        d_specs = [two] * nb
        y_specs = [pl.BlockSpec((1, 1, tok, width), lambda i, e: (chunk // 2, i, 0, 0))] * nb
        d_shapes = [jax.ShapeDtypeStruct((na, tok, width), BF)] * nb
        y_shapes = [jax.ShapeDtypeStruct((n_half, na, tok, width), BF)] * nb
    held = [*(kept or ()), *(y_kept or ())]
    n_in = 1 + 1 + len(c) + len(g) + 3
    n_out = len(d_shapes) + 1
    aliases = {n_in + k: n_out + k for k in range(len(kept or ()))}
    for k in range(len(y_kept or ())):
        aliases[n_in + len(kept or ()) + k] = n_out + 4 + k
    out = pl.pallas_call(
        functools.partial(expert_kernel, slots, na, nb, even, len(held)),
        grid_spec=pltpu.PrefetchScalarGridSpec(
            num_scalar_prefetch=1,
            grid=(na,),
            in_specs=[
                pl.BlockSpec((1, nb, 1, experts, tok), lambda i, e: (i, 0, chunk, 0, 0)),
                *([one, g_one] if even else [two] * nb + [g_two] * nb),
                fixed(router_t.shape), fixed(w1.shape), fixed(w2.shape),
                *[pl.BlockSpec(memory_space=pl.ANY)] * len(held),
            ],
            out_specs=[
                *d_specs,
                pl.BlockSpec((1, nb, 1, tok), lambda i, e: (i, 0, 0, 0)),
                by_rows(width), by_rows(FF), by_rows(width), by_rows(2 * FF),
                *y_specs,
            ],
        ),
        out_shape=[
            *d_shapes,
            jax.ShapeDtypeStruct((na, nb, 1, tok), F32),
            *[jax.ShapeDtypeStruct((nq * n_rows, n), BF) for n in (width, FF, width, 2 * FF)],
            *y_shapes,
        ],
        input_output_aliases=aliases,
        compiler_params=pltpu.CompilerParams(vmem_limit_bytes=VMEM_LIMIT),
        cost_estimate=pl.CostEstimate(
            flops=n_rows * width * FF * 12, bytes_accessed=30_000_000, transcendentals=n_rows * FF
        ),
        name="experts",
    )(expert, ranks, *c, *g, router_t, w1, w2, *held)
    n_d = len(d_shapes)
    return out[:n_d], out[n_d], out[n_out : n_out + 4], out[n_out + 4 :]


def body(
    n_experts,
    block_input,
    cotangent,
    routes,
    attn_gain,
    query_key_value_weight,
    attention_output_weight,
    ffn_gain,
    routing_weight,
    common_expert_gate_up_weight,
    common_expert_down_weight,
    expert_gate_up,
    expert_down,
):
    nq, nr, na, nb = (lax.axis_size(axis) for axis in ("q", "r", "a", "b"))
    q_at, r_at, a_at, b_at = (lax.axis_index(axis) for axis in ("q", "r", "a", "b"))
    n_ctx = nq * nr
    n_exp = na * nb
    ctx_rank = q_at * nr + r_at
    exp_rank = a_at * nb + b_at
    tok = block_input.shape[1]
    width = block_input.shape[2]
    half = tok // 2
    capacity = min(tok, 3 * TOP * tok // (2 * n_experts))
    slots = -(-capacity // 16) * 16
    row = jnp.arange(tok, dtype=jnp.int32)
    local_pos = jnp.where(
        row < half, ctx_rank * half + row, (2 * n_ctx - 1 - ctx_rank) * half + row - half
    )
    cosines, sines = rope_tables(local_pos, HEAD_DIM)
    sines = jnp.where(jnp.arange(HEAD_DIM)[None, :] < HEAD_DIM // 2, -sines, sines)
    tables = (cosines, sines)
    tokens_in = block_input[0].astype(F32)
    grad_low = cotangent[0]
    out_grad = grad_low.astype(F32)
    own_rows = query_key_value_weight.shape[0]
    down_rows = common_expert_down_weight.shape[0]

    named = jnp.any(
        routes[0][:, :, None] == jnp.arange(n_experts, dtype=jnp.int32)[None, None, :], axis=1
    )
    before = (row[:, None] < row[None, :]).astype(BF)
    rank = dot(named.astype(BF).T, before)
    rank = jnp.where(named.T, rank, -1.0)
    ranks = jnp.stack(direct_gather(rank, "q"))
    ranks = jnp.stack(ring_gather(ranks, "b"))
    ranks = jnp.stack(ring_gather(ranks, "a"))

    zeros = jnp.zeros((own_rows, 127), BF)
    front = jnp.concatenate([query_key_value_weight, attn_gain[:, None], zeros], axis=1)
    front_q = ring_gather(front, "q")
    rest = jnp.concatenate(
        [
            attention_output_weight,
            common_expert_gate_up_weight,
            common_expert_down_weight.reshape(own_rows, -1),
            ffn_gain[:, None],
            routing_weight,
            zeros[:, n_experts:],
        ],
        axis=1,
    )
    flat = common_expert_down_weight.size // own_rows
    front_q[-1] = after(front_q[-1], ranks)
    steps = dense_steps(nq)
    front_first = dense_start(front_q)

    gu_rows = expert_gate_up.shape[1]
    folded = expert_down.reshape(nq, -1, 2 * FF)
    both = jnp.concatenate([expert_gate_up, folded], axis=1)

    rest_q = ring_gather(pick("rest", rest, f1=front_q[1], f3=front_q[-1]), "q")
    g_q = [pick("g", grad_low, r1=rest_q[1], r3=rest_q[-1], f3=front_q[-1])]
    g_q.append(shift(g_q[0], "q"))
    front_first = [
        pick(f"mid{i}", v, r1=rest_q[1], r2=rest_q[2]) for i, v in enumerate(front_first)
    ]
    front_pieces = dense_end(*front_first)
    due = [pick("core2", front_pieces[0], r1=rest_q[1], r2=rest_q[2], r3=rest_q[3], g1=g_q[1])]
    qkv_weight, front_small = dense_place(front_pieces, steps, [3 * width, 128], due)
    for _ in range(nq - 2):
        g_q.append(shift(g_q[-1], "q"))
    rest_first = dense_start(
        [pick("rs1", part, fp=front_pieces, w=qkv_weight) for part in rest_q]
    )

    kv_chunks = []
    gain_one = front_small[:, 0].astype(F32)
    inv_one = rms_scale(tokens_in)
    normed = (tokens_in * inv_one * gain_one).astype(BF)
    normed = pick("norm", normed, rs=rest_first, g1=g_q[1], g2=g_q[2], g3=g_q[3])
    queries, kv_own = project(normed, qkv_weight, *tables)
    places = [
        jnp.stack(
            [ctx_rank]
            + [
                lax.rem(q_at - k + nq, nq) * nr + lax.rem(r_at - s + nr, nr)
                for s in range(nr)
            ]
        ).astype(jnp.int32)
        for k in range(nq)
    ]
    rest_pieces = dense_end(*(pick("rs2", v, q=queries, w=qkv_weight) for v in rest_first))
    state = None
    arrived = kv_own
    for k in range(nq):
        chunk = ring_gather(arrived, "r")
        if k < nq - 1:
            coming = shift(arrived, "q")
        if k == 1:
            g_even, g_odd = (
                pick("gs1", jnp.stack(g_q[low::2]), rp=rest_pieces, a1=arrived) for low in (0, 1)
            )
            g_even = jnp.stack(ring_gather(g_even, "b"))
            g_odd = jnp.stack(ring_gather(g_odd, "a"))
        state = attend_chunk(places[k], queries, chunk, state, k == nq - 1, n_ctx)
        kv_chunks.append(chunk)
        if k < nq - 1:
            if k == 0:
                arrived = pick("arr1", coming, s=state[0], g2=g_q[2], g3=g_q[3], rp=rest_pieces)
            if k == 1:
                arrived = pick("arr2", coming, s=state[0], gs=(g_even, g_odd), rp=rest_pieces)
            if k == 2:
                g_even, g_odd = ring_gather(g_even, "a"), ring_gather(g_odd, "b")
                arrived = pick("arr3", coming, s=state[0], gf=(g_even, g_odd))
    mixed, lse = state
    both = pick("wa", both, a3=arrived, c3=chunk[1:], q=queries, m=mixed)
    both = lax.all_to_all(both, "q", split_axis=0, concat_axis=0, tiled=True)
    mixed = pick("mix", mixed, gf=(g_even, g_odd))
    out_weight, shared_in, shared_out, rest_small = dense_place(
        rest_pieces, steps, [width, 2 * FF, flat, 128]
    )
    shared_out = shared_out.reshape(-1, width)
    gain_two = rest_small[:, 0].astype(F32)
    router = rest_small[:, 1 : 1 + n_experts]
    residual = tokens_in + dot(mixed, out_weight)
    inv_two = rms_scale(residual)
    second = (residual * inv_two * gain_two).astype(BF)
    expert = jnp.stack([exp_rank * nq + q_at, q_at, a_at, b_at]).astype(jnp.int32)
    router_t = router.T
    kept = None
    ys = [None, None]
    sum_first, dgates, decs = [], [], []
    c_q = ring_gather(second, "q")
    c_start = jnp.stack(ring_gather(c_q[0], "b"))
    c_planes = [plane_gather(c_q[0], True, c_start)]
    both = pick("wc", both, m=mixed, cs=c_start, c1=c_q[1], cp=c_planes[0])
    both = ring_gather(both, "r")
    kr = np.repeat(np.arange(nr, dtype=np.int32), nq)
    kq = np.tile(np.arange(nq, dtype=np.int32), nr)
    index = kq * nr + lax.rem(r_at - kr + nr, nr)
    w1, w2 = place(
        index.astype(jnp.int32),
        both,
        [((0, gu_rows), 0, 2 * FF), ((gu_rows, folded.shape[1]), 0, 2 * FF)],
    )
    w2 = w2.reshape(-1, width)
    g_even = [jnp.stack(g_even)]
    for k in range(nq):
        if k:
            ready = dict(w=w1) | {f"k{i}": v for i, v in enumerate(dgates)}
            rows = pick(f"c{k}a", c_q[k], **ready)
            first = jnp.stack(ring_gather(rows, "ba"[k % 2]))
            c_planes.append(plane_gather(rows, k % 2 == 0, pick(f"c{k}b", first, **ready)))
        c = c_planes[k]
        ready = {f"s{i}": v for i, v in enumerate(sum_first) if v is not None}
        if k == 3:
            ready["e1"] = dec_one = sum_end(sum_first[1], False)
        hold = pick(f"K{k}", ranks, **ready)
        dec, dgate, kept, ys[k % 2] = expert_chunk(
            k, nq, na, nb, expert, hold, c, (g_even, g_odd)[k % 2], router_t, w1, w2, kept, ys[k % 2], slots
        )
        dgates.append(dgate.reshape(na * nb, tok))
        ready = {f"k{i}": v for i, v in enumerate(dgates)}
        decs.append(dec)
        sum_first.append(None)
        if k:
            sum_first[k] = sum_start([pick(f"d{k}", v, **ready) for v in dec], k % 2 == 0)
    ready = {f"k{i}": v for i, v in enumerate(dgates)}
    sum_first[0] = sum_start([pick("d0", v, **ready) for v in decs[0]], True)
    firsts = sum_first
    dec_sums = [dec_one if k == 1 else sum_end(firsts[k], k % 2 == 0) for k in range(nq)]
    ready = {f"s{i}": v for i, v in enumerate(firsts)}
    xs, hs, deys, degs = kept[:4]
    gate_up_term = dot(pick("gu", xs, **ready), degs, TN).astype(BF)
    down_term = dot(pick("dn", hs, gu=gate_up_term, **ready), deys, TN).astype(BF)
    terms = [
        gate_up_term.reshape(nq, nr, gu_rows, 2 * FF),
        down_term.reshape(nq, nr, -1, 2 * FF),
    ]
    at = [lax.rem(r_at - k + nr, nr) for k in range(nr)]
    expert_rows = ring_sum(
        [
            jnp.concatenate(
                [lax.dynamic_index_in_dim(t, i, 1, keepdims=False) for t in terms], axis=1
            )
            for i in at
        ],
        "r",
    ).astype(BF)
    moving = dec_sums[1].astype(BF)
    for k in range(2, nq):
        term = dec_sums[k]
        term = pick(f"t{k}", term, gu=gate_up_term, dn=down_term, er=expert_rows)
        moving = (shift(moving, "q").astype(F32) + term).astype(BF)
    routed_grad = shift(moving, "q").astype(F32) + dec_sums[0]

    expert_rows = pick("ea", expert_rows, rg=routed_grad, t=moving)
    expert_rows = lax.all_to_all(expert_rows, "q", split_axis=0, concat_axis=0, tiled=True)

    ready = {f"k{i}": v for i, v in enumerate(dgates)}
    later = pick("sh", second, **ready)
    shared_pre = dot(later, shared_in)
    shared_gate, shared_up = shared_pre[:, :FF], shared_pre[:, FF:]
    shared_sig = jax.nn.sigmoid(shared_gate)
    shared_hidden = (shared_gate * shared_sig * shared_up).astype(BF)

    logits = jnp.where(named, dot(later, router), masked_value)
    raised = jnp.where(named, jnp.exp(logits - jnp.max(logits, axis=1, keepdims=True)), 0.0)
    gates = raised / jnp.sum(raised, axis=1, keepdims=True)
    n_all = nq * na * nb
    spot = np.arange(n_all, dtype=np.int32)
    spot = (
        lax.rem(q_at - spot // (na * nb) + nq, nq) * (na * nb)
        + lax.rem(a_at - spot // nb % na + na, na) * nb
        + lax.rem(b_at - spot % nb + nb, nb)
    )
    dgate = jnp.concatenate(dgates, axis=0)[spot]
    dgate = lax.all_to_all(dgate, ("q", "a", "b"), split_axis=0, concat_axis=0, tiled=True)
    dgate = jnp.swapaxes(dgate.reshape(nq, na * nb, tok), 0, 1).reshape(n_experts, tok).T
    grad_logits = gates * (dgate - jnp.sum(gates * dgate, axis=1, keepdims=True))
    grad_logits = grad_logits.astype(BF)

    shared_hidden_grad = dot(grad_low, shared_out, NT)
    shared_pre_grad = jnp.concatenate(
        [
            shared_hidden_grad * shared_up * shared_sig * (1.0 + shared_gate * (1.0 - shared_sig)),
            shared_hidden_grad * shared_gate * shared_sig,
        ],
        axis=1,
    ).astype(BF)
    second_grad = (
        dot(shared_pre_grad, shared_in, NT) + dot(grad_logits, router, NT) + routed_grad
    )
    ffn_gain_grad = jnp.sum(second_grad * residual * inv_two, axis=0)
    residual_grad = out_grad + norm_back(second_grad, residual, inv_two, gain_two)
    mixed_grad = residual_grad.astype(BF)
    heads_grad = dot(mixed_grad, out_weight, NT).astype(BF)

    y_first = [
        sum_start([pick("y1", v, rg=routed_grad, k=dgates[3]) for v in ys[p]], p == 0)
        for p in (0, 1)
    ]
    dq = None
    moving = None
    held = heads_grad
    for step, k in enumerate(list(range(1, nq)) + [0]):
        ready = dict(er=expert_rows, y=y_first, m=moving if step else ())
        held = pick(f"B{step}", held, **ready)
        dq, parts = attend_back_chunk(
            places[k], queries, held, mixed, lse, tables, kv_chunks[k], dq, k == 0, n_ctx
        )
        term = ring_sum(parts, "r")
        if k == 1:
            moving = term.astype(BF)
            first_move = moving
        elif k:
            moving = (shift(moving, "q").astype(F32) + term).astype(BF)
    late = dense_sum_core(
        [
            dot(normed, dq, TN).astype(BF),
            dot(mixed, mixed_grad, TN).astype(BF),
            dot(later, shared_pre_grad, TN).astype(BF),
            dot(shared_hidden, grad_low, TN).astype(BF).reshape(width, flat),
        ],
        own_rows,
    )
    y_sums = [sum_end(pick("y2", y_first[p], q=dq, m=moving, f=first_move), p == 0, 1) for p in (0, 1)]
    late = dense_sum_first(late)
    kv_back = finish_keys(
        shift(moving, "q"), pick("fin", term, late=late, ys=y_sums), *tables
    )

    gate_up_grad = expert_rows[:, :gu_rows].astype(F32)
    down_grad = expert_rows[:, gu_rows:].reshape(nq, -1, width).astype(F32)
    normed_grad = dot(dq, qkv_weight[:, :width], NT)
    normed_grad += dot(kv_back[0], qkv_weight[:, width : 2 * width], NT)
    normed_grad += dot(kv_back[1], qkv_weight[:, 2 * width :], NT)
    attn_gain_grad = jnp.sum(normed_grad * tokens_in * inv_one, axis=0)
    input_grad = residual_grad + norm_back(normed_grad, tokens_in, inv_one, gain_one)
    small_grad = jnp.concatenate(
        [
            attn_gain_grad[:, None],
            ffn_gain_grad[:, None],
            dot(second, grad_logits, TN),
            jnp.zeros((width, 126 - n_experts), F32),
        ],
        axis=1,
    ).astype(BF)
    key_value = dense_sum_core(
        [
            pick("kv1", dot(normed, kv_back[0], TN).astype(BF), late=late, ys=y_sums),
            dot(normed, kv_back[1], TN).astype(BF),
            small_grad,
        ],
        own_rows,
    )
    y_sums = pick("y3", y_sums, b=kv_back, kv=key_value, m=moving)
    y_terms = [y_sums[k % 2][k // 2] for k in range(nq)]
    late = dense_sum_second(*(pick("late2", v, b=kv_back, kv=key_value) for v in late))
    first_kv = dense_sum_first(pick("kv2", key_value, l=late))
    last_kv = dense_sum_second(*first_kv)
    y_moving = y_terms[1].astype(BF)
    for k in range(2, nq + 1):
        y_moving = shift(y_moving, "q")
        y_moving = pick(f"yz{k}", y_moving, kv=key_value, f=first_kv, l=late, z=last_kv)
        routed_sum = y_moving.astype(F32) + y_terms[k % nq]
        y_moving = routed_sum.astype(BF)
    late_grad = dense_sum_last(pick("late3", late, f=first_kv, kv=key_value, z=last_kv))
    kv_weight_grad = dense_sum_last(last_kv)
    layer_out = (residual + dot(shared_hidden, shared_out) + routed_sum).astype(BF)
    at_out, at_shared, at_down = width, 2 * width, 2 * width + 2 * FF
    return (
        layer_out[None],
        input_grad[None],
        kv_weight_grad[:, 2 * width],
        jnp.concatenate([late_grad[:, :at_out], kv_weight_grad[:, : 2 * width]], axis=1),
        late_grad[:, at_out:at_shared],
        kv_weight_grad[:, 2 * width + 1],
        kv_weight_grad[:, 2 * width + 2 : 2 * width + 2 + n_experts],
        late_grad[:, at_shared:at_down],
        late_grad[:, at_down:].reshape(down_rows, width),
        gate_up_grad,
        down_grad,
    )


def solution(mesh):
    n_ctx, n_exp = mesh.shape["ctx"], mesh.shape["exp"]

    def layer(*args):
        n_experts = args[10].shape[0]
        nq = n_experts // n_exp
        nb = 2
        fine = Mesh(
            np.asarray(mesh.devices).reshape(nq, n_ctx // nq, n_exp // nb, nb), ("q", "r", "a", "b")
        )
        ctx, exp, every = ("q", "r"), ("a", "b"), ("q", "r", "a", "b")
        tokens, flat, rows = P(exp, ctx, None), P(every), P(every, None)
        run = jax.shard_map(
            functools.partial(body, n_experts),
            mesh=fine,
            in_specs=(
                tokens, tokens, tokens, flat, rows, rows, flat, rows, rows, rows, tokens, tokens,
            ),
            out_specs=(tokens, tokens, flat, rows, rows, flat, rows, rows, rows, tokens, tokens),
            check_vma=False,
        )
        return run(*args)

    return layer
```

```python
import functools

import jax
import jax.numpy as jnp
import numpy as np
from jax import lax
from jax.experimental import pallas as pl
from jax.experimental.pallas import tpu as pltpu
from jax.sharding import Mesh
from jax.sharding import PartitionSpec as P

HEADS = 10
HEAD_DIM = 128
FF = 896
TOP = 7

norm_eps = 1e-06
rope_base = 10000.0
masked_value = -1e30
LOG2E = 1.4426950408889634

BF = jnp.bfloat16
F32 = jnp.float32
VMEM_LIMIT = 56 * 1024 * 1024


def rope_tables(positions, head_dim):
    halfway = head_dim // 2
    frequency = rope_base ** (-(jnp.arange(halfway).astype(F32) * 2.0 / head_dim))
    angles = positions.astype(F32)[:, None] * frequency[None, :]
    angles = jnp.concatenate([angles, angles], axis=1)
    return (jnp.cos(angles), jnp.sin(angles))


def rms_scale(values):
    return lax.rsqrt(jnp.mean(values * values, axis=1, keepdims=True) + norm_eps)


def norm_back(grad_in, values, inv_rms, gain_vec):
    scaled = grad_in * gain_vec
    return inv_rms * scaled - values * inv_rms**3 * jnp.mean(scaled * values, axis=1, keepdims=True)


def dot(a, b, dims=((1,), (0,))):
    return lax.dot_general(a, b, (dims, ((), ())), preferred_element_type=F32)


NT = ((1,), (1,))
TN = ((0,), (0,))


def shift(value, axis):
    n = lax.axis_size(axis)
    return lax.ppermute(value, axis, [(i, (i + 1) % n) for i in range(n)])


def ring_gather(value, axis):
    parts = [value]
    for _ in range(1, lax.axis_size(axis)):
        parts.append(shift(parts[-1], axis))
    return parts


def shift_by(value, axis, k):
    n = lax.axis_size(axis)
    return lax.ppermute(value, axis, [(i, (i + k) % n) for i in range(n)])


def direct_gather(value, axis):
    return [value] + [shift_by(value, axis, k) for k in range(1, lax.axis_size(axis))]


def ring_sum(blocks, axis, events=()):
    n = len(blocks)
    if n == 1:
        return blocks[0].astype(F32)
    moving = blocks[1].astype(BF)
    for k in range(2, n):
        moving = after(shift(moving, axis), *events)
        moving = (moving.astype(F32) + blocks[k].astype(F32)).astype(BF)
    return after(shift(moving, axis), *events).astype(F32) + blocks[0].astype(F32)


def ring_blocks(arrays, axis, dim):
    n = lax.axis_size(axis)
    index = lax.axis_index(axis)
    out = []
    for k in range(n):
        at = lax.rem(index - k + n, n)
        parts = [lax.dynamic_index_in_dim(v, at, dim, keepdims=False) for v in arrays]
        out.append(parts[0] if len(parts) == 1 else jnp.concatenate(parts, axis=-1))
    return out


ORDER = {
    "g": "r1",
    "mid1": "r1",
    "rs1": "fp",
    "norm": "rs g1",
    "gs1": "rp",
    "arr1": "g3 rp",
    "arr2": "s",
    "arr3": "s gf",
    "wa": "q",
    "wc": "cp",
    "c1b": "w",
    "c2b": "k0",
    "c3a": "k0",
    "K1": "s0",
    "gu": "s0",
    "dn": "s1",
    "t2": "er",
    "sh": "k2",
    "B1": "m",
    "B3": "er",
    "y1": "rg",
    "fin": "late",
    "kv1": "late",
    "kv2": "l",
    "yz2": "kv",
    "yz4": "l",
    "late3": "kv",
    "xg": "m",
    "dn0": "kv",
}


def pick(name, value, **events):
    chosen = [events[key] for key in ORDER.get(name, "").split() if key in events]
    return after(value, *jax.tree.leaves(chosen))


def after(value, *events):
    if not events:
        return value
    return lax.optimization_barrier((value, *events))[0]


def place_kernel(counts, cuts, index_ref, *refs):
    n = len(counts)
    pieces, outs, sems = refs[:n], refs[n:-1], refs[-1]
    t = 0
    for piece, count in zip(pieces, counts):
        for j in range(count):
            at = index_ref[t]
            t += 1
            for o, (rows, low, high) in enumerate(cuts):
                pltpu.make_async_copy(
                    piece.at[j, pl.ds(*rows), pl.ds(low, high - low)], outs[o].at[at], sems.at[o]
                ).start()
    for o in range(len(cuts)):
        pltpu.make_async_copy(outs[o], outs[o], sems.at[o]).wait()


def place(index, pieces, cuts):
    rows, total = pieces[0].shape[-2:]
    pieces = [piece.reshape(-1, rows, total) for piece in pieces]
    counts = [piece.shape[0] for piece in pieces]
    n = sum(counts)
    outs = pl.pallas_call(
        functools.partial(place_kernel, counts, cuts),
        in_specs=[pl.BlockSpec(memory_space=pltpu.SMEM)]
        + [pl.BlockSpec(memory_space=pl.ANY)] * len(pieces),
        out_specs=[pl.BlockSpec(memory_space=pltpu.VMEM)] * len(cuts),
        scratch_shapes=[pltpu.SemaphoreType.DMA((len(cuts),))],
        out_shape=[
            jax.ShapeDtypeStruct((n, c[0][1], c[2] - c[1]), pieces[0].dtype) for c in cuts
        ],
        compiler_params=pltpu.CompilerParams(vmem_limit_bytes=VMEM_LIMIT),
        cost_estimate=pl.CostEstimate(
            flops=0, bytes_accessed=4 * n * rows * total, transcendentals=0
        ),
        name="place",
    )(index, *pieces)
    return [out.reshape(-1, out.shape[2]) for out in outs]


def dense_steps(nq):
    half, na, nb = nq // 2, lax.axis_size("a"), lax.axis_size("b")
    steps = [[(kq, ka, kb) for kb in range(nb) for kq in range(half)] for ka in range(na)]
    return steps + [
        [(kq, ka, kb) for ka in range(na) for kq in range(half, nq)] for kb in range(nb)
    ]


def dense_start(along_q):
    half = len(along_q) // 2
    one = jnp.stack(ring_gather(jnp.stack(along_q[:half]), "b"))
    two = jnp.stack(ring_gather(jnp.stack(along_q[half:]), "a"))
    return one, two


def dense_end(one, two):
    return ring_gather(one, "a") + ring_gather(two, "b")


def dense_place(pieces, steps, widths, due=()):
    nq, nr, na, nb = (lax.axis_size(axis) for axis in ("q", "r", "a", "b"))
    rows, width = pieces[0].shape[-2:]
    flat = [piece.reshape(-1, rows, width) for piece in pieces]
    groups = [[0, na], [k for k in range(na + nb) if k not in (0, na)]]
    arrays, order = [], []
    for group in groups:
        own = jnp.concatenate([flat[k] for k in group], axis=0)
        if group is groups[1]:
            own = after(own, *due)
        entries = [s for k in group for s in steps[k]]
        for kr, part in enumerate(ring_gather(own, "r")):
            arrays.append(part)
            order += [(kr, *s) for s in entries]
    kr, kq, ka, kb = (np.array(column, np.int32) for column in zip(*order))
    index = lax.rem(lax.axis_index("q") - kq + nq, nq) * nr
    index = index + lax.rem(lax.axis_index("r") - kr + nr, nr)
    index = index * na + lax.rem(lax.axis_index("a") - ka + na, na)
    index = index * nb + lax.rem(lax.axis_index("b") - kb + nb, nb)
    edges = np.cumsum([0] + list(widths))
    cuts = [((0, rows), int(low), int(high)) for low, high in zip(edges[:-1], edges[1:])]
    return place(index.astype(jnp.int32), arrays, cuts)


def dense_sum_core(wholes, n_rows):
    nq, nr, na, nb = (lax.axis_size(axis) for axis in ("q", "r", "a", "b"))
    values = [whole.reshape(nq, nr, na, nb, n_rows, whole.shape[1]) for whole in wholes]
    return ring_sum(ring_blocks(values, "r", 1), "r").astype(BF)


def dense_sum_first(value):
    half = value.shape[0] // 2
    one = ring_sum(ring_blocks([value[:half]], "a", 1), "a").astype(BF)
    two = ring_sum(ring_blocks([value[half:]], "b", 2), "b").astype(BF)
    return one, two


def dense_sum_second(one, two):
    one = ring_sum(ring_blocks([one], "b", 1), "b")
    two = ring_sum(ring_blocks([two], "a", 1), "a")
    return jnp.concatenate([one, two], axis=0).astype(BF)


def dense_sum_last(value):
    return ring_sum(ring_blocks([value], "q", 0), "q")


def plane_gather(rows, even, first=None):
    inner, outer = ("b", "a") if even else ("a", "b")
    if first is None:
        first = jnp.stack(ring_gather(rows, inner))
    parts = ring_gather(first, outer)
    return [jnp.stack(parts)] if even else parts


def sum_start(parts, even, events=()):
    return ring_sum(parts, "a" if even else "b", events)


def sum_end(first, even, dim=0, events=()):
    n = first.shape[dim]
    parts = [lax.index_in_dim(first, k, dim, False) for k in range(n)]
    return ring_sum(parts, "b" if even else "a", events)


def project_kernel(n_query, x_ref, w_ref, cos_ref, sin_ref, q_ref, kv_ref):
    j = pl.program_id(0)
    made = dot(x_ref[...], w_ref[...])

    def turned():
        parts = []
        for low in range(0, made.shape[1], HEAD_DIM):
            u = made[:, low : low + HEAD_DIM]
            parts.append(u * cos_ref[...] + pltpu.roll(u, HEAD_DIM // 2, 1) * sin_ref[...])
        return jnp.concatenate(parts, axis=1).astype(BF)

    @pl.when(j < n_query)
    def _():
        q_ref[...] = turned()

    @pl.when((j >= n_query) & (j < 2 * n_query))
    def _():
        kv_ref[0] = turned()

    @pl.when(j >= 2 * n_query)
    def _():
        kv_ref[0] = made.astype(BF)


def project(normed, weight, cosines, signed_sine):
    tok, width = normed.shape
    block = 2 * HEAD_DIM
    n = width // block
    table = pl.BlockSpec((tok, HEAD_DIM), lambda j: (0, 0))
    return pl.pallas_call(
        functools.partial(project_kernel, n),
        grid=(3 * n,),
        in_specs=[
            pl.BlockSpec((tok, width), lambda j: (0, 0)),
            pl.BlockSpec((width, block), lambda j: (0, j)),
            table,
            table,
        ],
        out_specs=[
            pl.BlockSpec((tok, block), lambda j: (0, jnp.minimum(j, n - 1))),
            pl.BlockSpec(
                (1, tok, block),
                lambda j: (jnp.maximum(j - n, 0) // n, 0, jnp.maximum(j - n, 0) % n),
            ),
        ],
        out_shape=[
            jax.ShapeDtypeStruct((tok, width), BF),
            jax.ShapeDtypeStruct((2, tok, width), BF),
        ],
        compiler_params=pltpu.CompilerParams(vmem_limit_bytes=VMEM_LIMIT),
        cost_estimate=pl.CostEstimate(
            flops=6 * tok * width * width, bytes_accessed=6 * width * width, transcendentals=0
        ),
        name="project",
    )(normed, weight, cosines, signed_sine)


def turn_back(grad, cos, signed_sine):
    return grad * cos - pltpu.roll(grad, HEAD_DIM // 2, 1) * signed_sine


def finish_kernel(moved_ref, own_ref, cos_ref, sin_ref, out_ref):
    keys = moved_ref[0].astype(F32) + own_ref[0]
    out_ref[0] = turn_back(keys, cos_ref[...], sin_ref[...]).astype(BF)
    out_ref[1] = (moved_ref[1].astype(F32) + own_ref[1]).astype(BF)


def finish_keys(moved, own, cosines, signed_sine):
    _, tok, width = own.shape
    pair = pl.BlockSpec((2, tok, HEAD_DIM), lambda h: (0, 0, h))
    table = pl.BlockSpec((tok, HEAD_DIM), lambda h: (0, 0))
    return pl.pallas_call(
        finish_kernel,
        grid=(width // HEAD_DIM,),
        in_specs=[pair, pair, table, table],
        out_specs=pair,
        out_shape=jax.ShapeDtypeStruct((2, tok, width), BF),
        cost_estimate=pl.CostEstimate(
            flops=10 * tok * width, bytes_accessed=16 * tok * width, transcendentals=0
        ),
        name="finish_keys",
    )(moved, own, cosines, signed_sine)


def allowed_mask(own, other, n_ctx, half):
    row = lax.broadcasted_iota(jnp.int32, (2 * half, 2 * half), 0)
    col = lax.broadcasted_iota(jnp.int32, (2 * half, 2 * half), 1)
    last = 2 * n_ctx - 1
    query = row + jnp.where(row < half, own * half, (last - own) * half - half)
    key = col + jnp.where(col < half, other * half, (last - other) * half - half)
    return key <= query


def attend_kernel(n_ctx, n_src, first, last, place_ref, q_ref, *refs):
    kv_refs, refs = refs[:n_src], refs[n_src:]
    if not first:
        acc_in, ml_in = refs[:2]
        refs = refs[2:]
    out_ref, ml_ref = refs
    queries = q_ref[...]
    tok = queries.shape[0]
    scores = []
    for s in range(n_src):
        raw = dot(queries, kv_refs[s][0], NT) * (HEAD_DIM ** (-0.5) * LOG2E)
        mask = allowed_mask(place_ref[0], place_ref[1 + s], n_ctx, tok // 2)
        scores.append(jnp.where(mask, raw, masked_value))
    peak = functools.reduce(jnp.maximum, [jnp.max(s, axis=1, keepdims=True) for s in scores])
    if not first:
        old_peak = ml_in[0][:, 0:1]
        old_sum = ml_in[0][:, 64:65]
        peak = jnp.maximum(peak, old_peak)
    total = jnp.zeros_like(peak)
    mixed = jnp.zeros((tok, HEAD_DIM), F32)
    for s in range(n_src):
        raised = jnp.exp2(scores[s] - peak)
        total = total + jnp.sum(raised, axis=1, keepdims=True)
        mixed = mixed + dot(raised.astype(BF), kv_refs[s][1])
    if not first:
        decay = jnp.exp2(old_peak - peak)
        total = total + old_sum * decay
        mixed = mixed + acc_in[...] * decay
    if last:
        out_ref[...] = (mixed / total).astype(BF)
        ml_ref[0] = jnp.broadcast_to(peak + jnp.log2(total), (tok, 128))
    else:
        out_ref[...] = mixed
        lane = lax.broadcasted_iota(jnp.int32, (tok, 128), 1)
        ml_ref[0] = jnp.where(lane < 64, peak, total)


def attend_chunk(places, queries, kv_list, state, last, n_ctx):
    tok, width = queries.shape
    head = pl.BlockSpec((tok, HEAD_DIM), lambda h, p: (0, h))
    pair = pl.BlockSpec((2, tok, HEAD_DIM), lambda h, p: (0, 0, h))
    rows = pl.BlockSpec((1, tok, 128), lambda h, p: (h, 0, 0))
    first = state is None
    n = len(kv_list)
    pairs = tok * tok * n * HEADS
    return pl.pallas_call(
        functools.partial(attend_kernel, n_ctx, n, first, last),
        grid_spec=pltpu.PrefetchScalarGridSpec(
            num_scalar_prefetch=1,
            grid=(HEADS,),
            in_specs=[head] + [pair] * n + ([] if first else [head, rows]),
            out_specs=[head, rows],
        ),
        out_shape=[
            jax.ShapeDtypeStruct((tok, width), BF if last else F32),
            jax.ShapeDtypeStruct((HEADS, tok, 128), F32),
        ],
        compiler_params=pltpu.CompilerParams(vmem_limit_bytes=VMEM_LIMIT),
        cost_estimate=pl.CostEstimate(
            flops=4 * pairs * HEAD_DIM * 4, bytes_accessed=8 * tok * width, transcendentals=pairs
        ),
        name="attend",
    )(places, queries, *kv_list, *(() if first else state))


def attend_back_kernel(
    n_ctx, n_src, first, last, place_ref, q_ref, do_ref, o_ref, lse_ref, cos_ref, sin_ref, *refs
):
    kv_refs, refs = refs[:n_src], refs[n_src:]
    if not first:
        dq_in, refs = refs[0], refs[1:]
    dq_ref, dkv_refs = refs[0], refs[1:]
    queries = q_ref[...]
    grad = do_ref[...]
    tok = queries.shape[0]
    lse = lse_ref[0][:, 0:1]
    delta = jnp.sum(grad.astype(F32) * o_ref[...].astype(F32), axis=1, keepdims=True)
    scale = HEAD_DIM ** (-0.5)
    grad_query = jnp.zeros((tok, HEAD_DIM), F32)
    for s in range(n_src):
        keys, values = kv_refs[s][0], kv_refs[s][1]
        raw = dot(queries, keys, NT) * (scale * LOG2E)
        mask = allowed_mask(place_ref[0], place_ref[1 + s], n_ctx, tok // 2)
        probs = jnp.exp2(jnp.where(mask, raw, masked_value) - lse)
        grad_probs = dot(grad, values, NT)
        grad_scores = (probs * (grad_probs - delta)).astype(BF)
        grad_query = grad_query + dot(grad_scores, keys)
        dkv_refs[s][0] = (dot(grad_scores, queries, TN) * scale).astype(dkv_refs[s].dtype)
        dkv_refs[s][1] = dot(probs.astype(BF), grad, TN).astype(dkv_refs[s].dtype)
    grad_query = grad_query * scale
    if not first:
        grad_query = grad_query + dq_in[...]
    if last:
        grad_query = turn_back(grad_query, cos_ref[...], sin_ref[...]).astype(BF)
    dq_ref[...] = grad_query


def attend_back_chunk(places, queries, grad, mixed, lse, tables, kv_list, dq, last, n_ctx):
    tok, width = queries.shape
    head = pl.BlockSpec((tok, HEAD_DIM), lambda h, p: (0, h))
    pair = pl.BlockSpec((2, tok, HEAD_DIM), lambda h, p: (0, 0, h))
    rows = pl.BlockSpec((1, tok, 128), lambda h, p: (h, 0, 0))
    table = pl.BlockSpec((tok, HEAD_DIM), lambda h, p: (0, 0))
    first = dq is None
    n = len(kv_list)
    pairs = tok * tok * n * HEADS
    out = pl.pallas_call(
        functools.partial(attend_back_kernel, n_ctx, n, first, last),
        grid_spec=pltpu.PrefetchScalarGridSpec(
            num_scalar_prefetch=1,
            grid=(HEADS,),
            in_specs=[head, head, head, rows, table, table] + [pair] * n + ([] if first else [head]),
            out_specs=[head] + [pair] * n,
        ),
        out_shape=[jax.ShapeDtypeStruct((tok, width), BF if last else F32)]
        + [jax.ShapeDtypeStruct((2, tok, width), F32 if s == 0 else BF) for s in range(n)],
        compiler_params=pltpu.CompilerParams(vmem_limit_bytes=VMEM_LIMIT),
        cost_estimate=pl.CostEstimate(
            flops=10 * pairs * HEAD_DIM * 4, bytes_accessed=16 * tok * width, transcendentals=pairs
        ),
        name="attend_back",
    )(places, queries, grad, mixed, lse, *tables, *kv_list, *(() if first else (dq,)))
    return out[0], out[1:]


def expert_kernel(slots, na, nb, even, n_kept, e_ref, rank_ref, *refs):
    n_in, n_sum = (1, na) if even else (nb, nb)
    c_refs, g_refs, refs = refs[:n_in], refs[n_in : 2 * n_in], refs[2 * n_in :]
    wr_ref, w1_ref, w2_ref = refs[:3]
    refs = refs[3 + n_kept :]
    d_refs, dg_ref, refs = refs[:n_sum], refs[n_sum], refs[n_sum + 1 :]
    x_ref, h_ref, dey_ref, deg_ref = refs[:4]
    y_refs = refs[4:]
    tok = g_refs[0].shape[-2]
    experts = wr_ref.shape[0]
    me = e_ref[0]
    step = pl.program_id(0)
    picks, rows, grads, weights = [], [], [], []
    own = lax.broadcasted_iota(jnp.int32, (experts, tok), 0) == me
    slot = lax.broadcasted_iota(jnp.int32, (slots, tok), 0).astype(F32)
    for s in range(nb):
        tokens = c_refs[0][0, s] if even else c_refs[s][0]
        cot = g_refs[0][0, s, 0] if even else g_refs[s][0, 0]
        rank = rank_ref[0, s, 0]
        logits = dot(wr_ref[...], tokens, NT)
        logits = jnp.where(rank >= 0, logits, masked_value)
        raised = jnp.where(rank >= 0, jnp.exp(logits - jnp.max(logits, axis=0, keepdims=True)), 0.0)
        gates = raised / jnp.sum(raised, axis=0, keepdims=True)
        gate_row = jnp.sum(jnp.where(own, gates, 0.0), axis=0, keepdims=True)
        rank_row = jnp.sum(jnp.where(own, rank, 0.0), axis=0, keepdims=True)
        pick = jnp.where(slot == rank_row, 1.0, 0.0)
        weights.append(jnp.sum(pick * gate_row, axis=1, keepdims=True))
        pick_low = pick.astype(BF)
        picks.append((pick, pick_low))
        rows.append(dot(pick_low, tokens).astype(BF))
        grads.append(dot(pick_low, cot))
    x = jnp.concatenate(rows, axis=0)
    grad = jnp.concatenate(grads, axis=0)
    weight = jnp.concatenate(weights, axis=0)
    x_ref[...] = x
    dey = (weight * grad).astype(BF)
    dey_ref[...] = dey
    pre = dot(x, w1_ref[...])
    gate, up = pre[:, :FF], pre[:, FF:]
    sig = jax.nn.sigmoid(gate)
    act = gate * sig
    hidden = (act * up).astype(BF)
    h_ref[...] = hidden
    grad_hidden = dot(dey, w2_ref[...], NT)
    deg = jnp.concatenate(
        [
            (grad_hidden * up * sig * (1.0 + gate * (1.0 - sig))).astype(BF),
            (grad_hidden * act).astype(BF),
        ],
        axis=1,
    )
    deg_ref[...] = deg
    dec = dot(deg, w1_ref[...], NT).astype(BF)
    ey = dot(hidden, w2_ref[...]).astype(BF).astype(F32)
    dgate = jnp.sum(grad * ey, axis=1, keepdims=True)
    weighted = (weight * ey).astype(BF)
    d_all, y_all = [], []
    for s in range(nb):
        part = slice(s * slots, (s + 1) * slots)
        pick, pick_low = picks[s]
        d_all.append(dot(pick_low, dec[part], TN).astype(BF))
        y_all.append(dot(pick_low, weighted[part], TN).astype(BF))
        if not even:
            d_refs[s][0] = d_all[s]
            y_refs[s][0, 0] = y_all[s]
        dg_ref[0, s] = jnp.sum(pick * dgate[part], axis=0, keepdims=True)
    if even:
        for k in range(na):

            @pl.when(step == k)
            def _(k=k):
                for s in range(nb):
                    d_refs[k][s] = d_all[s]
                    y_refs[k][0, s] = y_all[s]


def expert_chunk(chunk, nq, na, nb, expert, ranks, c, g, router_t, w1, w2, kept, y_kept, slots):
    even = chunk % 2 == 0
    tok, width = c[0].shape[-2:]
    experts = router_t.shape[0]
    g_one = pl.BlockSpec((1, nb, 1, tok, width), lambda i, e: (i, 0, chunk // 2, 0, 0))
    g_two = pl.BlockSpec((1, 1, tok, width), lambda i, e: (i, chunk // 2, 0, 0))
    one = pl.BlockSpec((1, nb, tok, width), lambda i, e: (i, 0, 0, 0))
    two = pl.BlockSpec((1, tok, width), lambda i, e: (i, 0, 0))

    def fixed(shape):
        return pl.BlockSpec(shape, lambda i, e: (0,) * len(shape), pipeline_mode=pl.Buffered(1))

    def by_rows(n):
        return pl.BlockSpec((nb * slots, n), lambda i, e: (chunk * na + i, 0))

    n_rows = na * nb * slots
    n_half = nq // 2
    if even:
        d_specs = [pl.BlockSpec((nb, tok, width), lambda i, e: (0, 0, 0))] * na
        y_specs = [pl.BlockSpec((1, nb, tok, width), lambda i, e: (chunk // 2, 0, 0, 0))] * na
        d_shapes = [jax.ShapeDtypeStruct((nb, tok, width), BF)] * na
        y_shapes = [jax.ShapeDtypeStruct((n_half, nb, tok, width), BF)] * na
    else:
        d_specs = [two] * nb
        y_specs = [pl.BlockSpec((1, 1, tok, width), lambda i, e: (chunk // 2, i, 0, 0))] * nb
        d_shapes = [jax.ShapeDtypeStruct((na, tok, width), BF)] * nb
        y_shapes = [jax.ShapeDtypeStruct((n_half, na, tok, width), BF)] * nb
    held = [*(kept or ()), *(y_kept or ())]
    n_in = 1 + 1 + len(c) + len(g) + 3
    n_out = len(d_shapes) + 1
    aliases = {n_in + k: n_out + k for k in range(len(kept or ()))}
    for k in range(len(y_kept or ())):
        aliases[n_in + len(kept or ()) + k] = n_out + 4 + k
    out = pl.pallas_call(
        functools.partial(expert_kernel, slots, na, nb, even, len(held)),
        grid_spec=pltpu.PrefetchScalarGridSpec(
            num_scalar_prefetch=1,
            grid=(na,),
            in_specs=[
                pl.BlockSpec((1, nb, 1, experts, tok), lambda i, e: (i, 0, chunk, 0, 0)),
                *([one, g_one] if even else [two] * nb + [g_two] * nb),
                fixed(router_t.shape), fixed(w1.shape), fixed(w2.shape),
                *[pl.BlockSpec(memory_space=pl.ANY)] * len(held),
            ],
            out_specs=[
                *d_specs,
                pl.BlockSpec((1, nb, 1, tok), lambda i, e: (i, 0, 0, 0)),
                by_rows(width), by_rows(FF), by_rows(width), by_rows(2 * FF),
                *y_specs,
            ],
        ),
        out_shape=[
            *d_shapes,
            jax.ShapeDtypeStruct((na, nb, 1, tok), F32),
            *[jax.ShapeDtypeStruct((nq * n_rows, n), BF) for n in (width, FF, width, 2 * FF)],
            *y_shapes,
        ],
        input_output_aliases=aliases,
        compiler_params=pltpu.CompilerParams(vmem_limit_bytes=VMEM_LIMIT),
        cost_estimate=pl.CostEstimate(
            flops=n_rows * width * FF * 12, bytes_accessed=30_000_000, transcendentals=n_rows * FF
        ),
        name="experts",
    )(expert, ranks, *c, *g, router_t, w1, w2, *held)
    n_d = len(d_shapes)
    return out[:n_d], out[n_d], out[n_out : n_out + 4], out[n_out + 4 :]


def body(
    n_experts,
    block_input,
    cotangent,
    routes,
    attn_gain,
    query_key_value_weight,
    attention_output_weight,
    ffn_gain,
    routing_weight,
    common_expert_gate_up_weight,
    common_expert_down_weight,
    expert_gate_up,
    expert_down,
):
    nq, nr, na, nb = (lax.axis_size(axis) for axis in ("q", "r", "a", "b"))
    q_at, r_at, a_at, b_at = (lax.axis_index(axis) for axis in ("q", "r", "a", "b"))
    n_ctx = nq * nr
    n_exp = na * nb
    ctx_rank = q_at * nr + r_at
    exp_rank = a_at * nb + b_at
    tok = block_input.shape[1]
    width = block_input.shape[2]
    half = tok // 2
    capacity = min(tok, 3 * TOP * tok // (2 * n_experts))
    slots = -(-capacity // 16) * 16
    row = jnp.arange(tok, dtype=jnp.int32)
    local_pos = jnp.where(
        row < half, ctx_rank * half + row, (2 * n_ctx - 1 - ctx_rank) * half + row - half
    )
    cosines, sines = rope_tables(local_pos, HEAD_DIM)
    sines = jnp.where(jnp.arange(HEAD_DIM)[None, :] < HEAD_DIM // 2, -sines, sines)
    tables = (cosines, sines)
    tokens_in = block_input[0].astype(F32)
    grad_low = cotangent[0]
    out_grad = grad_low.astype(F32)
    own_rows = query_key_value_weight.shape[0]
    down_rows = common_expert_down_weight.shape[0]

    named = jnp.any(
        routes[0][:, :, None] == jnp.arange(n_experts, dtype=jnp.int32)[None, None, :], axis=1
    )
    before = (row[:, None] < row[None, :]).astype(BF)
    rank = dot(named.astype(BF).T, before)
    rank = jnp.where(named.T, rank, -1.0)
    ranks = jnp.stack(direct_gather(rank, "q"))
    ranks = jnp.stack(ring_gather(ranks, "b"))
    ranks = jnp.stack(ring_gather(ranks, "a"))

    zeros = jnp.zeros((own_rows, 127), BF)
    front = jnp.concatenate([query_key_value_weight, attn_gain[:, None], zeros], axis=1)
    front_q = ring_gather(front, "q")
    rest = jnp.concatenate(
        [
            attention_output_weight,
            common_expert_gate_up_weight,
            common_expert_down_weight.reshape(own_rows, -1),
            ffn_gain[:, None],
            routing_weight,
            zeros[:, n_experts:],
        ],
        axis=1,
    )
    flat = common_expert_down_weight.size // own_rows
    front_q[-1] = after(front_q[-1], ranks)
    steps = dense_steps(nq)
    front_first = dense_start(front_q)

    gu_rows = expert_gate_up.shape[1]
    folded = expert_down.reshape(nq, -1, 2 * FF)
    both = jnp.concatenate([expert_gate_up, folded], axis=1)

    rest_q = ring_gather(pick("rest", rest, f1=front_q[1], f3=front_q[-1]), "q")
    g_q = [pick("g", grad_low, r1=rest_q[1], r3=rest_q[-1], f3=front_q[-1])]
    g_q.append(shift(g_q[0], "q"))
    front_first = [
        pick(f"mid{i}", v, r1=rest_q[1], r2=rest_q[2]) for i, v in enumerate(front_first)
    ]
    front_pieces = dense_end(*front_first)
    due = [pick("core2", front_pieces[0], r1=rest_q[1], r2=rest_q[2], r3=rest_q[3], g1=g_q[1])]
    qkv_weight, front_small = dense_place(front_pieces, steps, [3 * width, 128], due)
    for _ in range(nq - 2):
        g_q.append(shift(g_q[-1], "q"))
    rest_first = dense_start(
        [pick("rs1", part, fp=front_pieces, w=qkv_weight) for part in rest_q]
    )

    kv_chunks = []
    gain_one = front_small[:, 0].astype(F32)
    inv_one = rms_scale(tokens_in)
    normed = (tokens_in * inv_one * gain_one).astype(BF)
    normed = pick("norm", normed, rs=rest_first, g1=g_q[1], g2=g_q[2], g3=g_q[3])
    queries, kv_own = project(normed, qkv_weight, *tables)
    places = [
        jnp.stack(
            [ctx_rank]
            + [
                lax.rem(q_at - k + nq, nq) * nr + lax.rem(r_at - s + nr, nr)
                for s in range(nr)
            ]
        ).astype(jnp.int32)
        for k in range(nq)
    ]
    rest_pieces = dense_end(*(pick("rs2", v, q=queries, w=qkv_weight) for v in rest_first))
    state = None
    arrived = kv_own
    for k in range(nq):
        chunk = ring_gather(arrived, "r")
        if k < nq - 1:
            coming = shift(arrived, "q")
        if k == 1:
            g_even, g_odd = (
                pick("gs1", jnp.stack(g_q[low::2]), rp=rest_pieces, a1=arrived) for low in (0, 1)
            )
            g_even = jnp.stack(ring_gather(g_even, "b"))
            g_odd = jnp.stack(ring_gather(g_odd, "a"))
        state = attend_chunk(places[k], queries, chunk, state, k == nq - 1, n_ctx)
        kv_chunks.append(chunk)
        if k < nq - 1:
            if k == 0:
                arrived = pick("arr1", coming, s=state[0], g2=g_q[2], g3=g_q[3], rp=rest_pieces)
            if k == 1:
                arrived = pick("arr2", coming, s=state[0], gs=(g_even, g_odd), rp=rest_pieces)
            if k == 2:
                g_even, g_odd = ring_gather(g_even, "a"), ring_gather(g_odd, "b")
                arrived = pick("arr3", coming, s=state[0], gf=(g_even, g_odd))
    mixed, lse = state
    both = pick("wa", both, a3=arrived, c3=chunk[1:], q=queries, m=mixed)
    both = lax.all_to_all(both, "q", split_axis=0, concat_axis=0, tiled=True)
    mixed = pick("mix", mixed, gf=(g_even, g_odd))
    out_weight, shared_in, shared_out, rest_small = dense_place(
        rest_pieces, steps, [width, 2 * FF, flat, 128]
    )
    shared_out = shared_out.reshape(-1, width)
    gain_two = rest_small[:, 0].astype(F32)
    router = rest_small[:, 1 : 1 + n_experts]
    residual = tokens_in + dot(mixed, out_weight)
    inv_two = rms_scale(residual)
    second = (residual * inv_two * gain_two).astype(BF)
    expert = jnp.stack([exp_rank * nq + q_at, q_at, a_at, b_at]).astype(jnp.int32)
    router_t = router.T
    kept = None
    ys = [None, None]
    sum_first, dgates, decs = [], [], []
    c_q = [second, shift(second, "q")]
    c_start = jnp.stack(ring_gather(c_q[0], "b"))
    c_planes = [plane_gather(c_q[0], True, c_start)]
    both = pick("wc", both, m=mixed, cs=c_start, c1=c_q[1], cp=c_planes[0])
    both = ring_gather(both, "r")
    kr = np.repeat(np.arange(nr, dtype=np.int32), nq)
    kq = np.tile(np.arange(nq, dtype=np.int32), nr)
    index = kq * nr + lax.rem(r_at - kr + nr, nr)
    w1, w2 = place(
        index.astype(jnp.int32),
        both,
        [((0, gu_rows), 0, 2 * FF), ((gu_rows, folded.shape[1]), 0, 2 * FF)],
    )
    w2 = w2.reshape(-1, width)
    for k in range(2, nq):
        c_q.append(shift(pick(f"cz{k}", c_q[-1], w=w1, cp=c_planes[0]), "q"))
    g_even = [jnp.stack(g_even)]
    for k in range(nq):
        if k:
            ready = dict(w=w1) | {f"k{i}": v for i, v in enumerate(dgates)}
            rows = pick(f"c{k}a", c_q[k], **ready)
            first = jnp.stack(ring_gather(rows, "ba"[k % 2]))
            c_planes.append(plane_gather(rows, k % 2 == 0, pick(f"c{k}b", first, **ready)))
        c = c_planes[k]
        ready = {f"s{i}": v for i, v in enumerate(sum_first) if v is not None}
        if k == 3:
            ready["e1"] = dec_one = sum_end(sum_first[1], False)
        hold = pick(f"K{k}", ranks, **ready)
        dec, dgate, kept, ys[k % 2] = expert_chunk(
            k, nq, na, nb, expert, hold, c, (g_even, g_odd)[k % 2], router_t, w1, w2, kept, ys[k % 2], slots
        )
        dgates.append(dgate.reshape(na * nb, tok))
        ready = {f"k{i}": v for i, v in enumerate(dgates)}
        decs.append(dec)
        sum_first.append(None)
        if k:
            sum_first[k] = sum_start([pick(f"d{k}", v, **ready) for v in dec], k % 2 == 0)
    ready = {f"k{i}": v for i, v in enumerate(dgates)}
    sum_first[0] = sum_start([pick("d0", v, **ready) for v in decs[0]], True)
    firsts = sum_first
    dec_sums = [dec_one if k == 1 else sum_end(firsts[k], k % 2 == 0) for k in range(nq)]
    ready = {f"s{i}": v for i, v in enumerate(firsts)}
    xs, hs, deys, degs = kept[:4]
    gate_up_term = dot(pick("gu", xs, **ready), degs, TN).astype(BF)
    down_term = dot(pick("dn", hs, gu=gate_up_term, **ready), deys, TN).astype(BF)
    terms = [
        gate_up_term.reshape(nq, nr, gu_rows, 2 * FF),
        down_term.reshape(nq, nr, -1, 2 * FF),
    ]
    at = [lax.rem(r_at - k + nr, nr) for k in range(nr)]
    expert_rows = ring_sum(
        [
            jnp.concatenate(
                [lax.dynamic_index_in_dim(t, i, 1, keepdims=False) for t in terms], axis=1
            )
            for i in at
        ],
        "r",
    ).astype(BF)
    moving = dec_sums[1].astype(BF)
    for k in range(2, nq):
        term = dec_sums[k]
        term = pick(f"t{k}", term, gu=gate_up_term, dn=down_term, er=expert_rows)
        moving = (shift(moving, "q").astype(F32) + term).astype(BF)
    routed_grad = shift(moving, "q").astype(F32) + dec_sums[0]

    expert_rows = pick("ea", expert_rows, rg=routed_grad, t=moving)
    expert_rows = lax.all_to_all(expert_rows, "q", split_axis=0, concat_axis=0, tiled=True)

    ready = {f"k{i}": v for i, v in enumerate(dgates)}
    later = pick("sh", second, **ready)
    shared_pre = dot(later, shared_in)
    shared_gate, shared_up = shared_pre[:, :FF], shared_pre[:, FF:]
    shared_sig = jax.nn.sigmoid(shared_gate)
    shared_hidden = (shared_gate * shared_sig * shared_up).astype(BF)

    logits = jnp.where(named, dot(later, router), masked_value)
    raised = jnp.where(named, jnp.exp(logits - jnp.max(logits, axis=1, keepdims=True)), 0.0)
    gates = raised / jnp.sum(raised, axis=1, keepdims=True)
    n_all = nq * na * nb
    spot = np.arange(n_all, dtype=np.int32)
    spot = (
        lax.rem(q_at - spot // (na * nb) + nq, nq) * (na * nb)
        + lax.rem(a_at - spot // nb % na + na, na) * nb
        + lax.rem(b_at - spot % nb + nb, nb)
    )
    dgate = jnp.concatenate(dgates, axis=0)[spot]
    dgate = lax.all_to_all(dgate, ("q", "a", "b"), split_axis=0, concat_axis=0, tiled=True)
    dgate = jnp.swapaxes(dgate.reshape(nq, na * nb, tok), 0, 1).reshape(n_experts, tok).T
    grad_logits = gates * (dgate - jnp.sum(gates * dgate, axis=1, keepdims=True))
    grad_logits = grad_logits.astype(BF)

    shared_hidden_grad = dot(grad_low, shared_out, NT)
    shared_pre_grad = jnp.concatenate(
        [
            shared_hidden_grad * shared_up * shared_sig * (1.0 + shared_gate * (1.0 - shared_sig)),
            shared_hidden_grad * shared_gate * shared_sig,
        ],
        axis=1,
    ).astype(BF)
    second_grad = (
        dot(shared_pre_grad, shared_in, NT) + dot(grad_logits, router, NT) + routed_grad
    )
    ffn_gain_grad = jnp.sum(second_grad * residual * inv_two, axis=0)
    residual_grad = out_grad + norm_back(second_grad, residual, inv_two, gain_two)
    mixed_grad = residual_grad.astype(BF)
    heads_grad = dot(mixed_grad, out_weight, NT).astype(BF)

    y_first = [
        sum_start([pick("y1", v, rg=routed_grad, k=dgates[3]) for v in ys[p]], p == 0)
        for p in (0, 1)
    ]
    dq = None
    moving = None
    held = heads_grad
    for step, k in enumerate(list(range(1, nq)) + [0]):
        ready = dict(er=expert_rows, y=y_first, m=moving if step else ())
        held = pick(f"B{step}", held, **ready)
        dq, parts = attend_back_chunk(
            places[k], queries, held, mixed, lse, tables, kv_chunks[k], dq, k == 0, n_ctx
        )
        term = ring_sum(parts, "r")
        if k == 1:
            moving = term.astype(BF)
            first_move = moving
        elif k:
            moving = (shift(moving, "q").astype(F32) + term).astype(BF)
    late = dense_sum_core(
        [
            dot(normed, dq, TN).astype(BF),
            dot(mixed, mixed_grad, TN).astype(BF),
            dot(later, shared_pre_grad, TN).astype(BF),
            dot(shared_hidden, grad_low, TN).astype(BF).reshape(width, flat),
            jnp.concatenate(
                [
                    ffn_gain_grad[:, None],
                    dot(later, grad_logits, TN),
                    jnp.zeros((width, 127 - n_experts), F32),
                ],
                axis=1,
            ).astype(BF),
        ],
        own_rows,
    )
    y_sums = [sum_end(pick("y2", y_first[p], q=dq, m=moving, f=first_move), p == 0, 1) for p in (0, 1)]
    late = dense_sum_first(late)
    kv_back = finish_keys(
        shift(moving, "q"), pick("fin", term, late=late, ys=y_sums), *tables
    )

    owned = pick("xg", expert_rows, b=kv_back, m=moving)
    gate_up_grad = owned[:, :gu_rows].astype(F32)
    down_grad = owned[:, gu_rows:].reshape(nq, -1, width).astype(F32)
    key_value = dense_sum_core(
        [
            pick("kv1", dot(normed, kv_back[0], TN).astype(BF), late=late, ys=y_sums),
            dot(normed, kv_back[1], TN).astype(BF),
        ],
        own_rows,
    )
    ready = dict(kv=key_value)
    normed_grad = dot(dq, qkv_weight[:, :width], NT)
    kv_low = pick("dn0", kv_back, **ready)
    normed_grad += dot(kv_low[0], qkv_weight[:, width : 2 * width], NT)
    normed_grad += dot(kv_low[1], qkv_weight[:, 2 * width :], NT)
    input_grad = residual_grad + norm_back(normed_grad, tokens_in, inv_one, gain_one)
    y_sums = pick("y3", y_sums, b=kv_back, kv=key_value, m=moving)
    y_terms = [y_sums[k % 2][k // 2] for k in range(nq)]
    late = dense_sum_second(*(pick("late2", v, b=kv_back, kv=key_value) for v in late))
    first_kv = dense_sum_first(pick("kv2", key_value, l=late))
    last_kv = dense_sum_second(*first_kv)
    y_moving = y_terms[1].astype(BF)
    for k in range(2, nq + 1):
        y_moving = shift(y_moving, "q")
        y_moving = pick(f"yz{k}", y_moving, kv=key_value, f=first_kv, l=late, z=last_kv)
        routed_sum = y_moving.astype(F32) + y_terms[k % nq]
        y_moving = routed_sum.astype(BF)
    late_grad = dense_sum_last(pick("late3", late, f=first_kv, kv=key_value, z=last_kv))
    kv_weight_grad = dense_sum_last(last_kv)
    layer_out = (residual + dot(shared_hidden, shared_out) + routed_sum).astype(BF)
    at_out, at_shared, at_down = width, 2 * width, 2 * width + 2 * FF
    at_small = at_down + flat
    qkv_weight_grad = jnp.concatenate([late_grad[:, :at_out], kv_weight_grad], axis=1)
    attn_gain_grad = jnp.sum(query_key_value_weight.astype(F32) * qkv_weight_grad, axis=1)
    attn_gain_grad = attn_gain_grad / attn_gain.astype(F32)
    return (
        layer_out[None],
        input_grad[None],
        attn_gain_grad,
        qkv_weight_grad,
        late_grad[:, at_out:at_shared],
        late_grad[:, at_small],
        late_grad[:, at_small + 1 : at_small + 1 + n_experts],
        late_grad[:, at_shared:at_down],
        late_grad[:, at_down:at_small].reshape(down_rows, width),
        gate_up_grad,
        down_grad,
    )


def solution(mesh):
    n_ctx, n_exp = mesh.shape["ctx"], mesh.shape["exp"]

    def layer(*args):
        n_experts = args[10].shape[0]
        nq = n_experts // n_exp
        nb = 2
        fine = Mesh(
            np.asarray(mesh.devices).reshape(nq, n_ctx // nq, n_exp // nb, nb), ("q", "r", "a", "b")
        )
        ctx, exp, every = ("q", "r"), ("a", "b"), ("q", "r", "a", "b")
        tokens, flat, rows = P(exp, ctx, None), P(every), P(every, None)
        run = jax.shard_map(
            functools.partial(body, n_experts),
            mesh=fine,
            in_specs=(
                tokens, tokens, tokens, flat, rows, rows, flat, rows, rows, rows, tokens, tokens,
            ),
            out_specs=(tokens, tokens, flat, rows, rows, flat, rows, rows, rows, tokens, tokens),
            check_vma=False,
        )
        return run(*args)

    return layer
```

```python
import functools

import jax
import jax.numpy as jnp
import numpy as np
from jax import lax
from jax.experimental import pallas as pl
from jax.experimental.pallas import tpu as pltpu
from jax.sharding import Mesh
from jax.sharding import PartitionSpec as P

HEADS = 10
HEAD_DIM = 128
FF = 896
TOP = 7

norm_eps = 1e-06
rope_base = 10000.0
masked_value = -1e30
LOG2E = 1.4426950408889634

BF = jnp.bfloat16
F32 = jnp.float32
VMEM_LIMIT = 56 * 1024 * 1024


def rope_tables(positions, head_dim):
    halfway = head_dim // 2
    frequency = rope_base ** (-(jnp.arange(halfway).astype(F32) * 2.0 / head_dim))
    angles = positions.astype(F32)[:, None] * frequency[None, :]
    angles = jnp.concatenate([angles, angles], axis=1)
    return (jnp.cos(angles), jnp.sin(angles))


def rms_scale(values):
    return lax.rsqrt(jnp.mean(values * values, axis=1, keepdims=True) + norm_eps)


def norm_back(grad_in, values, inv_rms, gain_vec):
    scaled = grad_in * gain_vec
    return inv_rms * scaled - values * inv_rms**3 * jnp.mean(scaled * values, axis=1, keepdims=True)


def dot(a, b, dims=((1,), (0,))):
    return lax.dot_general(a, b, (dims, ((), ())), preferred_element_type=F32)


NT = ((1,), (1,))
TN = ((0,), (0,))


def shift(value, axis):
    n = lax.axis_size(axis)
    return lax.ppermute(value, axis, [(i, (i + 1) % n) for i in range(n)])


def ring_gather(value, axis):
    parts = [value]
    for _ in range(1, lax.axis_size(axis)):
        parts.append(shift(parts[-1], axis))
    return parts


def shift_by(value, axis, k):
    n = lax.axis_size(axis)
    return lax.ppermute(value, axis, [(i, (i + k) % n) for i in range(n)])


def direct_gather(value, axis):
    return [value] + [shift_by(value, axis, k) for k in range(1, lax.axis_size(axis))]


def ring_sum(blocks, axis, events=()):
    n = len(blocks)
    if n == 1:
        return blocks[0].astype(F32)
    moving = blocks[1].astype(BF)
    for k in range(2, n):
        moving = after(shift(moving, axis), *events)
        moving = (moving.astype(F32) + blocks[k].astype(F32)).astype(BF)
    return after(shift(moving, axis), *events).astype(F32) + blocks[0].astype(F32)


def ring_blocks(arrays, axis, dim):
    n = lax.axis_size(axis)
    index = lax.axis_index(axis)
    out = []
    for k in range(n):
        at = lax.rem(index - k + n, n)
        parts = [lax.dynamic_index_in_dim(v, at, dim, keepdims=False) for v in arrays]
        out.append(parts[0] if len(parts) == 1 else jnp.concatenate(parts, axis=-1))
    return out


ORDER = {
    "rest": "f3",
    "g": "r3",
    "mid1": "r1",
    "rs1": "fp",
    "norm": "rs g2",
    "gs1": "rp",
    "arr2": "s gs",
    "arr3": "s gf",
    "wa": "q",
    "wc": "cp",
    "c1b": "w",
    "c2b": "w",
    "c3a": "w",
    "K1": "s0",
    "gu": "s1",
    "dn": "s1",
    "t2": "er",
    "B1": "m",
    "B3": "er",
    "y1": "rg",
    "fin": "late",
    "late2": "b",
    "kv2": "l",
    "yz2": "kv",
    "late3": "kv",
    "cz3": "cp",
    "dn0": "kv",
}


def pick(name, value, **events):
    chosen = [events[key] for key in ORDER.get(name, "").split() if key in events]
    return after(value, *jax.tree.leaves(chosen))


def after(value, *events):
    if not events:
        return value
    return lax.optimization_barrier((value, *events))[0]


def place_kernel(counts, cuts, index_ref, *refs):
    n = len(counts)
    pieces, outs, sems = refs[:n], refs[n:-1], refs[-1]
    t = 0
    for piece, count in zip(pieces, counts):
        for j in range(count):
            at = index_ref[t]
            t += 1
            for o, (rows, low, high) in enumerate(cuts):
                pltpu.make_async_copy(
                    piece.at[j, pl.ds(*rows), pl.ds(low, high - low)], outs[o].at[at], sems.at[o]
                ).start()
    for o in range(len(cuts)):
        pltpu.make_async_copy(outs[o], outs[o], sems.at[o]).wait()


def place(index, pieces, cuts):
    rows, total = pieces[0].shape[-2:]
    pieces = [piece.reshape(-1, rows, total) for piece in pieces]
    counts = [piece.shape[0] for piece in pieces]
    n = sum(counts)
    outs = pl.pallas_call(
        functools.partial(place_kernel, counts, cuts),
        in_specs=[pl.BlockSpec(memory_space=pltpu.SMEM)]
        + [pl.BlockSpec(memory_space=pl.ANY)] * len(pieces),
        out_specs=[pl.BlockSpec(memory_space=pltpu.VMEM)] * len(cuts),
        scratch_shapes=[pltpu.SemaphoreType.DMA((len(cuts),))],
        out_shape=[
            jax.ShapeDtypeStruct((n, c[0][1], c[2] - c[1]), pieces[0].dtype) for c in cuts
        ],
        compiler_params=pltpu.CompilerParams(vmem_limit_bytes=VMEM_LIMIT // 2),
        cost_estimate=pl.CostEstimate(
            flops=0, bytes_accessed=4 * n * rows * total, transcendentals=0
        ),
        name="place",
    )(index, *pieces)
    return [out.reshape(-1, out.shape[2]) for out in outs]


def dense_steps(nq):
    half, na, nb = nq // 2, lax.axis_size("a"), lax.axis_size("b")
    steps = [[(kq, ka, kb) for kb in range(nb) for kq in range(half)] for ka in range(na)]
    return steps + [
        [(kq, ka, kb) for ka in range(na) for kq in range(half, nq)] for kb in range(nb)
    ]


def dense_start(along_q):
    half = len(along_q) // 2
    one = jnp.stack(ring_gather(jnp.stack(along_q[:half]), "b"))
    two = jnp.stack(ring_gather(jnp.stack(along_q[half:]), "a"))
    return one, two


def dense_end(one, two):
    return ring_gather(one, "a") + ring_gather(two, "b")


def dense_place(pieces, steps, widths, due=()):
    nq, nr, na, nb = (lax.axis_size(axis) for axis in ("q", "r", "a", "b"))
    rows, width = pieces[0].shape[-2:]
    flat = [piece.reshape(-1, rows, width) for piece in pieces]
    groups = [[0, na], [k for k in range(na + nb) if k not in (0, na)]]
    arrays, order = [], []
    for group in groups:
        own = jnp.concatenate([flat[k] for k in group], axis=0)
        if group is groups[1]:
            own = after(own, *due)
        entries = [s for k in group for s in steps[k]]
        for kr, part in enumerate(ring_gather(own, "r")):
            arrays.append(part)
            order += [(kr, *s) for s in entries]
    kr, kq, ka, kb = (np.array(column, np.int32) for column in zip(*order))
    index = lax.rem(lax.axis_index("q") - kq + nq, nq) * nr
    index = index + lax.rem(lax.axis_index("r") - kr + nr, nr)
    index = index * na + lax.rem(lax.axis_index("a") - ka + na, na)
    index = index * nb + lax.rem(lax.axis_index("b") - kb + nb, nb)
    edges = np.cumsum([0] + list(widths))
    cuts = [((0, rows), int(low), int(high)) for low, high in zip(edges[:-1], edges[1:])]
    return place(index.astype(jnp.int32), arrays, cuts)


def dense_sum_core(wholes, n_rows):
    nq, nr, na, nb = (lax.axis_size(axis) for axis in ("q", "r", "a", "b"))
    values = [whole.reshape(nq, nr, na, nb, n_rows, whole.shape[1]) for whole in wholes]
    return ring_sum(ring_blocks(values, "r", 1), "r").astype(BF)


def dense_sum_first(value):
    half = value.shape[0] // 2
    one = ring_sum(ring_blocks([value[:half]], "a", 1), "a").astype(BF)
    two = ring_sum(ring_blocks([value[half:]], "b", 2), "b").astype(BF)
    return one, two


def dense_sum_second(one, two):
    one = ring_sum(ring_blocks([one], "b", 1), "b")
    two = ring_sum(ring_blocks([two], "a", 1), "a")
    return jnp.concatenate([one, two], axis=0).astype(BF)


def dense_sum_last(value):
    return ring_sum(ring_blocks([value], "q", 0), "q")


def plane_gather(rows, even, first=None):
    inner, outer = ("b", "a") if even else ("a", "b")
    if first is None:
        first = jnp.stack(ring_gather(rows, inner))
    parts = ring_gather(first, outer)
    return [jnp.stack(parts)] if even else parts


def sum_start(parts, even, events=()):
    return ring_sum(parts, "a" if even else "b", events)


def sum_end(first, even, dim=0, events=()):
    n = first.shape[dim]
    parts = [lax.index_in_dim(first, k, dim, False) for k in range(n)]
    return ring_sum(parts, "b" if even else "a", events)


def project_kernel(n_query, x_ref, w_ref, cos_ref, sin_ref, q_ref, kv_ref):
    j = pl.program_id(0)
    made = dot(x_ref[...], w_ref[...])

    def turned():
        parts = []
        for low in range(0, made.shape[1], HEAD_DIM):
            u = made[:, low : low + HEAD_DIM]
            parts.append(u * cos_ref[...] + pltpu.roll(u, HEAD_DIM // 2, 1) * sin_ref[...])
        return jnp.concatenate(parts, axis=1).astype(BF)

    @pl.when(j < n_query)
    def _():
        q_ref[...] = turned()

    @pl.when((j >= n_query) & (j < 2 * n_query))
    def _():
        kv_ref[0] = turned()

    @pl.when(j >= 2 * n_query)
    def _():
        kv_ref[0] = made.astype(BF)


def project(normed, weight, cosines, signed_sine):
    tok, width = normed.shape
    block = 2 * HEAD_DIM
    n = width // block
    table = pl.BlockSpec((tok, HEAD_DIM), lambda j: (0, 0))
    return pl.pallas_call(
        functools.partial(project_kernel, n),
        grid=(3 * n,),
        in_specs=[
            pl.BlockSpec((tok, width), lambda j: (0, 0)),
            pl.BlockSpec((width, block), lambda j: (0, j)),
            table,
            table,
        ],
        out_specs=[
            pl.BlockSpec((tok, block), lambda j: (0, jnp.minimum(j, n - 1))),
            pl.BlockSpec(
                (1, tok, block),
                lambda j: (jnp.maximum(j - n, 0) // n, 0, jnp.maximum(j - n, 0) % n),
            ),
        ],
        out_shape=[
            jax.ShapeDtypeStruct((tok, width), BF),
            jax.ShapeDtypeStruct((2, tok, width), BF),
        ],
        compiler_params=pltpu.CompilerParams(vmem_limit_bytes=VMEM_LIMIT // 2),
        cost_estimate=pl.CostEstimate(
            flops=6 * tok * width * width, bytes_accessed=6 * width * width, transcendentals=0
        ),
        name="project",
    )(normed, weight, cosines, signed_sine)


def turn_back(grad, cos, signed_sine):
    return grad * cos - pltpu.roll(grad, HEAD_DIM // 2, 1) * signed_sine


def finish_kernel(moved_ref, own_ref, cos_ref, sin_ref, out_ref):
    keys = moved_ref[0].astype(F32) + own_ref[0]
    out_ref[0] = turn_back(keys, cos_ref[...], sin_ref[...]).astype(BF)
    out_ref[1] = (moved_ref[1].astype(F32) + own_ref[1]).astype(BF)


def finish_keys(moved, own, cosines, signed_sine):
    _, tok, width = own.shape
    pair = pl.BlockSpec((2, tok, HEAD_DIM), lambda h: (0, 0, h))
    table = pl.BlockSpec((tok, HEAD_DIM), lambda h: (0, 0))
    return pl.pallas_call(
        finish_kernel,
        grid=(width // HEAD_DIM,),
        in_specs=[pair, pair, table, table],
        out_specs=pair,
        out_shape=jax.ShapeDtypeStruct((2, tok, width), BF),
        cost_estimate=pl.CostEstimate(
            flops=10 * tok * width, bytes_accessed=16 * tok * width, transcendentals=0
        ),
        name="finish_keys",
    )(moved, own, cosines, signed_sine)


def allowed_mask(own, other, n_ctx, half):
    row = lax.broadcasted_iota(jnp.int32, (2 * half, 2 * half), 0)
    col = lax.broadcasted_iota(jnp.int32, (2 * half, 2 * half), 1)
    last = 2 * n_ctx - 1
    query = row + jnp.where(row < half, own * half, (last - own) * half - half)
    key = col + jnp.where(col < half, other * half, (last - other) * half - half)
    return key <= query


def attend_kernel(n_ctx, n_src, first, last, place_ref, q_ref, *refs):
    kv_refs, refs = refs[:n_src], refs[n_src:]
    if not first:
        acc_in, ml_in = refs[:2]
        refs = refs[2:]
    out_ref, ml_ref = refs
    queries = q_ref[...]
    tok = queries.shape[0]
    scores = []
    for s in range(n_src):
        raw = dot(queries, kv_refs[s][0], NT) * (HEAD_DIM ** (-0.5) * LOG2E)
        mask = allowed_mask(place_ref[0], place_ref[1 + s], n_ctx, tok // 2)
        scores.append(jnp.where(mask, raw, masked_value))
    peak = functools.reduce(jnp.maximum, [jnp.max(s, axis=1, keepdims=True) for s in scores])
    if not first:
        old_peak = ml_in[0][:, 0:1]
        old_sum = ml_in[0][:, 64:65]
        peak = jnp.maximum(peak, old_peak)
    total = jnp.zeros_like(peak)
    mixed = jnp.zeros((tok, HEAD_DIM), F32)
    for s in range(n_src):
        raised = jnp.exp2(scores[s] - peak)
        total = total + jnp.sum(raised, axis=1, keepdims=True)
        mixed = mixed + dot(raised.astype(BF), kv_refs[s][1])
    if not first:
        decay = jnp.exp2(old_peak - peak)
        total = total + old_sum * decay
        mixed = mixed + acc_in[...] * decay
    if last:
        out_ref[...] = (mixed / total).astype(BF)
        ml_ref[0] = jnp.broadcast_to(peak + jnp.log2(total), (tok, 128))
    else:
        out_ref[...] = mixed
        lane = lax.broadcasted_iota(jnp.int32, (tok, 128), 1)
        ml_ref[0] = jnp.where(lane < 64, peak, total)


def attend_chunk(places, queries, kv_list, state, last, n_ctx):
    tok, width = queries.shape
    head = pl.BlockSpec((tok, HEAD_DIM), lambda h, p: (0, h))
    pair = pl.BlockSpec((2, tok, HEAD_DIM), lambda h, p: (0, 0, h))
    rows = pl.BlockSpec((1, tok, 128), lambda h, p: (h, 0, 0))
    first = state is None
    n = len(kv_list)
    pairs = tok * tok * n * HEADS
    return pl.pallas_call(
        functools.partial(attend_kernel, n_ctx, n, first, last),
        grid_spec=pltpu.PrefetchScalarGridSpec(
            num_scalar_prefetch=1,
            grid=(HEADS,),
            in_specs=[head] + [pair] * n + ([] if first else [head, rows]),
            out_specs=[head, rows],
        ),
        out_shape=[
            jax.ShapeDtypeStruct((tok, width), BF if last else F32),
            jax.ShapeDtypeStruct((HEADS, tok, 128), F32),
        ],
        compiler_params=pltpu.CompilerParams(vmem_limit_bytes=VMEM_LIMIT // 2),
        cost_estimate=pl.CostEstimate(
            flops=4 * pairs * HEAD_DIM * 4, bytes_accessed=8 * tok * width, transcendentals=pairs
        ),
        name="attend",
    )(places, queries, *kv_list, *(() if first else state))


def attend_back_kernel(
    n_ctx, n_src, first, last, place_ref, q_ref, do_ref, o_ref, lse_ref, cos_ref, sin_ref, *refs
):
    kv_refs, refs = refs[:n_src], refs[n_src:]
    if not first:
        dq_in, refs = refs[0], refs[1:]
    dq_ref, dkv_refs = refs[0], refs[1:]
    queries = q_ref[...]
    grad = do_ref[...]
    tok = queries.shape[0]
    lse = lse_ref[0][:, 0:1]
    delta = jnp.sum(grad.astype(F32) * o_ref[...].astype(F32), axis=1, keepdims=True)
    scale = HEAD_DIM ** (-0.5)
    grad_query = jnp.zeros((tok, HEAD_DIM), F32)
    for s in range(n_src):
        keys, values = kv_refs[s][0], kv_refs[s][1]
        raw = dot(queries, keys, NT) * (scale * LOG2E)
        mask = allowed_mask(place_ref[0], place_ref[1 + s], n_ctx, tok // 2)
        probs = jnp.exp2(jnp.where(mask, raw, masked_value) - lse)
        grad_probs = dot(grad, values, NT)
        grad_scores = (probs * (grad_probs - delta)).astype(BF)
        grad_query = grad_query + dot(grad_scores, keys)
        dkv_refs[s][0] = (dot(grad_scores, queries, TN) * scale).astype(dkv_refs[s].dtype)
        dkv_refs[s][1] = dot(probs.astype(BF), grad, TN).astype(dkv_refs[s].dtype)
    grad_query = grad_query * scale
    if not first:
        grad_query = grad_query + dq_in[...]
    if last:
        grad_query = turn_back(grad_query, cos_ref[...], sin_ref[...]).astype(BF)
    dq_ref[...] = grad_query


def attend_back_chunk(places, queries, grad, mixed, lse, tables, kv_list, dq, last, n_ctx):
    tok, width = queries.shape
    head = pl.BlockSpec((tok, HEAD_DIM), lambda h, p: (0, h))
    pair = pl.BlockSpec((2, tok, HEAD_DIM), lambda h, p: (0, 0, h))
    rows = pl.BlockSpec((1, tok, 128), lambda h, p: (h, 0, 0))
    table = pl.BlockSpec((tok, HEAD_DIM), lambda h, p: (0, 0))
    first = dq is None
    n = len(kv_list)
    pairs = tok * tok * n * HEADS
    out = pl.pallas_call(
        functools.partial(attend_back_kernel, n_ctx, n, first, last),
        grid_spec=pltpu.PrefetchScalarGridSpec(
            num_scalar_prefetch=1,
            grid=(HEADS,),
            in_specs=[head, head, head, rows, table, table] + [pair] * n + ([] if first else [head]),
            out_specs=[head] + [pair] * n,
        ),
        out_shape=[jax.ShapeDtypeStruct((tok, width), BF if last else F32)]
        + [jax.ShapeDtypeStruct((2, tok, width), F32 if s == 0 else BF) for s in range(n)],
        compiler_params=pltpu.CompilerParams(vmem_limit_bytes=VMEM_LIMIT // 2),
        cost_estimate=pl.CostEstimate(
            flops=10 * pairs * HEAD_DIM * 4, bytes_accessed=16 * tok * width, transcendentals=pairs
        ),
        name="attend_back",
    )(places, queries, grad, mixed, lse, *tables, *kv_list, *(() if first else (dq,)))
    return out[0], out[1:]


def expert_kernel(slots, na, nb, even, n_kept, e_ref, rank_ref, *refs):
    n_in, n_sum = (1, na) if even else (nb, nb)
    c_refs, g_refs, refs = refs[:n_in], refs[n_in : 2 * n_in], refs[2 * n_in :]
    wr_ref, w1_ref, w2_ref = refs[:3]
    refs = refs[3 + n_kept :]
    d_refs, dg_ref, refs = refs[:n_sum], refs[n_sum], refs[n_sum + 1 :]
    x_ref, h_ref, dey_ref, deg_ref = refs[:4]
    y_refs = refs[4:]
    tok = g_refs[0].shape[-2]
    experts = wr_ref.shape[0]
    me = e_ref[0]
    step = pl.program_id(0)
    picks, rows, grads, weights = [], [], [], []
    own = lax.broadcasted_iota(jnp.int32, (experts, tok), 0) == me
    slot = lax.broadcasted_iota(jnp.int32, (slots, tok), 0).astype(F32)
    for s in range(nb):
        tokens = c_refs[0][0, s] if even else c_refs[s][0]
        cot = g_refs[0][0, s, 0] if even else g_refs[s][0, 0]
        rank = rank_ref[0, s, 0]
        logits = dot(wr_ref[...], tokens, NT)
        logits = jnp.where(rank >= 0, logits, masked_value)
        raised = jnp.where(rank >= 0, jnp.exp(logits - jnp.max(logits, axis=0, keepdims=True)), 0.0)
        gates = raised / jnp.sum(raised, axis=0, keepdims=True)
        gate_row = jnp.sum(jnp.where(own, gates, 0.0), axis=0, keepdims=True)
        rank_row = jnp.sum(jnp.where(own, rank, 0.0), axis=0, keepdims=True)
        pick = jnp.where(slot == rank_row, 1.0, 0.0)
        weights.append(jnp.sum(pick * gate_row, axis=1, keepdims=True))
        pick_low = pick.astype(BF)
        picks.append((pick, pick_low))
        rows.append(dot(pick_low, tokens).astype(BF))
        grads.append(dot(pick_low, cot))
    x = jnp.concatenate(rows, axis=0)
    grad = jnp.concatenate(grads, axis=0)
    weight = jnp.concatenate(weights, axis=0)
    x_ref[...] = x
    dey = (weight * grad).astype(BF)
    dey_ref[...] = dey
    pre = dot(x, w1_ref[...])
    gate, up = pre[:, :FF], pre[:, FF:]
    sig = jax.nn.sigmoid(gate)
    act = gate * sig
    hidden = (act * up).astype(BF)
    h_ref[...] = hidden
    grad_hidden = dot(dey, w2_ref[...], NT)
    deg = jnp.concatenate(
        [
            (grad_hidden * up * sig * (1.0 + gate * (1.0 - sig))).astype(BF),
            (grad_hidden * act).astype(BF),
        ],
        axis=1,
    )
    deg_ref[...] = deg
    dec = dot(deg, w1_ref[...], NT).astype(BF)
    ey = dot(hidden, w2_ref[...]).astype(BF).astype(F32)
    dgate = jnp.sum(grad * ey, axis=1, keepdims=True)
    weighted = (weight * ey).astype(BF)
    d_all, y_all = [], []
    for s in range(nb):
        part = slice(s * slots, (s + 1) * slots)
        pick, pick_low = picks[s]
        d_all.append(dot(pick_low, dec[part], TN).astype(BF))
        y_all.append(dot(pick_low, weighted[part], TN).astype(BF))
        if not even:
            d_refs[s][0] = d_all[s]
            y_refs[s][0, 0] = y_all[s]
        dg_ref[0, s] = jnp.sum(pick * dgate[part], axis=0, keepdims=True)
    if even:
        for k in range(na):

            @pl.when(step == k)
            def _(k=k):
                for s in range(nb):
                    d_refs[k][s] = d_all[s]
                    y_refs[k][0, s] = y_all[s]


def expert_chunk(chunk, nq, na, nb, expert, ranks, c, g, router_t, w1, w2, kept, y_kept, slots):
    even = chunk % 2 == 0
    tok, width = c[0].shape[-2:]
    experts = router_t.shape[0]
    g_one = pl.BlockSpec((1, nb, 1, tok, width), lambda i, e: (i, 0, chunk // 2, 0, 0))
    g_two = pl.BlockSpec((1, 1, tok, width), lambda i, e: (i, chunk // 2, 0, 0))
    one = pl.BlockSpec((1, nb, tok, width), lambda i, e: (i, 0, 0, 0))
    two = pl.BlockSpec((1, tok, width), lambda i, e: (i, 0, 0))

    def fixed(shape):
        return pl.BlockSpec(shape, lambda i, e: (0,) * len(shape), pipeline_mode=pl.Buffered(1))

    def by_rows(n):
        return pl.BlockSpec((nb * slots, n), lambda i, e: (chunk * na + i, 0))

    n_rows = na * nb * slots
    n_half = nq // 2
    if even:
        d_specs = [pl.BlockSpec((nb, tok, width), lambda i, e: (0, 0, 0))] * na
        y_specs = [pl.BlockSpec((1, nb, tok, width), lambda i, e: (chunk // 2, 0, 0, 0))] * na
        d_shapes = [jax.ShapeDtypeStruct((nb, tok, width), BF)] * na
        y_shapes = [jax.ShapeDtypeStruct((n_half, nb, tok, width), BF)] * na
    else:
        d_specs = [two] * nb
        y_specs = [pl.BlockSpec((1, 1, tok, width), lambda i, e: (chunk // 2, i, 0, 0))] * nb
        d_shapes = [jax.ShapeDtypeStruct((na, tok, width), BF)] * nb
        y_shapes = [jax.ShapeDtypeStruct((n_half, na, tok, width), BF)] * nb
    held = [*(kept or ()), *(y_kept or ())]
    n_in = 1 + 1 + len(c) + len(g) + 3
    n_out = len(d_shapes) + 1
    aliases = {n_in + k: n_out + k for k in range(len(kept or ()))}
    for k in range(len(y_kept or ())):
        aliases[n_in + len(kept or ()) + k] = n_out + 4 + k
    out = pl.pallas_call(
        functools.partial(expert_kernel, slots, na, nb, even, len(held)),
        grid_spec=pltpu.PrefetchScalarGridSpec(
            num_scalar_prefetch=1,
            grid=(na,),
            in_specs=[
                pl.BlockSpec((1, nb, 1, experts, tok), lambda i, e: (i, 0, chunk, 0, 0)),
                *([one, g_one] if even else [two] * nb + [g_two] * nb),
                fixed(router_t.shape), fixed(w1.shape), fixed(w2.shape),
                *[pl.BlockSpec(memory_space=pl.ANY)] * len(held),
            ],
            out_specs=[
                *d_specs,
                pl.BlockSpec((1, nb, 1, tok), lambda i, e: (i, 0, 0, 0)),
                by_rows(width), by_rows(FF), by_rows(width), by_rows(2 * FF),
                *y_specs,
            ],
        ),
        out_shape=[
            *d_shapes,
            jax.ShapeDtypeStruct((na, nb, 1, tok), F32),
            *[jax.ShapeDtypeStruct((nq * n_rows, n), BF) for n in (width, FF, width, 2 * FF)],
            *y_shapes,
        ],
        input_output_aliases=aliases,
        compiler_params=pltpu.CompilerParams(vmem_limit_bytes=VMEM_LIMIT),
        cost_estimate=pl.CostEstimate(
            flops=n_rows * width * FF * 12, bytes_accessed=30_000_000, transcendentals=n_rows * FF
        ),
        name="experts",
    )(expert, ranks, *c, *g, router_t, w1, w2, *held)
    n_d = len(d_shapes)
    return out[:n_d], out[n_d], out[n_out : n_out + 4], out[n_out + 4 :]


def body(
    n_experts,
    block_input,
    cotangent,
    routes,
    attn_gain,
    query_key_value_weight,
    attention_output_weight,
    ffn_gain,
    routing_weight,
    common_expert_gate_up_weight,
    common_expert_down_weight,
    expert_gate_up,
    expert_down,
):
    nq, nr, na, nb = (lax.axis_size(axis) for axis in ("q", "r", "a", "b"))
    q_at, r_at, a_at, b_at = (lax.axis_index(axis) for axis in ("q", "r", "a", "b"))
    n_ctx = nq * nr
    n_exp = na * nb
    ctx_rank = q_at * nr + r_at
    exp_rank = a_at * nb + b_at
    tok = block_input.shape[1]
    width = block_input.shape[2]
    half = tok // 2
    capacity = min(tok, 3 * TOP * tok // (2 * n_experts))
    slots = -(-capacity // 16) * 16
    row = jnp.arange(tok, dtype=jnp.int32)
    local_pos = jnp.where(
        row < half, ctx_rank * half + row, (2 * n_ctx - 1 - ctx_rank) * half + row - half
    )
    cosines, sines = rope_tables(local_pos, HEAD_DIM)
    sines = jnp.where(jnp.arange(HEAD_DIM)[None, :] < HEAD_DIM // 2, -sines, sines)
    tables = (cosines, sines)
    tokens_in = block_input[0].astype(F32)
    grad_low = cotangent[0]
    out_grad = grad_low.astype(F32)
    own_rows = query_key_value_weight.shape[0]
    down_rows = common_expert_down_weight.shape[0]

    named = jnp.any(
        routes[0][:, :, None] == jnp.arange(n_experts, dtype=jnp.int32)[None, None, :], axis=1
    )
    before = (row[:, None] < row[None, :]).astype(BF)
    rank = dot(named.astype(BF).T, before)
    rank = jnp.where(named.T, rank, -1.0)
    ranks = jnp.stack(direct_gather(rank, "q"))
    ranks = jnp.stack(ring_gather(ranks, "b"))
    ranks = jnp.stack(ring_gather(ranks, "a"))

    zeros = jnp.zeros((own_rows, 127), BF)
    front = jnp.concatenate([query_key_value_weight, attn_gain[:, None], zeros], axis=1)
    front_q = ring_gather(front, "q")
    rest = jnp.concatenate(
        [
            attention_output_weight,
            common_expert_gate_up_weight,
            common_expert_down_weight.reshape(own_rows, -1),
            ffn_gain[:, None],
            routing_weight,
            zeros[:, n_experts:],
        ],
        axis=1,
    )
    flat = common_expert_down_weight.size // own_rows
    front_q[-1] = after(front_q[-1], ranks)
    steps = dense_steps(nq)
    front_first = dense_start(front_q)

    gu_rows = expert_gate_up.shape[1]
    folded = expert_down.reshape(nq, -1, 2 * FF)
    both = jnp.concatenate([expert_gate_up, folded], axis=1)

    rest_q = ring_gather(pick("rest", rest, f1=front_q[1], f3=front_q[-1]), "q")
    g_q = [pick("g", grad_low, r1=rest_q[1], r3=rest_q[-1], f3=front_q[-1])]
    g_q.append(shift(g_q[0], "q"))
    front_first = [
        pick(f"mid{i}", v, r1=rest_q[1], r2=rest_q[2]) for i, v in enumerate(front_first)
    ]
    front_pieces = dense_end(*front_first)
    due = [pick("core2", front_pieces[0], r1=rest_q[1], r2=rest_q[2], r3=rest_q[3], g1=g_q[1])]
    qkv_weight, front_small = dense_place(front_pieces, steps, [3 * width, 128], due)
    for _ in range(nq - 2):
        g_q.append(shift(g_q[-1], "q"))
    rest_first = dense_start(
        [pick("rs1", part, fp=front_pieces, w=qkv_weight) for part in rest_q]
    )

    kv_chunks = []
    gain_one = front_small[:, 0].astype(F32)
    inv_one = rms_scale(tokens_in)
    normed = (tokens_in * inv_one * gain_one).astype(BF)
    normed = pick("norm", normed, rs=rest_first, g1=g_q[1], g2=g_q[2], g3=g_q[3])
    queries, kv_own = project(normed, qkv_weight, *tables)
    places = [
        jnp.stack(
            [ctx_rank]
            + [
                lax.rem(q_at - k + nq, nq) * nr + lax.rem(r_at - s + nr, nr)
                for s in range(nr)
            ]
        ).astype(jnp.int32)
        for k in range(nq)
    ]
    rest_pieces = dense_end(*(pick("rs2", v, q=queries, w=qkv_weight) for v in rest_first))
    state = None
    arrived = kv_own
    for k in range(nq):
        chunk = ring_gather(arrived, "r")
        if k < nq - 1:
            coming = shift(arrived, "q")
        if k == 1:
            g_even, g_odd = (
                pick("gs1", jnp.stack(g_q[low::2]), rp=rest_pieces, a1=arrived) for low in (0, 1)
            )
            g_even = jnp.stack(ring_gather(g_even, "b"))
            g_odd = jnp.stack(ring_gather(g_odd, "a"))
        state = attend_chunk(places[k], queries, chunk, state, k == nq - 1, n_ctx)
        kv_chunks.append(chunk)
        if k < nq - 1:
            if k == 0:
                arrived = pick("arr1", coming, s=state[0], g2=g_q[2], g3=g_q[3], rp=rest_pieces)
            if k == 1:
                arrived = pick("arr2", coming, s=state[0], gs=(g_even, g_odd), rp=rest_pieces)
            if k == 2:
                g_even, g_odd = ring_gather(g_even, "a"), ring_gather(g_odd, "b")
                arrived = pick("arr3", coming, s=state[0], gf=(g_even, g_odd))
    mixed, lse = state
    both = pick("wa", both, a3=arrived, c3=chunk[1:], q=queries, m=mixed)
    both = lax.all_to_all(both, "q", split_axis=0, concat_axis=0, tiled=True)
    mixed = pick("mix", mixed, gf=(g_even, g_odd))
    out_weight, shared_in, shared_out, rest_small = dense_place(
        rest_pieces, steps, [width, 2 * FF, flat, 128]
    )
    shared_out = shared_out.reshape(-1, width)
    gain_two = rest_small[:, 0].astype(F32)
    router = rest_small[:, 1 : 1 + n_experts]
    residual = tokens_in + dot(mixed, out_weight)
    inv_two = rms_scale(residual)
    second = (residual * inv_two * gain_two).astype(BF)
    expert = jnp.stack([exp_rank * nq + q_at, q_at, a_at, b_at]).astype(jnp.int32)
    router_t = router.T
    kept = None
    ys = [None, None]
    sum_first, dgates, decs = [], [], []
    c_q = [second, shift(second, "q")]
    c_start = jnp.stack(ring_gather(c_q[0], "b"))
    c_planes = [plane_gather(c_q[0], True, c_start)]
    both = pick("wc", both, m=mixed, cs=c_start, c1=c_q[1], cp=c_planes[0])
    both = ring_gather(both, "r")
    kr = np.repeat(np.arange(nr, dtype=np.int32), nq)
    kq = np.tile(np.arange(nq, dtype=np.int32), nr)
    index = kq * nr + lax.rem(r_at - kr + nr, nr)
    w1, w2 = place(
        index.astype(jnp.int32),
        both,
        [((0, gu_rows), 0, 2 * FF), ((gu_rows, folded.shape[1]), 0, 2 * FF)],
    )
    w2 = w2.reshape(-1, width)
    for k in range(2, nq):
        c_q.append(shift(pick(f"cz{k}", c_q[-1], w=w1, cp=c_planes[0]), "q"))
    g_even = [jnp.stack(g_even)]
    for k in range(nq):
        if k:
            ready = dict(w=w1) | {f"k{i}": v for i, v in enumerate(dgates)}
            rows = pick(f"c{k}a", c_q[k], **ready)
            first = jnp.stack(ring_gather(rows, "ba"[k % 2]))
            c_planes.append(plane_gather(rows, k % 2 == 0, pick(f"c{k}b", first, **ready)))
        c = c_planes[k]
        ready = {f"s{i}": v for i, v in enumerate(sum_first) if v is not None}
        if k == 3:
            ready["e1"] = dec_one = sum_end(sum_first[1], False)
        hold = pick(f"K{k}", ranks, **ready)
        dec, dgate, kept, ys[k % 2] = expert_chunk(
            k, nq, na, nb, expert, hold, c, (g_even, g_odd)[k % 2], router_t, w1, w2, kept, ys[k % 2], slots
        )
        dgates.append(dgate.reshape(na * nb, tok))
        ready = {f"k{i}": v for i, v in enumerate(dgates)}
        decs.append(dec)
        sum_first.append(None)
        if k:
            sum_first[k] = sum_start([pick(f"d{k}", v, **ready) for v in dec], k % 2 == 0)
    ready = {f"k{i}": v for i, v in enumerate(dgates)}
    sum_first[0] = sum_start([pick("d0", v, **ready) for v in decs[0]], True)
    firsts = sum_first
    dec_sums = [dec_one if k == 1 else sum_end(firsts[k], k % 2 == 0) for k in range(nq)]
    ready = {f"s{i}": v for i, v in enumerate(firsts)}
    xs, hs, deys, degs = kept[:4]
    gate_up_term = dot(pick("gu", xs, **ready), degs, TN).astype(BF)
    down_term = dot(pick("dn", hs, gu=gate_up_term, **ready), deys, TN).astype(BF)
    terms = [
        gate_up_term.reshape(nq, nr, gu_rows, 2 * FF),
        down_term.reshape(nq, nr, -1, 2 * FF),
    ]
    at = [lax.rem(r_at - k + nr, nr) for k in range(nr)]
    expert_rows = ring_sum(
        [
            jnp.concatenate(
                [lax.dynamic_index_in_dim(t, i, 1, keepdims=False) for t in terms], axis=1
            )
            for i in at
        ],
        "r",
    ).astype(BF)
    moving = dec_sums[1].astype(BF)
    for k in range(2, nq):
        term = dec_sums[k]
        term = pick(f"t{k}", term, gu=gate_up_term, dn=down_term, er=expert_rows)
        moving = (shift(moving, "q").astype(F32) + term).astype(BF)
    routed_grad = shift(moving, "q").astype(F32) + dec_sums[0]

    expert_rows = pick("ea", expert_rows, rg=routed_grad, t=moving)
    expert_rows = lax.all_to_all(expert_rows, "q", split_axis=0, concat_axis=0, tiled=True)

    ready = {f"k{i}": v for i, v in enumerate(dgates)}
    later = pick("sh", second, **ready)
    shared_pre = dot(later, shared_in)
    shared_gate, shared_up = shared_pre[:, :FF], shared_pre[:, FF:]
    shared_sig = jax.nn.sigmoid(shared_gate)
    shared_hidden = (shared_gate * shared_sig * shared_up).astype(BF)

    logits = jnp.where(named, dot(later, router), masked_value)
    raised = jnp.where(named, jnp.exp(logits - jnp.max(logits, axis=1, keepdims=True)), 0.0)
    gates = raised / jnp.sum(raised, axis=1, keepdims=True)
    n_all = nq * na * nb
    spot = np.arange(n_all, dtype=np.int32)
    spot = (
        lax.rem(q_at - spot // (na * nb) + nq, nq) * (na * nb)
        + lax.rem(a_at - spot // nb % na + na, na) * nb
        + lax.rem(b_at - spot % nb + nb, nb)
    )
    dgate = jnp.concatenate(dgates, axis=0)[spot]
    dgate = lax.all_to_all(dgate, ("q", "a", "b"), split_axis=0, concat_axis=0, tiled=True)
    dgate = jnp.swapaxes(dgate.reshape(nq, na * nb, tok), 0, 1).reshape(n_experts, tok).T
    grad_logits = gates * (dgate - jnp.sum(gates * dgate, axis=1, keepdims=True))
    grad_logits = grad_logits.astype(BF)

    shared_hidden_grad = dot(grad_low, shared_out, NT)
    shared_pre_grad = jnp.concatenate(
        [
            shared_hidden_grad * shared_up * shared_sig * (1.0 + shared_gate * (1.0 - shared_sig)),
            shared_hidden_grad * shared_gate * shared_sig,
        ],
        axis=1,
    ).astype(BF)
    second_grad = (
        dot(shared_pre_grad, shared_in, NT) + dot(grad_logits, router, NT) + routed_grad
    )
    ffn_gain_grad = jnp.sum(second_grad * residual * inv_two, axis=0)
    residual_grad = out_grad + norm_back(second_grad, residual, inv_two, gain_two)
    mixed_grad = residual_grad.astype(BF)
    heads_grad = dot(mixed_grad, out_weight, NT).astype(BF)

    y_first = [
        sum_start([pick("y1", v, rg=routed_grad, k=dgates[3]) for v in ys[p]], p == 0)
        for p in (0, 1)
    ]
    dq = None
    moving = None
    held = heads_grad
    for step, k in enumerate(list(range(1, nq)) + [0]):
        ready = dict(er=expert_rows, y=y_first, m=moving if step else ())
        held = pick(f"B{step}", held, **ready)
        dq, parts = attend_back_chunk(
            places[k], queries, held, mixed, lse, tables, kv_chunks[k], dq, k == 0, n_ctx
        )
        term = ring_sum(parts, "r")
        if k == 1:
            moving = term.astype(BF)
            first_move = moving
        elif k:
            moving = (shift(moving, "q").astype(F32) + term).astype(BF)
    late = dense_sum_core(
        [
            dot(normed, dq, TN).astype(BF),
            dot(mixed, mixed_grad, TN).astype(BF),
            dot(later, shared_pre_grad, TN).astype(BF),
            dot(shared_hidden, grad_low, TN).astype(BF).reshape(width, flat),
            jnp.concatenate(
                [
                    ffn_gain_grad[:, None],
                    dot(later, grad_logits, TN),
                    jnp.zeros((width, 127 - n_experts), F32),
                ],
                axis=1,
            ).astype(BF),
        ],
        own_rows,
    )
    y_sums = [sum_end(pick("y2", y_first[p], q=dq, m=moving, f=first_move), p == 0, 1) for p in (0, 1)]
    late = dense_sum_first(late)
    kv_back = finish_keys(
        shift(moving, "q"), pick("fin", term, late=late, ys=y_sums), *tables
    )

    owned = pick("xg", expert_rows, b=kv_back, m=moving)
    gate_up_grad = owned[:, :gu_rows].astype(F32)
    down_grad = owned[:, gu_rows:].reshape(nq, -1, width).astype(F32)
    key_value = dense_sum_core(
        [
            pick("kv1", dot(normed, kv_back[0], TN).astype(BF), late=late, ys=y_sums),
            dot(normed, kv_back[1], TN).astype(BF),
        ],
        own_rows,
    )
    ready = dict(kv=key_value)
    normed_grad = dot(dq, qkv_weight[:, :width], NT)
    kv_low = pick("dn0", kv_back, **ready)
    normed_grad += dot(kv_low[0], qkv_weight[:, width : 2 * width], NT)
    normed_grad += dot(kv_low[1], qkv_weight[:, 2 * width :], NT)
    input_grad = residual_grad + norm_back(normed_grad, tokens_in, inv_one, gain_one)
    y_sums = pick("y3", y_sums, b=kv_back, kv=key_value, m=moving)
    y_terms = [y_sums[k % 2][k // 2] for k in range(nq)]
    late = dense_sum_second(*(pick("late2", v, b=kv_back, kv=key_value) for v in late))
    first_kv = dense_sum_first(pick("kv2", key_value, l=late))
    last_kv = dense_sum_second(*first_kv)
    y_moving = y_terms[1].astype(BF)
    for k in range(2, nq + 1):
        y_moving = shift(y_moving, "q")
        y_moving = pick(f"yz{k}", y_moving, kv=key_value, f=first_kv, l=late, z=last_kv)
        routed_sum = y_moving.astype(F32) + y_terms[k % nq]
        y_moving = routed_sum.astype(BF)
    late_grad = dense_sum_last(pick("late3", late, f=first_kv, kv=key_value, z=last_kv))
    kv_weight_grad = dense_sum_last(last_kv)
    layer_out = (residual + dot(shared_hidden, shared_out) + routed_sum).astype(BF)
    at_out, at_shared, at_down = width, 2 * width, 2 * width + 2 * FF
    at_small = at_down + flat
    qkv_weight_grad = jnp.concatenate([late_grad[:, :at_out], kv_weight_grad], axis=1)
    attn_gain_grad = jnp.sum(query_key_value_weight.astype(F32) * qkv_weight_grad, axis=1)
    attn_gain_grad = attn_gain_grad / attn_gain.astype(F32)
    return (
        layer_out[None],
        input_grad[None],
        attn_gain_grad,
        qkv_weight_grad,
        late_grad[:, at_out:at_shared],
        late_grad[:, at_small],
        late_grad[:, at_small + 1 : at_small + 1 + n_experts],
        late_grad[:, at_shared:at_down],
        late_grad[:, at_down:at_small].reshape(down_rows, width),
        gate_up_grad,
        down_grad,
    )


def solution(mesh):
    n_ctx, n_exp = mesh.shape["ctx"], mesh.shape["exp"]

    def layer(*args):
        n_experts = args[10].shape[0]
        nq = n_experts // n_exp
        nb = 2
        fine = Mesh(
            np.asarray(mesh.devices).reshape(nq, n_ctx // nq, n_exp // nb, nb), ("q", "r", "a", "b")
        )
        ctx, exp, every = ("q", "r"), ("a", "b"), ("q", "r", "a", "b")
        tokens, flat, rows = P(exp, ctx, None), P(every), P(every, None)
        run = jax.shard_map(
            functools.partial(body, n_experts),
            mesh=fine,
            in_specs=(
                tokens, tokens, tokens, flat, rows, rows, flat, rows, rows, rows, tokens, tokens,
            ),
            out_specs=(tokens, tokens, flat, rows, rows, flat, rows, rows, rows, tokens, tokens),
            check_vma=False,
        )
        return run(*args)

    return layer
```

```python
import functools

import jax
import jax.numpy as jnp
import numpy as np
from jax import lax
from jax.experimental import pallas as pl
from jax.experimental.pallas import tpu as pltpu
from jax.sharding import Mesh
from jax.sharding import PartitionSpec as P

HEADS = 10
HEAD_DIM = 128
FF = 896
TOP = 7

norm_eps = 1e-06
rope_base = 10000.0
masked_value = -1e30
LOG2E = 1.4426950408889634

BF = jnp.bfloat16
F32 = jnp.float32
VMEM_LIMIT = 56 * 1024 * 1024


def rope_tables(positions, head_dim):
    halfway = head_dim // 2
    frequency = rope_base ** (-(jnp.arange(halfway).astype(F32) * 2.0 / head_dim))
    angles = positions.astype(F32)[:, None] * frequency[None, :]
    angles = jnp.concatenate([angles, angles], axis=1)
    return (jnp.cos(angles), jnp.sin(angles))


def rms_scale(values):
    return lax.rsqrt(jnp.mean(values * values, axis=1, keepdims=True) + norm_eps)


def norm_back(grad_in, values, inv_rms, gain_vec):
    scaled = grad_in * gain_vec
    return inv_rms * scaled - values * inv_rms**3 * jnp.mean(scaled * values, axis=1, keepdims=True)


def dot(a, b, dims=((1,), (0,))):
    return lax.dot_general(a, b, (dims, ((), ())), preferred_element_type=F32)


NT = ((1,), (1,))
TN = ((0,), (0,))


def shift(value, axis):
    n = lax.axis_size(axis)
    return lax.ppermute(value, axis, [(i, (i + 1) % n) for i in range(n)])


def ring_gather(value, axis):
    parts = [value]
    for _ in range(1, lax.axis_size(axis)):
        parts.append(shift(parts[-1], axis))
    return parts


def shift_by(value, axis, k):
    n = lax.axis_size(axis)
    return lax.ppermute(value, axis, [(i, (i + k) % n) for i in range(n)])


def direct_gather(value, axis):
    return [value] + [shift_by(value, axis, k) for k in range(1, lax.axis_size(axis))]


def ring_sum(blocks, axis, events=()):
    n = len(blocks)
    if n == 1:
        return blocks[0].astype(F32)
    moving = blocks[1].astype(BF)
    for k in range(2, n):
        moving = after(shift(moving, axis), *events)
        moving = (moving.astype(F32) + blocks[k].astype(F32)).astype(BF)
    return after(shift(moving, axis), *events).astype(F32) + blocks[0].astype(F32)


def ring_blocks(arrays, axis, dim):
    n = lax.axis_size(axis)
    index = lax.axis_index(axis)
    out = []
    for k in range(n):
        at = lax.rem(index - k + n, n)
        parts = [lax.dynamic_index_in_dim(v, at, dim, keepdims=False) for v in arrays]
        out.append(parts[0] if len(parts) == 1 else jnp.concatenate(parts, axis=-1))
    return out


ORDER = {
    "rest": "f1",
    "g": "r3",
    "mid1": "r2",
    "core2": "r3",
    "rs1": "fp",
    "norm": "g2",
    "gs1": "rp",
    "arr1": "g3 rp",
    "arr2": "gs",
    "arr3": "s gf",
    "wa": "q",
    "wc": "m",
    "c1b": "w",
    "c2b": "k0",
    "c3a": "w",
    "c3b": "k0",
    "gu": "s1",
    "dn": "s1",
    "t2": "er",
    "sh": "k2",
    "B1": "m",
    "B3": "er",
    "y1": "rg",
    "fin": "late",
    "kv1": "ys",
    "kv2": "l",
    "yz3": "kv",
    "yz4": "z",
    "late3": "kv",
    "cz2": "w",
    "cz3": "cp",
    "xg": "m",
    "dn0": "kv",
}


def pick(name, value, **events):
    chosen = [events[key] for key in ORDER.get(name, "").split() if key in events]
    return after(value, *jax.tree.leaves(chosen))


def after(value, *events):
    if not events:
        return value
    return lax.optimization_barrier((value, *events))[0]


def place_kernel(counts, cuts, index_ref, *refs):
    n = len(counts)
    pieces, outs, sems = refs[:n], refs[n:-1], refs[-1]
    t = 0
    for piece, count in zip(pieces, counts):
        for j in range(count):
            at = index_ref[t]
            t += 1
            for o, (rows, low, high) in enumerate(cuts):
                pltpu.make_async_copy(
                    piece.at[j, pl.ds(*rows), pl.ds(low, high - low)], outs[o].at[at], sems.at[o]
                ).start()
    for o in range(len(cuts)):
        pltpu.make_async_copy(outs[o], outs[o], sems.at[o]).wait()


def place(index, pieces, cuts):
    rows, total = pieces[0].shape[-2:]
    pieces = [piece.reshape(-1, rows, total) for piece in pieces]
    counts = [piece.shape[0] for piece in pieces]
    n = sum(counts)
    outs = pl.pallas_call(
        functools.partial(place_kernel, counts, cuts),
        in_specs=[pl.BlockSpec(memory_space=pltpu.SMEM)]
        + [pl.BlockSpec(memory_space=pl.ANY)] * len(pieces),
        out_specs=[pl.BlockSpec(memory_space=pltpu.VMEM)] * len(cuts),
        scratch_shapes=[pltpu.SemaphoreType.DMA((len(cuts),))],
        out_shape=[
            jax.ShapeDtypeStruct((n, c[0][1], c[2] - c[1]), pieces[0].dtype) for c in cuts
        ],
        compiler_params=pltpu.CompilerParams(vmem_limit_bytes=VMEM_LIMIT // 2),
        cost_estimate=pl.CostEstimate(
            flops=0, bytes_accessed=4 * n * rows * total, transcendentals=0
        ),
        name="place",
    )(index, *pieces)
    return [out.reshape(-1, out.shape[2]) for out in outs]


def dense_steps(nq):
    half, na, nb = nq // 2, lax.axis_size("a"), lax.axis_size("b")
    steps = [[(kq, ka, kb) for kb in range(nb) for kq in range(half)] for ka in range(na)]
    return steps + [
        [(kq, ka, kb) for ka in range(na) for kq in range(half, nq)] for kb in range(nb)
    ]


def dense_start(along_q):
    half = len(along_q) // 2
    one = jnp.stack(ring_gather(jnp.stack(along_q[:half]), "b"))
    two = jnp.stack(ring_gather(jnp.stack(along_q[half:]), "a"))
    return one, two


def dense_end(one, two):
    return ring_gather(one, "a") + ring_gather(two, "b")


def dense_place(pieces, steps, widths, due=()):
    nq, nr, na, nb = (lax.axis_size(axis) for axis in ("q", "r", "a", "b"))
    rows, width = pieces[0].shape[-2:]
    flat = [piece.reshape(-1, rows, width) for piece in pieces]
    groups = [[0, na], [k for k in range(na + nb) if k not in (0, na)]]
    arrays, order = [], []
    for group in groups:
        own = jnp.concatenate([flat[k] for k in group], axis=0)
        if group is groups[1]:
            own = after(own, *due)
        entries = [s for k in group for s in steps[k]]
        for kr, part in enumerate(ring_gather(own, "r")):
            arrays.append(part)
            order += [(kr, *s) for s in entries]
    kr, kq, ka, kb = (np.array(column, np.int32) for column in zip(*order))
    index = lax.rem(lax.axis_index("q") - kq + nq, nq) * nr
    index = index + lax.rem(lax.axis_index("r") - kr + nr, nr)
    index = index * na + lax.rem(lax.axis_index("a") - ka + na, na)
    index = index * nb + lax.rem(lax.axis_index("b") - kb + nb, nb)
    edges = np.cumsum([0] + list(widths))
    cuts = [((0, rows), int(low), int(high)) for low, high in zip(edges[:-1], edges[1:])]
    return place(index.astype(jnp.int32), arrays, cuts)


def dense_sum_core(wholes, n_rows):
    nq, nr, na, nb = (lax.axis_size(axis) for axis in ("q", "r", "a", "b"))
    values = [whole.reshape(nq, nr, na, nb, n_rows, whole.shape[1]) for whole in wholes]
    return ring_sum(ring_blocks(values, "r", 1), "r").astype(BF)


def dense_sum_first(value):
    half = value.shape[0] // 2
    one = ring_sum(ring_blocks([value[:half]], "a", 1), "a").astype(BF)
    two = ring_sum(ring_blocks([value[half:]], "b", 2), "b").astype(BF)
    return one, two


def dense_sum_second(one, two):
    one = ring_sum(ring_blocks([one], "b", 1), "b")
    two = ring_sum(ring_blocks([two], "a", 1), "a")
    return jnp.concatenate([one, two], axis=0).astype(BF)


def dense_sum_last(value):
    return ring_sum(ring_blocks([value], "q", 0), "q")


def plane_gather(rows, even, first=None):
    inner, outer = ("b", "a") if even else ("a", "b")
    if first is None:
        first = jnp.stack(ring_gather(rows, inner))
    parts = ring_gather(first, outer)
    return [jnp.stack(parts)] if even else parts


def sum_start(parts, even, events=()):
    return ring_sum(parts, "a" if even else "b", events)


def sum_end(first, even, dim=0, events=()):
    n = first.shape[dim]
    parts = [lax.index_in_dim(first, k, dim, False) for k in range(n)]
    return ring_sum(parts, "b" if even else "a", events)


def project_kernel(n_query, x_ref, w_ref, cos_ref, sin_ref, q_ref, kv_ref):
    j = pl.program_id(0)
    made = dot(x_ref[...], w_ref[...])

    def turned():
        parts = []
        for low in range(0, made.shape[1], HEAD_DIM):
            u = made[:, low : low + HEAD_DIM]
            parts.append(u * cos_ref[...] + pltpu.roll(u, HEAD_DIM // 2, 1) * sin_ref[...])
        return jnp.concatenate(parts, axis=1).astype(BF)

    @pl.when(j < n_query)
    def _():
        q_ref[...] = turned()

    @pl.when((j >= n_query) & (j < 2 * n_query))
    def _():
        kv_ref[0] = turned()

    @pl.when(j >= 2 * n_query)
    def _():
        kv_ref[0] = made.astype(BF)


def project(normed, weight, cosines, signed_sine):
    tok, width = normed.shape
    block = 2 * HEAD_DIM
    n = width // block
    table = pl.BlockSpec((tok, HEAD_DIM), lambda j: (0, 0))
    return pl.pallas_call(
        functools.partial(project_kernel, n),
        grid=(3 * n,),
        in_specs=[
            pl.BlockSpec((tok, width), lambda j: (0, 0)),
            pl.BlockSpec((width, block), lambda j: (0, j)),
            table,
            table,
        ],
        out_specs=[
            pl.BlockSpec((tok, block), lambda j: (0, jnp.minimum(j, n - 1))),
            pl.BlockSpec(
                (1, tok, block),
                lambda j: (jnp.maximum(j - n, 0) // n, 0, jnp.maximum(j - n, 0) % n),
            ),
        ],
        out_shape=[
            jax.ShapeDtypeStruct((tok, width), BF),
            jax.ShapeDtypeStruct((2, tok, width), BF),
        ],
        compiler_params=pltpu.CompilerParams(vmem_limit_bytes=VMEM_LIMIT // 2),
        cost_estimate=pl.CostEstimate(
            flops=6 * tok * width * width, bytes_accessed=6 * width * width, transcendentals=0
        ),
        name="project",
    )(normed, weight, cosines, signed_sine)


def turn_back(grad, cos, signed_sine):
    return grad * cos - pltpu.roll(grad, HEAD_DIM // 2, 1) * signed_sine


def finish_kernel(moved_ref, own_ref, cos_ref, sin_ref, out_ref):
    keys = moved_ref[0].astype(F32) + own_ref[0]
    out_ref[0] = turn_back(keys, cos_ref[...], sin_ref[...]).astype(BF)
    out_ref[1] = (moved_ref[1].astype(F32) + own_ref[1]).astype(BF)


def finish_keys(moved, own, cosines, signed_sine):
    _, tok, width = own.shape
    pair = pl.BlockSpec((2, tok, HEAD_DIM), lambda h: (0, 0, h))
    table = pl.BlockSpec((tok, HEAD_DIM), lambda h: (0, 0))
    return pl.pallas_call(
        finish_kernel,
        grid=(width // HEAD_DIM,),
        in_specs=[pair, pair, table, table],
        out_specs=pair,
        out_shape=jax.ShapeDtypeStruct((2, tok, width), BF),
        cost_estimate=pl.CostEstimate(
            flops=10 * tok * width, bytes_accessed=16 * tok * width, transcendentals=0
        ),
        name="finish_keys",
    )(moved, own, cosines, signed_sine)


def allowed_mask(own, other, n_ctx, half):
    row = lax.broadcasted_iota(jnp.int32, (2 * half, 2 * half), 0)
    col = lax.broadcasted_iota(jnp.int32, (2 * half, 2 * half), 1)
    last = 2 * n_ctx - 1
    query = row + jnp.where(row < half, own * half, (last - own) * half - half)
    key = col + jnp.where(col < half, other * half, (last - other) * half - half)
    return key <= query


def attend_kernel(n_ctx, n_src, first, last, place_ref, q_ref, *refs):
    kv_refs, refs = refs[:n_src], refs[n_src:]
    if not first:
        acc_in, ml_in = refs[:2]
        refs = refs[2:]
    out_ref, ml_ref = refs
    queries = q_ref[...]
    tok = queries.shape[0]
    scores = []
    for s in range(n_src):
        raw = dot(queries, kv_refs[s][0], NT) * (HEAD_DIM ** (-0.5) * LOG2E)
        mask = allowed_mask(place_ref[0], place_ref[1 + s], n_ctx, tok // 2)
        scores.append(jnp.where(mask, raw, masked_value))
    peak = functools.reduce(jnp.maximum, [jnp.max(s, axis=1, keepdims=True) for s in scores])
    if not first:
        old_peak = ml_in[0][:, 0:1]
        old_sum = ml_in[0][:, 64:65]
        peak = jnp.maximum(peak, old_peak)
    total = jnp.zeros_like(peak)
    mixed = jnp.zeros((tok, HEAD_DIM), F32)
    for s in range(n_src):
        raised = jnp.exp2(scores[s] - peak)
        total = total + jnp.sum(raised, axis=1, keepdims=True)
        mixed = mixed + dot(raised.astype(BF), kv_refs[s][1])
    if not first:
        decay = jnp.exp2(old_peak - peak)
        total = total + old_sum * decay
        mixed = mixed + acc_in[...] * decay
    if last:
        out_ref[...] = (mixed / total).astype(BF)
        ml_ref[0] = jnp.broadcast_to(peak + jnp.log2(total), (tok, 128))
    else:
        out_ref[...] = mixed
        lane = lax.broadcasted_iota(jnp.int32, (tok, 128), 1)
        ml_ref[0] = jnp.where(lane < 64, peak, total)


def attend_chunk(places, queries, kv_list, state, last, n_ctx):
    tok, width = queries.shape
    head = pl.BlockSpec((tok, HEAD_DIM), lambda h, p: (0, h))
    pair = pl.BlockSpec((2, tok, HEAD_DIM), lambda h, p: (0, 0, h))
    rows = pl.BlockSpec((1, tok, 128), lambda h, p: (h, 0, 0))
    first = state is None
    n = len(kv_list)
    pairs = tok * tok * n * HEADS
    return pl.pallas_call(
        functools.partial(attend_kernel, n_ctx, n, first, last),
        grid_spec=pltpu.PrefetchScalarGridSpec(
            num_scalar_prefetch=1,
            grid=(HEADS,),
            in_specs=[head] + [pair] * n + ([] if first else [head, rows]),
            out_specs=[head, rows],
        ),
        out_shape=[
            jax.ShapeDtypeStruct((tok, width), BF if last else F32),
            jax.ShapeDtypeStruct((HEADS, tok, 128), F32),
        ],
        compiler_params=pltpu.CompilerParams(vmem_limit_bytes=VMEM_LIMIT // 2),
        cost_estimate=pl.CostEstimate(
            flops=4 * pairs * HEAD_DIM * 4, bytes_accessed=8 * tok * width, transcendentals=pairs
        ),
        name="attend",
    )(places, queries, *kv_list, *(() if first else state))


def attend_back_kernel(
    n_ctx, n_src, first, last, place_ref, q_ref, do_ref, o_ref, lse_ref, cos_ref, sin_ref, *refs
):
    kv_refs, refs = refs[:n_src], refs[n_src:]
    if not first:
        dq_in, refs = refs[0], refs[1:]
    dq_ref, dkv_refs = refs[0], refs[1:]
    queries = q_ref[...]
    grad = do_ref[...]
    tok = queries.shape[0]
    lse = lse_ref[0][:, 0:1]
    delta = jnp.sum(grad.astype(F32) * o_ref[...].astype(F32), axis=1, keepdims=True)
    scale = HEAD_DIM ** (-0.5)
    grad_query = jnp.zeros((tok, HEAD_DIM), F32)
    for s in range(n_src):
        keys, values = kv_refs[s][0], kv_refs[s][1]
        raw = dot(queries, keys, NT) * (scale * LOG2E)
        mask = allowed_mask(place_ref[0], place_ref[1 + s], n_ctx, tok // 2)
        probs = jnp.exp2(jnp.where(mask, raw, masked_value) - lse)
        grad_probs = dot(grad, values, NT)
        grad_scores = (probs * (grad_probs - delta)).astype(BF)
        grad_query = grad_query + dot(grad_scores, keys)
        dkv_refs[s][0] = (dot(grad_scores, queries, TN) * scale).astype(dkv_refs[s].dtype)
        dkv_refs[s][1] = dot(probs.astype(BF), grad, TN).astype(dkv_refs[s].dtype)
    grad_query = grad_query * scale
    if not first:
        grad_query = grad_query + dq_in[...]
    if last:
        grad_query = turn_back(grad_query, cos_ref[...], sin_ref[...]).astype(BF)
    dq_ref[...] = grad_query


def attend_back_chunk(places, queries, grad, mixed, lse, tables, kv_list, dq, last, n_ctx):
    tok, width = queries.shape
    head = pl.BlockSpec((tok, HEAD_DIM), lambda h, p: (0, h))
    pair = pl.BlockSpec((2, tok, HEAD_DIM), lambda h, p: (0, 0, h))
    rows = pl.BlockSpec((1, tok, 128), lambda h, p: (h, 0, 0))
    table = pl.BlockSpec((tok, HEAD_DIM), lambda h, p: (0, 0))
    first = dq is None
    n = len(kv_list)
    pairs = tok * tok * n * HEADS
    out = pl.pallas_call(
        functools.partial(attend_back_kernel, n_ctx, n, first, last),
        grid_spec=pltpu.PrefetchScalarGridSpec(
            num_scalar_prefetch=1,
            grid=(HEADS,),
            in_specs=[head, head, head, rows, table, table] + [pair] * n + ([] if first else [head]),
            out_specs=[head] + [pair] * n,
        ),
        out_shape=[jax.ShapeDtypeStruct((tok, width), BF if last else F32)]
        + [jax.ShapeDtypeStruct((2, tok, width), F32 if s == 0 else BF) for s in range(n)],
        compiler_params=pltpu.CompilerParams(vmem_limit_bytes=VMEM_LIMIT // 2),
        cost_estimate=pl.CostEstimate(
            flops=10 * pairs * HEAD_DIM * 4, bytes_accessed=16 * tok * width, transcendentals=pairs
        ),
        name="attend_back",
    )(places, queries, grad, mixed, lse, *tables, *kv_list, *(() if first else (dq,)))
    return out[0], out[1:]


def expert_kernel(slots, na, nb, even, n_kept, e_ref, rank_ref, *refs):
    n_in, n_sum = (1, na) if even else (nb, nb)
    c_refs, g_refs, refs = refs[:n_in], refs[n_in : 2 * n_in], refs[2 * n_in :]
    wr_ref, w1_ref, w2_ref = refs[:3]
    refs = refs[3 + n_kept :]
    d_refs, dg_ref, refs = refs[:n_sum], refs[n_sum], refs[n_sum + 1 :]
    x_ref, h_ref, dey_ref, deg_ref = refs[:4]
    y_refs = refs[4:]
    tok = g_refs[0].shape[-2]
    experts = wr_ref.shape[0]
    me = e_ref[0]
    step = pl.program_id(0)
    picks, rows, grads, weights = [], [], [], []
    own = lax.broadcasted_iota(jnp.int32, (experts, tok), 0) == me
    slot = lax.broadcasted_iota(jnp.int32, (slots, tok), 0).astype(F32)
    for s in range(nb):
        tokens = c_refs[0][0, s] if even else c_refs[s][0]
        cot = g_refs[0][0, s, 0] if even else g_refs[s][0, 0]
        rank = rank_ref[0, s, 0]
        logits = dot(wr_ref[...], tokens, NT)
        logits = jnp.where(rank >= 0, logits, masked_value)
        raised = jnp.where(rank >= 0, jnp.exp(logits - jnp.max(logits, axis=0, keepdims=True)), 0.0)
        gates = raised / jnp.sum(raised, axis=0, keepdims=True)
        gate_row = jnp.sum(jnp.where(own, gates, 0.0), axis=0, keepdims=True)
        rank_row = jnp.sum(jnp.where(own, rank, 0.0), axis=0, keepdims=True)
        pick = jnp.where(slot == rank_row, 1.0, 0.0)
        weights.append(jnp.sum(pick * gate_row, axis=1, keepdims=True))
        pick_low = pick.astype(BF)
        picks.append((pick, pick_low))
        rows.append(dot(pick_low, tokens).astype(BF))
        grads.append(dot(pick_low, cot))
    x = jnp.concatenate(rows, axis=0)
    grad = jnp.concatenate(grads, axis=0)
    weight = jnp.concatenate(weights, axis=0)
    x_ref[...] = x
    dey = (weight * grad).astype(BF)
    dey_ref[...] = dey
    pre = dot(x, w1_ref[...])
    gate, up = pre[:, :FF], pre[:, FF:]
    sig = jax.nn.sigmoid(gate)
    act = gate * sig
    hidden = (act * up).astype(BF)
    h_ref[...] = hidden
    grad_hidden = dot(dey, w2_ref[...], NT)
    deg = jnp.concatenate(
        [
            (grad_hidden * up * sig * (1.0 + gate * (1.0 - sig))).astype(BF),
            (grad_hidden * act).astype(BF),
        ],
        axis=1,
    )
    deg_ref[...] = deg
    dec = dot(deg, w1_ref[...], NT).astype(BF)
    ey = dot(hidden, w2_ref[...]).astype(BF).astype(F32)
    dgate = jnp.sum(grad * ey, axis=1, keepdims=True)
    weighted = (weight * ey).astype(BF)
    d_all, y_all = [], []
    for s in range(nb):
        part = slice(s * slots, (s + 1) * slots)
        pick, pick_low = picks[s]
        d_all.append(dot(pick_low, dec[part], TN).astype(BF))
        y_all.append(dot(pick_low, weighted[part], TN).astype(BF))
        if not even:
            d_refs[s][0] = d_all[s]
            y_refs[s][0, 0] = y_all[s]
        dg_ref[0, s] = jnp.sum(pick * dgate[part], axis=0, keepdims=True)
    if even:
        for k in range(na):

            @pl.when(step == k)
            def _(k=k):
                for s in range(nb):
                    d_refs[k][s] = d_all[s]
                    y_refs[k][0, s] = y_all[s]


def expert_chunk(chunk, nq, na, nb, expert, ranks, c, g, router_t, w1, w2, kept, y_kept, slots):
    even = chunk % 2 == 0
    tok, width = c[0].shape[-2:]
    experts = router_t.shape[0]
    g_one = pl.BlockSpec((1, nb, 1, tok, width), lambda i, e: (i, 0, chunk // 2, 0, 0))
    g_two = pl.BlockSpec((1, 1, tok, width), lambda i, e: (i, chunk // 2, 0, 0))
    one = pl.BlockSpec((1, nb, tok, width), lambda i, e: (i, 0, 0, 0))
    two = pl.BlockSpec((1, tok, width), lambda i, e: (i, 0, 0))

    def fixed(shape):
        return pl.BlockSpec(shape, lambda i, e: (0,) * len(shape), pipeline_mode=pl.Buffered(1))

    def by_rows(n):
        return pl.BlockSpec((nb * slots, n), lambda i, e: (chunk * na + i, 0))

    n_rows = na * nb * slots
    n_half = nq // 2
    if even:
        d_specs = [pl.BlockSpec((nb, tok, width), lambda i, e: (0, 0, 0))] * na
        y_specs = [pl.BlockSpec((1, nb, tok, width), lambda i, e: (chunk // 2, 0, 0, 0))] * na
        d_shapes = [jax.ShapeDtypeStruct((nb, tok, width), BF)] * na
        y_shapes = [jax.ShapeDtypeStruct((n_half, nb, tok, width), BF)] * na
    else:
        d_specs = [two] * nb
        y_specs = [pl.BlockSpec((1, 1, tok, width), lambda i, e: (chunk // 2, i, 0, 0))] * nb
        d_shapes = [jax.ShapeDtypeStruct((na, tok, width), BF)] * nb
        y_shapes = [jax.ShapeDtypeStruct((n_half, na, tok, width), BF)] * nb
    held = [*(kept or ()), *(y_kept or ())]
    n_in = 1 + 1 + len(c) + len(g) + 3
    n_out = len(d_shapes) + 1
    aliases = {n_in + k: n_out + k for k in range(len(kept or ()))}
    for k in range(len(y_kept or ())):
        aliases[n_in + len(kept or ()) + k] = n_out + 4 + k
    out = pl.pallas_call(
        functools.partial(expert_kernel, slots, na, nb, even, len(held)),
        grid_spec=pltpu.PrefetchScalarGridSpec(
            num_scalar_prefetch=1,
            grid=(na,),
            in_specs=[
                pl.BlockSpec((1, nb, 1, experts, tok), lambda i, e: (i, 0, chunk, 0, 0)),
                *([one, g_one] if even else [two] * nb + [g_two] * nb),
                fixed(router_t.shape), fixed(w1.shape), fixed(w2.shape),
                *[pl.BlockSpec(memory_space=pl.ANY)] * len(held),
            ],
            out_specs=[
                *d_specs,
                pl.BlockSpec((1, nb, 1, tok), lambda i, e: (i, 0, 0, 0)),
                by_rows(width), by_rows(FF), by_rows(width), by_rows(2 * FF),
                *y_specs,
            ],
        ),
        out_shape=[
            *d_shapes,
            jax.ShapeDtypeStruct((na, nb, 1, tok), F32),
            *[jax.ShapeDtypeStruct((nq * n_rows, n), BF) for n in (width, FF, width, 2 * FF)],
            *y_shapes,
        ],
        input_output_aliases=aliases,
        compiler_params=pltpu.CompilerParams(vmem_limit_bytes=VMEM_LIMIT),
        cost_estimate=pl.CostEstimate(
            flops=n_rows * width * FF * 12, bytes_accessed=30_000_000, transcendentals=n_rows * FF
        ),
        name="experts",
    )(expert, ranks, *c, *g, router_t, w1, w2, *held)
    n_d = len(d_shapes)
    return out[:n_d], out[n_d], out[n_out : n_out + 4], out[n_out + 4 :]


def body(
    n_experts,
    block_input,
    cotangent,
    routes,
    attn_gain,
    query_key_value_weight,
    attention_output_weight,
    ffn_gain,
    routing_weight,
    common_expert_gate_up_weight,
    common_expert_down_weight,
    expert_gate_up,
    expert_down,
):
    nq, nr, na, nb = (lax.axis_size(axis) for axis in ("q", "r", "a", "b"))
    q_at, r_at, a_at, b_at = (lax.axis_index(axis) for axis in ("q", "r", "a", "b"))
    n_ctx = nq * nr
    n_exp = na * nb
    ctx_rank = q_at * nr + r_at
    exp_rank = a_at * nb + b_at
    tok = block_input.shape[1]
    width = block_input.shape[2]
    half = tok // 2
    capacity = min(tok, 3 * TOP * tok // (2 * n_experts))
    slots = -(-capacity // 16) * 16
    row = jnp.arange(tok, dtype=jnp.int32)
    local_pos = jnp.where(
        row < half, ctx_rank * half + row, (2 * n_ctx - 1 - ctx_rank) * half + row - half
    )
    cosines, sines = rope_tables(local_pos, HEAD_DIM)
    sines = jnp.where(jnp.arange(HEAD_DIM)[None, :] < HEAD_DIM // 2, -sines, sines)
    tables = (cosines, sines)
    tokens_in = block_input[0].astype(F32)
    grad_low = cotangent[0]
    out_grad = grad_low.astype(F32)
    own_rows = query_key_value_weight.shape[0]
    down_rows = common_expert_down_weight.shape[0]

    named = jnp.any(
        routes[0][:, :, None] == jnp.arange(n_experts, dtype=jnp.int32)[None, None, :], axis=1
    )
    before = (row[:, None] < row[None, :]).astype(BF)
    rank = dot(named.astype(BF).T, before)
    rank = jnp.where(named.T, rank, -1.0)
    ranks = jnp.stack(direct_gather(rank, "q"))
    ranks = jnp.stack(ring_gather(ranks, "b"))
    ranks = jnp.stack(ring_gather(ranks, "a"))

    zeros = jnp.zeros((own_rows, 127), BF)
    front = jnp.concatenate([query_key_value_weight, attn_gain[:, None], zeros], axis=1)
    front_q = ring_gather(front, "q")
    rest = jnp.concatenate(
        [
            attention_output_weight,
            common_expert_gate_up_weight,
            common_expert_down_weight.reshape(own_rows, -1),
            ffn_gain[:, None],
            routing_weight,
            zeros[:, n_experts:],
        ],
        axis=1,
    )
    flat = common_expert_down_weight.size // own_rows
    front_q[-1] = after(front_q[-1], ranks)
    steps = dense_steps(nq)
    front_first = dense_start(front_q)

    gu_rows = expert_gate_up.shape[1]
    folded = expert_down.reshape(nq, -1, 2 * FF)
    both = jnp.concatenate([expert_gate_up, folded], axis=1)

    rest_q = ring_gather(pick("rest", rest, f1=front_q[1], f3=front_q[-1]), "q")
    g_q = [pick("g", grad_low, r1=rest_q[1], r3=rest_q[-1], f3=front_q[-1])]
    g_q.append(shift(g_q[0], "q"))
    front_first = [
        pick(f"mid{i}", v, r1=rest_q[1], r2=rest_q[2]) for i, v in enumerate(front_first)
    ]
    front_pieces = dense_end(*front_first)
    due = [pick("core2", front_pieces[0], r1=rest_q[1], r2=rest_q[2], r3=rest_q[3], g1=g_q[1])]
    qkv_weight, front_small = dense_place(front_pieces, steps, [3 * width, 128], due)
    for _ in range(nq - 2):
        g_q.append(shift(g_q[-1], "q"))
    rest_first = dense_start(
        [pick("rs1", part, fp=front_pieces, w=qkv_weight) for part in rest_q]
    )

    kv_chunks = []
    gain_one = front_small[:, 0].astype(F32)
    inv_one = rms_scale(tokens_in)
    normed = (tokens_in * inv_one * gain_one).astype(BF)
    normed = pick("norm", normed, rs=rest_first, g1=g_q[1], g2=g_q[2], g3=g_q[3])
    queries, kv_own = project(normed, qkv_weight, *tables)
    places = [
        jnp.stack(
            [ctx_rank]
            + [
                lax.rem(q_at - k + nq, nq) * nr + lax.rem(r_at - s + nr, nr)
                for s in range(nr)
            ]
        ).astype(jnp.int32)
        for k in range(nq)
    ]
    rest_pieces = dense_end(*(pick("rs2", v, q=queries, w=qkv_weight) for v in rest_first))
    state = None
    arrived = kv_own
    for k in range(nq):
        chunk = ring_gather(arrived, "r")
        if k < nq - 1:
            coming = shift(arrived, "q")
        if k == 1:
            g_even, g_odd = (
                pick("gs1", jnp.stack(g_q[low::2]), rp=rest_pieces, a1=arrived) for low in (0, 1)
            )
            g_even = jnp.stack(ring_gather(g_even, "b"))
            g_odd = jnp.stack(ring_gather(g_odd, "a"))
        state = attend_chunk(places[k], queries, chunk, state, k == nq - 1, n_ctx)
        kv_chunks.append(chunk)
        if k < nq - 1:
            if k == 0:
                arrived = pick("arr1", coming, s=state[0], g2=g_q[2], g3=g_q[3], rp=rest_pieces)
            if k == 1:
                arrived = pick("arr2", coming, s=state[0], gs=(g_even, g_odd), rp=rest_pieces)
            if k == 2:
                g_even, g_odd = ring_gather(g_even, "a"), ring_gather(g_odd, "b")
                arrived = pick("arr3", coming, s=state[0], gf=(g_even, g_odd))
    mixed, lse = state
    both = pick("wa", both, a3=arrived, c3=chunk[1:], q=queries, m=mixed)
    both = lax.all_to_all(both, "q", split_axis=0, concat_axis=0, tiled=True)
    mixed = pick("mix", mixed, gf=(g_even, g_odd))
    out_weight, shared_in, shared_out, rest_small = dense_place(
        rest_pieces, steps, [width, 2 * FF, flat, 128]
    )
    shared_out = shared_out.reshape(-1, width)
    gain_two = rest_small[:, 0].astype(F32)
    router = rest_small[:, 1 : 1 + n_experts]
    residual = tokens_in + dot(mixed, out_weight)
    inv_two = rms_scale(residual)
    second = (residual * inv_two * gain_two).astype(BF)
    expert = jnp.stack([exp_rank * nq + q_at, q_at, a_at, b_at]).astype(jnp.int32)
    router_t = router.T
    kept = None
    ys = [None, None]
    sum_first, dgates, decs = [], [], []
    c_q = ring_gather(second, "q")
    c_start = jnp.stack(ring_gather(c_q[0], "b"))
    c_planes = [plane_gather(c_q[0], True, c_start)]
    both = pick("wc", both, m=mixed, cs=c_start, c1=c_q[1], cp=c_planes[0])
    both = ring_gather(both, "r")
    kr = np.repeat(np.arange(nr, dtype=np.int32), nq)
    kq = np.tile(np.arange(nq, dtype=np.int32), nr)
    index = kq * nr + lax.rem(r_at - kr + nr, nr)
    w1, w2 = place(
        index.astype(jnp.int32),
        both,
        [((0, gu_rows), 0, 2 * FF), ((gu_rows, folded.shape[1]), 0, 2 * FF)],
    )
    w2 = w2.reshape(-1, width)
    g_even = [jnp.stack(g_even)]
    for k in range(nq):
        if k:
            ready = dict(w=w1) | {f"k{i}": v for i, v in enumerate(dgates)}
            rows = pick(f"c{k}a", c_q[k], **ready)
            first = jnp.stack(ring_gather(rows, "ba"[k % 2]))
            c_planes.append(plane_gather(rows, k % 2 == 0, pick(f"c{k}b", first, **ready)))
        c = c_planes[k]
        ready = {f"s{i}": v for i, v in enumerate(sum_first) if v is not None}
        if k == 3:
            ready["e1"] = dec_one = sum_end(sum_first[1], False)
        hold = pick(f"K{k}", ranks, **ready)
        dec, dgate, kept, ys[k % 2] = expert_chunk(
            k, nq, na, nb, expert, hold, c, (g_even, g_odd)[k % 2], router_t, w1, w2, kept, ys[k % 2], slots
        )
        dgates.append(dgate.reshape(na * nb, tok))
        ready = {f"k{i}": v for i, v in enumerate(dgates)}
        decs.append(dec)
        sum_first.append(None)
        if k:
            sum_first[k] = sum_start([pick(f"d{k}", v, **ready) for v in dec], k % 2 == 0)
    ready = {f"k{i}": v for i, v in enumerate(dgates)}
    sum_first[0] = sum_start([pick("d0", v, **ready) for v in decs[0]], True)
    firsts = sum_first
    dec_sums = [dec_one if k == 1 else sum_end(firsts[k], k % 2 == 0) for k in range(nq)]
    ready = {f"s{i}": v for i, v in enumerate(firsts)}
    xs, hs, deys, degs = kept[:4]
    gate_up_term = dot(pick("gu", xs, **ready), degs, TN).astype(BF)
    down_term = dot(pick("dn", hs, gu=gate_up_term, **ready), deys, TN).astype(BF)
    terms = [
        gate_up_term.reshape(nq, nr, gu_rows, 2 * FF),
        down_term.reshape(nq, nr, -1, 2 * FF),
    ]
    at = [lax.rem(r_at - k + nr, nr) for k in range(nr)]
    expert_rows = ring_sum(
        [
            jnp.concatenate(
                [lax.dynamic_index_in_dim(t, i, 1, keepdims=False) for t in terms], axis=1
            )
            for i in at
        ],
        "r",
    ).astype(BF)
    moving = dec_sums[1].astype(BF)
    for k in range(2, nq):
        term = dec_sums[k]
        term = pick(f"t{k}", term, gu=gate_up_term, dn=down_term, er=expert_rows)
        moving = (shift(moving, "q").astype(F32) + term).astype(BF)
    routed_grad = shift(moving, "q").astype(F32) + dec_sums[0]

    expert_rows = pick("ea", expert_rows, rg=routed_grad, t=moving)
    expert_rows = lax.all_to_all(expert_rows, "q", split_axis=0, concat_axis=0, tiled=True)

    ready = {f"k{i}": v for i, v in enumerate(dgates)}
    later = pick("sh", second, **ready)
    shared_pre = dot(later, shared_in)
    shared_gate, shared_up = shared_pre[:, :FF], shared_pre[:, FF:]
    shared_sig = jax.nn.sigmoid(shared_gate)
    shared_hidden = (shared_gate * shared_sig * shared_up).astype(BF)

    logits = jnp.where(named, dot(later, router), masked_value)
    raised = jnp.where(named, jnp.exp(logits - jnp.max(logits, axis=1, keepdims=True)), 0.0)
    gates = raised / jnp.sum(raised, axis=1, keepdims=True)
    n_all = nq * na * nb
    spot = np.arange(n_all, dtype=np.int32)
    spot = (
        lax.rem(q_at - spot // (na * nb) + nq, nq) * (na * nb)
        + lax.rem(a_at - spot // nb % na + na, na) * nb
        + lax.rem(b_at - spot % nb + nb, nb)
    )
    dgate = jnp.concatenate(dgates, axis=0)[spot]
    dgate = lax.all_to_all(dgate, ("q", "a", "b"), split_axis=0, concat_axis=0, tiled=True)
    dgate = jnp.swapaxes(dgate.reshape(nq, na * nb, tok), 0, 1).reshape(n_experts, tok).T
    grad_logits = gates * (dgate - jnp.sum(gates * dgate, axis=1, keepdims=True))
    grad_logits = grad_logits.astype(BF)

    shared_hidden_grad = dot(grad_low, shared_out, NT)
    shared_pre_grad = jnp.concatenate(
        [
            shared_hidden_grad * shared_up * shared_sig * (1.0 + shared_gate * (1.0 - shared_sig)),
            shared_hidden_grad * shared_gate * shared_sig,
        ],
        axis=1,
    ).astype(BF)
    second_grad = (
        dot(shared_pre_grad, shared_in, NT) + dot(grad_logits, router, NT) + routed_grad
    )
    ffn_gain_grad = jnp.sum(second_grad * residual * inv_two, axis=0)
    residual_grad = out_grad + norm_back(second_grad, residual, inv_two, gain_two)
    mixed_grad = residual_grad.astype(BF)
    heads_grad = dot(mixed_grad, out_weight, NT).astype(BF)

    y_first = [
        sum_start([pick("y1", v, rg=routed_grad, k=dgates[3]) for v in ys[p]], p == 0)
        for p in (0, 1)
    ]
    dq = None
    moving = None
    held = heads_grad
    for step, k in enumerate(list(range(1, nq)) + [0]):
        ready = dict(er=expert_rows, y=y_first, m=moving if step else ())
        held = pick(f"B{step}", held, **ready)
        dq, parts = attend_back_chunk(
            places[k], queries, held, mixed, lse, tables, kv_chunks[k], dq, k == 0, n_ctx
        )
        term = ring_sum(parts, "r")
        if k == 1:
            moving = term.astype(BF)
            first_move = moving
        elif k:
            moving = (shift(moving, "q").astype(F32) + term).astype(BF)
    late = dense_sum_core(
        [
            dot(normed, dq, TN).astype(BF),
            dot(mixed, mixed_grad, TN).astype(BF),
            dot(later, shared_pre_grad, TN).astype(BF),
            dot(shared_hidden, grad_low, TN).astype(BF).reshape(width, flat),
        ],
        own_rows,
    )
    y_sums = [sum_end(pick("y2", y_first[p], q=dq, m=moving, f=first_move), p == 0, 1) for p in (0, 1)]
    late = dense_sum_first(late)
    kv_back = finish_keys(
        shift(moving, "q"), pick("fin", term, late=late, ys=y_sums), *tables
    )

    gate_up_grad = expert_rows[:, :gu_rows].astype(F32)
    down_grad = expert_rows[:, gu_rows:].reshape(nq, -1, width).astype(F32)
    normed_grad = dot(dq, qkv_weight[:, :width], NT)
    normed_grad += dot(kv_back[0], qkv_weight[:, width : 2 * width], NT)
    normed_grad += dot(kv_back[1], qkv_weight[:, 2 * width :], NT)
    attn_gain_grad = jnp.sum(normed_grad * tokens_in * inv_one, axis=0)
    input_grad = residual_grad + norm_back(normed_grad, tokens_in, inv_one, gain_one)
    small_grad = jnp.concatenate(
        [
            attn_gain_grad[:, None],
            ffn_gain_grad[:, None],
            dot(second, grad_logits, TN),
            jnp.zeros((width, 126 - n_experts), F32),
        ],
        axis=1,
    ).astype(BF)
    key_value = dense_sum_core(
        [
            pick("kv1", dot(normed, kv_back[0], TN).astype(BF), late=late, ys=y_sums),
            dot(normed, kv_back[1], TN).astype(BF),
            small_grad,
        ],
        own_rows,
    )
    y_sums = pick("y3", y_sums, b=kv_back, kv=key_value, m=moving)
    y_terms = [y_sums[k % 2][k // 2] for k in range(nq)]
    late = dense_sum_second(*(pick("late2", v, b=kv_back, kv=key_value) for v in late))
    first_kv = dense_sum_first(pick("kv2", key_value, l=late))
    last_kv = dense_sum_second(*first_kv)
    y_moving = y_terms[1].astype(BF)
    for k in range(2, nq + 1):
        y_moving = shift(y_moving, "q")
        y_moving = pick(f"yz{k}", y_moving, kv=key_value, f=first_kv, l=late, z=last_kv)
        routed_sum = y_moving.astype(F32) + y_terms[k % nq]
        y_moving = routed_sum.astype(BF)
    late_grad = dense_sum_last(pick("late3", late, f=first_kv, kv=key_value, z=last_kv))
    kv_weight_grad = dense_sum_last(last_kv)
    layer_out = (residual + dot(shared_hidden, shared_out) + routed_sum).astype(BF)
    at_out, at_shared, at_down = width, 2 * width, 2 * width + 2 * FF
    return (
        layer_out[None],
        input_grad[None],
        kv_weight_grad[:, 2 * width],
        jnp.concatenate([late_grad[:, :at_out], kv_weight_grad[:, : 2 * width]], axis=1),
        late_grad[:, at_out:at_shared],
        kv_weight_grad[:, 2 * width + 1],
        kv_weight_grad[:, 2 * width + 2 : 2 * width + 2 + n_experts],
        late_grad[:, at_shared:at_down],
        late_grad[:, at_down:].reshape(down_rows, width),
        gate_up_grad,
        down_grad,
    )


def solution(mesh):
    n_ctx, n_exp = mesh.shape["ctx"], mesh.shape["exp"]

    def layer(*args):
        n_experts = args[10].shape[0]
        nq = n_experts // n_exp
        nb = 2
        fine = Mesh(
            np.asarray(mesh.devices).reshape(nq, n_ctx // nq, n_exp // nb, nb), ("q", "r", "a", "b")
        )
        ctx, exp, every = ("q", "r"), ("a", "b"), ("q", "r", "a", "b")
        tokens, flat, rows = P(exp, ctx, None), P(every), P(every, None)
        run = jax.shard_map(
            functools.partial(body, n_experts),
            mesh=fine,
            in_specs=(
                tokens, tokens, tokens, flat, rows, rows, flat, rows, rows, rows, tokens, tokens,
            ),
            out_specs=(tokens, tokens, flat, rows, rows, flat, rows, rows, rows, tokens, tokens),
            check_vma=False,
        )
        return run(*args)

    return layer
```

```python
import functools

import jax
import jax.numpy as jnp
import numpy as np
from jax import lax
from jax.experimental import pallas as pl
from jax.experimental.pallas import tpu as pltpu
from jax.sharding import Mesh
from jax.sharding import PartitionSpec as P

HEADS = 10
HEAD_DIM = 128
FF = 896
TOP = 7

norm_eps = 1e-06
rope_base = 10000.0
masked_value = -1e30
LOG2E = 1.4426950408889634

BF = jnp.bfloat16
F32 = jnp.float32
VMEM_LIMIT = 56 * 1024 * 1024


def rope_tables(positions, head_dim):
    halfway = head_dim // 2
    frequency = rope_base ** (-(jnp.arange(halfway).astype(F32) * 2.0 / head_dim))
    angles = positions.astype(F32)[:, None] * frequency[None, :]
    angles = jnp.concatenate([angles, angles], axis=1)
    return (jnp.cos(angles), jnp.sin(angles))


def rms_scale(values):
    return lax.rsqrt(jnp.mean(values * values, axis=1, keepdims=True) + norm_eps)


def norm_back(grad_in, values, inv_rms, gain_vec):
    scaled = grad_in * gain_vec
    return inv_rms * scaled - values * inv_rms**3 * jnp.mean(scaled * values, axis=1, keepdims=True)


def dot(a, b, dims=((1,), (0,))):
    return lax.dot_general(a, b, (dims, ((), ())), preferred_element_type=F32)


NT = ((1,), (1,))
TN = ((0,), (0,))


def shift(value, axis):
    n = lax.axis_size(axis)
    return lax.ppermute(value, axis, [(i, (i + 1) % n) for i in range(n)])


def ring_gather(value, axis):
    parts = [value]
    for _ in range(1, lax.axis_size(axis)):
        parts.append(shift(parts[-1], axis))
    return parts


def shift_by(value, axis, k):
    n = lax.axis_size(axis)
    return lax.ppermute(value, axis, [(i, (i + k) % n) for i in range(n)])


def direct_gather(value, axis):
    return [value] + [shift_by(value, axis, k) for k in range(1, lax.axis_size(axis))]


def ring_sum(blocks, axis, events=()):
    n = len(blocks)
    if n == 1:
        return blocks[0].astype(F32)
    moving = blocks[1].astype(BF)
    for k in range(2, n):
        moving = after(shift(moving, axis), *events)
        moving = (moving.astype(F32) + blocks[k].astype(F32)).astype(BF)
    return after(shift(moving, axis), *events).astype(F32) + blocks[0].astype(F32)


def ring_blocks(arrays, axis, dim):
    n = lax.axis_size(axis)
    index = lax.axis_index(axis)
    out = []
    for k in range(n):
        at = lax.rem(index - k + n, n)
        parts = [lax.dynamic_index_in_dim(v, at, dim, keepdims=False) for v in arrays]
        out.append(parts[0] if len(parts) == 1 else jnp.concatenate(parts, axis=-1))
    return out


ORDER = {
    "rest": "f1",
    "g": "r3",
    "mid1": "r2",
    "core2": "r3",
    "rs1": "fp",
    "gs1": "rp",
    "arr1": "g3 rp",
    "arr2": "gs",
    "arr3": "s gf",
    "wa": "q",
    "mix": "gf",
    "wc": "m",
    "c1b": "w",
    "c2b": "k0",
    "c3a": "w",
    "c3b": "k0",
    "gu": "s1",
    "dn": "s1",
    "t2": "er",
    "sh": "k2",
    "B1": "m",
    "B3": "er",
    "y1": "rg",
    "fin": "late",
    "kv1": "ys",
    "kv2": "l",
    "yz3": "kv",
    "yz4": "f",
    "late3": "kv",
    "cz2": "w",
    "cz3": "cp",
    "xg": "m",
    "dn0": "kv",
}


def pick(name, value, **events):
    chosen = [events[key] for key in ORDER.get(name, "").split() if key in events]
    return after(value, *jax.tree.leaves(chosen))


def after(value, *events):
    if not events:
        return value
    return lax.optimization_barrier((value, *events))[0]


def place_kernel(counts, cuts, index_ref, *refs):
    n = len(counts)
    pieces, outs, sems = refs[:n], refs[n:-1], refs[-1]
    t = 0
    for piece, count in zip(pieces, counts):
        for j in range(count):
            at = index_ref[t]
            t += 1
            for o, (rows, low, high) in enumerate(cuts):
                pltpu.make_async_copy(
                    piece.at[j, pl.ds(*rows), pl.ds(low, high - low)], outs[o].at[at], sems.at[o]
                ).start()
    for o in range(len(cuts)):
        pltpu.make_async_copy(outs[o], outs[o], sems.at[o]).wait()


def place(index, pieces, cuts):
    rows, total = pieces[0].shape[-2:]
    pieces = [piece.reshape(-1, rows, total) for piece in pieces]
    counts = [piece.shape[0] for piece in pieces]
    n = sum(counts)
    outs = pl.pallas_call(
        functools.partial(place_kernel, counts, cuts),
        in_specs=[pl.BlockSpec(memory_space=pltpu.SMEM)]
        + [pl.BlockSpec(memory_space=pl.ANY)] * len(pieces),
        out_specs=[pl.BlockSpec(memory_space=pltpu.VMEM)] * len(cuts),
        scratch_shapes=[pltpu.SemaphoreType.DMA((len(cuts),))],
        out_shape=[
            jax.ShapeDtypeStruct((n, c[0][1], c[2] - c[1]), pieces[0].dtype) for c in cuts
        ],
        compiler_params=pltpu.CompilerParams(vmem_limit_bytes=VMEM_LIMIT // 2),
        cost_estimate=pl.CostEstimate(
            flops=0, bytes_accessed=4 * n * rows * total, transcendentals=0
        ),
        name="place",
    )(index, *pieces)
    return [out.reshape(-1, out.shape[2]) for out in outs]


def dense_steps(nq):
    half, na, nb = nq // 2, lax.axis_size("a"), lax.axis_size("b")
    steps = [[(kq, ka, kb) for kb in range(nb) for kq in range(half)] for ka in range(na)]
    return steps + [
        [(kq, ka, kb) for ka in range(na) for kq in range(half, nq)] for kb in range(nb)
    ]


def dense_start(along_q):
    half = len(along_q) // 2
    one = jnp.stack(ring_gather(jnp.stack(along_q[:half]), "b"))
    two = jnp.stack(ring_gather(jnp.stack(along_q[half:]), "a"))
    return one, two


def dense_end(one, two):
    return ring_gather(one, "a") + ring_gather(two, "b")


def dense_place(pieces, steps, widths, due=()):
    nq, nr, na, nb = (lax.axis_size(axis) for axis in ("q", "r", "a", "b"))
    rows, width = pieces[0].shape[-2:]
    flat = [piece.reshape(-1, rows, width) for piece in pieces]
    groups = [[0, na], [k for k in range(na + nb) if k not in (0, na)]]
    arrays, order = [], []
    for group in groups:
        own = jnp.concatenate([flat[k] for k in group], axis=0)
        if group is groups[1]:
            own = after(own, *due)
        entries = [s for k in group for s in steps[k]]
        for kr, part in enumerate(ring_gather(own, "r")):
            arrays.append(part)
            order += [(kr, *s) for s in entries]
    kr, kq, ka, kb = (np.array(column, np.int32) for column in zip(*order))
    index = lax.rem(lax.axis_index("q") - kq + nq, nq) * nr
    index = index + lax.rem(lax.axis_index("r") - kr + nr, nr)
    index = index * na + lax.rem(lax.axis_index("a") - ka + na, na)
    index = index * nb + lax.rem(lax.axis_index("b") - kb + nb, nb)
    edges = np.cumsum([0] + list(widths))
    cuts = [((0, rows), int(low), int(high)) for low, high in zip(edges[:-1], edges[1:])]
    return place(index.astype(jnp.int32), arrays, cuts)


def dense_sum_core(wholes, n_rows):
    nq, nr, na, nb = (lax.axis_size(axis) for axis in ("q", "r", "a", "b"))
    values = [whole.reshape(nq, nr, na, nb, n_rows, whole.shape[1]) for whole in wholes]
    return ring_sum(ring_blocks(values, "r", 1), "r").astype(BF)


def dense_sum_first(value):
    half = value.shape[0] // 2
    one = ring_sum(ring_blocks([value[:half]], "a", 1), "a").astype(BF)
    two = ring_sum(ring_blocks([value[half:]], "b", 2), "b").astype(BF)
    return one, two


def dense_sum_second(one, two):
    one = ring_sum(ring_blocks([one], "b", 1), "b")
    two = ring_sum(ring_blocks([two], "a", 1), "a")
    return jnp.concatenate([one, two], axis=0).astype(BF)


def dense_sum_last(value):
    return ring_sum(ring_blocks([value], "q", 0), "q")


def plane_gather(rows, even, first=None):
    inner, outer = ("b", "a") if even else ("a", "b")
    if first is None:
        first = jnp.stack(ring_gather(rows, inner))
    parts = ring_gather(first, outer)
    return [jnp.stack(parts)] if even else parts


def sum_start(parts, even, events=()):
    return ring_sum(parts, "a" if even else "b", events)


def sum_end(first, even, dim=0, events=()):
    n = first.shape[dim]
    parts = [lax.index_in_dim(first, k, dim, False) for k in range(n)]
    return ring_sum(parts, "b" if even else "a", events)


def project_kernel(n_query, x_ref, w_ref, cos_ref, sin_ref, q_ref, kv_ref):
    j = pl.program_id(0)
    made = dot(x_ref[...], w_ref[...])

    def turned():
        parts = []
        for low in range(0, made.shape[1], HEAD_DIM):
            u = made[:, low : low + HEAD_DIM]
            parts.append(u * cos_ref[...] + pltpu.roll(u, HEAD_DIM // 2, 1) * sin_ref[...])
        return jnp.concatenate(parts, axis=1).astype(BF)

    @pl.when(j < n_query)
    def _():
        q_ref[...] = turned()

    @pl.when((j >= n_query) & (j < 2 * n_query))
    def _():
        kv_ref[0] = turned()

    @pl.when(j >= 2 * n_query)
    def _():
        kv_ref[0] = made.astype(BF)


def project(normed, weight, cosines, signed_sine):
    tok, width = normed.shape
    block = 2 * HEAD_DIM
    n = width // block
    table = pl.BlockSpec((tok, HEAD_DIM), lambda j: (0, 0))
    return pl.pallas_call(
        functools.partial(project_kernel, n),
        grid=(3 * n,),
        in_specs=[
            pl.BlockSpec((tok, width), lambda j: (0, 0)),
            pl.BlockSpec((width, block), lambda j: (0, j)),
            table,
            table,
        ],
        out_specs=[
            pl.BlockSpec((tok, block), lambda j: (0, jnp.minimum(j, n - 1))),
            pl.BlockSpec(
                (1, tok, block),
                lambda j: (jnp.maximum(j - n, 0) // n, 0, jnp.maximum(j - n, 0) % n),
            ),
        ],
        out_shape=[
            jax.ShapeDtypeStruct((tok, width), BF),
            jax.ShapeDtypeStruct((2, tok, width), BF),
        ],
        compiler_params=pltpu.CompilerParams(vmem_limit_bytes=VMEM_LIMIT // 2),
        cost_estimate=pl.CostEstimate(
            flops=6 * tok * width * width, bytes_accessed=6 * width * width, transcendentals=0
        ),
        name="project",
    )(normed, weight, cosines, signed_sine)


def turn_back(grad, cos, signed_sine):
    return grad * cos - pltpu.roll(grad, HEAD_DIM // 2, 1) * signed_sine


def finish_kernel(moved_ref, own_ref, cos_ref, sin_ref, out_ref):
    keys = moved_ref[0].astype(F32) + own_ref[0]
    out_ref[0] = turn_back(keys, cos_ref[...], sin_ref[...]).astype(BF)
    out_ref[1] = (moved_ref[1].astype(F32) + own_ref[1]).astype(BF)


def finish_keys(moved, own, cosines, signed_sine):
    _, tok, width = own.shape
    pair = pl.BlockSpec((2, tok, HEAD_DIM), lambda h: (0, 0, h))
    table = pl.BlockSpec((tok, HEAD_DIM), lambda h: (0, 0))
    return pl.pallas_call(
        finish_kernel,
        grid=(width // HEAD_DIM,),
        in_specs=[pair, pair, table, table],
        out_specs=pair,
        out_shape=jax.ShapeDtypeStruct((2, tok, width), BF),
        cost_estimate=pl.CostEstimate(
            flops=10 * tok * width, bytes_accessed=16 * tok * width, transcendentals=0
        ),
        name="finish_keys",
    )(moved, own, cosines, signed_sine)


def allowed_mask(own, other, n_ctx, half):
    row = lax.broadcasted_iota(jnp.int32, (2 * half, 2 * half), 0)
    col = lax.broadcasted_iota(jnp.int32, (2 * half, 2 * half), 1)
    last = 2 * n_ctx - 1
    query = row + jnp.where(row < half, own * half, (last - own) * half - half)
    key = col + jnp.where(col < half, other * half, (last - other) * half - half)
    return key <= query


def attend_kernel(n_ctx, n_src, first, last, place_ref, q_ref, *refs):
    kv_refs, refs = refs[:n_src], refs[n_src:]
    if not first:
        acc_in, ml_in = refs[:2]
        refs = refs[2:]
    out_ref, ml_ref = refs
    queries = q_ref[...]
    tok = queries.shape[0]
    scores = []
    for s in range(n_src):
        raw = dot(queries, kv_refs[s][0], NT) * (HEAD_DIM ** (-0.5) * LOG2E)
        mask = allowed_mask(place_ref[0], place_ref[1 + s], n_ctx, tok // 2)
        scores.append(jnp.where(mask, raw, masked_value))
    peak = functools.reduce(jnp.maximum, [jnp.max(s, axis=1, keepdims=True) for s in scores])
    if not first:
        old_peak = ml_in[0][:, 0:1]
        old_sum = ml_in[0][:, 64:65]
        peak = jnp.maximum(peak, old_peak)
    total = jnp.zeros_like(peak)
    mixed = jnp.zeros((tok, HEAD_DIM), F32)
    for s in range(n_src):
        raised = jnp.exp2(scores[s] - peak)
        total = total + jnp.sum(raised, axis=1, keepdims=True)
        mixed = mixed + dot(raised.astype(BF), kv_refs[s][1])
    if not first:
        decay = jnp.exp2(old_peak - peak)
        total = total + old_sum * decay
        mixed = mixed + acc_in[...] * decay
    if last:
        out_ref[...] = (mixed / total).astype(BF)
        ml_ref[0] = jnp.broadcast_to(peak + jnp.log2(total), (tok, 128))
    else:
        out_ref[...] = mixed
        lane = lax.broadcasted_iota(jnp.int32, (tok, 128), 1)
        ml_ref[0] = jnp.where(lane < 64, peak, total)


def attend_chunk(places, queries, kv_list, state, last, n_ctx):
    tok, width = queries.shape
    head = pl.BlockSpec((tok, HEAD_DIM), lambda h, p: (0, h))
    pair = pl.BlockSpec((2, tok, HEAD_DIM), lambda h, p: (0, 0, h))
    rows = pl.BlockSpec((1, tok, 128), lambda h, p: (h, 0, 0))
    first = state is None
    n = len(kv_list)
    pairs = tok * tok * n * HEADS
    return pl.pallas_call(
        functools.partial(attend_kernel, n_ctx, n, first, last),
        grid_spec=pltpu.PrefetchScalarGridSpec(
            num_scalar_prefetch=1,
            grid=(HEADS,),
            in_specs=[head] + [pair] * n + ([] if first else [head, rows]),
            out_specs=[head, rows],
        ),
        out_shape=[
            jax.ShapeDtypeStruct((tok, width), BF if last else F32),
            jax.ShapeDtypeStruct((HEADS, tok, 128), F32),
        ],
        compiler_params=pltpu.CompilerParams(vmem_limit_bytes=VMEM_LIMIT // 2),
        cost_estimate=pl.CostEstimate(
            flops=4 * pairs * HEAD_DIM * 4, bytes_accessed=8 * tok * width, transcendentals=pairs
        ),
        name="attend",
    )(places, queries, *kv_list, *(() if first else state))


def attend_back_kernel(
    n_ctx, n_src, first, last, place_ref, q_ref, do_ref, o_ref, lse_ref, cos_ref, sin_ref, *refs
):
    kv_refs, refs = refs[:n_src], refs[n_src:]
    if not first:
        dq_in, refs = refs[0], refs[1:]
    dq_ref, dkv_refs = refs[0], refs[1:]
    queries = q_ref[...]
    grad = do_ref[...]
    tok = queries.shape[0]
    lse = lse_ref[0][:, 0:1]
    delta = jnp.sum(grad.astype(F32) * o_ref[...].astype(F32), axis=1, keepdims=True)
    scale = HEAD_DIM ** (-0.5)
    grad_query = jnp.zeros((tok, HEAD_DIM), F32)
    for s in range(n_src):
        keys, values = kv_refs[s][0], kv_refs[s][1]
        raw = dot(queries, keys, NT) * (scale * LOG2E)
        mask = allowed_mask(place_ref[0], place_ref[1 + s], n_ctx, tok // 2)
        probs = jnp.exp2(jnp.where(mask, raw, masked_value) - lse)
        grad_probs = dot(grad, values, NT)
        grad_scores = (probs * (grad_probs - delta)).astype(BF)
        grad_query = grad_query + dot(grad_scores, keys)
        dkv_refs[s][0] = (dot(grad_scores, queries, TN) * scale).astype(dkv_refs[s].dtype)
        dkv_refs[s][1] = dot(probs.astype(BF), grad, TN).astype(dkv_refs[s].dtype)
    grad_query = grad_query * scale
    if not first:
        grad_query = grad_query + dq_in[...]
    if last:
        grad_query = turn_back(grad_query, cos_ref[...], sin_ref[...]).astype(BF)
    dq_ref[...] = grad_query


def attend_back_chunk(places, queries, grad, mixed, lse, tables, kv_list, dq, last, n_ctx):
    tok, width = queries.shape
    head = pl.BlockSpec((tok, HEAD_DIM), lambda h, p: (0, h))
    pair = pl.BlockSpec((2, tok, HEAD_DIM), lambda h, p: (0, 0, h))
    rows = pl.BlockSpec((1, tok, 128), lambda h, p: (h, 0, 0))
    table = pl.BlockSpec((tok, HEAD_DIM), lambda h, p: (0, 0))
    first = dq is None
    n = len(kv_list)
    pairs = tok * tok * n * HEADS
    out = pl.pallas_call(
        functools.partial(attend_back_kernel, n_ctx, n, first, last),
        grid_spec=pltpu.PrefetchScalarGridSpec(
            num_scalar_prefetch=1,
            grid=(HEADS,),
            in_specs=[head, head, head, rows, table, table] + [pair] * n + ([] if first else [head]),
            out_specs=[head] + [pair] * n,
        ),
        out_shape=[jax.ShapeDtypeStruct((tok, width), BF if last else F32)]
        + [jax.ShapeDtypeStruct((2, tok, width), F32 if s == 0 else BF) for s in range(n)],
        compiler_params=pltpu.CompilerParams(vmem_limit_bytes=VMEM_LIMIT // 2),
        cost_estimate=pl.CostEstimate(
            flops=10 * pairs * HEAD_DIM * 4, bytes_accessed=16 * tok * width, transcendentals=pairs
        ),
        name="attend_back",
    )(places, queries, grad, mixed, lse, *tables, *kv_list, *(() if first else (dq,)))
    return out[0], out[1:]


def expert_kernel(slots, na, nb, even, n_kept, e_ref, rank_ref, *refs):
    n_in, n_sum = (1, na) if even else (nb, nb)
    c_refs, g_refs, refs = refs[:n_in], refs[n_in : 2 * n_in], refs[2 * n_in :]
    wr_ref, w1_ref, w2_ref = refs[:3]
    refs = refs[3 + n_kept :]
    d_refs, dg_ref, refs = refs[:n_sum], refs[n_sum], refs[n_sum + 1 :]
    x_ref, h_ref, dey_ref, deg_ref = refs[:4]
    y_refs = refs[4:]
    tok = g_refs[0].shape[-2]
    experts = wr_ref.shape[0]
    me = e_ref[0]
    step = pl.program_id(0)
    picks, rows, grads, weights = [], [], [], []
    own = lax.broadcasted_iota(jnp.int32, (experts, tok), 0) == me
    slot = lax.broadcasted_iota(jnp.int32, (slots, tok), 0).astype(F32)
    for s in range(nb):
        tokens = c_refs[0][0, s] if even else c_refs[s][0]
        cot = g_refs[0][0, s, 0] if even else g_refs[s][0, 0]
        rank = rank_ref[0, s, 0]
        logits = dot(wr_ref[...], tokens, NT)
        logits = jnp.where(rank >= 0, logits, masked_value)
        raised = jnp.where(rank >= 0, jnp.exp(logits - jnp.max(logits, axis=0, keepdims=True)), 0.0)
        gates = raised / jnp.sum(raised, axis=0, keepdims=True)
        gate_row = jnp.sum(jnp.where(own, gates, 0.0), axis=0, keepdims=True)
        rank_row = jnp.sum(jnp.where(own, rank, 0.0), axis=0, keepdims=True)
        pick = jnp.where(slot == rank_row, 1.0, 0.0)
        weights.append(jnp.sum(pick * gate_row, axis=1, keepdims=True))
        pick_low = pick.astype(BF)
        picks.append((pick, pick_low))
        rows.append(dot(pick_low, tokens).astype(BF))
        grads.append(dot(pick_low, cot))
    x = jnp.concatenate(rows, axis=0)
    grad = jnp.concatenate(grads, axis=0)
    weight = jnp.concatenate(weights, axis=0)
    x_ref[...] = x
    dey = (weight * grad).astype(BF)
    dey_ref[...] = dey
    pre = dot(x, w1_ref[...])
    gate, up = pre[:, :FF], pre[:, FF:]
    sig = jax.nn.sigmoid(gate)
    act = gate * sig
    hidden = (act * up).astype(BF)
    h_ref[...] = hidden
    grad_hidden = dot(dey, w2_ref[...], NT)
    deg = jnp.concatenate(
        [
            (grad_hidden * up * sig * (1.0 + gate * (1.0 - sig))).astype(BF),
            (grad_hidden * act).astype(BF),
        ],
        axis=1,
    )
    deg_ref[...] = deg
    dec = dot(deg, w1_ref[...], NT).astype(BF)
    ey = dot(hidden, w2_ref[...]).astype(BF).astype(F32)
    dgate = jnp.sum(grad * ey, axis=1, keepdims=True)
    weighted = (weight * ey).astype(BF)
    d_all, y_all = [], []
    for s in range(nb):
        part = slice(s * slots, (s + 1) * slots)
        pick, pick_low = picks[s]
        d_all.append(dot(pick_low, dec[part], TN).astype(BF))
        y_all.append(dot(pick_low, weighted[part], TN).astype(BF))
        if not even:
            d_refs[s][0] = d_all[s]
            y_refs[s][0, 0] = y_all[s]
        dg_ref[0, s] = jnp.sum(pick * dgate[part], axis=0, keepdims=True)
    if even:
        for k in range(na):

            @pl.when(step == k)
            def _(k=k):
                for s in range(nb):
                    d_refs[k][s] = d_all[s]
                    y_refs[k][0, s] = y_all[s]


def expert_chunk(chunk, nq, na, nb, expert, ranks, c, g, router_t, w1, w2, kept, y_kept, slots):
    even = chunk % 2 == 0
    tok, width = c[0].shape[-2:]
    experts = router_t.shape[0]
    g_one = pl.BlockSpec((1, nb, 1, tok, width), lambda i, e: (i, 0, chunk // 2, 0, 0))
    g_two = pl.BlockSpec((1, 1, tok, width), lambda i, e: (i, chunk // 2, 0, 0))
    one = pl.BlockSpec((1, nb, tok, width), lambda i, e: (i, 0, 0, 0))
    two = pl.BlockSpec((1, tok, width), lambda i, e: (i, 0, 0))

    def fixed(shape):
        return pl.BlockSpec(shape, lambda i, e: (0,) * len(shape), pipeline_mode=pl.Buffered(1))

    def by_rows(n):
        return pl.BlockSpec((nb * slots, n), lambda i, e: (chunk * na + i, 0))

    n_rows = na * nb * slots
    n_half = nq // 2
    if even:
        d_specs = [pl.BlockSpec((nb, tok, width), lambda i, e: (0, 0, 0))] * na
        y_specs = [pl.BlockSpec((1, nb, tok, width), lambda i, e: (chunk // 2, 0, 0, 0))] * na
        d_shapes = [jax.ShapeDtypeStruct((nb, tok, width), BF)] * na
        y_shapes = [jax.ShapeDtypeStruct((n_half, nb, tok, width), BF)] * na
    else:
        d_specs = [two] * nb
        y_specs = [pl.BlockSpec((1, 1, tok, width), lambda i, e: (chunk // 2, i, 0, 0))] * nb
        d_shapes = [jax.ShapeDtypeStruct((na, tok, width), BF)] * nb
        y_shapes = [jax.ShapeDtypeStruct((n_half, na, tok, width), BF)] * nb
    held = [*(kept or ()), *(y_kept or ())]
    n_in = 1 + 1 + len(c) + len(g) + 3
    n_out = len(d_shapes) + 1
    aliases = {n_in + k: n_out + k for k in range(len(kept or ()))}
    for k in range(len(y_kept or ())):
        aliases[n_in + len(kept or ()) + k] = n_out + 4 + k
    out = pl.pallas_call(
        functools.partial(expert_kernel, slots, na, nb, even, len(held)),
        grid_spec=pltpu.PrefetchScalarGridSpec(
            num_scalar_prefetch=1,
            grid=(na,),
            in_specs=[
                pl.BlockSpec((1, nb, 1, experts, tok), lambda i, e: (i, 0, chunk, 0, 0)),
                *([one, g_one] if even else [two] * nb + [g_two] * nb),
                fixed(router_t.shape), fixed(w1.shape), fixed(w2.shape),
                *[pl.BlockSpec(memory_space=pl.ANY)] * len(held),
            ],
            out_specs=[
                *d_specs,
                pl.BlockSpec((1, nb, 1, tok), lambda i, e: (i, 0, 0, 0)),
                by_rows(width), by_rows(FF), by_rows(width), by_rows(2 * FF),
                *y_specs,
            ],
        ),
        out_shape=[
            *d_shapes,
            jax.ShapeDtypeStruct((na, nb, 1, tok), F32),
            *[jax.ShapeDtypeStruct((nq * n_rows, n), BF) for n in (width, FF, width, 2 * FF)],
            *y_shapes,
        ],
        input_output_aliases=aliases,
        compiler_params=pltpu.CompilerParams(vmem_limit_bytes=VMEM_LIMIT),
        cost_estimate=pl.CostEstimate(
            flops=n_rows * width * FF * 12, bytes_accessed=30_000_000, transcendentals=n_rows * FF
        ),
        name="experts",
    )(expert, ranks, *c, *g, router_t, w1, w2, *held)
    n_d = len(d_shapes)
    return out[:n_d], out[n_d], out[n_out : n_out + 4], out[n_out + 4 :]


def body(
    n_experts,
    block_input,
    cotangent,
    routes,
    attn_gain,
    query_key_value_weight,
    attention_output_weight,
    ffn_gain,
    routing_weight,
    common_expert_gate_up_weight,
    common_expert_down_weight,
    expert_gate_up,
    expert_down,
):
    nq, nr, na, nb = (lax.axis_size(axis) for axis in ("q", "r", "a", "b"))
    q_at, r_at, a_at, b_at = (lax.axis_index(axis) for axis in ("q", "r", "a", "b"))
    n_ctx = nq * nr
    n_exp = na * nb
    ctx_rank = q_at * nr + r_at
    exp_rank = a_at * nb + b_at
    tok = block_input.shape[1]
    width = block_input.shape[2]
    half = tok // 2
    capacity = min(tok, 3 * TOP * tok // (2 * n_experts))
    slots = -(-capacity // 16) * 16
    row = jnp.arange(tok, dtype=jnp.int32)
    local_pos = jnp.where(
        row < half, ctx_rank * half + row, (2 * n_ctx - 1 - ctx_rank) * half + row - half
    )
    cosines, sines = rope_tables(local_pos, HEAD_DIM)
    sines = jnp.where(jnp.arange(HEAD_DIM)[None, :] < HEAD_DIM // 2, -sines, sines)
    tables = (cosines, sines)
    tokens_in = block_input[0].astype(F32)
    grad_low = cotangent[0]
    out_grad = grad_low.astype(F32)
    own_rows = query_key_value_weight.shape[0]
    down_rows = common_expert_down_weight.shape[0]

    named = jnp.any(
        routes[0][:, :, None] == jnp.arange(n_experts, dtype=jnp.int32)[None, None, :], axis=1
    )
    before = (row[:, None] < row[None, :]).astype(BF)
    rank = dot(named.astype(BF).T, before)
    rank = jnp.where(named.T, rank, -1.0)
    ranks = jnp.stack(direct_gather(rank, "q"))
    ranks = jnp.stack(ring_gather(ranks, "b"))
    ranks = jnp.stack(ring_gather(ranks, "a"))

    zeros = jnp.zeros((own_rows, 127), BF)
    front = jnp.concatenate([query_key_value_weight, attn_gain[:, None], zeros], axis=1)
    front_q = ring_gather(front, "q")
    rest = jnp.concatenate(
        [
            attention_output_weight,
            common_expert_gate_up_weight,
            common_expert_down_weight.reshape(own_rows, -1),
            ffn_gain[:, None],
            routing_weight,
            zeros[:, n_experts:],
        ],
        axis=1,
    )
    flat = common_expert_down_weight.size // own_rows
    front_q[-1] = after(front_q[-1], ranks)
    steps = dense_steps(nq)
    front_first = dense_start(front_q)

    gu_rows = expert_gate_up.shape[1]
    folded = expert_down.reshape(nq, -1, 2 * FF)
    both = jnp.concatenate([expert_gate_up, folded], axis=1)

    rest_q = ring_gather(pick("rest", rest, f1=front_q[1], f3=front_q[-1]), "q")
    g_q = [pick("g", grad_low, r1=rest_q[1], r3=rest_q[-1], f3=front_q[-1])]
    g_q.append(shift(g_q[0], "q"))
    front_first = [
        pick(f"mid{i}", v, r1=rest_q[1], r2=rest_q[2]) for i, v in enumerate(front_first)
    ]
    front_pieces = dense_end(*front_first)
    due = [pick("core2", front_pieces[0], r1=rest_q[1], r2=rest_q[2], r3=rest_q[3], g1=g_q[1])]
    qkv_weight, front_small = dense_place(front_pieces, steps, [3 * width, 128], due)
    for _ in range(nq - 2):
        g_q.append(shift(g_q[-1], "q"))
    rest_first = dense_start(
        [pick("rs1", part, fp=front_pieces, w=qkv_weight) for part in rest_q]
    )

    kv_chunks = []
    gain_one = front_small[:, 0].astype(F32)
    inv_one = rms_scale(tokens_in)
    normed = (tokens_in * inv_one * gain_one).astype(BF)
    normed = pick("norm", normed, rs=rest_first, g1=g_q[1], g2=g_q[2], g3=g_q[3])
    queries, kv_own = project(normed, qkv_weight, *tables)
    places = [
        jnp.stack(
            [ctx_rank]
            + [
                lax.rem(q_at - k + nq, nq) * nr + lax.rem(r_at - s + nr, nr)
                for s in range(nr)
            ]
        ).astype(jnp.int32)
        for k in range(nq)
    ]
    rest_pieces = dense_end(*(pick("rs2", v, q=queries, w=qkv_weight) for v in rest_first))
    state = None
    arrived = kv_own
    for k in range(nq):
        chunk = ring_gather(arrived, "r")
        if k < nq - 1:
            coming = shift(arrived, "q")
        if k == 1:
            g_even, g_odd = (
                pick("gs1", jnp.stack(g_q[low::2]), rp=rest_pieces, a1=arrived) for low in (0, 1)
            )
            g_even = jnp.stack(ring_gather(g_even, "b"))
            g_odd = jnp.stack(ring_gather(g_odd, "a"))
        state = attend_chunk(places[k], queries, chunk, state, k == nq - 1, n_ctx)
        kv_chunks.append(chunk)
        if k < nq - 1:
            if k == 0:
                arrived = pick("arr1", coming, s=state[0], g2=g_q[2], g3=g_q[3], rp=rest_pieces)
            if k == 1:
                arrived = pick("arr2", coming, s=state[0], gs=(g_even, g_odd), rp=rest_pieces)
            if k == 2:
                g_even, g_odd = ring_gather(g_even, "a"), ring_gather(g_odd, "b")
                arrived = pick("arr3", coming, s=state[0], gf=(g_even, g_odd))
    mixed, lse = state
    both = pick("wa", both, a3=arrived, c3=chunk[1:], q=queries, m=mixed)
    both = lax.all_to_all(both, "q", split_axis=0, concat_axis=0, tiled=True)
    mixed = pick("mix", mixed, gf=(g_even, g_odd))
    out_weight, shared_in, shared_out, rest_small = dense_place(
        rest_pieces, steps, [width, 2 * FF, flat, 128]
    )
    shared_out = shared_out.reshape(-1, width)
    gain_two = rest_small[:, 0].astype(F32)
    router = rest_small[:, 1 : 1 + n_experts]
    residual = tokens_in + dot(mixed, out_weight)
    inv_two = rms_scale(residual)
    second = (residual * inv_two * gain_two).astype(BF)
    expert = jnp.stack([exp_rank * nq + q_at, q_at, a_at, b_at]).astype(jnp.int32)
    router_t = router.T
    kept = None
    ys = [None, None]
    sum_first, dgates, decs = [], [], []
    c_q = ring_gather(second, "q")
    c_start = jnp.stack(ring_gather(c_q[0], "b"))
    c_planes = [plane_gather(c_q[0], True, c_start)]
    both = pick("wc", both, m=mixed, cs=c_start, c1=c_q[1], cp=c_planes[0])
    both = ring_gather(both, "r")
    kr = np.repeat(np.arange(nr, dtype=np.int32), nq)
    kq = np.tile(np.arange(nq, dtype=np.int32), nr)
    index = kq * nr + lax.rem(r_at - kr + nr, nr)
    w1, w2 = place(
        index.astype(jnp.int32),
        both,
        [((0, gu_rows), 0, 2 * FF), ((gu_rows, folded.shape[1]), 0, 2 * FF)],
    )
    w2 = w2.reshape(-1, width)
    g_even = [jnp.stack(g_even)]
    for k in range(nq):
        if k:
            ready = dict(w=w1) | {f"k{i}": v for i, v in enumerate(dgates)}
            rows = pick(f"c{k}a", c_q[k], **ready)
            first = jnp.stack(ring_gather(rows, "ba"[k % 2]))
            c_planes.append(plane_gather(rows, k % 2 == 0, pick(f"c{k}b", first, **ready)))
        c = c_planes[k]
        ready = {f"s{i}": v for i, v in enumerate(sum_first) if v is not None}
        if k == 3:
            ready["e1"] = dec_one = sum_end(sum_first[1], False)
        hold = pick(f"K{k}", ranks, **ready)
        dec, dgate, kept, ys[k % 2] = expert_chunk(
            k, nq, na, nb, expert, hold, c, (g_even, g_odd)[k % 2], router_t, w1, w2, kept, ys[k % 2], slots
        )
        dgates.append(dgate.reshape(na * nb, tok))
        ready = {f"k{i}": v for i, v in enumerate(dgates)}
        decs.append(dec)
        sum_first.append(None)
        if k:
            sum_first[k] = sum_start([pick(f"d{k}", v, **ready) for v in dec], k % 2 == 0)
    ready = {f"k{i}": v for i, v in enumerate(dgates)}
    sum_first[0] = sum_start([pick("d0", v, **ready) for v in decs[0]], True)
    firsts = sum_first
    dec_sums = [dec_one if k == 1 else sum_end(firsts[k], k % 2 == 0) for k in range(nq)]
    ready = {f"s{i}": v for i, v in enumerate(firsts)}
    xs, hs, deys, degs = kept[:4]
    gate_up_term = dot(pick("gu", xs, **ready), degs, TN).astype(BF)
    down_term = dot(pick("dn", hs, gu=gate_up_term, **ready), deys, TN).astype(BF)
    terms = [
        gate_up_term.reshape(nq, nr, gu_rows, 2 * FF),
        down_term.reshape(nq, nr, -1, 2 * FF),
    ]
    at = [lax.rem(r_at - k + nr, nr) for k in range(nr)]
    expert_rows = ring_sum(
        [
            jnp.concatenate(
                [lax.dynamic_index_in_dim(t, i, 1, keepdims=False) for t in terms], axis=1
            )
            for i in at
        ],
        "r",
    ).astype(BF)
    moving = dec_sums[1].astype(BF)
    for k in range(2, nq):
        term = dec_sums[k]
        term = pick(f"t{k}", term, gu=gate_up_term, dn=down_term, er=expert_rows)
        moving = (shift(moving, "q").astype(F32) + term).astype(BF)
    routed_grad = shift(moving, "q").astype(F32) + dec_sums[0]

    expert_rows = pick("ea", expert_rows, rg=routed_grad, t=moving)
    expert_rows = lax.all_to_all(expert_rows, "q", split_axis=0, concat_axis=0, tiled=True)

    ready = {f"k{i}": v for i, v in enumerate(dgates)}
    later = pick("sh", second, **ready)
    shared_pre = dot(later, shared_in)
    shared_gate, shared_up = shared_pre[:, :FF], shared_pre[:, FF:]
    shared_sig = jax.nn.sigmoid(shared_gate)
    shared_hidden = (shared_gate * shared_sig * shared_up).astype(BF)

    logits = jnp.where(named, dot(later, router), masked_value)
    raised = jnp.where(named, jnp.exp(logits - jnp.max(logits, axis=1, keepdims=True)), 0.0)
    gates = raised / jnp.sum(raised, axis=1, keepdims=True)
    n_all = nq * na * nb
    spot = np.arange(n_all, dtype=np.int32)
    spot = (
        lax.rem(q_at - spot // (na * nb) + nq, nq) * (na * nb)
        + lax.rem(a_at - spot // nb % na + na, na) * nb
        + lax.rem(b_at - spot % nb + nb, nb)
    )
    dgate = jnp.concatenate(dgates, axis=0)[spot]
    dgate = lax.all_to_all(dgate, ("q", "a", "b"), split_axis=0, concat_axis=0, tiled=True)
    dgate = jnp.swapaxes(dgate.reshape(nq, na * nb, tok), 0, 1).reshape(n_experts, tok).T
    grad_logits = gates * (dgate - jnp.sum(gates * dgate, axis=1, keepdims=True))
    grad_logits = grad_logits.astype(BF)

    shared_hidden_grad = dot(grad_low, shared_out, NT)
    shared_pre_grad = jnp.concatenate(
        [
            shared_hidden_grad * shared_up * shared_sig * (1.0 + shared_gate * (1.0 - shared_sig)),
            shared_hidden_grad * shared_gate * shared_sig,
        ],
        axis=1,
    ).astype(BF)
    second_grad = (
        dot(shared_pre_grad, shared_in, NT) + dot(grad_logits, router, NT) + routed_grad
    )
    ffn_gain_grad = jnp.sum(second_grad * residual * inv_two, axis=0)
    residual_grad = out_grad + norm_back(second_grad, residual, inv_two, gain_two)
    mixed_grad = residual_grad.astype(BF)
    heads_grad = dot(mixed_grad, out_weight, NT).astype(BF)

    y_first = [
        sum_start([pick("y1", v, rg=routed_grad, k=dgates[3]) for v in ys[p]], p == 0)
        for p in (0, 1)
    ]
    dq = None
    moving = None
    held = heads_grad
    for step, k in enumerate(list(range(1, nq)) + [0]):
        ready = dict(er=expert_rows, y=y_first, m=moving if step else ())
        held = pick(f"B{step}", held, **ready)
        dq, parts = attend_back_chunk(
            places[k], queries, held, mixed, lse, tables, kv_chunks[k], dq, k == 0, n_ctx
        )
        term = ring_sum(parts, "r")
        if k == 1:
            moving = term.astype(BF)
            first_move = moving
        elif k:
            moving = (shift(moving, "q").astype(F32) + term).astype(BF)
    late = dense_sum_core(
        [
            dot(normed, dq, TN).astype(BF),
            dot(mixed, mixed_grad, TN).astype(BF),
            dot(later, shared_pre_grad, TN).astype(BF),
            dot(shared_hidden, grad_low, TN).astype(BF).reshape(width, flat),
        ],
        own_rows,
    )
    y_sums = [sum_end(pick("y2", y_first[p], q=dq, m=moving, f=first_move), p == 0, 1) for p in (0, 1)]
    late = dense_sum_first(late)
    kv_back = finish_keys(
        shift(moving, "q"), pick("fin", term, late=late, ys=y_sums), *tables
    )

    gate_up_grad = expert_rows[:, :gu_rows].astype(F32)
    down_grad = expert_rows[:, gu_rows:].reshape(nq, -1, width).astype(F32)
    normed_grad = dot(dq, qkv_weight[:, :width], NT)
    normed_grad += dot(kv_back[0], qkv_weight[:, width : 2 * width], NT)
    normed_grad += dot(kv_back[1], qkv_weight[:, 2 * width :], NT)
    attn_gain_grad = jnp.sum(normed_grad * tokens_in * inv_one, axis=0)
    input_grad = residual_grad + norm_back(normed_grad, tokens_in, inv_one, gain_one)
    small_grad = jnp.concatenate(
        [
            attn_gain_grad[:, None],
            ffn_gain_grad[:, None],
            dot(second, grad_logits, TN),
            jnp.zeros((width, 126 - n_experts), F32),
        ],
        axis=1,
    ).astype(BF)
    key_value = dense_sum_core(
        [
            pick("kv1", dot(normed, kv_back[0], TN).astype(BF), late=late, ys=y_sums),
            dot(normed, kv_back[1], TN).astype(BF),
            small_grad,
        ],
        own_rows,
    )
    y_sums = pick("y3", y_sums, b=kv_back, kv=key_value, m=moving)
    y_terms = [y_sums[k % 2][k // 2] for k in range(nq)]
    late = dense_sum_second(*(pick("late2", v, b=kv_back, kv=key_value) for v in late))
    first_kv = dense_sum_first(pick("kv2", key_value, l=late))
    last_kv = dense_sum_second(*first_kv)
    y_moving = y_terms[1].astype(BF)
    for k in range(2, nq + 1):
        y_moving = shift(y_moving, "q")
        y_moving = pick(f"yz{k}", y_moving, kv=key_value, f=first_kv, l=late, z=last_kv)
        routed_sum = y_moving.astype(F32) + y_terms[k % nq]
        y_moving = routed_sum.astype(BF)
    late_grad = dense_sum_last(pick("late3", late, f=first_kv, kv=key_value, z=last_kv))
    kv_weight_grad = dense_sum_last(last_kv)
    layer_out = (residual + dot(shared_hidden, shared_out) + routed_sum).astype(BF)
    at_out, at_shared, at_down = width, 2 * width, 2 * width + 2 * FF
    return (
        layer_out[None],
        input_grad[None],
        kv_weight_grad[:, 2 * width],
        jnp.concatenate([late_grad[:, :at_out], kv_weight_grad[:, : 2 * width]], axis=1),
        late_grad[:, at_out:at_shared],
        kv_weight_grad[:, 2 * width + 1],
        kv_weight_grad[:, 2 * width + 2 : 2 * width + 2 + n_experts],
        late_grad[:, at_shared:at_down],
        late_grad[:, at_down:].reshape(down_rows, width),
        gate_up_grad,
        down_grad,
    )


def solution(mesh):
    n_ctx, n_exp = mesh.shape["ctx"], mesh.shape["exp"]

    def layer(*args):
        n_experts = args[10].shape[0]
        nq = n_experts // n_exp
        nb = 2
        fine = Mesh(
            np.asarray(mesh.devices).reshape(nq, n_ctx // nq, n_exp // nb, nb), ("q", "r", "a", "b")
        )
        ctx, exp, every = ("q", "r"), ("a", "b"), ("q", "r", "a", "b")
        tokens, flat, rows = P(exp, ctx, None), P(every), P(every, None)
        run = jax.shard_map(
            functools.partial(body, n_experts),
            mesh=fine,
            in_specs=(
                tokens, tokens, tokens, flat, rows, rows, flat, rows, rows, rows, tokens, tokens,
            ),
            out_specs=(tokens, tokens, flat, rows, rows, flat, rows, rows, rows, tokens, tokens),
            check_vma=False,
        )
        return run(*args)

    return layer
```
